512 devices in a mesh: dp: 32 (over z, y_lo), fsdp: 16 (over y_hi, x, core).
Axes of the slice: x: 4, y: 8 (y_hi: 2, y_lo: 4; y = y_hi * 4 + y_lo), z: 8, core: 2. Of those that a mesh axis runs over, the one named last changes fastest.
Arguments:
- images: bfloat16 [65536, 1152], P(('dp', 'fsdp')), may hold values from -0.017944336 to 0.017944336
- pooled: bfloat16 [65536, 1152], P(('dp', 'fsdp')), may hold values from -0.0625 to 0.0625
- head_weight: bfloat16 [1152, 1152], P('fsdp'), may hold values from -0.1875 to 0.1875
- head_bias: float32 [1152], replicated, may hold values from -0.018 to 0.018
- log_scale: float32 [1], replicated, may hold values from 4.3 to 4.7
- bias: float32 [1], replicated, may hold values from -3 to -1
Outputs:
- row_loss: float32 [65536], P(('dp', 'fsdp'))
- image_grad: bfloat16 [65536, 1152], P(('dp', 'fsdp'))
- pooled_grad: bfloat16 [65536, 1152], P(('dp', 'fsdp'))
- head_grad: float32 [36864, 1152], P(('dp', 'fsdp'))
The draws below stay inside these ranges and needn't reach their ends.
All inputs are finite; a program needn't handle non-finite values.
Results may differ from the reference program's by a relative error of at most 0.025.
Values may be sent and summed in bfloat16 or wider, within the bound.
A program may use at most 64 MiB of HBM per device.

```python
import jax
import jax.numpy as jnp
from jax import lax

EMBED_WIDTH = 1152
PAIRS_PER_DEVICE = 128
STEPS = 4
TOKENS = 65536
N_DP = 32
N_FSDP = 16


def strengthened(values, stream_key, source, target, blocks, factor):
    def block_of(position):
        return (jnp.arange(values.shape[position]) // (values.shape[position] // blocks)).reshape((-1,) + (1,) * (values.ndim - 1 - position))

    one_side = jax.random.permutation(stream_key, blocks)[block_of(target)]
    far = (block_of(target) + blocks // 2) % blocks
    return jnp.where((block_of(source) == one_side) | (block_of(source) == far), factor * values, values)


def level_of(own_key, extent, cuts, smallest, largest):
    level = 1.0
    for position, blocks in cuts:
        heights = jax.random.uniform(jax.random.fold_in(jax.random.fold_in(own_key, 6), position), (blocks,), jnp.float32, smallest / len(cuts), largest / len(cuts))
        level = level * jnp.repeat(jnp.exp(heights), extent[position] // blocks).reshape((-1,) + (1,) * (len(extent) - 1 - position))
    return level


def noise(rng, shape, width, most, shards=(), kind=jnp.bfloat16):
    values = jax.random.normal(rng, shape, jnp.float32) * width
    if len(shards) > 0:
        values = level_of(rng, shape, shards, -0.22, 0.18) * values
    return jnp.clip(values, min=-most, max=most).astype(kind)


def gaussian_with(stream_key, extent, deviation, bound, pieces, heavy, kind=jnp.bfloat16):
    entries = deviation * jax.random.normal(stream_key, extent, jnp.float32)
    if pieces:
        entries = entries * level_of(stream_key, extent, pieces, -0.22, 0.18)
    return jnp.clip(strengthened(entries, jax.random.fold_in(stream_key, 3), *heavy), -bound, bound).astype(kind)


def setup_inputs(seed: int = 0) -> dict:
    keys = jax.random.split(jax.random.key(seed), 7)
    return {
        "images": noise(keys[0], (TOKENS, EMBED_WIDTH), 0.003, 0.017944336, ((0, 512),)),
        "pooled": gaussian_with(keys[1], (TOKENS, EMBED_WIDTH), 0.003, 0.0625, ((0, 512),), (0, 1, 128, 5.5)),
        "head_weight": noise(keys[2], (EMBED_WIDTH, EMBED_WIDTH), EMBED_WIDTH ** -0.5, 0.1875, ((0, 16),)),
        "head_bias": noise(keys[3], (EMBED_WIDTH,), 0.003, 0.018, (), jnp.float32),
        "log_scale": jnp.clip(jax.random.uniform(keys[4], (1,), jnp.float32, 4.3, 4.7), 4.3, 4.7),
        "bias": jnp.clip(jax.random.uniform(keys[5], (1,), jnp.float32, -3.0, -1.0), -3.0, -1.0),
    }


def normalize(v):
    total = lax.optimization_barrier(jnp.sum(v * v, axis=-1, keepdims=True))
    scale_r = lax.rsqrt(total + 1e-06)
    return (v * scale_r, scale_r)

def reference(images, pooled, head_weight, head_bias, log_scale, bias):
    temper = jnp.exp(log_scale[0])
    offset = bias[0]
    image_features, xr = normalize(images.astype(jnp.float32))
    normalized_image = image_features.astype(jnp.bfloat16)
    u_pre = jnp.dot(pooled, head_weight, preferred_element_type=jnp.float32) + head_bias
    ztxt, zr = normalize(u_pre)
    zhat = ztxt.astype(jnp.bfloat16)
    normalized_image_grouped = normalized_image.reshape(N_DP, N_FSDP, PAIRS_PER_DEVICE, EMBED_WIDTH).astype(jnp.float32)
    zh4 = zhat.reshape(N_DP, N_FSDP, PAIRS_PER_DEVICE, EMBED_WIDTH).astype(jnp.float32)
    eye_mask = jnp.eye(PAIRS_PER_DEVICE, dtype=bool)
    loss_sum = jnp.zeros((N_DP, N_FSDP, PAIRS_PER_DEVICE), jnp.float32)
    dx_sum = jnp.zeros((N_DP, N_FSDP, PAIRS_PER_DEVICE, EMBED_WIDTH), jnp.float32)
    dz_sum = jnp.zeros((N_DP, N_FSDP, PAIRS_PER_DEVICE, EMBED_WIDTH), jnp.float32)
    for step in range(STEPS):
        textk = jnp.roll(zh4, step, axis=0)
        cosine = jnp.einsum('abic,abjc->abij', normalized_image_grouped, textk)
        logits = temper * cosine + offset
        if step == 0:
            label = jnp.where(eye_mask, 1.0, -1.0).astype(jnp.float32)
        else:
            label = -jnp.ones((PAIRS_PER_DEVICE, PAIRS_PER_DEVICE), jnp.float32)
        loss_sum = loss_sum + lax.optimization_barrier(jnp.sum(jax.nn.softplus(-label * logits), axis=-1)) / PAIRS_PER_DEVICE
        bias_gradient = (-label * jax.nn.sigmoid(-label * logits) * temper / PAIRS_PER_DEVICE).astype(jnp.bfloat16).astype(jnp.float32)
        dx_sum = dx_sum + jnp.einsum('abij,abjc->abic', bias_gradient, textk)
        text_gradient_step = jnp.einsum('abij,abic->abjc', bias_gradient, normalized_image_grouped)
        dz_sum = dz_sum + jnp.roll(text_gradient_step, -step, axis=0)
    dx = dx_sum.reshape(TOKENS, EMBED_WIDTH)
    dz = dz_sum.reshape(TOKENS, EMBED_WIDTH)
    image_grad = (xr * (dx - image_features * lax.optimization_barrier(jnp.sum(image_features * dx, axis=-1, keepdims=True)))).astype(jnp.bfloat16)
    dzb = (zr * (dz - ztxt * lax.optimization_barrier(jnp.sum(ztxt * dz, axis=-1, keepdims=True)))).astype(jnp.bfloat16)
    pooled_grad = jnp.dot(dzb, head_weight.T, preferred_element_type=jnp.float32).astype(jnp.bfloat16)
    p4 = pooled.reshape(N_DP, N_FSDP, PAIRS_PER_DEVICE, EMBED_WIDTH)
    d4 = dzb.reshape(N_DP, N_FSDP, PAIRS_PER_DEVICE, EMBED_WIDTH)

    def group_sum(pair):
        pgroup, dgroup = pair
        terms = jnp.einsum('fbi,fbj->fij', pgroup.astype(jnp.float32), dgroup.astype(jnp.float32))
        rounded = lax.optimization_barrier(terms.astype(jnp.bfloat16))
        return lax.optimization_barrier(jnp.sum(rounded.astype(jnp.float32), axis=0))
    head_grad = lax.map(group_sum, (p4, d4)).reshape(N_DP * EMBED_WIDTH, EMBED_WIDTH)
    return (loss_sum.reshape(TOKENS), image_grad, pooled_grad, head_grad)
```

```python
import jax
import jax.numpy as jnp
from jax import lax
from jax.experimental import pallas as pl
from jax.experimental.pallas import tpu as pltpu
from jax.sharding import PartitionSpec as P

MESH = pl.DeviceIdType.MESH
F32 = jnp.float32
BF16 = jnp.bfloat16
NT = (((1,), (1,)), ((), ()))

ROWS = 128
WIDTH = 1152
SHARD = 72
CHIP = 144
UNIT = 80
PART = 64
AHEAD = 48
TILE = 384
ORDER = ((0, 2), (1, 2), (0, 1), (1, 1), (0, 3), (1, 3), (0, 0), (1, 0))


def normalize(v):
    r = lax.rsqrt(jnp.sum(v * v, axis=-1, keepdims=True) + 1e-06)
    return v * r, r


def kernel(
    img, pool, wsh, hb, log_scale, bias,
    loss_out, img_out, pool_out, head_out,
    wtmp, wf, xbuf, pbuf, xhat, ximg, zhat, ztxt, dz, dx, dzb, pt, ssum,
    tbuf, rbuf, stage, far, near, yout, yin,
    w_s, w_r, x_s, x_r, p_s, p_r, t_s, t_r, g_s, g_r,
):
    dp = lax.axis_index("dp")
    f = lax.axis_index("fsdp")
    j = lax.rem(dp, 4)
    yh = lax.div(f, 8)
    x = lax.rem(lax.div(f, 2), 4)
    c = lax.rem(f, 2)
    base = yh * 8 + c

    sib = (dp, f + 1 - 2 * c)
    xp = (dp, base + 2 * lax.rem(x + 1, 4))
    xm = (dp, base + 2 * lax.rem(x + 3, 4))
    zp = (lax.rem(dp + 4, 32), f)
    zm = (lax.rem(dp + 28, 32), f)
    wrap_up = lax.div(j + 1, 4)
    up = (dp + 1 - 4 * wrap_up, lax.rem(f + 8 * wrap_up, 16))
    wrap_dn = lax.div(3 - j, 3)
    dn = (dp - 1 + 4 * wrap_dn, lax.rem(f + 8 * wrap_dn, 16))
    opp = (dp, lax.rem(f + 8, 16))

    barrier = pltpu.get_barrier_semaphore()
    for who in (sib, xp, xm, zp, zm, up, dn, opp):
        pl.semaphore_signal(barrier, inc=1, device_id=who, device_id_type=MESH)
    pl.semaphore_wait(barrier, 8)

    def copy(src, dst, send, recv, who):
        return pltpu.make_async_remote_copy(
            src_ref=src, dst_ref=dst, send_sem=send, recv_sem=recv, device_id=who, device_id_type=MESH
        )

    def send_x(k, src):
        @pl.when(jnp.logical_and(k <= 3 - j, j >= 1))
        def _():
            copy(src, xbuf.at[k + 1], x_s.at[k], x_r.at[k + 1], dn).start()

        @pl.when(jnp.logical_and(k > 3 - j, j <= 2))
        def _():
            copy(src, xbuf.at[k - 1], x_s.at[k], x_r.at[k - 1], up).start()

    def send_p(k, src):
        @pl.when(jnp.logical_and(k <= j, j <= 2))
        def _():
            copy(src, pbuf.at[k + 1], p_s.at[k], p_r.at[k + 1], up).start()

        @pl.when(jnp.logical_and(k > j, j >= 1))
        def _():
            copy(src, pbuf.at[k - 1], p_s.at[k], p_r.at[k - 1], dn).start()

    def wait_x(k):
        copy(xbuf.at[k], xbuf.at[k], x_s.at[k], x_r.at[k], up).wait_recv()

    def wait_p(k):
        copy(pbuf.at[k], pbuf.at[k], p_s.at[k], p_r.at[k], up).wait_recv()

    def x_done(k, src):
        @pl.when(jnp.logical_or(jnp.logical_and(k <= 3 - j, j >= 1), jnp.logical_and(k > 3 - j, j <= 2)))
        def _():
            copy(src, xbuf.at[1], x_s.at[k], x_r.at[1], up).wait_send()

    def p_done(k, src):
        @pl.when(jnp.logical_or(jnp.logical_and(k <= j, j <= 2), jnp.logical_and(k > j, j >= 1)))
        def _():
            copy(src, pbuf.at[1], p_s.at[k], p_r.at[1], up).wait_send()

    xk0 = 1 + 2 * lax.div(j, 3)
    xk1 = 2 + lax.div(j, 2) - lax.div(j, 3)
    xk2 = 6 - xk0 - xk1
    pk0 = 1 + 2 * lax.div(3 - j, 3)
    pk1 = 2 + lax.rem(lax.div(j + 1, 2), 2)
    pk2 = 6 - pk0 - pk1

    w_swap = copy(wsh, wtmp, w_s.at[0], w_r.at[0], sib)
    w_swap.start()
    x_hop = copy(img, xbuf.at[4], x_s.at[5], x_r.at[4], zm)
    p_hop = copy(pool, pbuf.at[4], p_s.at[5], p_r.at[4], zp)

    @pl.when(j <= 2)
    def _():
        x_hop.start()

    send_x(0, img)

    @pl.when(j >= 1)
    def _():
        p_hop.start()

    send_p(0, pool)

    v, xr = normalize(img[...].astype(F32))
    ximg[...] = v
    xhat[...] = v.astype(BF16)

    def chip(h, off):
        return h * 4 + lax.rem(x + off, 4)

    def rows_of(m, start, size):
        return wf.at[pl.ds(pl.multiple_of(m * CHIP + start, 16), size), :]

    def unit(m):
        return rows_of(m, 64 * c, UNIT)

    def w_copy(src, dst, ident, who, send=None):
        return copy(src, dst, w_s.at[ident if send is None else send], w_r.at[ident], who)

    w_sent = []

    def w_go(src, ident, who):
        d = w_copy(src, src, ident, who)
        d.start()
        w_sent.append(d)

    mine = chip(yh, 0)
    theirs = chip(1 - yh, 0)
    w_swap.wait_recv()
    own_rows = wsh[...].astype(F32)
    sib_rows = wtmp[...].astype(F32)
    first = c == 0
    wf[pl.ds(pl.multiple_of(mine * CHIP, 16), CHIP), :] = jnp.concatenate(
        [jnp.where(first, own_rows, sib_rows), jnp.where(first, sib_rows, own_rows)], axis=0
    ).astype(BF16)

    w_edge_up = w_copy(unit(mine), unit(mine), 9, up)
    w_edge_dn = w_copy(unit(mine), unit(mine), 9, dn)
    w_pass_up = w_copy(unit(theirs), unit(theirs), 9, up, 10)
    w_pass_dn = w_copy(unit(theirs), unit(theirs), 9, dn, 10)

    @pl.when(j == 3)
    def _():
        w_edge_up.start()

    @pl.when(j == 0)
    def _():
        w_edge_dn.start()

    w_go(unit(mine), 1, xp)
    w_go(unit(mine), 2, xm)

    pt[...] = pool[...].astype(F32).T.astype(BF16)

    def to_sibling(m, ident):
        w_go(rows_of(m, 80 * c, PART), ident, sib)

    def near_units(r, h):
        for d, (off, onward) in enumerate(((3, xp), (1, xm))):
            m = chip(h, off)
            w_copy(unit(m), unit(m), 1 + 2 * r + d, xp).wait_recv()
            if d == 0:
                w_go(rows_of(m, 64 * c, AHEAD), 5 + 2 * r, onward)
            else:
                w_go(rows_of(m, 64 * c + AHEAD, UNIT - AHEAD), 6 + 2 * r, onward)
            to_sibling(m, 11 + 4 * r + d)

    def far_units(r, h):
        m = chip(h, 2)
        part = rows_of(m, 64 * c, AHEAD)
        w_copy(part, part, 5 + 2 * r, xp).wait_recv()
        part = rows_of(m, 64 * c + AHEAD, UNIT - AHEAD)
        w_copy(part, part, 6 + 2 * r, xp).wait_recv()
        to_sibling(m, 13 + 4 * r)

    other = w_copy(unit(theirs), unit(theirs), 9, xp)
    near_units(0, yh)

    outer = jnp.logical_or(j == 0, j == 3)
    inner = jnp.logical_and(j >= 1, j <= 2)

    @pl.when(outer)
    def _():
        other.wait_recv()

    @pl.when(j == 0)
    def _():
        w_pass_up.start()

    @pl.when(j == 3)
    def _():
        w_pass_dn.start()

    @pl.when(j <= 2)
    def _():
        wait_x(1)
        send_x(1, xbuf.at[1])
        wait_x(4)
        send_x(4, xbuf.at[4])

    far_units(0, yh)

    @pl.when(inner)
    def _():
        other.wait_recv()

    w_go(unit(theirs), 3, xp)
    w_go(unit(theirs), 4, xm)
    to_sibling(theirs, 14)

    @pl.when(j <= 2)
    def _():
        wait_x(xk1)
        send_x(xk1, xbuf.at[xk1])

    @pl.when(j >= 1)
    def _():
        wait_p(4)
        send_p(4, pbuf.at[4])

    near_units(1, 1 - yh)
    far_units(1, 1 - yh)

    @pl.when(inner)
    def _():
        wait_x(xk2)
        send_x(xk2, xbuf.at[xk2])

    @pl.when(j >= 1)
    def _():
        wait_p(1)
        send_p(1, pbuf.at[1])

    for ident, m in (
        (11, chip(yh, 3)), (12, chip(yh, 1)), (13, chip(yh, 2)), (14, theirs),
        (15, chip(1 - yh, 3)), (16, chip(1 - yh, 1)), (17, chip(1 - yh, 2)),
    ):
        got = rows_of(m, 80 - 80 * c, PART)
        w_copy(got, got, ident, sib).wait_recv()

    temper = jnp.exp(jnp.full((1, 128), log_scale[0], F32))
    offset = jnp.full((1, 128), bias[0], F32)
    gain = temper * (1.0 / ROWS)
    eye = lax.broadcasted_iota(jnp.int32, (ROWS, ROWS), 0) == lax.broadcasted_iota(jnp.int32, (ROWS, ROWS), 1)

    def project(block, out):
        @pl.loop(0, WIDTH // TILE)
        def _(n):
            cols = pl.ds(pl.multiple_of(n * TILE, TILE), TILE)
            out[:, cols] = jnp.dot(block[...], wf[:, cols], preferred_element_type=F32) + hb[:, cols]

    def weights(a, b, own):
        l = temper * lax.dot_general(a, b, NT, preferred_element_type=F32) + offset
        m = jnp.where(eye, -l, l) if own else l
        g = gain / (1.0 + jnp.exp(-m))
        if own:
            g = jnp.where(eye, -g, g)
        return m, g.astype(BF16)

    def softplus(m):
        return jnp.maximum(m, 0.0) + jnp.log1p(jnp.exp(-jnp.abs(m)))

    project(pool, ztxt)
    v, zr = normalize(ztxt[...])
    ztxt[...] = v
    zhat[...] = v.astype(BF16)

    _, g = weights(zhat[...], xhat[...], True)
    dz[...] = jnp.dot(g, xhat[...], preferred_element_type=F32)
    for i, k in enumerate((xk0, xk1, xk2)):
        @pl.when(outer if i == 2 else j == 3)
        def _():
            wait_x(k)

        xh = normalize(xbuf[k].astype(F32))[0].astype(BF16)
        _, g = weights(zhat[...], xh, False)
        dz[...] += jnp.dot(g, xh, preferred_element_type=F32)

    v = ztxt[...]
    d = dz[...]
    dzb[...] = (zr * (d - v * jnp.sum(v * d, axis=-1, keepdims=True))).astype(BF16)

    for i, (h, off) in enumerate(ORDER):
        m = chip(h, off)
        t = jnp.dot(
            pt[pl.ds(pl.multiple_of(m * CHIP, 16), CHIP), :], dzb[...], preferred_element_type=F32
        ).astype(BF16).astype(F32)
        tbuf[0, i] = t[:SHARD].astype(BF16)
        tbuf[1, i] = t[SHARD:].astype(BF16)
        copy(tbuf.at[1 - c, i], rbuf.at[i], t_s.at[i], t_r.at[i], sib).start()

    @pl.when(inner)
    def _():
        wait_p(pk1)
        send_p(pk1, pbuf.at[pk1])

    def pair_sum(i):
        copy(rbuf.at[i], rbuf.at[i], t_s.at[i], t_r.at[i], sib).wait_recv()
        return tbuf[c, i].astype(F32) + rbuf[i].astype(F32)

    g_sent = []

    def g_go(value, ident, dst, who):
        stage[ident] = value.astype(BF16)
        d = copy(stage.at[ident], dst, g_s.at[ident], g_r.at[ident], who)
        d.start()
        g_sent.append(d)

    def g_wait(ref, ident):
        copy(ref, ref, g_s.at[ident], g_r.at[ident], xp).wait_recv()
        return ref[...].astype(F32)

    g_go(pair_sum(0), 0, far.at[0], xp)
    g_go(pair_sum(1), 1, far.at[1], xm)
    g_go(pair_sum(3), 2, near.at[0, 1], xp)
    g_go(pair_sum(4), 3, near.at[1, 0], xm)
    g_go(pair_sum(2) + g_wait(far.at[0], 0), 4, near.at[0, 0], xp)
    g_go(pair_sum(5) + g_wait(far.at[1], 1), 5, near.at[1, 1], xm)

    @pl.when(inner)
    def _():
        wait_p(pk2)
        send_p(pk2, pbuf.at[pk2])

    m, g = weights(xhat[...], zhat[...], True)
    ssum[...] = softplus(m)
    dx[...] = jnp.dot(g, zhat[...], preferred_element_type=F32)

    def text(k, u):
        project(pbuf.at[k], u)
        zh = normalize(u[...])[0].astype(BF16)
        m, g = weights(xhat[...], zh, False)
        ssum[...] += softplus(m)
        dx[...] += jnp.dot(g, zh, preferred_element_type=F32)

    @pl.when(j == 0)
    def _():
        wait_p(pk0)

    text(pk0, dz)

    @pl.loop(0, WIDTH // TILE)
    def _(n):
        cols = pl.ds(pl.multiple_of(n * TILE, TILE), TILE)
        pool_out[:, cols] = lax.dot_general(
            dzb[...], wf[cols, :], NT, preferred_element_type=F32
        ).astype(BF16)

    total = []
    for h in range(2):
        total.append(pair_sum(6 + h) + g_wait(near.at[0, h], 4 - 2 * h) + g_wait(near.at[1, h], 3 + 2 * h))
    low = yh == 0
    yout[...] = jnp.where(low, total[1], total[0]).astype(BF16)
    head_out[...] = jnp.where(low, total[0], total[1])
    y_copy = copy(yout, yin, g_s.at[6], g_r.at[6], opp)
    y_copy.start()

    for k in (pk1, pk2):
        @pl.when(outer)
        def _():
            wait_p(k)

        text(k, dz)

    loss_out[...] = jnp.sum(ssum[...].T, axis=0, keepdims=True) * (1.0 / ROWS)
    v = ximg[...]
    d = dx[...]
    img_out[...] = (xr * (d - v * jnp.sum(v * d, axis=-1, keepdims=True))).astype(BF16)

    y_copy.wait_recv()
    head_out[...] += yin[...].astype(F32)

    w_swap.wait_send()
    for d in w_sent:
        d.wait_send()

    @pl.when(j == 3)
    def _():
        w_edge_up.wait_send()
        w_pass_dn.wait_send()

    @pl.when(j == 0)
    def _():
        w_edge_dn.wait_send()
        w_pass_up.wait_send()

    @pl.when(j <= 2)
    def _():
        x_hop.wait_send()

    @pl.when(j >= 1)
    def _():
        p_hop.wait_send()

    x_done(0, img)
    p_done(0, pool)
    for k in range(1, 4):
        x_done(k, xbuf.at[k])
        p_done(k, pbuf.at[k])
    x_done(4, xbuf.at[4])
    p_done(4, pbuf.at[4])
    for i in range(8):
        copy(tbuf.at[1 - c, i], rbuf.at[i], t_s.at[i], t_r.at[i], sib).wait_send()
    for d in g_sent:
        d.wait_send()
    y_copy.wait_send()


def per_device(images, pooled, head_weight, head_bias, log_scale, bias):
    vmem = pl.BlockSpec(memory_space=pltpu.VMEM)
    smem = pl.BlockSpec(memory_space=pltpu.SMEM)
    block = (ROWS, WIDTH)
    slab = (SHARD, WIDTH)
    dma = pltpu.SemaphoreType.DMA
    loss, image_grad, pooled_grad, head_grad = pl.pallas_call(
        kernel,
        out_shape=(
            jax.ShapeDtypeStruct((1, ROWS), F32),
            jax.ShapeDtypeStruct(block, BF16),
            jax.ShapeDtypeStruct(block, BF16),
            jax.ShapeDtypeStruct(slab, F32),
        ),
        in_specs=[vmem, vmem, vmem, vmem, smem, smem],
        out_specs=(vmem, vmem, vmem, vmem),
        scratch_shapes=[
            pltpu.VMEM(slab, BF16),
            pltpu.VMEM((WIDTH, WIDTH), BF16),
            pltpu.VMEM((5,) + block, BF16),
            pltpu.VMEM((5,) + block, BF16),
            pltpu.VMEM(block, BF16),
            pltpu.VMEM(block, F32),
            pltpu.VMEM(block, BF16),
            pltpu.VMEM(block, F32),
            pltpu.VMEM(block, F32),
            pltpu.VMEM(block, F32),
            pltpu.VMEM(block, BF16),
            pltpu.VMEM((WIDTH, ROWS), BF16),
            pltpu.VMEM((ROWS, ROWS), F32),
            pltpu.VMEM((2, 8) + slab, BF16),
            pltpu.VMEM((8,) + slab, BF16),
            pltpu.VMEM((6,) + slab, BF16),
            pltpu.VMEM((2,) + slab, BF16),
            pltpu.VMEM((2, 2) + slab, BF16),
            pltpu.VMEM(slab, BF16),
            pltpu.VMEM(slab, BF16),
            dma((18,)), dma((18,)),
            dma((6,)), dma((6,)),
            dma((6,)), dma((6,)),
            dma((8,)), dma((8,)),
            dma((7,)), dma((7,)),
        ],
        compiler_params=pltpu.CompilerParams(
            collective_id=0, has_side_effects=True, vmem_limit_bytes=40 * 1024 * 1024
        ),
        cost_estimate=pl.CostEstimate(flops=4_000_000_000, bytes_accessed=6_000_000, transcendentals=300_000),
    )(images, pooled, head_weight, head_bias.reshape(1, WIDTH), log_scale, bias)
    return loss.reshape(ROWS), image_grad, pooled_grad, head_grad


def solution(mesh):
    in_specs = (P(("dp", "fsdp"), None), P(("dp", "fsdp"), None), P("fsdp", None), P(), P(), P())
    out_specs = (
        P(("dp", "fsdp")),
        P(("dp", "fsdp"), None),
        P(("dp", "fsdp"), None),
        P(("dp", "fsdp"), None),
    )
    return jax.shard_map(
        per_device, mesh=mesh, in_specs=in_specs, out_specs=out_specs, check_vma=False
    )
```

```python
import jax
import jax.numpy as jnp
from jax import lax
from jax.experimental import pallas as pl
from jax.experimental.pallas import tpu as pltpu
from jax.sharding import PartitionSpec as P

MESH = pl.DeviceIdType.MESH
F32 = jnp.float32
BF16 = jnp.bfloat16
NT = (((1,), (1,)), ((), ()))

ROWS = 128
WIDTH = 1152
SHARD = 72
CHIP = 144
UNIT = 80
PART = 64
AHEAD = 48
TILE = 384
VMEM_GRANT = 60 * 1024 * 1024
HALF = 64
SPLIT = 640
ORDER = (2, 1, 3, 0)


def normalize(v):
    r = lax.rsqrt(jnp.sum(v * v, axis=-1, keepdims=True) + 1e-06)
    return v * r, r


def kernel(
    img_hbm, pool_hbm, wsh_hbm, hb_hbm, log_scale, bias,
    loss_hbm, img_grad_hbm, pool_grad_hbm, head_grad_hbm,
    img, pool, wsh, hb, loss_out, img_out, pool_out, head_out,
    wtmp, wf, xbuf, pbuf, xhat, ximg, zhat, ztxt, dz, dx, dzb, pt, ssum,
    t_a, t_b, r_a, r_b, st_a, st_b, far_a, far_b, near_a, near_b,
    y_a, y_b, pass_a, pass_b, in_a, in_b,
    xg, gdx, gsum, gdx_out, gsum_out, gdx_in, gsum_in,
    l_s, o_s, w_s, w_r, x_s, x_r, p_s, p_r, t_s, t_r, g_s, g_r, h_s, h_r,
):
    loads = [
        pltpu.make_async_copy(src, dst, l_s.at[i])
        for i, (src, dst) in enumerate(
            ((wsh_hbm, wsh), (img_hbm, img), (pool_hbm, pool), (hb_hbm, hb.at[0]))
        )
    ]
    for d in loads:
        d.start()
    stores = [
        pltpu.make_async_copy(src, dst, o_s.at[i])
        for i, (src, dst) in enumerate(
            ((loss_out, loss_hbm), (img_out, img_grad_hbm), (pool_out, pool_grad_hbm), (head_out, head_grad_hbm))
        )
    ]

    dp = lax.axis_index("dp")
    f = lax.axis_index("fsdp")
    j = lax.rem(dp, 4)
    yh = lax.div(f, 8)
    x = lax.rem(lax.div(f, 2), 4)
    c = lax.rem(f, 2)
    base = yh * 8 + c

    sib = (dp, f + 1 - 2 * c)
    xp = (dp, base + 2 * lax.rem(x + 1, 4))
    xm = (dp, base + 2 * lax.rem(x + 3, 4))
    zp = (lax.rem(dp + 4, 32), f)
    zm = (lax.rem(dp + 28, 32), f)
    wrap_up = lax.div(j + 1, 4)
    up = (dp + 1 - 4 * wrap_up, lax.rem(f + 8 * wrap_up, 16))
    wrap_dn = lax.div(3 - j, 3)
    dn = (dp - 1 + 4 * wrap_dn, lax.rem(f + 8 * wrap_dn, 16))
    wrap = lax.div(j + 2, 4)
    up2 = (dp + 2 - 4 * wrap, lax.rem(f + 8 * wrap, 16))
    wrap = lax.div(3 - j, 2)
    dn2 = (dp - 2 + 4 * wrap, lax.rem(f + 8 * wrap, 16))

    barrier = pltpu.get_barrier_semaphore()
    for who in (sib, xp, xm, zp, zm, up, dn, up2, dn2):
        pl.semaphore_signal(barrier, inc=1, device_id=who, device_id_type=MESH)
    pl.semaphore_wait(barrier, 9)
    for d in loads:
        d.wait()

    def copy(src, dst, send, recv, who):
        return pltpu.make_async_remote_copy(
            src_ref=src, dst_ref=dst, send_sem=send, recv_sem=recv, device_id=who, device_id_type=MESH
        )

    def part(ref, h):
        return ref.at[pl.ds(HALF * h, HALF), :]

    def send_x(k, src, h):
        @pl.when(jnp.logical_and(k <= 3 - j, j >= 1))
        def _():
            copy(part(src, h), part(xbuf.at[k + 1], h), x_s.at[k, h], x_r.at[k + 1, h], dn).start()

        @pl.when(jnp.logical_and(k > 3 - j, j <= 2))
        def _():
            copy(part(src, h), part(xbuf.at[k - 1], h), x_s.at[k, h], x_r.at[k - 1, h], up).start()

    def send_p(k, src, h):
        @pl.when(jnp.logical_and(k <= j, j <= 1))
        def _():
            copy(part(src, h), part(pbuf.at[k + 1], h), p_s.at[k, h], p_r.at[k + 1, h], up).start()

        @pl.when(jnp.logical_and(k > j, j >= 2))
        def _():
            copy(part(src, h), part(pbuf.at[k - 1], h), p_s.at[k, h], p_r.at[k - 1, h], dn).start()

    def wait_x(k, h, whole=False):
        dst = xbuf.at[k] if whole else part(xbuf.at[k], h)
        copy(dst, dst, x_s.at[k, h], x_r.at[k, h], up).wait_recv()

    def wait_p(k, h):
        dst = part(pbuf.at[k], h)
        copy(dst, dst, p_s.at[k, h], p_r.at[k, h], up).wait_recv()

    def pass_x(k, h):
        wait_x(k, h)
        send_x(k, xbuf.at[k], h)

    def pass_p(k):
        for h in range(2):
            wait_p(k, h)
            send_p(k, pbuf.at[k], h)

    def x_done(k, src):
        @pl.when(jnp.logical_or(jnp.logical_and(k <= 3 - j, j >= 1), jnp.logical_and(k > 3 - j, j <= 2)))
        def _():
            for h in range(2):
                copy(part(src, h), part(xbuf.at[1], h), x_s.at[k, h], x_r.at[1, h], up).wait_send()

    def p_done(k, src):
        @pl.when(jnp.logical_or(jnp.logical_and(k <= j, j <= 1), jnp.logical_and(k > j, j >= 2)))
        def _():
            for h in range(2):
                copy(part(src, h), part(pbuf.at[1], h), p_s.at[k, h], p_r.at[1, h], up).wait_send()

    middle = lax.rem(lax.div(j + 1, 2), 2)
    outer = middle == 0
    inner = middle == 1
    xk0 = 1 + 2 * lax.div(j, 3)
    xk1 = 2 + middle
    xk2 = 6 - xk0 - xk1
    guest = copy(img, xbuf.at[5], x_s.at[6, 0], x_r.at[5, 0], up)

    w_swap = copy(wsh, wtmp, w_s.at[0], w_r.at[0], sib)
    w_swap.start()
    x_hop = [copy(part(img, h), part(xbuf.at[4], h), x_s.at[5, h], x_r.at[4, h], zm) for h in range(2)]
    p_hop = [copy(part(pool, h), part(pbuf.at[4], h), p_s.at[5, h], p_r.at[4, h], zp) for h in range(2)]

    @pl.when(j <= 2)
    def _():
        for d in x_hop:
            d.start()

    send_x(0, img, 0)
    send_x(0, img, 1)
    send_p(0, pool, 0)

    @pl.when(j >= 1)
    def _():
        for d in p_hop:
            d.start()

    v, xr = normalize(img[...].astype(F32))
    ximg[...] = v
    xhat[...] = v.astype(BF16)

    def chip(h, off):
        return h * 4 + lax.rem(x + off, 4)

    def rows_of(m, start, size):
        return wf.at[pl.ds(pl.multiple_of(m * CHIP + start, 16), size), :]

    def unit(m):
        return rows_of(m, 64 * c, UNIT)

    def w_copy(src, dst, ident, who, send=None):
        return copy(src, dst, w_s.at[ident if send is None else send], w_r.at[ident], who)

    w_sent = []

    def w_go(src, ident, who):
        d = w_copy(src, src, ident, who)
        d.start()
        w_sent.append(d)

    mine = chip(yh, 0)
    theirs = chip(1 - yh, 0)
    w_swap.wait_recv()
    own_rows = wsh[...].astype(F32)
    sib_rows = wtmp[...].astype(F32)
    first = c == 0
    wf[pl.ds(pl.multiple_of(mine * CHIP, 16), CHIP), :] = jnp.concatenate(
        [jnp.where(first, own_rows, sib_rows), jnp.where(first, sib_rows, own_rows)], axis=0
    ).astype(BF16)

    w_edge_up = w_copy(unit(mine), unit(mine), 9, up)
    w_edge_dn = w_copy(unit(mine), unit(mine), 9, dn)
    w_pass_up = w_copy(unit(theirs), unit(theirs), 9, up, 10)
    w_pass_dn = w_copy(unit(theirs), unit(theirs), 9, dn, 10)

    @pl.when(j == 3)
    def _():
        w_edge_up.start()

    @pl.when(j == 0)
    def _():
        w_edge_dn.start()

    w_go(unit(mine), 1, xp)
    w_go(unit(mine), 2, xm)

    pt[...] = pool[...].astype(F32).T.astype(BF16)

    def to_sibling(m, ident):
        w_go(rows_of(m, 80 * c, PART), ident, sib)

    def near_units(r, h):
        for d, (off, onward) in enumerate(((3, xp), (1, xm))):
            m = chip(h, off)
            w_copy(unit(m), unit(m), 1 + 2 * r + d, xp).wait_recv()
            if d == 0:
                w_go(rows_of(m, 64 * c, AHEAD), 5 + 2 * r, onward)
            else:
                w_go(rows_of(m, 64 * c + AHEAD, UNIT - AHEAD), 6 + 2 * r, onward)
            to_sibling(m, 11 + 4 * r + d)

    def far_units(r, h):
        m = chip(h, 2)
        part = rows_of(m, 64 * c, AHEAD)
        w_copy(part, part, 5 + 2 * r, xp).wait_recv()
        part = rows_of(m, 64 * c + AHEAD, UNIT - AHEAD)
        w_copy(part, part, 6 + 2 * r, xp).wait_recv()
        to_sibling(m, 13 + 4 * r)

    other = w_copy(unit(theirs), unit(theirs), 9, xp)
    theirs_xp = w_copy(unit(theirs), unit(theirs), 3, xp)
    theirs_xm = w_copy(unit(theirs), unit(theirs), 4, xm)
    theirs_part = rows_of(theirs, 80 * c, PART)
    theirs_sib = w_copy(theirs_part, theirs_part, 14, sib)
    w_sent.extend((theirs_xp, theirs_xm, theirs_sib))

    def send_theirs():
        theirs_xp.start()
        theirs_xm.start()
        theirs_sib.start()

    for h in range(2):
        @pl.when(j <= 2)
        def _():
            pass_x(4, h)

        @pl.when(inner)
        def _():
            pass_x(1, h)

    near_units(0, yh)

    @pl.when(outer)
    def _():
        other.wait_recv()

    @pl.when(j == 0)
    def _():
        w_pass_up.start()

    @pl.when(j == 3)
    def _():
        w_pass_dn.start()

    @pl.when(outer)
    def _():
        send_theirs()

    @pl.when(inner)
    def _():
        pass_x(3, 0)

    @pl.when(j == 0)
    def _():
        send_p(0, pool, 1)
        guest.start()

    @pl.when(j == 3)
    def _():
        pass_p(4)

    far_units(0, yh)

    @pl.when(inner)
    def _():
        pass_x(3, 1)
        other.wait_recv()
        send_theirs()
        pass_x(2, 0)

    near_units(1, 1 - yh)

    @pl.when(inner)
    def _():
        pass_x(2, 1)

    @pl.when(j == 1)
    def _():
        send_p(0, pool, 1)
        pass_p(1)

    @pl.when(j == 2)
    def _():
        pass_p(4)

    far_units(1, 1 - yh)

    @pl.when(j == 2)
    def _():
        pass_p(3)

    for ident, m in (
        (11, chip(yh, 3)), (12, chip(yh, 1)), (13, chip(yh, 2)), (14, theirs),
        (15, chip(1 - yh, 3)), (16, chip(1 - yh, 1)), (17, chip(1 - yh, 2)),
    ):
        got = rows_of(m, 80 - 80 * c, PART)
        w_copy(got, got, ident, sib).wait_recv()

    temper = jnp.exp(jnp.full((1, 128), log_scale[0], F32))
    offset = jnp.full((1, 128), bias[0], F32)
    gain = temper * (1.0 / ROWS)
    eye = lax.broadcasted_iota(jnp.int32, (ROWS, ROWS), 0) == lax.broadcasted_iota(jnp.int32, (ROWS, ROWS), 1)

    def project(block, out):
        @pl.loop(0, WIDTH // TILE)
        def _(n):
            cols = pl.ds(pl.multiple_of(n * TILE, TILE), TILE)
            out[:, cols] = jnp.dot(block[...], wf[:, cols], preferred_element_type=F32) + hb[:, cols]

    def weights(a, b, own):
        l = temper * lax.dot_general(a, b, NT, preferred_element_type=F32) + offset
        m = jnp.where(eye, -l, l) if own else l
        g = gain / (1.0 + jnp.exp(-m))
        if own:
            g = jnp.where(eye, -g, g)
        return m, g.astype(BF16)

    def softplus(m):
        return jnp.maximum(m, 0.0) + jnp.log1p(jnp.exp(-jnp.abs(m)))

    project(pool, ztxt)
    v, zr = normalize(ztxt[...])
    ztxt[...] = v
    zhat[...] = v.astype(BF16)

    _, g = weights(zhat[...], xhat[...], True)
    dz[...] = jnp.dot(g, xhat[...], preferred_element_type=F32)
    for i, k in enumerate((xk0, xk1, xk2)):
        @pl.when(outer)
        def _():
            wait_x(k, 0)
            wait_x(k, 1)

        xh = normalize(xbuf[k].astype(F32))[0].astype(BF16)
        _, g = weights(zhat[...], xh, False)
        dz[...] += jnp.dot(g, xh, preferred_element_type=F32)

    v = ztxt[...]
    d = dz[...]
    dzb[...] = (zr * (d - v * jnp.sum(v * d, axis=-1, keepdims=True))).astype(BF16)

    def term(n):
        m = chip(1 - yh if n < 4 else yh, ORDER[n % 4])
        t = jnp.dot(
            pt[pl.ds(pl.multiple_of(m * CHIP, 16), CHIP), :], dzb[...], preferred_element_type=F32
        )
        for o, u in enumerate((t[:SHARD].astype(BF16), t[SHARD:].astype(BF16))):
            t_a[o, n] = u[:, :SPLIT]
            t_b[o, n] = u[:, SPLIT:]
        copy(t_a.at[1 - c, n], r_a.at[n], t_s.at[0, n], t_r.at[0, n], sib).start()
        copy(t_b.at[1 - c, n], r_b.at[n], t_s.at[1, n], t_r.at[1, n], sib).start()

    def pair_a(n):
        copy(r_a.at[n], r_a.at[n], t_s.at[0, n], t_r.at[0, n], sib).wait_recv()
        return t_a[c, n].astype(F32) + r_a[n].astype(F32)

    def pair_b(n):
        copy(r_b.at[n], r_b.at[n], t_s.at[1, n], t_r.at[1, n], sib).wait_recv()
        return t_b[c, n].astype(F32) + r_b[n].astype(F32)

    g_sent = []

    def g_go(src, value, ident, dst, who):
        src[...] = value.astype(BF16)
        d = copy(src, dst, g_s.at[ident], g_r.at[ident], who)
        d.start()
        g_sent.append(d)

    def g_wait(ref, ident):
        copy(ref, ref, g_s.at[ident], g_r.at[ident], xp).wait_recv()
        return ref[...].astype(F32)

    def first_sends(g):
        n = 4 * g
        g_go(st_a.at[g, 0], pair_a(n), 6 * g, far_a.at[g], xp)
        g_go(st_b.at[g, 0], pair_b(n), 6 * g + 1, far_b.at[g], xm)
        g_go(st_b.at[g, 1], pair_b(n + 1), 6 * g + 2, near_b.at[g, 0], xp)
        g_go(st_a.at[g, 1], pair_a(n + 2), 6 * g + 3, near_a.at[g, 1], xm)

    def second_sends(g):
        n = 4 * g
        g_go(st_a.at[g, 2], pair_a(n + 1) + g_wait(far_a.at[g], 6 * g), 6 * g + 4, near_a.at[g, 0], xp)
        g_go(st_b.at[g, 2], pair_b(n + 2) + g_wait(far_b.at[g], 6 * g + 1), 6 * g + 5, near_b.at[g, 1], xm)

    def sums(g):
        n = 4 * g + 3
        a = pair_a(n) + g_wait(near_a.at[g, 0], 6 * g + 4) + g_wait(near_a.at[g, 1], 6 * g + 3)
        b = pair_b(n) + g_wait(near_b.at[g, 0], 6 * g + 2) + g_wait(near_b.at[g, 1], 6 * g + 5)
        return a, b

    def host(zh, add):
        m, g = weights(xg[...], zh, False)
        if add:
            gsum[...] += softplus(m)
            gdx[...] += jnp.dot(g, zh, preferred_element_type=F32)
        else:
            gsum[...] = softplus(m)
            gdx[...] = jnp.dot(g, zh, preferred_element_type=F32)

    def text(k):
        project(pbuf.at[k], dz)
        return normalize(dz[...])[0].astype(BF16)

    def own_text(zh):
        m, g = weights(xhat[...], zh, False)
        ssum[...] += softplus(m)
        dx[...] += jnp.dot(g, zh, preferred_element_type=F32)

    def back():
        @pl.loop(0, WIDTH // TILE)
        def _(n):
            cols = pl.ds(pl.multiple_of(n * TILE, TILE), TILE)
            pool_out[:, cols] = lax.dot_general(
                dzb[...], wf[cols, :], NT, preferred_element_type=F32
            ).astype(BF16)

        stores[2].start()

    gdx_up = copy(gdx_out, gdx_in, h_s.at[0], h_r.at[0], up)
    gdx_dn = copy(gdx_out, gdx_in, h_s.at[0], h_r.at[0], dn)
    gsum_up = copy(gsum_out, gsum_in, h_s.at[1], h_r.at[1], up)
    gsum_dn = copy(gsum_out, gsum_in, h_s.at[1], h_r.at[1], dn)

    for n in range(3):
        term(n)
    first_sends(0)
    for n in range(3, 7):
        term(n)

    m, g = weights(xhat[...], zhat[...], True)
    ssum[...] = softplus(m)
    dx[...] = jnp.dot(g, zhat[...], preferred_element_type=F32)

    @pl.when(j == 1)
    def _():
        wait_p(4, 0)
        wait_p(4, 1)
        wait_x(5, 0, whole=True)

    @pl.when(inner)
    def _():
        xg[...] = normalize(xbuf[9 - 4 * j].astype(F32))[0].astype(BF16)

    @pl.when(j == 1)
    def _():
        host(text(4), False)

    @pl.when(j == 2)
    def _():
        host(zhat[...], False)

    second_sends(0)
    first_sends(1)
    term(7)

    @pl.when(j == 2)
    def _():
        wait_p(1, 0)
        wait_p(1, 1)

    @pl.when(inner)
    def _():
        zh = text(1)
        own_text(zh)

        @pl.when(j == 2)
        def _():
            host(zh, True)

    second_sends(1)

    @pl.when(j == 1)
    def _():
        wait_p(3, 0)
        wait_p(3, 1)

    @pl.when(inner)
    def _():
        zh = text(3)
        own_text(zh)

        @pl.when(j == 1)
        def _():
            host(zh, True)

    a, b = sums(0)
    g_go(y_a, a, 12, pass_a, up2)
    g_go(y_b, b, 13, pass_b, dn2)

    @pl.when(inner)
    def _():
        wait_p(2, 0)
        wait_p(2, 1)
        zh = text(2)
        host(zh, True)
        gdx_out[...] = gdx[...].astype(BF16)
        gsum_out[...] = jnp.sum(gsum[...].T, axis=0, keepdims=True)

        @pl.when(j == 1)
        def _():
            gdx_dn.start()
            gsum_dn.start()

        @pl.when(j == 2)
        def _():
            gdx_up.start()
            gsum_up.start()

        own_text(zh)

    @pl.when(outer)
    def _():
        back()

    a, b = sums(1)
    head_out[:, :SPLIT] = a
    head_out[:, SPLIT:] = b

    onward = []
    for ref, ident, dst, who in ((pass_a, 12, in_a, up2), (pass_b, 13, in_b, dn2)):
        copy(ref, ref, g_s.at[ident], g_r.at[ident], xp).wait_recv()
        d = copy(ref, dst, g_s.at[ident + 2], g_r.at[ident + 2], who)
        d.start()
        onward.append(d)

    @pl.when(inner)
    def _():
        back()

    @pl.when(outer)
    def _():
        gdx_up.wait_recv()
        gsum_up.wait_recv()
        dx[...] += gdx_in[...].astype(F32)
        loss_out[...] = (jnp.sum(ssum[...].T, axis=0, keepdims=True) + gsum_in[...]) * (1.0 / ROWS)

    @pl.when(inner)
    def _():
        loss_out[...] = jnp.sum(ssum[...].T, axis=0, keepdims=True) * (1.0 / ROWS)

    stores[0].start()
    v = ximg[...]
    d = dx[...]
    img_out[...] = (xr * (d - v * jnp.sum(v * d, axis=-1, keepdims=True))).astype(BF16)
    stores[1].start()

    head_out[:, :SPLIT] += g_wait(in_a, 14)
    head_out[:, SPLIT:] += g_wait(in_b, 15)
    stores[3].start()

    w_swap.wait_send()
    for d in w_sent:
        d.wait_send()

    @pl.when(j == 3)
    def _():
        w_edge_up.wait_send()
        w_pass_dn.wait_send()

    @pl.when(j == 0)
    def _():
        w_edge_dn.wait_send()
        w_pass_up.wait_send()

    @pl.when(j <= 2)
    def _():
        for d in x_hop:
            d.wait_send()

    @pl.when(j >= 1)
    def _():
        for d in p_hop:
            d.wait_send()

    @pl.when(j == 0)
    def _():
        guest.wait_send()

    @pl.when(inner)
    def _():
        gdx_up.wait_send()
        gsum_up.wait_send()

    x_done(0, img)
    p_done(0, pool)
    for k in range(1, 4):
        x_done(k, xbuf.at[k])
        p_done(k, pbuf.at[k])
    x_done(4, xbuf.at[4])
    p_done(4, pbuf.at[4])
    for n in range(8):
        copy(t_a.at[1 - c, n], r_a.at[n], t_s.at[0, n], t_r.at[0, n], sib).wait_send()
        copy(t_b.at[1 - c, n], r_b.at[n], t_s.at[1, n], t_r.at[1, n], sib).wait_send()
    for d in g_sent + onward:
        d.wait_send()
    for d in stores:
        d.wait()


def finish(*refs):
    into, out = refs[12], refs[13]
    loads = [pltpu.make_async_copy(refs[i], refs[8 + i], into.at[i]) for i in range(4)]
    stores = [pltpu.make_async_copy(refs[8 + i], refs[4 + i], out.at[i]) for i in range(4)]
    for d in loads:
        d.start()
    for d, e in zip(loads, stores):
        d.wait()
        e.start()
    for e in stores:
        e.wait()


def per_device(images, pooled, head_weight, head_bias, log_scale, bias):
    smem = pl.BlockSpec(memory_space=pltpu.SMEM)
    hbm = pl.BlockSpec(memory_space=pltpu.HBM)
    block = (ROWS, WIDTH)
    slab = (SHARD, WIDTH)
    slab_a = (SHARD, SPLIT)
    slab_b = (SHARD, WIDTH - SPLIT)
    dma = pltpu.SemaphoreType.DMA
    results = (
        jax.ShapeDtypeStruct((1, ROWS), F32),
        jax.ShapeDtypeStruct(block, BF16),
        jax.ShapeDtypeStruct(block, BF16),
        jax.ShapeDtypeStruct(slab, F32),
    )
    made = pl.pallas_call(
        kernel,
        out_shape=results,
        in_specs=[hbm, hbm, hbm, hbm, smem, smem],
        out_specs=(hbm, hbm, hbm, hbm),
        scratch_shapes=[
            pltpu.VMEM(block, BF16),
            pltpu.VMEM(block, BF16),
            pltpu.VMEM(slab, BF16),
            pltpu.VMEM((1, WIDTH), F32),
            pltpu.VMEM((1, ROWS), F32),
            pltpu.VMEM(block, BF16),
            pltpu.VMEM(block, BF16),
            pltpu.VMEM(slab, F32),
            pltpu.VMEM(slab, BF16),
            pltpu.VMEM((WIDTH, WIDTH), BF16),
            pltpu.VMEM((6,) + block, BF16),
            pltpu.VMEM((5,) + block, BF16),
            pltpu.VMEM(block, BF16),
            pltpu.VMEM(block, F32),
            pltpu.VMEM(block, BF16),
            pltpu.VMEM(block, F32),
            pltpu.VMEM(block, F32),
            pltpu.VMEM(block, F32),
            pltpu.VMEM(block, BF16),
            pltpu.VMEM((WIDTH, ROWS), BF16),
            pltpu.VMEM((ROWS, ROWS), F32),
            pltpu.VMEM((2, 8) + slab_a, BF16),
            pltpu.VMEM((2, 8) + slab_b, BF16),
            pltpu.VMEM((8,) + slab_a, BF16),
            pltpu.VMEM((8,) + slab_b, BF16),
            pltpu.VMEM((2, 3) + slab_a, BF16),
            pltpu.VMEM((2, 3) + slab_b, BF16),
            pltpu.VMEM((2,) + slab_a, BF16),
            pltpu.VMEM((2,) + slab_b, BF16),
            pltpu.VMEM((2, 2) + slab_a, BF16),
            pltpu.VMEM((2, 2) + slab_b, BF16),
            pltpu.VMEM(slab_a, BF16),
            pltpu.VMEM(slab_b, BF16),
            pltpu.VMEM(slab_a, BF16),
            pltpu.VMEM(slab_b, BF16),
            pltpu.VMEM(slab_a, BF16),
            pltpu.VMEM(slab_b, BF16),
            pltpu.VMEM(block, BF16),
            pltpu.VMEM(block, F32),
            pltpu.VMEM((ROWS, ROWS), F32),
            pltpu.VMEM(block, BF16),
            pltpu.VMEM((1, ROWS), F32),
            pltpu.VMEM(block, BF16),
            pltpu.VMEM((1, ROWS), F32),
            dma((4,)), dma((4,)),
            dma((18,)), dma((18,)),
            dma((7, 2)), dma((6, 2)),
            dma((6, 2)), dma((5, 2)),
            dma((2, 8)), dma((2, 8)),
            dma((16,)), dma((16,)),
            dma((2,)), dma((2,)),
        ],
        compiler_params=pltpu.CompilerParams(
            collective_id=0, has_side_effects=True, vmem_limit_bytes=VMEM_GRANT
        ),
        cost_estimate=pl.CostEstimate(flops=4_000_000_000, bytes_accessed=6_000_000, transcendentals=300_000),
    )(images, pooled, head_weight, head_bias, log_scale, bias)
    loss, image_grad, pooled_grad, head_grad = pl.pallas_call(
        finish,
        out_shape=results,
        in_specs=[hbm] * 4,
        out_specs=(hbm,) * 4,
        scratch_shapes=[pltpu.VMEM(r.shape, r.dtype) for r in results] + [dma((4,)), dma((4,))],
        compiler_params=pltpu.CompilerParams(vmem_limit_bytes=VMEM_GRANT),
    )(*made)
    return loss.reshape(ROWS), image_grad, pooled_grad, head_grad


def solution(mesh):
    in_specs = (P(("dp", "fsdp"), None), P(("dp", "fsdp"), None), P("fsdp", None), P(), P(), P())
    out_specs = (
        P(("dp", "fsdp")),
        P(("dp", "fsdp"), None),
        P(("dp", "fsdp"), None),
        P(("dp", "fsdp"), None),
    )
    return jax.shard_map(
        per_device, mesh=mesh, in_specs=in_specs, out_specs=out_specs, check_vma=False
    )
```

```python
import jax
import jax.numpy as jnp
from jax import lax
from jax.experimental import pallas as pl
from jax.experimental.pallas import tpu as pltpu
from jax.sharding import PartitionSpec as P

MESH = pl.DeviceIdType.MESH
F32 = jnp.float32
BF16 = jnp.bfloat16
NT = (((1,), (1,)), ((), ()))

ROWS = 128
WIDTH = 1152
SHARD = 72
CHIP = 144
UNIT = 80
PART = 64
AHEAD = 48
TILE = 384
VMEM_GRANT = 60 * 1024 * 1024
HALF = 64
SPLIT = 640
ORDER = (2, 1, 3, 0)


def normalize(v):
    r = lax.rsqrt(jnp.sum(v * v, axis=-1, keepdims=True) + 1e-06)
    return v * r, r


def kernel(
    img_hbm, pool_hbm, wsh_hbm, hb_hbm, log_scale, bias,
    loss_hbm, img_grad_hbm, pool_grad_hbm, head_grad_hbm,
    img, pool, wsh, hb, loss_out, img_out, pool_out, head_out,
    wtmp, wf, xbuf, pbuf, xb, zb, ximg, ztxt, u, dzb, pt,
    t_a, t_b, r_a, r_b, st_a, st_b, far_a, far_b, near_a, near_b,
    y_a, y_b, pass_a, pass_b, in_a, in_b,
    gdx_out, gsum_out, gdx_in, gsum_in,
    l_s, o_s, w_s, w_r, x_s, x_r, p_s, p_r, t_s, t_r, g_s, g_r, h_s, h_r,
):
    loads = [
        pltpu.make_async_copy(src, dst, l_s.at[i])
        for i, (src, dst) in enumerate(
            ((wsh_hbm, wsh), (img_hbm, img), (pool_hbm, pool), (hb_hbm, hb.at[0]))
        )
    ]
    for d in loads:
        d.start()
    stores = [
        pltpu.make_async_copy(src, dst, o_s.at[i])
        for i, (src, dst) in enumerate(
            ((loss_out, loss_hbm), (img_out, img_grad_hbm), (pool_out, pool_grad_hbm), (head_out, head_grad_hbm))
        )
    ]

    dp = lax.axis_index("dp")
    f = lax.axis_index("fsdp")
    j = lax.rem(dp, 4)
    yh = lax.div(f, 8)
    x = lax.rem(lax.div(f, 2), 4)
    c = lax.rem(f, 2)
    base = yh * 8 + c

    sib = (dp, f + 1 - 2 * c)
    xp = (dp, base + 2 * lax.rem(x + 1, 4))
    xm = (dp, base + 2 * lax.rem(x + 3, 4))
    zp = (lax.rem(dp + 4, 32), f)
    zm = (lax.rem(dp + 28, 32), f)
    wrap_up = lax.div(j + 1, 4)
    up = (dp + 1 - 4 * wrap_up, lax.rem(f + 8 * wrap_up, 16))
    wrap_dn = lax.div(3 - j, 3)
    dn = (dp - 1 + 4 * wrap_dn, lax.rem(f + 8 * wrap_dn, 16))
    wrap = lax.div(j + 2, 4)
    up2 = (dp + 2 - 4 * wrap, lax.rem(f + 8 * wrap, 16))
    wrap = lax.div(3 - j, 2)
    dn2 = (dp - 2 + 4 * wrap, lax.rem(f + 8 * wrap, 16))

    barrier = pltpu.get_barrier_semaphore()
    for who in (sib, xp, xm, zp, zm, up, dn, up2, dn2):
        pl.semaphore_signal(barrier, inc=1, device_id=who, device_id_type=MESH)
    pl.semaphore_wait(barrier, 9)
    for d in loads:
        d.wait()

    def copy(src, dst, send, recv, who):
        return pltpu.make_async_remote_copy(
            src_ref=src, dst_ref=dst, send_sem=send, recv_sem=recv, device_id=who, device_id_type=MESH
        )

    def part(ref, h):
        return ref.at[pl.ds(HALF * h, HALF), :]

    def send_x(k, src, h):
        @pl.when(jnp.logical_and(k <= 3 - j, j >= 1))
        def _():
            copy(part(src, h), part(xbuf.at[k + 1], h), x_s.at[k, h], x_r.at[k + 1, h], dn).start()

        @pl.when(jnp.logical_and(k > 3 - j, j <= 2))
        def _():
            copy(part(src, h), part(xbuf.at[k - 1], h), x_s.at[k, h], x_r.at[k - 1, h], up).start()

    def send_p(k, src, h):
        @pl.when(jnp.logical_and(k <= j, j <= 1))
        def _():
            copy(part(src, h), part(pbuf.at[k + 1], h), p_s.at[k, h], p_r.at[k + 1, h], up).start()

        @pl.when(jnp.logical_and(k > j, j >= 2))
        def _():
            copy(part(src, h), part(pbuf.at[k - 1], h), p_s.at[k, h], p_r.at[k - 1, h], dn).start()

    def wait_x(k, h, whole=False):
        dst = xbuf.at[k] if whole else part(xbuf.at[k], h)
        copy(dst, dst, x_s.at[k, h], x_r.at[k, h], up).wait_recv()

    def quarter(k, q):
        return xbuf.at[k, pl.ds(HALF // 2 * q, HALF // 2), :]

    hop_in = [copy(quarter(4, q), quarter(4, q), x_s.at[5, q], x_r.at[4, q], zm) for q in range(4)]
    hop_up = [copy(quarter(4, q), quarter(3, q), x_s.at[4, q], x_r.at[3, q // 2], up) for q in range(4)]

    def wait_p(k, h):
        dst = part(pbuf.at[k], h)
        copy(dst, dst, p_s.at[k, h], p_r.at[k, h], up).wait_recv()

    def pass_x(k, h):
        wait_x(k, h)
        send_x(k, xbuf.at[k], h)

    def pass_p(k):
        for h in range(2):
            wait_p(k, h)
            send_p(k, pbuf.at[k], h)

    def x_done(k, src):
        @pl.when(jnp.logical_or(jnp.logical_and(k <= 3 - j, j >= 1), jnp.logical_and(k > 3 - j, j <= 2)))
        def _():
            for h in range(2):
                copy(part(src, h), part(xbuf.at[1], h), x_s.at[k, h], x_r.at[1, h], up).wait_send()

    def p_done(k, src):
        @pl.when(jnp.logical_or(jnp.logical_and(k <= j, j <= 1), jnp.logical_and(k > j, j >= 2)))
        def _():
            for h in range(2):
                copy(part(src, h), part(pbuf.at[1], h), p_s.at[k, h], p_r.at[1, h], up).wait_send()

    middle = lax.rem(lax.div(j + 1, 2), 2)
    outer = middle == 0
    inner = middle == 1
    xk0 = 1 + 2 * lax.div(j, 3)
    xk1 = 2 + middle
    xk2 = 6 - xk0 - xk1
    guest = copy(img, xbuf.at[5], x_s.at[6, 0], x_r.at[5, 0], up)

    w_swap = copy(wsh, wtmp, w_s.at[0], w_r.at[0], sib)
    w_swap.start()
    x_hop = [
        copy(img.at[pl.ds(HALF // 2 * q, HALF // 2), :], quarter(4, q), x_s.at[5, q], x_r.at[4, q], zm)
        for q in range(4)
    ]
    p_hop = [copy(part(pool, h), part(pbuf.at[4], h), p_s.at[5, h], p_r.at[4, h], zp) for h in range(2)]

    @pl.when(j <= 2)
    def _():
        for d in x_hop:
            d.start()

    send_x(0, img, 0)
    send_x(0, img, 1)
    send_p(0, pool, 0)

    @pl.when(j >= 1)
    def _():
        for d in p_hop:
            d.start()

    v, xr = normalize(img[...].astype(F32))
    ximg[...] = v
    xb[0] = v.astype(BF16)

    def chip(h, off):
        return h * 4 + lax.rem(x + off, 4)

    def rows_of(m, start, size):
        return wf.at[pl.ds(pl.multiple_of(m * CHIP + start, 16), size), :]

    def unit(m):
        return rows_of(m, 64 * c, UNIT)

    def w_copy(src, dst, ident, who, send=None):
        return copy(src, dst, w_s.at[ident if send is None else send], w_r.at[ident], who)

    w_sent = []

    def w_go(src, ident, who):
        d = w_copy(src, src, ident, who)
        d.start()
        w_sent.append(d)

    mine = chip(yh, 0)
    theirs = chip(1 - yh, 0)
    w_swap.wait_recv()
    own_rows = wsh[...].astype(F32)
    sib_rows = wtmp[...].astype(F32)
    first = c == 0
    wf[pl.ds(pl.multiple_of(mine * CHIP, 16), CHIP), :] = jnp.concatenate(
        [jnp.where(first, own_rows, sib_rows), jnp.where(first, sib_rows, own_rows)], axis=0
    ).astype(BF16)

    w_edge_up = w_copy(unit(mine), unit(mine), 9, up)
    w_edge_dn = w_copy(unit(mine), unit(mine), 9, dn)
    w_pass_up = w_copy(unit(theirs), unit(theirs), 9, up, 10)
    w_pass_dn = w_copy(unit(theirs), unit(theirs), 9, dn, 10)

    @pl.when(j == 3)
    def _():
        w_edge_up.start()

    @pl.when(j == 0)
    def _():
        w_edge_dn.start()

    w_go(unit(mine), 1, xp)
    w_go(unit(mine), 2, xm)

    pt[...] = pool[...].astype(F32).T.astype(BF16)

    def to_sibling(m, ident):
        w_go(rows_of(m, 80 * c, PART), ident, sib)

    def near_units(r, h):
        for d, (off, onward) in enumerate(((3, xp), (1, xm))):
            m = chip(h, off)
            w_copy(unit(m), unit(m), 1 + 2 * r + d, xp).wait_recv()
            if d == 0:
                w_go(rows_of(m, 64 * c, AHEAD), 5 + 2 * r, onward)
            else:
                w_go(rows_of(m, 64 * c + AHEAD, UNIT - AHEAD), 6 + 2 * r, onward)
            to_sibling(m, 11 + 4 * r + d)

    def far_units(r, h):
        m = chip(h, 2)
        part = rows_of(m, 64 * c, AHEAD)
        w_copy(part, part, 5 + 2 * r, xp).wait_recv()
        part = rows_of(m, 64 * c + AHEAD, UNIT - AHEAD)
        w_copy(part, part, 6 + 2 * r, xp).wait_recv()
        to_sibling(m, 13 + 4 * r)

    other = w_copy(unit(theirs), unit(theirs), 9, xp)
    theirs_xp = w_copy(unit(theirs), unit(theirs), 3, xp)
    theirs_xm = w_copy(unit(theirs), unit(theirs), 4, xm)
    theirs_part = rows_of(theirs, 80 * c, PART)
    theirs_sib = w_copy(theirs_part, theirs_part, 14, sib)
    w_sent.extend((theirs_xp, theirs_xm, theirs_sib))

    def send_theirs():
        theirs_xp.start()
        theirs_xm.start()
        theirs_sib.start()

    for h in range(2):
        @pl.when(j <= 2)
        def _():
            for q in (2 * h, 2 * h + 1):
                hop_in[q].wait_recv()
                hop_up[q].start()

        @pl.when(inner)
        def _():
            pass_x(1, h)

    near_units(0, yh)

    @pl.when(outer)
    def _():
        other.wait_recv()

    @pl.when(j == 0)
    def _():
        w_pass_up.start()

    @pl.when(j == 3)
    def _():
        w_pass_dn.start()

    @pl.when(outer)
    def _():
        send_theirs()

    @pl.when(inner)
    def _():
        pass_x(3, 0)

    @pl.when(j == 0)
    def _():
        send_p(0, pool, 1)
        guest.start()

    @pl.when(j == 3)
    def _():
        pass_p(4)

    far_units(0, yh)

    @pl.when(inner)
    def _():
        pass_x(3, 1)
        other.wait_recv()
        send_theirs()
        pass_x(2, 0)

    near_units(1, 1 - yh)

    @pl.when(inner)
    def _():
        pass_x(2, 1)

    @pl.when(j == 1)
    def _():
        send_p(0, pool, 1)
        pass_p(1)

    @pl.when(j == 2)
    def _():
        pass_p(4)

    far_units(1, 1 - yh)

    @pl.when(j == 2)
    def _():
        pass_p(3)

    def ready(k):
        xb[k] = normalize(xbuf[k].astype(F32))[0].astype(BF16)

    @pl.when(inner)
    def _():
        for k in range(1, 4):
            ready(k)

    for ident, m in (
        (11, chip(yh, 3)), (12, chip(yh, 1)), (13, chip(yh, 2)), (14, theirs),
        (15, chip(1 - yh, 3)), (16, chip(1 - yh, 1)), (17, chip(1 - yh, 2)),
    ):
        got = rows_of(m, 80 - 80 * c, PART)
        w_copy(got, got, ident, sib).wait_recv()

    temper = jnp.exp(jnp.full((1, 1), log_scale[0], F32))
    offset = jnp.full((1, 1), bias[0], F32)
    gain = temper * (1.0 / ROWS)

    def project(block, out):
        for start in range(0, WIDTH, 512):
            cols = pl.ds(start, min(512, WIDTH - start))
            out[:, cols] = jnp.dot(block, wf[:, cols], preferred_element_type=F32) + hb[:, cols]

    def weights(a, b, own):
        l = temper * lax.dot_general(a, b, NT, preferred_element_type=F32) + offset
        if own:
            eye = lax.broadcasted_iota(jnp.int32, l.shape, 0) == lax.broadcasted_iota(jnp.int32, l.shape, 1)
            l = jnp.where(eye, -l, l)
        g = gain / (1.0 + jnp.exp(-l))
        if own:
            g = jnp.where(eye, -g, g)
        return l, g.astype(BF16)

    def losses(m):
        e = jnp.maximum(m, 0.0) + jnp.log1p(jnp.exp(-jnp.abs(m)))
        total = e[:, :ROWS]
        for start in range(ROWS, m.shape[1], ROWS):
            total = total + e[:, start:start + ROWS]
        return jnp.sum(total.T, axis=0, keepdims=True)

    def image_side(d, row):
        loss_out[...] = row * (1.0 / ROWS)
        stores[0].start()
        v = ximg[...]
        img_out[...] = (xr * (d - v * jnp.sum(v * d, axis=-1, keepdims=True))).astype(BF16)
        stores[1].start()

    project(pool[...], ztxt)
    v, zr = normalize(ztxt[...])
    ztxt[...] = v
    zb[0] = v.astype(BF16)

    @pl.when(outer)
    def _():
        for k in (xk0, xk1, xk2):
            wait_x(k, 0)
            wait_x(k, 1)
            ready(k)

    seen = xb[0:4].reshape(4 * ROWS, WIDTH)
    _, g = weights(zb[0], seen, True)
    d = jnp.dot(g, seen, preferred_element_type=F32)
    v = ztxt[...]
    dzb[...] = (zr * (d - v * jnp.sum(v * d, axis=-1, keepdims=True))).astype(BF16)

    def term(n):
        m = chip(1 - yh if n < 4 else yh, ORDER[n % 4])
        t = jnp.dot(
            pt[pl.ds(pl.multiple_of(m * CHIP, 16), CHIP), :], dzb[...], preferred_element_type=F32
        )
        for o, u in enumerate((t[:SHARD].astype(BF16), t[SHARD:].astype(BF16))):
            t_a[o, n] = u[:, :SPLIT]
            t_b[o, n] = u[:, SPLIT:]
        copy(t_a.at[1 - c, n], r_a.at[n], t_s.at[0, n], t_r.at[0, n], sib).start()
        copy(t_b.at[1 - c, n], r_b.at[n], t_s.at[1, n], t_r.at[1, n], sib).start()

    def pair_a(n):
        copy(r_a.at[n], r_a.at[n], t_s.at[0, n], t_r.at[0, n], sib).wait_recv()
        return t_a[c, n].astype(F32) + r_a[n].astype(F32)

    def pair_b(n):
        copy(r_b.at[n], r_b.at[n], t_s.at[1, n], t_r.at[1, n], sib).wait_recv()
        return t_b[c, n].astype(F32) + r_b[n].astype(F32)

    g_sent = []

    def g_go(src, value, ident, dst, who):
        src[...] = value.astype(BF16)
        d = copy(src, dst, g_s.at[ident], g_r.at[ident], who)
        d.start()
        g_sent.append(d)

    def g_wait(ref, ident):
        copy(ref, ref, g_s.at[ident], g_r.at[ident], xp).wait_recv()
        return ref[...].astype(F32)

    def first_sends(g):
        n = 4 * g
        g_go(st_a.at[g, 0], pair_a(n), 6 * g, far_a.at[g], xp)
        g_go(st_b.at[g, 0], pair_b(n), 6 * g + 1, far_b.at[g], xm)
        g_go(st_b.at[g, 1], pair_b(n + 1), 6 * g + 2, near_b.at[g, 0], xp)
        g_go(st_a.at[g, 1], pair_a(n + 2), 6 * g + 3, near_a.at[g, 1], xm)

    def second_sends(g):
        n = 4 * g
        g_go(st_a.at[g, 2], pair_a(n + 1) + g_wait(far_a.at[g], 6 * g), 6 * g + 4, near_a.at[g, 0], xp)
        g_go(st_b.at[g, 2], pair_b(n + 2) + g_wait(far_b.at[g], 6 * g + 1), 6 * g + 5, near_b.at[g, 1], xm)

    def sums(g):
        n = 4 * g + 3
        a = pair_a(n) + g_wait(near_a.at[g, 0], 6 * g + 4) + g_wait(near_a.at[g, 1], 6 * g + 3)
        b = pair_b(n) + g_wait(near_b.at[g, 0], 6 * g + 2) + g_wait(near_b.at[g, 1], 6 * g + 5)
        return a, b

    def back():
        @pl.loop(0, WIDTH // TILE)
        def _(n):
            cols = pl.ds(pl.multiple_of(n * TILE, TILE), TILE)
            pool_out[:, cols] = lax.dot_general(
                dzb[...], wf[cols, :], NT, preferred_element_type=F32
            ).astype(BF16)

        stores[2].start()

    gdx_up = copy(gdx_out, gdx_in, h_s.at[0], h_r.at[0], up)
    gdx_dn = copy(gdx_out, gdx_in, h_s.at[0], h_r.at[0], dn)
    gsum_up = copy(gsum_out, gsum_in, h_s.at[1], h_r.at[1], up)
    gsum_dn = copy(gsum_out, gsum_in, h_s.at[1], h_r.at[1], dn)

    for n in range(3):
        term(n)
    first_sends(0)
    for n in range(3, 8):
        term(n)
    first_sends(1)

    @pl.when(j == 1)
    def _():
        for h in range(2):
            wait_p(4, h)
            wait_p(3, h)
        wait_x(5, 0, whole=True)
        ready(5)

    @pl.when(j == 2)
    def _():
        for h in range(2):
            wait_p(1, h)

    @pl.when(inner)
    def _():
        for h in range(2):
            wait_p(2, h)
        project(pbuf[1:5].reshape(4 * ROWS, WIDTH), u)

    second_sends(0)

    @pl.when(inner)
    def _():
        @pl.loop(1, 5)
        def _(k):
            zb[k] = normalize(u[pl.ds(pl.multiple_of((k - 1) * ROWS, ROWS), ROWS), :])[0].astype(BF16)

        hosted = zb[pl.ds(4 - 2 * j, 3)].reshape(3 * ROWS, WIDTH)
        m, g = weights(xb[9 - 4 * j], hosted, False)
        gdx_out[...] = jnp.dot(g, hosted, preferred_element_type=F32).astype(BF16)
        gsum_out[...] = losses(m)

        @pl.when(j == 1)
        def _():
            gdx_dn.start()
            gsum_dn.start()

        @pl.when(j == 2)
        def _():
            gdx_up.start()
            gsum_up.start()

    @pl.when(outer)
    def _():
        back()

    a, b = sums(0)
    g_go(y_a, a, 12, pass_a, up2)
    g_go(y_b, b, 13, pass_b, dn2)
    second_sends(1)

    @pl.when(inner)
    def _():
        texts = zb[0:4].reshape(4 * ROWS, WIDTH)
        m, g = weights(xb[0], texts, True)
        image_side(jnp.dot(g, texts, preferred_element_type=F32), losses(m))

    a, b = sums(1)
    head_out[:, :SPLIT] = a
    head_out[:, SPLIT:] = b

    onward = []
    for ref, ident, dst, who in ((pass_a, 12, in_a, up2), (pass_b, 13, in_b, dn2)):
        copy(ref, ref, g_s.at[ident], g_r.at[ident], xp).wait_recv()
        d = copy(ref, dst, g_s.at[ident + 2], g_r.at[ident + 2], who)
        d.start()
        onward.append(d)

    @pl.when(inner)
    def _():
        back()

    @pl.when(outer)
    def _():
        m, g = weights(xb[0], zb[0], True)
        row = losses(m)
        d = jnp.dot(g, zb[0], preferred_element_type=F32)
        gsum_up.wait_recv()
        gdx_up.wait_recv()
        image_side(d + gdx_in[...].astype(F32), row + gsum_in[...])

    head_out[:, :SPLIT] += g_wait(in_a, 14)
    head_out[:, SPLIT:] += g_wait(in_b, 15)
    stores[3].start()

    w_swap.wait_send()
    for d in w_sent:
        d.wait_send()

    @pl.when(j == 3)
    def _():
        w_edge_up.wait_send()
        w_pass_dn.wait_send()

    @pl.when(j == 0)
    def _():
        w_edge_dn.wait_send()
        w_pass_up.wait_send()

    @pl.when(j <= 2)
    def _():
        for d in x_hop + hop_up:
            d.wait_send()

    @pl.when(j >= 1)
    def _():
        for d in p_hop:
            d.wait_send()

    @pl.when(j == 0)
    def _():
        guest.wait_send()

    @pl.when(inner)
    def _():
        gdx_up.wait_send()
        gsum_up.wait_send()

    x_done(0, img)
    p_done(0, pool)
    for k in range(1, 4):
        x_done(k, xbuf.at[k])
        p_done(k, pbuf.at[k])
    p_done(4, pbuf.at[4])
    for n in range(8):
        copy(t_a.at[1 - c, n], r_a.at[n], t_s.at[0, n], t_r.at[0, n], sib).wait_send()
        copy(t_b.at[1 - c, n], r_b.at[n], t_s.at[1, n], t_r.at[1, n], sib).wait_send()
    for d in g_sent + onward:
        d.wait_send()
    for d in stores:
        d.wait()


def finish(*refs):
    into, out = refs[12], refs[13]
    loads = [pltpu.make_async_copy(refs[i], refs[8 + i], into.at[i]) for i in range(4)]
    stores = [pltpu.make_async_copy(refs[8 + i], refs[4 + i], out.at[i]) for i in range(4)]
    for d in loads:
        d.start()
    for d, e in zip(loads, stores):
        d.wait()
        e.start()
    for e in stores:
        e.wait()


def per_device(images, pooled, head_weight, head_bias, log_scale, bias):
    smem = pl.BlockSpec(memory_space=pltpu.SMEM)
    hbm = pl.BlockSpec(memory_space=pltpu.HBM)
    block = (ROWS, WIDTH)
    slab = (SHARD, WIDTH)
    slab_a = (SHARD, SPLIT)
    slab_b = (SHARD, WIDTH - SPLIT)
    dma = pltpu.SemaphoreType.DMA
    results = (
        jax.ShapeDtypeStruct((1, ROWS), F32),
        jax.ShapeDtypeStruct(block, BF16),
        jax.ShapeDtypeStruct(block, BF16),
        jax.ShapeDtypeStruct(slab, F32),
    )
    made = pl.pallas_call(
        kernel,
        out_shape=results,
        in_specs=[hbm, hbm, hbm, hbm, smem, smem],
        out_specs=(hbm, hbm, hbm, hbm),
        scratch_shapes=[
            pltpu.VMEM(block, BF16),
            pltpu.VMEM(block, BF16),
            pltpu.VMEM(slab, BF16),
            pltpu.VMEM((1, WIDTH), F32),
            pltpu.VMEM((1, ROWS), F32),
            pltpu.VMEM(block, BF16),
            pltpu.VMEM(block, BF16),
            pltpu.VMEM(slab, F32),
            pltpu.VMEM(slab, BF16),
            pltpu.VMEM((WIDTH, WIDTH), BF16),
            pltpu.VMEM((6,) + block, BF16),
            pltpu.VMEM((5,) + block, BF16),
            pltpu.VMEM((6,) + block, BF16),
            pltpu.VMEM((5,) + block, BF16),
            pltpu.VMEM(block, F32),
            pltpu.VMEM(block, F32),
            pltpu.VMEM((4 * ROWS, WIDTH), F32),
            pltpu.VMEM(block, BF16),
            pltpu.VMEM((WIDTH, ROWS), BF16),
            pltpu.VMEM((2, 8) + slab_a, BF16),
            pltpu.VMEM((2, 8) + slab_b, BF16),
            pltpu.VMEM((8,) + slab_a, BF16),
            pltpu.VMEM((8,) + slab_b, BF16),
            pltpu.VMEM((2, 3) + slab_a, BF16),
            pltpu.VMEM((2, 3) + slab_b, BF16),
            pltpu.VMEM((2,) + slab_a, BF16),
            pltpu.VMEM((2,) + slab_b, BF16),
            pltpu.VMEM((2, 2) + slab_a, BF16),
            pltpu.VMEM((2, 2) + slab_b, BF16),
            pltpu.VMEM(slab_a, BF16),
            pltpu.VMEM(slab_b, BF16),
            pltpu.VMEM(slab_a, BF16),
            pltpu.VMEM(slab_b, BF16),
            pltpu.VMEM(slab_a, BF16),
            pltpu.VMEM(slab_b, BF16),
            pltpu.VMEM(block, BF16),
            pltpu.VMEM((1, ROWS), F32),
            pltpu.VMEM(block, BF16),
            pltpu.VMEM((1, ROWS), F32),
            dma((4,)), dma((4,)),
            dma((18,)), dma((18,)),
            dma((7, 4)), dma((6, 4)),
            dma((6, 2)), dma((5, 2)),
            dma((2, 8)), dma((2, 8)),
            dma((16,)), dma((16,)),
            dma((2,)), dma((2,)),
        ],
        compiler_params=pltpu.CompilerParams(
            collective_id=0, has_side_effects=True, vmem_limit_bytes=VMEM_GRANT
        ),
        cost_estimate=pl.CostEstimate(flops=4_000_000_000, bytes_accessed=6_000_000, transcendentals=300_000),
    )(images, pooled, head_weight, head_bias, log_scale, bias)
    loss, image_grad, pooled_grad, head_grad = pl.pallas_call(
        finish,
        out_shape=results,
        in_specs=[hbm] * 4,
        out_specs=(hbm,) * 4,
        scratch_shapes=[pltpu.VMEM(r.shape, r.dtype) for r in results] + [dma((4,)), dma((4,))],
        compiler_params=pltpu.CompilerParams(vmem_limit_bytes=VMEM_GRANT),
    )(*made)
    return loss.reshape(ROWS), image_grad, pooled_grad, head_grad


def solution(mesh):
    in_specs = (P(("dp", "fsdp"), None), P(("dp", "fsdp"), None), P("fsdp", None), P(), P(), P())
    out_specs = (
        P(("dp", "fsdp")),
        P(("dp", "fsdp"), None),
        P(("dp", "fsdp"), None),
        P(("dp", "fsdp"), None),
    )
    return jax.shard_map(
        per_device, mesh=mesh, in_specs=in_specs, out_specs=out_specs, check_vma=False
    )
```

```python
import jax
import jax.numpy as jnp
from jax import lax
from jax.experimental import pallas as pl
from jax.experimental.pallas import tpu as pltpu
from jax.sharding import PartitionSpec as P

MESH = pl.DeviceIdType.MESH
F32 = jnp.float32
BF16 = jnp.bfloat16
NT = (((1,), (1,)), ((), ()))

ROWS = 128
WIDTH = 1152
SHARD = 72
CHIP = 144
UNIT = 80
PART = 64
AHEAD = 48
TILE = 384
VMEM_GRANT = 60 * 1024 * 1024
HALF = 64
SPLIT = 640
ORDER = (2, 1, 3, 0)


def normalize(v):
    r = lax.rsqrt(jnp.sum(v * v, axis=-1, keepdims=True) + 1e-06)
    return v * r, r


def kernel(
    img_hbm, pool_hbm, wsh_hbm, hb_hbm, log_scale, bias,
    loss_hbm, img_grad_hbm, pool_grad_hbm, head_grad_hbm,
    img, pool, wsh, hb, loss_out, img_out, pool_out, head_out,
    wtmp, wf, xbuf, pbuf, xb, zb, ximg, ztxt, u, dzb, pt,
    t_a, t_b, r_a, r_b, st_a, st_b, far_a, far_b, near_a, near_b,
    y_a, y_b, pass_a, pass_b, in_a, in_b,
    gdx_out, gsum_out, gdx_in, gsum_in,
    l_s, o_s, w_s, w_r, x_s, x_r, p_s, p_r, t_s, t_r, g_s, g_r, h_s, h_r,
):
    loads = [
        pltpu.make_async_copy(src, dst, l_s.at[i])
        for i, (src, dst) in enumerate(
            ((wsh_hbm, wsh), (img_hbm, img), (pool_hbm, pool), (hb_hbm, hb.at[0]))
        )
    ]
    for d in loads:
        d.start()
    stores = [
        pltpu.make_async_copy(src, dst, o_s.at[i])
        for i, (src, dst) in enumerate(
            ((loss_out, loss_hbm), (img_out, img_grad_hbm), (pool_out, pool_grad_hbm), (head_out, head_grad_hbm))
        )
    ]

    dp = lax.axis_index("dp")
    f = lax.axis_index("fsdp")
    j = lax.rem(dp, 4)
    yh = lax.div(f, 8)
    x = lax.rem(lax.div(f, 2), 4)
    c = lax.rem(f, 2)
    base = yh * 8 + c

    sib = (dp, f + 1 - 2 * c)
    xp = (dp, base + 2 * lax.rem(x + 1, 4))
    xm = (dp, base + 2 * lax.rem(x + 3, 4))
    zp = (lax.rem(dp + 4, 32), f)
    zm = (lax.rem(dp + 28, 32), f)
    wrap_up = lax.div(j + 1, 4)
    up = (dp + 1 - 4 * wrap_up, lax.rem(f + 8 * wrap_up, 16))
    wrap_dn = lax.div(3 - j, 3)
    dn = (dp - 1 + 4 * wrap_dn, lax.rem(f + 8 * wrap_dn, 16))
    wrap = lax.div(j + 2, 4)
    up2 = (dp + 2 - 4 * wrap, lax.rem(f + 8 * wrap, 16))
    wrap = lax.div(3 - j, 2)
    dn2 = (dp - 2 + 4 * wrap, lax.rem(f + 8 * wrap, 16))

    barrier = pltpu.get_barrier_semaphore()
    for who in (sib, xp, xm, zp, zm, up, dn, up2, dn2):
        pl.semaphore_signal(barrier, inc=1, device_id=who, device_id_type=MESH)
    pl.semaphore_wait(barrier, 9)
    for d in loads:
        d.wait()

    def copy(src, dst, send, recv, who):
        return pltpu.make_async_remote_copy(
            src_ref=src, dst_ref=dst, send_sem=send, recv_sem=recv, device_id=who, device_id_type=MESH
        )

    def part(ref, h):
        return ref.at[pl.ds(HALF * h, HALF), :]

    def send_x(k, src, h):
        @pl.when(jnp.logical_and(k <= 3 - j, j >= 1))
        def _():
            copy(part(src, h), part(xbuf.at[k + 1], h), x_s.at[k, h], x_r.at[k + 1, h], dn).start()

        @pl.when(jnp.logical_and(k > 3 - j, j <= 2))
        def _():
            copy(part(src, h), part(xbuf.at[k - 1], h), x_s.at[k, h], x_r.at[k - 1, h], up).start()

    def send_p(k, src, h):
        @pl.when(jnp.logical_and(k <= j, j <= 1))
        def _():
            copy(part(src, h), part(pbuf.at[k + 1], h), p_s.at[k, h], p_r.at[k + 1, h], up).start()

        @pl.when(jnp.logical_and(k > j, j >= 2))
        def _():
            copy(part(src, h), part(pbuf.at[k - 1], h), p_s.at[k, h], p_r.at[k - 1, h], dn).start()

    def wait_x(k, h, whole=False):
        dst = xbuf.at[k] if whole else part(xbuf.at[k], h)
        copy(dst, dst, x_s.at[k, h], x_r.at[k, h], up).wait_recv()

    def quarter(k, q):
        return xbuf.at[k, pl.ds(HALF // 2 * q, HALF // 2), :]

    hop_in = [copy(quarter(4, q), quarter(4, q), x_s.at[5, q], x_r.at[4, q], zm) for q in range(4)]
    hop_up = [copy(quarter(4, q), quarter(3, q), x_s.at[4, q], x_r.at[3, q // 2], up) for q in range(4)]

    def wait_p(k, h):
        dst = part(pbuf.at[k], h)
        copy(dst, dst, p_s.at[k, h], p_r.at[k, h], up).wait_recv()

    def pass_x(k, h):
        wait_x(k, h)
        send_x(k, xbuf.at[k], h)

    def pass_p(k):
        for h in range(2):
            wait_p(k, h)
            send_p(k, pbuf.at[k], h)

    def x_done(k, src):
        @pl.when(jnp.logical_or(jnp.logical_and(k <= 3 - j, j >= 1), jnp.logical_and(k > 3 - j, j <= 2)))
        def _():
            for h in range(2):
                copy(part(src, h), part(xbuf.at[1], h), x_s.at[k, h], x_r.at[1, h], up).wait_send()

    def p_done(k, src):
        @pl.when(jnp.logical_or(jnp.logical_and(k <= j, j <= 1), jnp.logical_and(k > j, j >= 2)))
        def _():
            for h in range(2):
                copy(part(src, h), part(pbuf.at[1], h), p_s.at[k, h], p_r.at[1, h], up).wait_send()

    middle = lax.rem(lax.div(j + 1, 2), 2)
    outer = middle == 0
    inner = middle == 1
    xk0 = 1 + 2 * lax.div(j, 3)
    xk1 = 2 + middle
    xk2 = 6 - xk0 - xk1
    guest = copy(img, xbuf.at[5], x_s.at[6, 0], x_r.at[5, 0], up)

    w_swap = copy(wsh, wtmp, w_s.at[0], w_r.at[0], sib)
    w_swap.start()
    x_hop = [
        copy(img.at[pl.ds(HALF // 2 * q, HALF // 2), :], quarter(4, q), x_s.at[5, q], x_r.at[4, q], zm)
        for q in range(4)
    ]
    p_hop = [copy(part(pool, h), part(pbuf.at[4], h), p_s.at[5, h], p_r.at[4, h], zp) for h in range(2)]

    @pl.when(j <= 2)
    def _():
        for d in x_hop:
            d.start()

    send_x(0, img, 0)
    send_x(0, img, 1)

    @pl.when(j == 1)
    def _():
        send_p(0, pool, 0)

    @pl.when(j >= 1)
    def _():
        for d in p_hop:
            d.start()

    v, xr = normalize(img[...].astype(F32))
    ximg[...] = v
    xb[0] = v.astype(BF16)

    def chip(h, off):
        return h * 4 + lax.rem(x + off, 4)

    def rows_of(m, start, size):
        return wf.at[pl.ds(pl.multiple_of(m * CHIP + start, 16), size), :]

    def piece(m, p):
        return rows_of(m, 64 * c, AHEAD) if p == 0 else rows_of(m, 64 * c + AHEAD, UNIT - AHEAD)

    def w_copy(src, dst, ident, who, send=None):
        return copy(src, dst, w_s.at[ident if send is None else send], w_r.at[ident], who)

    w_sent = []

    def w_go(src, ident, who):
        d = w_copy(src, src, ident, who)
        d.start()
        w_sent.append(d)

    mine = chip(yh, 0)
    theirs = chip(1 - yh, 0)
    w_swap.wait_recv()
    own_rows = wsh[...].astype(F32)
    sib_rows = wtmp[...].astype(F32)
    first = c == 0
    wf[pl.ds(pl.multiple_of(mine * CHIP, 16), CHIP), :] = jnp.concatenate(
        [jnp.where(first, own_rows, sib_rows), jnp.where(first, sib_rows, own_rows)], axis=0
    ).astype(BF16)

    edge_up = [w_copy(piece(mine, p), piece(mine, p), 13 + p, up) for p in range(2)]
    edge_dn = [w_copy(piece(mine, p), piece(mine, p), 13 + p, dn) for p in range(2)]
    pass_up = [w_copy(piece(theirs, p), piece(theirs, p), 13 + p, up, 15 + p) for p in range(2)]
    pass_dn = [w_copy(piece(theirs, p), piece(theirs, p), 13 + p, dn, 15 + p) for p in range(2)]

    @pl.when(j == 3)
    def _():
        for d in edge_up:
            d.start()

    @pl.when(j == 0)
    def _():
        for d in edge_dn:
            d.start()

    def along_x(r, m):
        return {
            (d, p): w_copy(piece(m, p), piece(m, p), 1 + 4 * r + 2 * d + p, xp if d == 0 else xm)
            for d in range(2)
            for p in range(2)
        }

    mine_x = along_x(0, mine)
    theirs_x = along_x(1, theirs)
    for key in ((0, 0), (1, 1), (0, 1), (1, 0)):
        mine_x[key].start()
    w_sent.extend(mine_x.values())
    w_sent.extend(theirs_x.values())

    pt[...] = pool[...].astype(F32).T.astype(BF16)

    def to_sibling(m, ident):
        w_go(rows_of(m, 80 * c, PART), ident, sib)

    def near_first(r, h):
        for d, (off, onward) in enumerate(((3, xp), (1, xm))):
            got = piece(chip(h, off), d)
            w_copy(got, got, 1 + 4 * r + 3 * d, xp).wait_recv()
            w_go(got, 9 + 2 * r + d, onward)

    def near_rest(r, h):
        for d, off in enumerate((3, 1)):
            m = chip(h, off)
            got = piece(m, 1 - d)
            w_copy(got, got, 2 + 4 * r + d, xp).wait_recv()
            to_sibling(m, 17 + 4 * r + d)

    def far_units(r, h):
        m = chip(h, 2)
        for p in range(2):
            w_copy(piece(m, p), piece(m, p), 9 + 2 * r + p, xp).wait_recv()
        to_sibling(m, 19 + 4 * r)

    edge_in = [w_copy(piece(theirs, p), piece(theirs, p), 13 + p, xp) for p in range(2)]
    theirs_part = rows_of(theirs, 80 * c, PART)
    theirs_sib = w_copy(theirs_part, theirs_part, 20, sib)
    w_sent.append(theirs_sib)

    def theirs_first():
        edge_in[0].wait_recv()

        @pl.when(j == 0)
        def _():
            pass_up[0].start()

        @pl.when(j == 3)
        def _():
            pass_dn[0].start()

        theirs_x[0, 0].start()

    def theirs_rest():
        edge_in[1].wait_recv()

        @pl.when(j == 0)
        def _():
            pass_up[1].start()

        @pl.when(j == 3)
        def _():
            pass_dn[1].start()

        for key in ((1, 1), (0, 1), (1, 0)):
            theirs_x[key].start()
        theirs_sib.start()

    def hop_on(h):
        @pl.when(j <= 2)
        def _():
            for q in (2 * h, 2 * h + 1):
                hop_in[q].wait_recv()
                hop_up[q].start()

        @pl.when(inner)
        def _():
            pass_x(1, h)

    hop_on(0)

    @pl.when(outer)
    def _():
        theirs_first()

    near_first(0, yh)

    @pl.when(outer)
    def _():
        theirs_rest()

    hop_on(1)
    near_rest(0, yh)

    @pl.when(j == 0)
    def _():
        send_p(0, pool, 0)
        send_p(0, pool, 1)
        guest.start()

    @pl.when(j == 3)
    def _():
        pass_p(4)

    @pl.when(inner)
    def _():
        pass_x(3, 0)
        theirs_first()

    far_units(0, yh)

    @pl.when(inner)
    def _():
        pass_x(3, 1)
        theirs_rest()
        pass_x(2, 0)

    near_first(1, 1 - yh)

    @pl.when(inner)
    def _():
        pass_x(2, 1)

    near_rest(1, 1 - yh)

    @pl.when(j == 1)
    def _():
        send_p(0, pool, 1)
        pass_p(1)

    @pl.when(j == 2)
    def _():
        pass_p(4)

    far_units(1, 1 - yh)

    @pl.when(j == 2)
    def _():
        pass_p(3)

    def ready(k):
        xb[k] = normalize(xbuf[k].astype(F32))[0].astype(BF16)

    @pl.when(inner)
    def _():
        for k in range(1, 4):
            ready(k)

    for ident, m in (
        (17, chip(yh, 3)), (18, chip(yh, 1)), (19, chip(yh, 2)), (20, theirs),
        (21, chip(1 - yh, 3)), (22, chip(1 - yh, 1)), (23, chip(1 - yh, 2)),
    ):
        got = rows_of(m, 80 - 80 * c, PART)
        w_copy(got, got, ident, sib).wait_recv()

    temper = jnp.exp(jnp.full((1, 1), log_scale[0], F32))
    offset = jnp.full((1, 1), bias[0], F32)
    gain = temper * (1.0 / ROWS)

    def project(block, out):
        for start in range(0, WIDTH, 512):
            cols = pl.ds(start, min(512, WIDTH - start))
            out[:, cols] = jnp.dot(block, wf[:, cols], preferred_element_type=F32) + hb[:, cols]

    def weights(a, b, own):
        l = temper * lax.dot_general(a, b, NT, preferred_element_type=F32) + offset
        if own:
            eye = lax.broadcasted_iota(jnp.int32, l.shape, 0) == lax.broadcasted_iota(jnp.int32, l.shape, 1)
            l = jnp.where(eye, -l, l)
        g = gain / (1.0 + jnp.exp(-l))
        if own:
            g = jnp.where(eye, -g, g)
        return l, g.astype(BF16)

    def losses(m):
        e = jnp.maximum(m, 0.0) + jnp.log1p(jnp.exp(-jnp.abs(m)))
        total = e[:, :ROWS]
        for start in range(ROWS, m.shape[1], ROWS):
            total = total + e[:, start:start + ROWS]
        return jnp.sum(total.T, axis=0, keepdims=True)

    def image_side(d, row):
        loss_out[...] = row * (1.0 / ROWS)
        stores[0].start()
        v = ximg[...]
        img_out[...] = (xr * (d - v * jnp.sum(v * d, axis=-1, keepdims=True))).astype(BF16)
        stores[1].start()

    project(pool[...], ztxt)
    v, zr = normalize(ztxt[...])
    ztxt[...] = v
    zb[0] = v.astype(BF16)

    @pl.when(outer)
    def _():
        for k in (xk0, xk1, xk2):
            wait_x(k, 0)
            wait_x(k, 1)
            ready(k)

    seen = xb[0:4].reshape(4 * ROWS, WIDTH)
    _, g = weights(zb[0], seen, True)
    d = jnp.dot(g, seen, preferred_element_type=F32)
    v = ztxt[...]
    dzb[...] = (zr * (d - v * jnp.sum(v * d, axis=-1, keepdims=True))).astype(BF16)

    def term(n):
        m = chip(1 - yh if n < 4 else yh, ORDER[n % 4])
        t = jnp.dot(
            pt[pl.ds(pl.multiple_of(m * CHIP, 16), CHIP), :], dzb[...], preferred_element_type=F32
        )
        for o, u in enumerate((t[:SHARD].astype(BF16), t[SHARD:].astype(BF16))):
            t_a[o, n] = u[:, :SPLIT]
            t_b[o, n] = u[:, SPLIT:]
        copy(t_a.at[1 - c, n], r_a.at[n], t_s.at[0, n], t_r.at[0, n], sib).start()
        copy(t_b.at[1 - c, n], r_b.at[n], t_s.at[1, n], t_r.at[1, n], sib).start()

    def pair_a(n):
        copy(r_a.at[n], r_a.at[n], t_s.at[0, n], t_r.at[0, n], sib).wait_recv()
        return t_a[c, n].astype(F32) + r_a[n].astype(F32)

    def pair_b(n):
        copy(r_b.at[n], r_b.at[n], t_s.at[1, n], t_r.at[1, n], sib).wait_recv()
        return t_b[c, n].astype(F32) + r_b[n].astype(F32)

    g_sent = []

    def g_go(src, value, ident, dst, who):
        src[...] = value.astype(BF16)
        d = copy(src, dst, g_s.at[ident], g_r.at[ident], who)
        d.start()
        g_sent.append(d)

    def g_wait(ref, ident):
        copy(ref, ref, g_s.at[ident], g_r.at[ident], xp).wait_recv()
        return ref[...].astype(F32)

    def first_sends(g):
        n = 4 * g
        g_go(st_a.at[g, 0], pair_a(n), 6 * g, far_a.at[g], xp)
        g_go(st_b.at[g, 0], pair_b(n), 6 * g + 1, far_b.at[g], xm)
        g_go(st_b.at[g, 1], pair_b(n + 1), 6 * g + 2, near_b.at[g, 0], xp)
        g_go(st_a.at[g, 1], pair_a(n + 2), 6 * g + 3, near_a.at[g, 1], xm)

    def second_sends(g):
        n = 4 * g
        g_go(st_a.at[g, 2], pair_a(n + 1) + g_wait(far_a.at[g], 6 * g), 6 * g + 4, near_a.at[g, 0], xp)
        g_go(st_b.at[g, 2], pair_b(n + 2) + g_wait(far_b.at[g], 6 * g + 1), 6 * g + 5, near_b.at[g, 1], xm)

    def sums(g):
        n = 4 * g + 3
        a = pair_a(n) + g_wait(near_a.at[g, 0], 6 * g + 4) + g_wait(near_a.at[g, 1], 6 * g + 3)
        b = pair_b(n) + g_wait(near_b.at[g, 0], 6 * g + 2) + g_wait(near_b.at[g, 1], 6 * g + 5)
        return a, b

    def back():
        @pl.loop(0, WIDTH // TILE)
        def _(n):
            cols = pl.ds(pl.multiple_of(n * TILE, TILE), TILE)
            pool_out[:, cols] = lax.dot_general(
                dzb[...], wf[cols, :], NT, preferred_element_type=F32
            ).astype(BF16)

        stores[2].start()

    gdx_up = copy(gdx_out, gdx_in, h_s.at[0], h_r.at[0], up)
    gdx_dn = copy(gdx_out, gdx_in, h_s.at[0], h_r.at[0], dn)
    gsum_up = copy(gsum_out, gsum_in, h_s.at[1], h_r.at[1], up)
    gsum_dn = copy(gsum_out, gsum_in, h_s.at[1], h_r.at[1], dn)

    for n in range(3):
        term(n)
    first_sends(0)
    for n in range(3, 8):
        term(n)
    first_sends(1)

    @pl.when(j == 1)
    def _():
        for h in range(2):
            wait_p(4, h)
            wait_p(3, h)
        wait_x(5, 0, whole=True)
        ready(5)

    @pl.when(j == 2)
    def _():
        for h in range(2):
            wait_p(1, h)

    @pl.when(inner)
    def _():
        for h in range(2):
            wait_p(2, h)
        project(pbuf[1:5].reshape(4 * ROWS, WIDTH), u)

    second_sends(0)

    @pl.when(inner)
    def _():
        @pl.loop(1, 5)
        def _(k):
            zb[k] = normalize(u[pl.ds(pl.multiple_of((k - 1) * ROWS, ROWS), ROWS), :])[0].astype(BF16)

        hosted = zb[pl.ds(4 - 2 * j, 3)].reshape(3 * ROWS, WIDTH)
        m, g = weights(xb[9 - 4 * j], hosted, False)
        gdx_out[...] = jnp.dot(g, hosted, preferred_element_type=F32).astype(BF16)
        gsum_out[...] = losses(m)

        @pl.when(j == 1)
        def _():
            gdx_dn.start()
            gsum_dn.start()

        @pl.when(j == 2)
        def _():
            gdx_up.start()
            gsum_up.start()

    @pl.when(outer)
    def _():
        back()

    a, b = sums(0)
    g_go(y_a, a, 12, pass_a, up2)
    g_go(y_b, b, 13, pass_b, dn2)
    second_sends(1)

    @pl.when(inner)
    def _():
        texts = zb[0:4].reshape(4 * ROWS, WIDTH)
        m, g = weights(xb[0], texts, True)
        image_side(jnp.dot(g, texts, preferred_element_type=F32), losses(m))

    a, b = sums(1)
    head_out[:, :SPLIT] = a
    head_out[:, SPLIT:] = b

    onward = []
    for ref, ident, dst, who in ((pass_a, 12, in_a, up2), (pass_b, 13, in_b, dn2)):
        copy(ref, ref, g_s.at[ident], g_r.at[ident], xp).wait_recv()
        d = copy(ref, dst, g_s.at[ident + 2], g_r.at[ident + 2], who)
        d.start()
        onward.append(d)

    @pl.when(inner)
    def _():
        back()

    @pl.when(outer)
    def _():
        m, g = weights(xb[0], zb[0], True)
        row = losses(m)
        d = jnp.dot(g, zb[0], preferred_element_type=F32)
        gsum_up.wait_recv()
        gdx_up.wait_recv()
        image_side(d + gdx_in[...].astype(F32), row + gsum_in[...])

    head_out[:, :SPLIT] += g_wait(in_a, 14)
    head_out[:, SPLIT:] += g_wait(in_b, 15)
    stores[3].start()

    w_swap.wait_send()
    for d in w_sent:
        d.wait_send()

    @pl.when(j == 3)
    def _():
        for d in edge_up + pass_dn:
            d.wait_send()

    @pl.when(j == 0)
    def _():
        for d in edge_dn + pass_up:
            d.wait_send()

    @pl.when(j <= 2)
    def _():
        for d in x_hop + hop_up:
            d.wait_send()

    @pl.when(j >= 1)
    def _():
        for d in p_hop:
            d.wait_send()

    @pl.when(j == 0)
    def _():
        guest.wait_send()

    @pl.when(inner)
    def _():
        gdx_up.wait_send()
        gsum_up.wait_send()

    x_done(0, img)
    p_done(0, pool)
    for k in range(1, 4):
        x_done(k, xbuf.at[k])
        p_done(k, pbuf.at[k])
    p_done(4, pbuf.at[4])
    for n in range(8):
        copy(t_a.at[1 - c, n], r_a.at[n], t_s.at[0, n], t_r.at[0, n], sib).wait_send()
        copy(t_b.at[1 - c, n], r_b.at[n], t_s.at[1, n], t_r.at[1, n], sib).wait_send()
    for d in g_sent + onward:
        d.wait_send()
    for d in stores:
        d.wait()


def finish(*refs):
    into, out = refs[12], refs[13]
    loads = [pltpu.make_async_copy(refs[i], refs[8 + i], into.at[i]) for i in range(4)]
    stores = [pltpu.make_async_copy(refs[8 + i], refs[4 + i], out.at[i]) for i in range(4)]
    for d in loads:
        d.start()
    for d, e in zip(loads, stores):
        d.wait()
        e.start()
    for e in stores:
        e.wait()


def per_device(images, pooled, head_weight, head_bias, log_scale, bias):
    smem = pl.BlockSpec(memory_space=pltpu.SMEM)
    hbm = pl.BlockSpec(memory_space=pltpu.HBM)
    block = (ROWS, WIDTH)
    slab = (SHARD, WIDTH)
    slab_a = (SHARD, SPLIT)
    slab_b = (SHARD, WIDTH - SPLIT)
    dma = pltpu.SemaphoreType.DMA
    results = (
        jax.ShapeDtypeStruct((1, ROWS), F32),
        jax.ShapeDtypeStruct(block, BF16),
        jax.ShapeDtypeStruct(block, BF16),
        jax.ShapeDtypeStruct(slab, F32),
    )
    made = pl.pallas_call(
        kernel,
        out_shape=results,
        in_specs=[hbm, hbm, hbm, hbm, smem, smem],
        out_specs=(hbm, hbm, hbm, hbm),
        scratch_shapes=[
            pltpu.VMEM(block, BF16),
            pltpu.VMEM(block, BF16),
            pltpu.VMEM(slab, BF16),
            pltpu.VMEM((1, WIDTH), F32),
            pltpu.VMEM((1, ROWS), F32),
            pltpu.VMEM(block, BF16),
            pltpu.VMEM(block, BF16),
            pltpu.VMEM(slab, F32),
            pltpu.VMEM(slab, BF16),
            pltpu.VMEM((WIDTH, WIDTH), BF16),
            pltpu.VMEM((6,) + block, BF16),
            pltpu.VMEM((5,) + block, BF16),
            pltpu.VMEM((6,) + block, BF16),
            pltpu.VMEM((5,) + block, BF16),
            pltpu.VMEM(block, F32),
            pltpu.VMEM(block, F32),
            pltpu.VMEM((4 * ROWS, WIDTH), F32),
            pltpu.VMEM(block, BF16),
            pltpu.VMEM((WIDTH, ROWS), BF16),
            pltpu.VMEM((2, 8) + slab_a, BF16),
            pltpu.VMEM((2, 8) + slab_b, BF16),
            pltpu.VMEM((8,) + slab_a, BF16),
            pltpu.VMEM((8,) + slab_b, BF16),
            pltpu.VMEM((2, 3) + slab_a, BF16),
            pltpu.VMEM((2, 3) + slab_b, BF16),
            pltpu.VMEM((2,) + slab_a, BF16),
            pltpu.VMEM((2,) + slab_b, BF16),
            pltpu.VMEM((2, 2) + slab_a, BF16),
            pltpu.VMEM((2, 2) + slab_b, BF16),
            pltpu.VMEM(slab_a, BF16),
            pltpu.VMEM(slab_b, BF16),
            pltpu.VMEM(slab_a, BF16),
            pltpu.VMEM(slab_b, BF16),
            pltpu.VMEM(slab_a, BF16),
            pltpu.VMEM(slab_b, BF16),
            pltpu.VMEM(block, BF16),
            pltpu.VMEM((1, ROWS), F32),
            pltpu.VMEM(block, BF16),
            pltpu.VMEM((1, ROWS), F32),
            dma((4,)), dma((4,)),
            dma((24,)), dma((24,)),
            dma((7, 4)), dma((6, 4)),
            dma((6, 2)), dma((5, 2)),
            dma((2, 8)), dma((2, 8)),
            dma((16,)), dma((16,)),
            dma((2,)), dma((2,)),
        ],
        compiler_params=pltpu.CompilerParams(
            collective_id=0, has_side_effects=True, vmem_limit_bytes=VMEM_GRANT
        ),
        cost_estimate=pl.CostEstimate(flops=4_000_000_000, bytes_accessed=6_000_000, transcendentals=300_000),
    )(images, pooled, head_weight, head_bias, log_scale, bias)
    loss, image_grad, pooled_grad, head_grad = pl.pallas_call(
        finish,
        out_shape=results,
        in_specs=[hbm] * 4,
        out_specs=(hbm,) * 4,
        scratch_shapes=[pltpu.VMEM(r.shape, r.dtype) for r in results] + [dma((4,)), dma((4,))],
        compiler_params=pltpu.CompilerParams(vmem_limit_bytes=VMEM_GRANT),
    )(*made)
    return loss.reshape(ROWS), image_grad, pooled_grad, head_grad


def solution(mesh):
    in_specs = (P(("dp", "fsdp"), None), P(("dp", "fsdp"), None), P("fsdp", None), P(), P(), P())
    out_specs = (
        P(("dp", "fsdp")),
        P(("dp", "fsdp"), None),
        P(("dp", "fsdp"), None),
        P(("dp", "fsdp"), None),
    )
    return jax.shard_map(
        per_device, mesh=mesh, in_specs=in_specs, out_specs=out_specs, check_vma=False
    )
```

```python
import jax
import jax.numpy as jnp
from jax import lax
from jax.experimental import pallas as pl
from jax.experimental.pallas import tpu as pltpu
from jax.sharding import PartitionSpec as P

MESH = pl.DeviceIdType.MESH
F32 = jnp.float32
BF16 = jnp.bfloat16
NT = (((1,), (1,)), ((), ()))

ROWS = 128
WIDTH = 1152
SHARD = 72
CHIP = 144
UNIT = 80
PART = 64
AHEAD = 48
TILE = 384
VMEM_GRANT = 60 * 1024 * 1024
HALF = 64
SPLIT = 640
ORDER = (2, 1, 3, 0)


def normalize(v):
    r = lax.rsqrt(jnp.sum(v * v, axis=-1, keepdims=True) + 1e-06)
    return v * r, r


def kernel(
    img_hbm, pool_hbm, wsh_hbm, hb_hbm, log_scale, bias,
    loss_hbm, img_grad_hbm, pool_grad_hbm, head_grad_hbm,
    img, pool, wsh, hb, loss_out, img_out, pool_out, head_out,
    wtmp, wf, xbuf, pbuf, xb, zb, ximg, ztxt, u, dzb, psib, ptf, pt, terms,
    st_a, st_b, far_a, far_b, near_a, near_b,
    y_a, y_b, pass_a, pass_b, in_a, in_b,
    gdx_out, gsum_out, gdx_in, gsum_in,
    l_s, o_s, w_s, w_r, x_s, x_r, p_s, p_r, g_s, g_r, h_s, h_r,
):
    loads = [
        pltpu.make_async_copy(src, dst, l_s.at[i])
        for i, (src, dst) in enumerate(
            ((wsh_hbm, wsh), (img_hbm, img), (pool_hbm, pool), (hb_hbm, hb.at[0]))
        )
    ]
    for d in loads:
        d.start()
    stores = [
        pltpu.make_async_copy(src, dst, o_s.at[i])
        for i, (src, dst) in enumerate(
            ((loss_out, loss_hbm), (img_out, img_grad_hbm), (pool_out, pool_grad_hbm), (head_out, head_grad_hbm))
        )
    ]

    dp = lax.axis_index("dp")
    f = lax.axis_index("fsdp")
    j = lax.rem(dp, 4)
    yh = lax.div(f, 8)
    x = lax.rem(lax.div(f, 2), 4)
    c = lax.rem(f, 2)
    base = yh * 8 + c

    sib = (dp, f + 1 - 2 * c)
    xp = (dp, base + 2 * lax.rem(x + 1, 4))
    xm = (dp, base + 2 * lax.rem(x + 3, 4))
    zp = (lax.rem(dp + 4, 32), f)
    zm = (lax.rem(dp + 28, 32), f)
    wrap_up = lax.div(j + 1, 4)
    up = (dp + 1 - 4 * wrap_up, lax.rem(f + 8 * wrap_up, 16))
    wrap_dn = lax.div(3 - j, 3)
    dn = (dp - 1 + 4 * wrap_dn, lax.rem(f + 8 * wrap_dn, 16))
    wrap = lax.div(j + 2, 4)
    up2 = (dp + 2 - 4 * wrap, lax.rem(f + 8 * wrap, 16))
    wrap = lax.div(3 - j, 2)
    dn2 = (dp - 2 + 4 * wrap, lax.rem(f + 8 * wrap, 16))

    barrier = pltpu.get_barrier_semaphore()
    for who in (sib, xp, xm, zp, zm, up, dn, up2, dn2):
        pl.semaphore_signal(barrier, inc=1, device_id=who, device_id_type=MESH)
    pl.semaphore_wait(barrier, 9)
    for d in loads:
        d.wait()

    def copy(src, dst, send, recv, who):
        return pltpu.make_async_remote_copy(
            src_ref=src, dst_ref=dst, send_sem=send, recv_sem=recv, device_id=who, device_id_type=MESH
        )

    def part(ref, h):
        return ref.at[pl.ds(HALF * h, HALF), :]

    def send_x(k, src, h):
        @pl.when(jnp.logical_and(k <= 3 - j, j >= 1))
        def _():
            copy(part(src, h), part(xbuf.at[k + 1], h), x_s.at[k, h], x_r.at[k + 1, h], dn).start()

        @pl.when(jnp.logical_and(k > 3 - j, j <= 2))
        def _():
            copy(part(src, h), part(xbuf.at[k - 1], h), x_s.at[k, h], x_r.at[k - 1, h], up).start()

    def send_p(k, src, h):
        @pl.when(jnp.logical_and(k <= j, j <= 1))
        def _():
            copy(part(src, h), part(pbuf.at[k + 1], h), p_s.at[k, h], p_r.at[k + 1, h], up).start()

        @pl.when(jnp.logical_and(k > j, j >= 2))
        def _():
            copy(part(src, h), part(pbuf.at[k - 1], h), p_s.at[k, h], p_r.at[k - 1, h], dn).start()

    def wait_x(k, h, whole=False):
        dst = xbuf.at[k] if whole else part(xbuf.at[k], h)
        copy(dst, dst, x_s.at[k, h], x_r.at[k, h], up).wait_recv()

    def quarter(k, q):
        return xbuf.at[k, pl.ds(HALF // 2 * q, HALF // 2), :]

    hop_in = [copy(quarter(4, q), quarter(4, q), x_s.at[5, q], x_r.at[4, q], zm) for q in range(4)]
    hop_up = [copy(quarter(4, q), quarter(3, q), x_s.at[4, q], x_r.at[3, q // 2], up) for q in range(4)]

    def wait_p(k, h):
        dst = part(pbuf.at[k], h)
        copy(dst, dst, p_s.at[k, h], p_r.at[k, h], up).wait_recv()

    def pass_x(k, h):
        wait_x(k, h)
        send_x(k, xbuf.at[k], h)

    def pass_p(k):
        for h in range(2):
            wait_p(k, h)
            send_p(k, pbuf.at[k], h)

    def x_done(k, src):
        @pl.when(jnp.logical_or(jnp.logical_and(k <= 3 - j, j >= 1), jnp.logical_and(k > 3 - j, j <= 2)))
        def _():
            for h in range(2):
                copy(part(src, h), part(xbuf.at[1], h), x_s.at[k, h], x_r.at[1, h], up).wait_send()

    def p_done(k, src):
        @pl.when(jnp.logical_or(jnp.logical_and(k <= j, j <= 1), jnp.logical_and(k > j, j >= 2)))
        def _():
            for h in range(2):
                copy(part(src, h), part(pbuf.at[1], h), p_s.at[k, h], p_r.at[1, h], up).wait_send()

    middle = lax.rem(lax.div(j + 1, 2), 2)
    outer = middle == 0
    inner = middle == 1
    xk0 = 1 + 2 * lax.div(j, 3)
    xk1 = 2 + middle
    xk2 = 6 - xk0 - xk1
    guest = copy(img, xbuf.at[5], x_s.at[6, 0], x_r.at[5, 0], up)

    w_swap = copy(wsh, wtmp, w_s.at[0], w_r.at[0], sib)
    w_swap.start()
    pool_swap = copy(pool, psib, h_s.at[2], h_r.at[2], sib)
    x_hop = [
        copy(img.at[pl.ds(HALF // 2 * q, HALF // 2), :], quarter(4, q), x_s.at[5, q], x_r.at[4, q], zm)
        for q in range(4)
    ]
    p_hop = [copy(part(pool, h), part(pbuf.at[4], h), p_s.at[5, h], p_r.at[4, h], zp) for h in range(2)]

    @pl.when(j <= 2)
    def _():
        for d in x_hop:
            d.start()

    send_x(0, img, 0)
    send_x(0, img, 1)

    @pl.when(j == 1)
    def _():
        send_p(0, pool, 0)

    @pl.when(j >= 1)
    def _():
        for d in p_hop:
            d.start()

    v, xr = normalize(img[...].astype(F32))
    ximg[...] = v
    xb[0] = v.astype(BF16)

    def chip(h, off):
        return h * 4 + lax.rem(x + off, 4)

    def rows_of(m, start, size):
        return wf.at[pl.ds(pl.multiple_of(m * CHIP + start, 16), size), :]

    def piece(m, p):
        return rows_of(m, 64 * c, AHEAD) if p == 0 else rows_of(m, 64 * c + AHEAD, UNIT - AHEAD)

    def w_copy(src, dst, ident, who, send=None):
        return copy(src, dst, w_s.at[ident if send is None else send], w_r.at[ident], who)

    w_sent = []

    def w_go(src, ident, who):
        d = w_copy(src, src, ident, who)
        d.start()
        w_sent.append(d)

    mine = chip(yh, 0)
    theirs = chip(1 - yh, 0)
    w_swap.wait_recv()
    own_rows = wsh[...].astype(F32)
    sib_rows = wtmp[...].astype(F32)
    first = c == 0
    wf[pl.ds(pl.multiple_of(mine * CHIP, 16), CHIP), :] = jnp.concatenate(
        [jnp.where(first, own_rows, sib_rows), jnp.where(first, sib_rows, own_rows)], axis=0
    ).astype(BF16)

    edge_up = [w_copy(piece(mine, p), piece(mine, p), 13 + p, up) for p in range(2)]
    edge_dn = [w_copy(piece(mine, p), piece(mine, p), 13 + p, dn) for p in range(2)]
    pass_up = [w_copy(piece(theirs, p), piece(theirs, p), 13 + p, up, 15 + p) for p in range(2)]
    pass_dn = [w_copy(piece(theirs, p), piece(theirs, p), 13 + p, dn, 15 + p) for p in range(2)]

    @pl.when(j == 3)
    def _():
        for d in edge_up:
            d.start()

    @pl.when(j == 0)
    def _():
        for d in edge_dn:
            d.start()

    def along_x(r, m):
        return {
            (d, p): w_copy(piece(m, p), piece(m, p), 1 + 4 * r + 2 * d + p, xp if d == 0 else xm)
            for d in range(2)
            for p in range(2)
        }

    mine_x = along_x(0, mine)
    theirs_x = along_x(1, theirs)
    for key in ((0, 0), (1, 1), (0, 1), (1, 0)):
        mine_x[key].start()
    w_sent.extend(mine_x.values())
    w_sent.extend(theirs_x.values())
    pool_swap.start()

    def slab_rows(n):
        m = chip(1 - yh if n < 4 else yh, ORDER[n % 4])
        return ptf[pl.ds(pl.multiple_of(m * CHIP + SHARD * c, 8), SHARD), :]

    def transpose_into(ref, start):
        ptf[...] = ref[...].astype(F32).T
        for n in range(0, 8, 2):
            pt[SHARD * n:SHARD * (n + 2), start:start + ROWS] = jnp.concatenate(
                [slab_rows(n), slab_rows(n + 1)], axis=0
            ).astype(BF16)

    def to_sibling(m, ident):
        w_go(rows_of(m, 80 * c, PART), ident, sib)

    def near_first(r, h):
        for d, (off, onward) in enumerate(((3, xp), (1, xm))):
            got = piece(chip(h, off), d)
            w_copy(got, got, 1 + 4 * r + 3 * d, xp).wait_recv()
            w_go(got, 9 + 2 * r + d, onward)

    def near_rest(r, h):
        for d, off in enumerate((3, 1)):
            m = chip(h, off)
            got = piece(m, 1 - d)
            w_copy(got, got, 2 + 4 * r + d, xp).wait_recv()
            to_sibling(m, 17 + 4 * r + d)

    def far_units(r, h):
        m = chip(h, 2)
        for p in range(2):
            w_copy(piece(m, p), piece(m, p), 9 + 2 * r + p, xp).wait_recv()
        to_sibling(m, 19 + 4 * r)

    edge_in = [w_copy(piece(theirs, p), piece(theirs, p), 13 + p, xp) for p in range(2)]
    theirs_part = rows_of(theirs, 80 * c, PART)
    theirs_sib = w_copy(theirs_part, theirs_part, 20, sib)
    w_sent.append(theirs_sib)

    def theirs_first():
        edge_in[0].wait_recv()

        @pl.when(j == 0)
        def _():
            pass_up[0].start()

        @pl.when(j == 3)
        def _():
            pass_dn[0].start()

        theirs_x[0, 0].start()

    def theirs_rest():
        edge_in[1].wait_recv()

        @pl.when(j == 0)
        def _():
            pass_up[1].start()

        @pl.when(j == 3)
        def _():
            pass_dn[1].start()

        for key in ((1, 1), (0, 1), (1, 0)):
            theirs_x[key].start()
        theirs_sib.start()

    def hop_on(h):
        @pl.when(j <= 2)
        def _():
            for q in (2 * h, 2 * h + 1):
                hop_in[q].wait_recv()
                hop_up[q].start()

        @pl.when(inner)
        def _():
            pass_x(1, h)

    hop_on(0)
    transpose_into(pool, 0)

    @pl.when(outer)
    def _():
        theirs_first()

    near_first(0, yh)

    @pl.when(outer)
    def _():
        theirs_rest()

    hop_on(1)
    near_rest(0, yh)
    pool_swap.wait_recv()
    transpose_into(psib, ROWS)

    @pl.when(j == 0)
    def _():
        send_p(0, pool, 0)
        send_p(0, pool, 1)
        guest.start()

    @pl.when(j == 3)
    def _():
        pass_p(4)

    @pl.when(inner)
    def _():
        pass_x(3, 0)
        theirs_first()

    far_units(0, yh)

    @pl.when(inner)
    def _():
        pass_x(3, 1)
        theirs_rest()
        pass_x(2, 0)

    near_first(1, 1 - yh)

    @pl.when(inner)
    def _():
        pass_x(2, 1)

    near_rest(1, 1 - yh)

    @pl.when(j == 1)
    def _():
        send_p(0, pool, 1)
        pass_p(1)

    @pl.when(j == 2)
    def _():
        pass_p(4)

    far_units(1, 1 - yh)

    @pl.when(j == 2)
    def _():
        pass_p(3)

    def ready(k):
        xb[k] = normalize(xbuf[k].astype(F32))[0].astype(BF16)

    @pl.when(inner)
    def _():
        for k in range(1, 4):
            ready(k)

    for ident, m in (
        (17, chip(yh, 3)), (18, chip(yh, 1)), (19, chip(yh, 2)), (20, theirs),
        (21, chip(1 - yh, 3)), (22, chip(1 - yh, 1)), (23, chip(1 - yh, 2)),
    ):
        got = rows_of(m, 80 - 80 * c, PART)
        w_copy(got, got, ident, sib).wait_recv()

    temper = jnp.exp(jnp.full((1, 1), log_scale[0], F32))
    offset = jnp.full((1, 1), bias[0], F32)
    gain = temper * (1.0 / ROWS)

    def project(block, out):
        for start in range(0, WIDTH, 512):
            cols = pl.ds(start, min(512, WIDTH - start))
            out[:, cols] = jnp.dot(block, wf[:, cols], preferred_element_type=F32) + hb[:, cols]

    def weights(a, b, own):
        l = temper * lax.dot_general(a, b, NT, preferred_element_type=F32) + offset
        if own:
            eye = lax.broadcasted_iota(jnp.int32, l.shape, 0) == lax.broadcasted_iota(jnp.int32, l.shape, 1)
            l = jnp.where(eye, -l, l)
        g = gain / (1.0 + jnp.exp(-l))
        if own:
            g = jnp.where(eye, -g, g)
        return l, g.astype(BF16)

    def losses(m):
        e = jnp.maximum(m, 0.0) + jnp.log1p(jnp.exp(-jnp.abs(m)))
        total = e[:, :ROWS]
        for start in range(ROWS, m.shape[1], ROWS):
            total = total + e[:, start:start + ROWS]
        return jnp.sum(total.T, axis=0, keepdims=True)

    def image_side(d, row):
        loss_out[...] = row * (1.0 / ROWS)
        stores[0].start()
        v = ximg[...]
        img_out[...] = (xr * (d - v * jnp.sum(v * d, axis=-1, keepdims=True))).astype(BF16)
        stores[1].start()

    project(pool[...], ztxt)
    v, zr = normalize(ztxt[...])
    ztxt[...] = v
    zb[0] = v.astype(BF16)

    def text_grad(a, own):
        _, g = weights(zb[0], a, own)
        return jnp.dot(g, a, preferred_element_type=F32)

    def text_side(d):
        v = ztxt[...]
        dzb[:ROWS] = (zr * (d - v * jnp.sum(v * d, axis=-1, keepdims=True))).astype(BF16)

    @pl.when(inner)
    def _():
        text_side(text_grad(xb[0:4].reshape(4 * ROWS, WIDTH), True))

    @pl.when(outer)
    def _():
        for k in (xk0, xk1):
            wait_x(k, 0)
            wait_x(k, 1)
            ready(k)
        u[:ROWS] = text_grad(xb[0], True) + text_grad(xb[xk0], False) + text_grad(xb[xk1], False)
        wait_x(xk2, 0)
        wait_x(xk2, 1)
        ready(xk2)
        text_side(u[:ROWS] + text_grad(xb[xk2], False))

    pair = copy(dzb.at[:ROWS], dzb.at[ROWS:], h_s.at[3], h_r.at[3], sib)
    pair.start()

    def make(n):
        t = jnp.dot(pt[SHARD * n:SHARD * (n + 2), :], dzb[...], preferred_element_type=F32)
        terms[n] = t[:SHARD]
        terms[n + 1] = t[SHARD:]

    def pair_a(n):
        return terms[n, :, :SPLIT]

    def pair_b(n):
        return terms[n, :, SPLIT:]

    g_sent = []

    def g_go(src, value, ident, dst, who):
        src[...] = value.astype(BF16)
        d = copy(src, dst, g_s.at[ident], g_r.at[ident], who)
        d.start()
        g_sent.append(d)

    def g_wait(ref, ident):
        copy(ref, ref, g_s.at[ident], g_r.at[ident], xp).wait_recv()
        return ref[...].astype(F32)

    def first_sends(g):
        n = 4 * g
        g_go(st_a.at[g, 0], pair_a(n), 6 * g, far_a.at[g], xp)
        g_go(st_b.at[g, 0], pair_b(n), 6 * g + 1, far_b.at[g], xm)
        g_go(st_b.at[g, 1], pair_b(n + 1), 6 * g + 2, near_b.at[g, 0], xp)
        g_go(st_a.at[g, 1], pair_a(n + 2), 6 * g + 3, near_a.at[g, 1], xm)

    def second_sends(g):
        n = 4 * g
        g_go(st_a.at[g, 2], pair_a(n + 1) + g_wait(far_a.at[g], 6 * g), 6 * g + 4, near_a.at[g, 0], xp)
        g_go(st_b.at[g, 2], pair_b(n + 2) + g_wait(far_b.at[g], 6 * g + 1), 6 * g + 5, near_b.at[g, 1], xm)

    def sums(g):
        n = 4 * g + 3
        a = pair_a(n) + g_wait(near_a.at[g, 0], 6 * g + 4) + g_wait(near_a.at[g, 1], 6 * g + 3)
        b = pair_b(n) + g_wait(near_b.at[g, 0], 6 * g + 2) + g_wait(near_b.at[g, 1], 6 * g + 5)
        return a, b

    def back():
        @pl.loop(0, WIDTH // TILE)
        def _(n):
            cols = pl.ds(pl.multiple_of(n * TILE, TILE), TILE)
            pool_out[:, cols] = lax.dot_general(
                dzb[:ROWS], wf[cols, :], NT, preferred_element_type=F32
            ).astype(BF16)

        stores[2].start()

    gdx_up = copy(gdx_out, gdx_in, h_s.at[0], h_r.at[0], up)
    gdx_dn = copy(gdx_out, gdx_in, h_s.at[0], h_r.at[0], dn)
    gsum_up = copy(gsum_out, gsum_in, h_s.at[1], h_r.at[1], up)
    gsum_dn = copy(gsum_out, gsum_in, h_s.at[1], h_r.at[1], dn)

    @pl.when(outer)
    def _():
        m, g = weights(xb[0], zb[0], True)
        u[ROWS:2 * ROWS] = jnp.dot(g, zb[0], preferred_element_type=F32)
        loss_out[...] = losses(m)

    pair.wait_recv()
    make(0)
    make(2)
    first_sends(0)
    make(4)
    make(6)

    @pl.when(outer)
    def _():
        back()

    second_sends(0)
    first_sends(1)

    @pl.when(j == 1)
    def _():
        for h in range(2):
            wait_p(4, h)
            wait_p(3, h)
        wait_x(5, 0, whole=True)
        ready(5)

    @pl.when(j == 2)
    def _():
        for h in range(2):
            wait_p(1, h)

    @pl.when(inner)
    def _():
        for h in range(2):
            wait_p(2, h)
        project(pbuf[1:5].reshape(4 * ROWS, WIDTH), u)

    a, b = sums(0)
    g_go(y_a, a, 12, pass_a, up2)
    g_go(y_b, b, 13, pass_b, dn2)

    onward = [
        copy(pass_a, in_a, g_s.at[14], g_r.at[14], up2),
        copy(pass_b, in_b, g_s.at[15], g_r.at[15], dn2),
    ]

    def relay():
        for ref, ident, d in ((pass_a, 12, onward[0]), (pass_b, 13, onward[1])):
            copy(ref, ref, g_s.at[ident], g_r.at[ident], xp).wait_recv()
            d.start()

    @pl.when(outer)
    def _():
        relay()

    second_sends(1)

    @pl.when(inner)
    def _():
        @pl.loop(1, 5)
        def _(k):
            zb[k] = normalize(u[pl.ds(pl.multiple_of((k - 1) * ROWS, ROWS), ROWS), :])[0].astype(BF16)

        hosted = zb[pl.ds(4 - 2 * j, 3)].reshape(3 * ROWS, WIDTH)
        m, g = weights(xb[9 - 4 * j], hosted, False)
        gdx_out[...] = jnp.dot(g, hosted, preferred_element_type=F32).astype(BF16)
        gsum_out[...] = losses(m)

        @pl.when(j == 1)
        def _():
            gdx_dn.start()
            gsum_dn.start()

        @pl.when(j == 2)
        def _():
            gdx_up.start()
            gsum_up.start()

        texts = zb[0:4].reshape(4 * ROWS, WIDTH)
        m, g = weights(xb[0], texts, True)
        image_side(jnp.dot(g, texts, preferred_element_type=F32), losses(m))
        back()

    a, b = sums(1)
    head_out[:, :SPLIT] = a
    head_out[:, SPLIT:] = b

    @pl.when(inner)
    def _():
        relay()

    @pl.when(outer)
    def _():
        gsum_up.wait_recv()
        gdx_up.wait_recv()
        image_side(u[ROWS:2 * ROWS] + gdx_in[...].astype(F32), loss_out[...] + gsum_in[...])

    head_out[:, :SPLIT] += g_wait(in_a, 14)
    head_out[:, SPLIT:] += g_wait(in_b, 15)
    stores[3].start()

    w_swap.wait_send()
    for d in w_sent:
        d.wait_send()

    @pl.when(j == 3)
    def _():
        for d in edge_up + pass_dn:
            d.wait_send()

    @pl.when(j == 0)
    def _():
        for d in edge_dn + pass_up:
            d.wait_send()

    @pl.when(j <= 2)
    def _():
        for d in x_hop + hop_up:
            d.wait_send()

    @pl.when(j >= 1)
    def _():
        for d in p_hop:
            d.wait_send()

    @pl.when(j == 0)
    def _():
        guest.wait_send()

    @pl.when(inner)
    def _():
        gdx_up.wait_send()
        gsum_up.wait_send()

    x_done(0, img)
    p_done(0, pool)
    for k in range(1, 4):
        x_done(k, xbuf.at[k])
        p_done(k, pbuf.at[k])
    p_done(4, pbuf.at[4])
    pool_swap.wait_send()
    pair.wait_send()
    for d in g_sent + onward:
        d.wait_send()
    for d in stores:
        d.wait()


def finish(*refs):
    into, out = refs[12], refs[13]
    loads = [pltpu.make_async_copy(refs[i], refs[8 + i], into.at[i]) for i in range(4)]
    stores = [pltpu.make_async_copy(refs[8 + i], refs[4 + i], out.at[i]) for i in range(4)]
    for d in loads:
        d.start()
    for d, e in zip(loads, stores):
        d.wait()
        e.start()
    for e in stores:
        e.wait()


def per_device(images, pooled, head_weight, head_bias, log_scale, bias):
    smem = pl.BlockSpec(memory_space=pltpu.SMEM)
    hbm = pl.BlockSpec(memory_space=pltpu.HBM)
    block = (ROWS, WIDTH)
    slab = (SHARD, WIDTH)
    slab_a = (SHARD, SPLIT)
    slab_b = (SHARD, WIDTH - SPLIT)
    dma = pltpu.SemaphoreType.DMA
    results = (
        jax.ShapeDtypeStruct((1, ROWS), F32),
        jax.ShapeDtypeStruct(block, BF16),
        jax.ShapeDtypeStruct(block, BF16),
        jax.ShapeDtypeStruct(slab, F32),
    )
    made = pl.pallas_call(
        kernel,
        out_shape=results,
        in_specs=[hbm, hbm, hbm, hbm, smem, smem],
        out_specs=(hbm, hbm, hbm, hbm),
        scratch_shapes=[
            pltpu.VMEM(block, BF16),
            pltpu.VMEM(block, BF16),
            pltpu.VMEM(slab, BF16),
            pltpu.VMEM((1, WIDTH), F32),
            pltpu.VMEM((1, ROWS), F32),
            pltpu.VMEM(block, BF16),
            pltpu.VMEM(block, BF16),
            pltpu.VMEM(slab, F32),
            pltpu.VMEM(slab, BF16),
            pltpu.VMEM((WIDTH, WIDTH), BF16),
            pltpu.VMEM((6,) + block, BF16),
            pltpu.VMEM((5,) + block, BF16),
            pltpu.VMEM((6,) + block, BF16),
            pltpu.VMEM((5,) + block, BF16),
            pltpu.VMEM(block, F32),
            pltpu.VMEM(block, F32),
            pltpu.VMEM((4 * ROWS, WIDTH), F32),
            pltpu.VMEM((2 * ROWS, WIDTH), BF16),
            pltpu.VMEM(block, BF16),
            pltpu.VMEM((WIDTH, ROWS), F32),
            pltpu.VMEM((8 * SHARD, 2 * ROWS), BF16),
            pltpu.VMEM((8,) + slab, F32),
            pltpu.VMEM((2, 3) + slab_a, BF16),
            pltpu.VMEM((2, 3) + slab_b, BF16),
            pltpu.VMEM((2,) + slab_a, BF16),
            pltpu.VMEM((2,) + slab_b, BF16),
            pltpu.VMEM((2, 2) + slab_a, BF16),
            pltpu.VMEM((2, 2) + slab_b, BF16),
            pltpu.VMEM(slab_a, BF16),
            pltpu.VMEM(slab_b, BF16),
            pltpu.VMEM(slab_a, BF16),
            pltpu.VMEM(slab_b, BF16),
            pltpu.VMEM(slab_a, BF16),
            pltpu.VMEM(slab_b, BF16),
            pltpu.VMEM(block, BF16),
            pltpu.VMEM((1, ROWS), F32),
            pltpu.VMEM(block, BF16),
            pltpu.VMEM((1, ROWS), F32),
            dma((4,)), dma((4,)),
            dma((24,)), dma((24,)),
            dma((7, 4)), dma((6, 4)),
            dma((6, 2)), dma((5, 2)),
            dma((16,)), dma((16,)),
            dma((4,)), dma((4,)),
        ],
        compiler_params=pltpu.CompilerParams(
            collective_id=0, has_side_effects=True, vmem_limit_bytes=VMEM_GRANT
        ),
        cost_estimate=pl.CostEstimate(flops=4_000_000_000, bytes_accessed=6_000_000, transcendentals=300_000),
    )(images, pooled, head_weight, head_bias, log_scale, bias)
    loss, image_grad, pooled_grad, head_grad = pl.pallas_call(
        finish,
        out_shape=results,
        in_specs=[hbm] * 4,
        out_specs=(hbm,) * 4,
        scratch_shapes=[pltpu.VMEM(r.shape, r.dtype) for r in results] + [dma((4,)), dma((4,))],
        compiler_params=pltpu.CompilerParams(vmem_limit_bytes=VMEM_GRANT),
    )(*made)
    return loss.reshape(ROWS), image_grad, pooled_grad, head_grad


def solution(mesh):
    in_specs = (P(("dp", "fsdp"), None), P(("dp", "fsdp"), None), P("fsdp", None), P(), P(), P())
    out_specs = (
        P(("dp", "fsdp")),
        P(("dp", "fsdp"), None),
        P(("dp", "fsdp"), None),
        P(("dp", "fsdp"), None),
    )
    return jax.shard_map(
        per_device, mesh=mesh, in_specs=in_specs, out_specs=out_specs, check_vma=False
    )
```

```python
import jax
import jax.numpy as jnp
from jax import lax
from jax.experimental import pallas as pl
from jax.experimental.pallas import tpu as pltpu
from jax.sharding import PartitionSpec as P

MESH = pl.DeviceIdType.MESH
F32 = jnp.float32
BF16 = jnp.bfloat16
NT = (((1,), (1,)), ((), ()))

ROWS = 128
WIDTH = 1152
SHARD = 72
CHIP = 144
UNIT = 80
PART = 64
AHEAD = 48
TILE = 384
VMEM_GRANT = 60 * 1024 * 1024
HALF = 64
SPLIT = 640
PLACE = {1: 0, 3: 1, 4: 2, 2: 3}
ORDER = (2, 1, 3, 0)


def normalize(v):
    r = lax.rsqrt(jnp.sum(v * v, axis=-1, keepdims=True) + 1e-06)
    return v * r, r


def kernel(
    img_hbm, pool_hbm, wsh_hbm, hb_hbm, log_scale, bias,
    loss_hbm, img_grad_hbm, pool_grad_hbm, head_grad_hbm,
    img, pool, wsh, hb, loss_out, img_out, pool_out, head_out,
    wtmp, wf, xbuf, pbuf, xb, zb, ximg, ztxt, u, dzb, psib, ptf, pt, terms,
    st_a, st_b, far_a, far_b, near_a, near_b,
    y_a, y_b, pass_a, pass_b, in_a, in_b,
    gdx, gdx_out, gsum_out, gdx_in, gsum_in,
    l_s, o_s, w_s, w_r, x_s, x_r, p_s, p_r, g_s, g_r, h_s, h_r,
):
    loads = [
        pltpu.make_async_copy(src, dst, l_s.at[i])
        for i, (src, dst) in enumerate(
            ((wsh_hbm, wsh), (img_hbm, img), (pool_hbm, pool), (hb_hbm, hb.at[0]))
        )
    ]
    for d in loads:
        d.start()
    stores = [
        pltpu.make_async_copy(src, dst, o_s.at[i])
        for i, (src, dst) in enumerate(
            ((loss_out, loss_hbm), (img_out, img_grad_hbm), (pool_out, pool_grad_hbm), (head_out, head_grad_hbm))
        )
    ]

    dp = lax.axis_index("dp")
    f = lax.axis_index("fsdp")
    j = lax.rem(dp, 4)
    yh = lax.div(f, 8)
    x = lax.rem(lax.div(f, 2), 4)
    c = lax.rem(f, 2)
    base = yh * 8 + c

    sib = (dp, f + 1 - 2 * c)
    xp = (dp, base + 2 * lax.rem(x + 1, 4))
    xm = (dp, base + 2 * lax.rem(x + 3, 4))
    zp = (lax.rem(dp + 4, 32), f)
    zm = (lax.rem(dp + 28, 32), f)
    wrap_up = lax.div(j + 1, 4)
    up = (dp + 1 - 4 * wrap_up, lax.rem(f + 8 * wrap_up, 16))
    wrap_dn = lax.div(3 - j, 3)
    dn = (dp - 1 + 4 * wrap_dn, lax.rem(f + 8 * wrap_dn, 16))
    wrap = lax.div(j + 2, 4)
    up2 = (dp + 2 - 4 * wrap, lax.rem(f + 8 * wrap, 16))
    wrap = lax.div(3 - j, 2)
    dn2 = (dp - 2 + 4 * wrap, lax.rem(f + 8 * wrap, 16))

    barrier = pltpu.get_barrier_semaphore()
    for who in (sib, xp, xm, zp, zm, up, dn, up2, dn2):
        pl.semaphore_signal(barrier, inc=1, device_id=who, device_id_type=MESH)
    pl.semaphore_wait(barrier, 9)
    for d in loads:
        d.wait()

    def copy(src, dst, send, recv, who):
        return pltpu.make_async_remote_copy(
            src_ref=src, dst_ref=dst, send_sem=send, recv_sem=recv, device_id=who, device_id_type=MESH
        )

    def part(ref, h):
        return ref.at[pl.ds(HALF * h, HALF), :]

    def send_x(k, src, h):
        @pl.when(jnp.logical_and(k <= 3 - j, j >= 1))
        def _():
            copy(part(src, h), part(xbuf.at[k + 1], h), x_s.at[k, h], x_r.at[k + 1, h], dn).start()

        @pl.when(jnp.logical_and(k > 3 - j, j <= 2))
        def _():
            copy(part(src, h), part(xbuf.at[k - 1], h), x_s.at[k, h], x_r.at[k - 1, h], up).start()

    def send_p(k, src, h):
        if k < 4:
          @pl.when(jnp.logical_and(k <= j, j <= 1))
          def _():
            copy(part(src, h), part(pbuf.at[PLACE[k + 1]], h), p_s.at[k, h], p_r.at[k + 1, h], up).start()

        if k > 2:
          @pl.when(jnp.logical_and(k > j, j >= 2))
          def _():
            copy(part(src, h), part(pbuf.at[PLACE[k - 1]], h), p_s.at[k, h], p_r.at[k - 1, h], dn).start()

    def wait_x(k, h, whole=False):
        dst = xbuf.at[k] if whole else part(xbuf.at[k], h)
        copy(dst, dst, x_s.at[k, h], x_r.at[k, h], up).wait_recv()

    def quarter(k, q):
        return xbuf.at[k, pl.ds(HALF // 2 * q, HALF // 2), :]

    hop_in = [copy(quarter(4, q), quarter(4, q), x_s.at[5, q], x_r.at[4, q], zm) for q in range(4)]
    hop_up = [copy(quarter(4, q), quarter(3, q), x_s.at[4, q], x_r.at[3, q // 2], up) for q in range(4)]

    def wait_p(k, h):
        dst = part(pbuf.at[PLACE[k]], h)
        copy(dst, dst, p_s.at[k, h], p_r.at[k, h], up).wait_recv()

    def pass_x(k, h):
        wait_x(k, h)
        send_x(k, xbuf.at[k], h)

    def pass_p(k):
        for h in range(2):
            wait_p(k, h)
            send_p(k, pbuf.at[PLACE[k]], h)

    def x_done(k, src):
        @pl.when(jnp.logical_or(jnp.logical_and(k <= 3 - j, j >= 1), jnp.logical_and(k > 3 - j, j <= 2)))
        def _():
            for h in range(2):
                copy(part(src, h), part(xbuf.at[1], h), x_s.at[k, h], x_r.at[1, h], up).wait_send()

    def p_done(k, src):
        @pl.when(jnp.logical_or(jnp.logical_and(k <= j, j <= 1), jnp.logical_and(k > j, j >= 2)))
        def _():
            for h in range(2):
                copy(part(src, h), part(pbuf.at[0], h), p_s.at[k, h], p_r.at[1, h], up).wait_send()

    middle = lax.rem(lax.div(j + 1, 2), 2)
    outer = middle == 0
    inner = middle == 1
    xk0 = 1 + 2 * lax.div(j, 3)
    xk1 = 2 + middle
    xk2 = 6 - xk0 - xk1
    guest = copy(img, xbuf.at[5], x_s.at[6, 0], x_r.at[5, 0], up)

    w_swap = copy(wsh, wtmp, w_s.at[0], w_r.at[0], sib)
    w_swap.start()
    pool_swap = copy(pool, psib, h_s.at[2], h_r.at[2], sib)
    x_hop = [
        copy(img.at[pl.ds(HALF // 2 * q, HALF // 2), :], quarter(4, q), x_s.at[5, q], x_r.at[4, q], zm)
        for q in range(4)
    ]
    p_hop = [copy(part(pool, h), part(pbuf.at[PLACE[4]], h), p_s.at[5, h], p_r.at[4, h], zp) for h in range(2)]

    @pl.when(j <= 2)
    def _():
        for d in x_hop:
            d.start()

    send_x(0, img, 0)
    send_x(0, img, 1)

    @pl.when(j == 1)
    def _():
        send_p(0, pool, 0)

    @pl.when(j >= 1)
    def _():
        for d in p_hop:
            d.start()

    v, xr = normalize(img[...].astype(F32))
    ximg[...] = v
    xb[0] = v.astype(BF16)

    def chip(h, off):
        return h * 4 + lax.rem(x + off, 4)

    def rows_of(m, start, size):
        return wf.at[pl.ds(pl.multiple_of(m * CHIP + start, 16), size), :]

    def piece(m, p):
        return rows_of(m, 64 * c, AHEAD) if p == 0 else rows_of(m, 64 * c + AHEAD, UNIT - AHEAD)

    def w_copy(src, dst, ident, who, send=None):
        return copy(src, dst, w_s.at[ident if send is None else send], w_r.at[ident], who)

    w_sent = []

    def w_go(src, ident, who):
        d = w_copy(src, src, ident, who)
        d.start()
        w_sent.append(d)

    mine = chip(yh, 0)
    theirs = chip(1 - yh, 0)
    w_swap.wait_recv()
    own_rows = wsh[...].astype(F32)
    sib_rows = wtmp[...].astype(F32)
    first = c == 0
    wf[pl.ds(pl.multiple_of(mine * CHIP, 16), CHIP), :] = jnp.concatenate(
        [jnp.where(first, own_rows, sib_rows), jnp.where(first, sib_rows, own_rows)], axis=0
    ).astype(BF16)

    edge_up = [w_copy(piece(mine, p), piece(mine, p), 13 + p, up) for p in range(2)]
    edge_dn = [w_copy(piece(mine, p), piece(mine, p), 13 + p, dn) for p in range(2)]
    pass_up = [w_copy(piece(theirs, p), piece(theirs, p), 13 + p, up, 15 + p) for p in range(2)]
    pass_dn = [w_copy(piece(theirs, p), piece(theirs, p), 13 + p, dn, 15 + p) for p in range(2)]

    @pl.when(j == 3)
    def _():
        for d in edge_up:
            d.start()

    @pl.when(j == 0)
    def _():
        for d in edge_dn:
            d.start()

    def along_x(r, m):
        return {
            (d, p): w_copy(piece(m, p), piece(m, p), 1 + 4 * r + 2 * d + p, xp if d == 0 else xm)
            for d in range(2)
            for p in range(2)
        }

    mine_x = along_x(0, mine)
    theirs_x = along_x(1, theirs)
    for key in ((0, 0), (1, 1), (0, 1), (1, 0)):
        mine_x[key].start()
    w_sent.extend(mine_x.values())
    w_sent.extend(theirs_x.values())
    pool_swap.start()

    def slab_rows(n):
        m = chip(1 - yh if n < 4 else yh, ORDER[n % 4])
        return ptf[pl.ds(pl.multiple_of(m * CHIP + SHARD * c, 8), SHARD), :]

    def transpose_into(ref, start):
        ptf[...] = ref[...].astype(F32).T
        for n in range(0, 8, 2):
            pt[SHARD * n:SHARD * (n + 2), start:start + ROWS] = jnp.concatenate(
                [slab_rows(n), slab_rows(n + 1)], axis=0
            ).astype(BF16)

    def to_sibling(m, ident):
        w_go(rows_of(m, 80 * c, PART), ident, sib)

    def near_first(r, h):
        for d, (off, onward) in enumerate(((3, xp), (1, xm))):
            got = piece(chip(h, off), d)
            w_copy(got, got, 1 + 4 * r + 3 * d, xp).wait_recv()
            w_go(got, 9 + 2 * r + d, onward)

    def near_rest(r, h):
        for d, off in enumerate((3, 1)):
            m = chip(h, off)
            got = piece(m, 1 - d)
            w_copy(got, got, 2 + 4 * r + d, xp).wait_recv()
            to_sibling(m, 17 + 4 * r + d)

    def far_units(r, h):
        m = chip(h, 2)
        for p in range(2):
            w_copy(piece(m, p), piece(m, p), 9 + 2 * r + p, xp).wait_recv()
        to_sibling(m, 19 + 4 * r)

    edge_in = [w_copy(piece(theirs, p), piece(theirs, p), 13 + p, xp) for p in range(2)]
    theirs_part = rows_of(theirs, 80 * c, PART)
    theirs_sib = w_copy(theirs_part, theirs_part, 20, sib)
    w_sent.append(theirs_sib)

    def theirs_first():
        edge_in[0].wait_recv()

        @pl.when(j == 0)
        def _():
            pass_up[0].start()

        @pl.when(j == 3)
        def _():
            pass_dn[0].start()

        theirs_x[0, 0].start()

    def theirs_rest():
        edge_in[1].wait_recv()

        @pl.when(j == 0)
        def _():
            pass_up[1].start()

        @pl.when(j == 3)
        def _():
            pass_dn[1].start()

        for key in ((1, 1), (0, 1), (1, 0)):
            theirs_x[key].start()
        theirs_sib.start()

    def hop_on(h):
        @pl.when(j <= 2)
        def _():
            for q in (2 * h, 2 * h + 1):
                hop_in[q].wait_recv()
                hop_up[q].start()

        @pl.when(inner)
        def _():
            pass_x(1, h)

    hop_on(0)
    transpose_into(pool, 0)

    @pl.when(outer)
    def _():
        theirs_first()

    near_first(0, yh)

    @pl.when(outer)
    def _():
        theirs_rest()

    hop_on(1)
    near_rest(0, yh)
    pool_swap.wait_recv()
    transpose_into(psib, ROWS)

    @pl.when(j == 0)
    def _():
        send_p(0, pool, 0)
        send_p(0, pool, 1)
        guest.start()

    @pl.when(j == 3)
    def _():
        pass_p(4)

    @pl.when(inner)
    def _():
        pass_x(3, 0)
        theirs_first()

    far_units(0, yh)

    @pl.when(inner)
    def _():
        pass_x(3, 1)
        theirs_rest()
        pass_x(2, 0)

    @pl.when(j == 2)
    def _():
        pass_p(4)

    @pl.when(j == 1)
    def _():
        pass_x(2, 1)

    near_first(1, 1 - yh)

    @pl.when(j == 2)
    def _():
        pass_x(2, 1)

    @pl.when(j == 1)
    def _():
        send_p(0, pool, 1)

    near_rest(1, 1 - yh)

    @pl.when(j == 1)
    def _():
        pass_p(1)

    @pl.when(j == 2)
    def _():
        pass_p(3)

    far_units(1, 1 - yh)

    def ready(k):
        xb[k] = normalize(xbuf[k].astype(F32))[0].astype(BF16)

    @pl.when(inner)
    def _():
        for k in range(1, 4):
            ready(k)

    for ident, m in (
        (17, chip(yh, 3)), (18, chip(yh, 1)), (19, chip(yh, 2)), (20, theirs),
        (21, chip(1 - yh, 3)), (22, chip(1 - yh, 1)), (23, chip(1 - yh, 2)),
    ):
        got = rows_of(m, 80 - 80 * c, PART)
        w_copy(got, got, ident, sib).wait_recv()

    temper = jnp.exp(jnp.full((1, 1), log_scale[0], F32))
    offset = jnp.full((1, 1), bias[0], F32)
    gain = temper * (1.0 / ROWS)

    def project(block, out):
        for start in range(0, WIDTH, 512):
            cols = pl.ds(start, min(512, WIDTH - start))
            out[:, cols] = jnp.dot(block, wf[:, cols], preferred_element_type=F32) + hb[:, cols]

    def weights(a, b, own):
        l = temper * lax.dot_general(a, b, NT, preferred_element_type=F32) + offset
        if own:
            eye = lax.broadcasted_iota(jnp.int32, l.shape, 0) == lax.broadcasted_iota(jnp.int32, l.shape, 1)
            l = jnp.where(eye, -l, l)
        g = gain / (1.0 + jnp.exp(-l))
        if own:
            g = jnp.where(eye, -g, g)
        return l, g.astype(BF16)

    def losses(m):
        e = jnp.maximum(m, 0.0) + jnp.log1p(jnp.exp(-jnp.abs(m)))
        total = e[:, :ROWS]
        for start in range(ROWS, m.shape[1], ROWS):
            total = total + e[:, start:start + ROWS]
        return jnp.sum(total.T, axis=0, keepdims=True)

    def image_side(d, row):
        loss_out[...] = row * (1.0 / ROWS)
        stores[0].start()
        v = ximg[...]
        img_out[...] = (xr * (d - v * jnp.sum(v * d, axis=-1, keepdims=True))).astype(BF16)
        stores[1].start()

    project(pool[...], ztxt)
    v, zr = normalize(ztxt[...])
    ztxt[...] = v
    zb[0] = v.astype(BF16)

    def text_grad(a, own):
        _, g = weights(zb[0], a, own)
        return jnp.dot(g, a, preferred_element_type=F32)

    def text_side(d):
        v = ztxt[...]
        dzb[:ROWS] = (zr * (d - v * jnp.sum(v * d, axis=-1, keepdims=True))).astype(BF16)

    @pl.when(inner)
    def _():
        text_side(text_grad(xb[0:4].reshape(4 * ROWS, WIDTH), True))

    @pl.when(outer)
    def _():
        for k in (xk0, xk1):
            wait_x(k, 0)
            wait_x(k, 1)
            ready(k)
        u[:ROWS] = text_grad(xb[0], True) + text_grad(xb[xk0], False) + text_grad(xb[xk1], False)
        wait_x(xk2, 0)
        wait_x(xk2, 1)
        ready(xk2)
        text_side(u[:ROWS] + text_grad(xb[xk2], False))

    pair = copy(dzb.at[:ROWS], dzb.at[ROWS:], h_s.at[3], h_r.at[3], sib)
    pair.start()

    def make(n):
        t = jnp.dot(pt[SHARD * n:SHARD * (n + 2), :], dzb[...], preferred_element_type=F32)
        terms[n] = t[:SHARD]
        terms[n + 1] = t[SHARD:]

    def pair_a(n):
        return terms[n, :, :SPLIT]

    def pair_b(n):
        return terms[n, :, SPLIT:]

    g_sent = []

    def g_go(src, value, ident, dst, who):
        src[...] = value.astype(BF16)
        d = copy(src, dst, g_s.at[ident], g_r.at[ident], who)
        d.start()
        g_sent.append(d)

    def g_wait(ref, ident):
        copy(ref, ref, g_s.at[ident], g_r.at[ident], xp).wait_recv()
        return ref[...].astype(F32)

    def far_sends(g):
        n = 4 * g
        g_go(st_a.at[g, 0], pair_a(n), 6 * g, far_a.at[g], xp)
        g_go(st_b.at[g, 0], pair_b(n), 6 * g + 1, far_b.at[g], xm)

    def near_sends(g):
        n = 4 * g
        g_go(st_b.at[g, 1], pair_b(n + 1), 6 * g + 2, near_b.at[g, 0], xp)
        g_go(st_a.at[g, 1], pair_a(n + 2), 6 * g + 3, near_a.at[g, 1], xm)

    def second_sends(g):
        n = 4 * g
        g_go(st_a.at[g, 2], pair_a(n + 1) + g_wait(far_a.at[g], 6 * g), 6 * g + 4, near_a.at[g, 0], xp)
        g_go(st_b.at[g, 2], pair_b(n + 2) + g_wait(far_b.at[g], 6 * g + 1), 6 * g + 5, near_b.at[g, 1], xm)

    def sums(g):
        n = 4 * g + 3
        a = pair_a(n) + g_wait(near_a.at[g, 0], 6 * g + 4) + g_wait(near_a.at[g, 1], 6 * g + 3)
        b = pair_b(n) + g_wait(near_b.at[g, 0], 6 * g + 2) + g_wait(near_b.at[g, 1], 6 * g + 5)
        return a, b

    def back():
        @pl.loop(0, WIDTH // TILE)
        def _(n):
            cols = pl.ds(pl.multiple_of(n * TILE, TILE), TILE)
            pool_out[:, cols] = lax.dot_general(
                dzb[:ROWS], wf[cols, :], NT, preferred_element_type=F32
            ).astype(BF16)

        stores[2].start()

    gdx_up = copy(gdx_out, gdx_in, h_s.at[0], h_r.at[0], up)
    gdx_dn = copy(gdx_out, gdx_in, h_s.at[0], h_r.at[0], dn)
    gsum_up = copy(gsum_out, gsum_in, h_s.at[1], h_r.at[1], up)
    gsum_dn = copy(gsum_out, gsum_in, h_s.at[1], h_r.at[1], dn)

    @pl.when(outer)
    def _():
        m, g = weights(xb[0], zb[0], True)
        u[ROWS:2 * ROWS] = jnp.dot(g, zb[0], preferred_element_type=F32)
        loss_out[...] = losses(m)

    def texts_done(first, last):
        for n in range(first, last):
            v = u[ROWS * (n - 1):ROWS * n]
            zb[n] = normalize(v)[0].astype(BF16)

    def meet(image, texts, own):
        m, g = weights(image, texts, own)
        return jnp.dot(g, texts, preferred_element_type=F32), losses(m)

    @pl.when(j == 1)
    def _():
        for h in range(2):
            wait_p(3, h)
            wait_p(4, h)
        wait_x(5, 0, whole=True)
        ready(5)

    @pl.when(j == 2)
    def _():
        for h in range(2):
            wait_p(1, h)

    @pl.when(inner)
    def _():
        project(pbuf[0:3].reshape(3 * ROWS, WIDTH), u.at[:3 * ROWS])

    pair.wait_recv()
    make(0)
    far_sends(0)
    make(2)
    near_sends(0)
    make(4)
    make(6)

    @pl.when(inner)
    def _():
        texts_done(1, 4)
        d, row = meet(xb[9 - 4 * j], zb[pl.ds(4 - 2 * j, 2)].reshape(2 * ROWS, WIDTH), False)
        gdx[...] = d
        gsum_out[...] = row

    @pl.when(outer)
    def _():
        back()

    second_sends(0)
    far_sends(1)
    near_sends(1)

    @pl.when(inner)
    def _():
        for h in range(2):
            wait_p(2, h)
        project(pbuf[3], u.at[3 * ROWS:])
        texts_done(4, 5)
        d, row = meet(xb[9 - 4 * j], zb[4], False)
        gdx_out[...] = (gdx[...] + d).astype(BF16)
        gsum_out[...] += row

        @pl.when(j == 1)
        def _():
            gdx_dn.start()
            gsum_dn.start()

        @pl.when(j == 2)
        def _():
            gdx_up.start()
            gsum_up.start()

    a, b = sums(0)
    g_go(y_a, a, 12, pass_a, up2)
    g_go(y_b, b, 13, pass_b, dn2)

    onward = [
        copy(pass_a, in_a, g_s.at[14], g_r.at[14], up2),
        copy(pass_b, in_b, g_s.at[15], g_r.at[15], dn2),
    ]

    def relay():
        for ref, ident, d in ((pass_a, 12, onward[0]), (pass_b, 13, onward[1])):
            copy(ref, ref, g_s.at[ident], g_r.at[ident], xp).wait_recv()
            d.start()

    @pl.when(outer)
    def _():
        relay()

    second_sends(1)

    @pl.when(inner)
    def _():
        d, row = meet(xb[0], zb[0:3].reshape(3 * ROWS, WIDTH), True)
        e, more = meet(xb[0], zb[4], False)
        image_side(d + e, row + more)
        back()

    a, b = sums(1)
    head_out[:, :SPLIT] = a
    head_out[:, SPLIT:] = b

    @pl.when(inner)
    def _():
        relay()

    @pl.when(outer)
    def _():
        gsum_up.wait_recv()
        gdx_up.wait_recv()
        image_side(u[ROWS:2 * ROWS] + gdx_in[...].astype(F32), loss_out[...] + gsum_in[...])

    head_out[:, :SPLIT] += g_wait(in_a, 14)
    head_out[:, SPLIT:] += g_wait(in_b, 15)
    stores[3].start()

    w_swap.wait_send()
    for d in w_sent:
        d.wait_send()

    @pl.when(j == 3)
    def _():
        for d in edge_up + pass_dn:
            d.wait_send()

    @pl.when(j == 0)
    def _():
        for d in edge_dn + pass_up:
            d.wait_send()

    @pl.when(j <= 2)
    def _():
        for d in x_hop + hop_up:
            d.wait_send()

    @pl.when(j >= 1)
    def _():
        for d in p_hop:
            d.wait_send()

    @pl.when(j == 0)
    def _():
        guest.wait_send()

    @pl.when(inner)
    def _():
        gdx_up.wait_send()
        gsum_up.wait_send()

    x_done(0, img)
    p_done(0, pool)
    for k in range(1, 4):
        x_done(k, xbuf.at[k])
        p_done(k, pbuf.at[0])
    p_done(4, pbuf.at[0])
    pool_swap.wait_send()
    pair.wait_send()
    for d in g_sent + onward:
        d.wait_send()
    for d in stores:
        d.wait()


def finish(*refs):
    into, out = refs[12], refs[13]
    loads = [pltpu.make_async_copy(refs[i], refs[8 + i], into.at[i]) for i in range(4)]
    stores = [pltpu.make_async_copy(refs[8 + i], refs[4 + i], out.at[i]) for i in range(4)]
    for d in loads:
        d.start()
    for d, e in zip(loads, stores):
        d.wait()
        e.start()
    for e in stores:
        e.wait()


def per_device(images, pooled, head_weight, head_bias, log_scale, bias):
    smem = pl.BlockSpec(memory_space=pltpu.SMEM)
    hbm = pl.BlockSpec(memory_space=pltpu.HBM)
    block = (ROWS, WIDTH)
    slab = (SHARD, WIDTH)
    slab_a = (SHARD, SPLIT)
    slab_b = (SHARD, WIDTH - SPLIT)
    dma = pltpu.SemaphoreType.DMA
    results = (
        jax.ShapeDtypeStruct((1, ROWS), F32),
        jax.ShapeDtypeStruct(block, BF16),
        jax.ShapeDtypeStruct(block, BF16),
        jax.ShapeDtypeStruct(slab, F32),
    )
    made = pl.pallas_call(
        kernel,
        out_shape=results,
        in_specs=[hbm, hbm, hbm, hbm, smem, smem],
        out_specs=(hbm, hbm, hbm, hbm),
        scratch_shapes=[
            pltpu.VMEM(block, BF16),
            pltpu.VMEM(block, BF16),
            pltpu.VMEM(slab, BF16),
            pltpu.VMEM((1, WIDTH), F32),
            pltpu.VMEM((1, ROWS), F32),
            pltpu.VMEM(block, BF16),
            pltpu.VMEM(block, BF16),
            pltpu.VMEM(slab, F32),
            pltpu.VMEM(slab, BF16),
            pltpu.VMEM((WIDTH, WIDTH), BF16),
            pltpu.VMEM((6,) + block, BF16),
            pltpu.VMEM((4,) + block, BF16),
            pltpu.VMEM((6,) + block, BF16),
            pltpu.VMEM((5,) + block, BF16),
            pltpu.VMEM(block, F32),
            pltpu.VMEM(block, F32),
            pltpu.VMEM((4 * ROWS, WIDTH), F32),
            pltpu.VMEM((2 * ROWS, WIDTH), BF16),
            pltpu.VMEM(block, BF16),
            pltpu.VMEM((WIDTH, ROWS), F32),
            pltpu.VMEM((8 * SHARD, 2 * ROWS), BF16),
            pltpu.VMEM((8,) + slab, F32),
            pltpu.VMEM((2, 3) + slab_a, BF16),
            pltpu.VMEM((2, 3) + slab_b, BF16),
            pltpu.VMEM((2,) + slab_a, BF16),
            pltpu.VMEM((2,) + slab_b, BF16),
            pltpu.VMEM((2, 2) + slab_a, BF16),
            pltpu.VMEM((2, 2) + slab_b, BF16),
            pltpu.VMEM(slab_a, BF16),
            pltpu.VMEM(slab_b, BF16),
            pltpu.VMEM(slab_a, BF16),
            pltpu.VMEM(slab_b, BF16),
            pltpu.VMEM(slab_a, BF16),
            pltpu.VMEM(slab_b, BF16),
            pltpu.VMEM(block, F32),
            pltpu.VMEM(block, BF16),
            pltpu.VMEM((1, ROWS), F32),
            pltpu.VMEM(block, BF16),
            pltpu.VMEM((1, ROWS), F32),
            dma((4,)), dma((4,)),
            dma((24,)), dma((24,)),
            dma((7, 4)), dma((6, 4)),
            dma((6, 2)), dma((5, 2)),
            dma((16,)), dma((16,)),
            dma((4,)), dma((4,)),
        ],
        compiler_params=pltpu.CompilerParams(
            collective_id=0, has_side_effects=True, vmem_limit_bytes=VMEM_GRANT
        ),
        cost_estimate=pl.CostEstimate(flops=4_000_000_000, bytes_accessed=6_000_000, transcendentals=300_000),
    )(images, pooled, head_weight, head_bias, log_scale, bias)
    loss, image_grad, pooled_grad, head_grad = pl.pallas_call(
        finish,
        out_shape=results,
        in_specs=[hbm] * 4,
        out_specs=(hbm,) * 4,
        scratch_shapes=[pltpu.VMEM(r.shape, r.dtype) for r in results] + [dma((4,)), dma((4,))],
        compiler_params=pltpu.CompilerParams(vmem_limit_bytes=VMEM_GRANT),
    )(*made)
    return loss.reshape(ROWS), image_grad, pooled_grad, head_grad


def solution(mesh):
    in_specs = (P(("dp", "fsdp"), None), P(("dp", "fsdp"), None), P("fsdp", None), P(), P(), P())
    out_specs = (
        P(("dp", "fsdp")),
        P(("dp", "fsdp"), None),
        P(("dp", "fsdp"), None),
        P(("dp", "fsdp"), None),
    )
    return jax.shard_map(
        per_device, mesh=mesh, in_specs=in_specs, out_specs=out_specs, check_vma=False
    )
```

```python
import jax
import jax.numpy as jnp
from jax import lax
from jax.experimental import pallas as pl
from jax.experimental.pallas import tpu as pltpu
from jax.sharding import PartitionSpec as P

MESH = pl.DeviceIdType.MESH
F32 = jnp.float32
BF16 = jnp.bfloat16
NT = (((1,), (1,)), ((), ()))

ROWS = 128
WIDTH = 1152
SHARD = 72
CHIP = 144
UNIT = 80
PART = 64
AHEAD = 48
TILE = 384
VMEM_GRANT = 44 * 1024 * 1024
HALF = 64
PIECES = ((0, 384, 1), (640, 256, -1), (384, 256, 1), (896, 256, -1))
PLACE = {1: 0, 3: 1, 4: 2, 2: 3}
ORDER = (2, 1, 3, 0)


def normalize(v):
    r = lax.rsqrt(jnp.sum(v * v, axis=-1, keepdims=True) + 1e-06)
    return v * r, r


def kernel(
    img_hbm, pool_hbm, wsh_hbm, hb_hbm, log_scale, bias,
    loss_out, img_out, pool_out, head_out,
    img, pool, wsh, hb,
    wtmp, wf, xbuf, pbuf, xb, zb, ximg, ztxt, u, dzb, psib, ptf, pt, terms,
    g_out, g_far, g_near,
    y_out, y_pass, y_in,
    gdx, gdx_out, gsum_out, gdx_in, gsum_in,
    l_s, w_s, w_r, x_s, x_r, p_s, p_r, g_s, g_r, h_s, h_r,
):
    loads = [
        pltpu.make_async_copy(src, dst, l_s.at[i])
        for i, (src, dst) in enumerate(
            ((wsh_hbm, wsh), (img_hbm, img), (pool_hbm, pool), (hb_hbm, hb.at[0]))
        )
    ]
    for d in loads:
        d.start()
    dp = lax.axis_index("dp")
    f = lax.axis_index("fsdp")
    j = lax.rem(dp, 4)
    yh = lax.div(f, 8)
    x = lax.rem(lax.div(f, 2), 4)
    c = lax.rem(f, 2)
    base = yh * 8 + c

    sib = (dp, f + 1 - 2 * c)
    xp = (dp, base + 2 * lax.rem(x + 1, 4))
    xm = (dp, base + 2 * lax.rem(x + 3, 4))
    zp = (lax.rem(dp + 4, 32), f)
    zm = (lax.rem(dp + 28, 32), f)
    wrap_up = lax.div(j + 1, 4)
    up = (dp + 1 - 4 * wrap_up, lax.rem(f + 8 * wrap_up, 16))
    wrap_dn = lax.div(3 - j, 3)
    dn = (dp - 1 + 4 * wrap_dn, lax.rem(f + 8 * wrap_dn, 16))
    wrap = lax.div(j + 2, 4)
    up2 = (dp + 2 - 4 * wrap, lax.rem(f + 8 * wrap, 16))
    wrap = lax.div(3 - j, 2)
    dn2 = (dp - 2 + 4 * wrap, lax.rem(f + 8 * wrap, 16))

    barrier = pltpu.get_barrier_semaphore()
    for who in (sib, xp, xm, zp, zm, up, dn, up2, dn2):
        pl.semaphore_signal(barrier, inc=1, device_id=who, device_id_type=MESH)
    pl.semaphore_wait(barrier, 9)
    for d in loads:
        d.wait()

    def copy(src, dst, send, recv, who):
        return pltpu.make_async_remote_copy(
            src_ref=src, dst_ref=dst, send_sem=send, recv_sem=recv, device_id=who, device_id_type=MESH
        )

    def part(ref, h):
        return ref.at[pl.ds(HALF * h, HALF), :]

    def send_x(k, src, h):
        @pl.when(jnp.logical_and(k <= 3 - j, j >= 1))
        def _():
            copy(part(src, h), part(xbuf.at[k + 1], h), x_s.at[k, h], x_r.at[k + 1, h], dn).start()

        @pl.when(jnp.logical_and(k > 3 - j, j <= 2))
        def _():
            copy(part(src, h), part(xbuf.at[k - 1], h), x_s.at[k, h], x_r.at[k - 1, h], up).start()

    def send_p(k, src, h):
        if k < 4:
          @pl.when(jnp.logical_and(k <= j, j <= 1))
          def _():
            copy(part(src, h), part(pbuf.at[PLACE[k + 1]], h), p_s.at[k, h], p_r.at[k + 1, h], up).start()

        if k > 2:
          @pl.when(jnp.logical_and(k > j, j >= 2))
          def _():
            copy(part(src, h), part(pbuf.at[PLACE[k - 1]], h), p_s.at[k, h], p_r.at[k - 1, h], dn).start()

    def wait_x(k, h, whole=False):
        dst = xbuf.at[k] if whole else part(xbuf.at[k], h)
        copy(dst, dst, x_s.at[k, h], x_r.at[k, h], up).wait_recv()

    def quarter(k, q):
        return xbuf.at[k, pl.ds(HALF // 2 * q, HALF // 2), :]

    hop_in = [copy(quarter(4, q), quarter(4, q), x_s.at[5, q], x_r.at[4, q], zm) for q in range(4)]
    hop_up = [copy(quarter(4, q), quarter(3, q), x_s.at[4, q], x_r.at[3, q // 2], up) for q in range(4)]

    def wait_p(k, h):
        dst = part(pbuf.at[PLACE[k]], h)
        copy(dst, dst, p_s.at[k, h], p_r.at[k, h], up).wait_recv()

    def pass_x(k, h):
        wait_x(k, h)
        send_x(k, xbuf.at[k], h)

    def pass_p(k):
        for h in range(2):
            wait_p(k, h)
            send_p(k, pbuf.at[PLACE[k]], h)

    def x_done(k, src):
        @pl.when(jnp.logical_or(jnp.logical_and(k <= 3 - j, j >= 1), jnp.logical_and(k > 3 - j, j <= 2)))
        def _():
            for h in range(2):
                copy(part(src, h), part(xbuf.at[1], h), x_s.at[k, h], x_r.at[1, h], up).wait_send()

    def p_done(k, src):
        @pl.when(jnp.logical_or(jnp.logical_and(k <= j, j <= 1), jnp.logical_and(k > j, j >= 2)))
        def _():
            for h in range(2):
                copy(part(src, h), part(pbuf.at[0], h), p_s.at[k, h], p_r.at[1, h], up).wait_send()

    middle = lax.rem(lax.div(j + 1, 2), 2)
    outer = middle == 0
    inner = middle == 1
    xk0 = 1 + 2 * lax.div(j, 3)
    xk1 = 2 + middle
    xk2 = 6 - xk0 - xk1
    guest = copy(img, xbuf.at[5], x_s.at[6, 0], x_r.at[5, 0], up)

    w_swap = copy(wsh, wtmp, w_s.at[0], w_r.at[0], sib)
    w_swap.start()
    pool_swap = copy(pool, psib, h_s.at[2], h_r.at[2], sib)
    x_hop = [
        copy(img.at[pl.ds(HALF // 2 * q, HALF // 2), :], quarter(4, q), x_s.at[5, q], x_r.at[4, q], zm)
        for q in range(4)
    ]
    p_hop = [copy(part(pool, h), part(pbuf.at[PLACE[4]], h), p_s.at[5, h], p_r.at[4, h], zp) for h in range(2)]

    @pl.when(j <= 2)
    def _():
        for d in x_hop:
            d.start()

    send_x(0, img, 0)
    send_x(0, img, 1)

    @pl.when(j == 1)
    def _():
        send_p(0, pool, 0)

    @pl.when(j >= 1)
    def _():
        for d in p_hop:
            d.start()

    v, xr = normalize(img[...].astype(F32))
    ximg[...] = v
    xb[0] = v.astype(BF16)

    def chip(h, off):
        return h * 4 + lax.rem(x + off, 4)

    def rows_of(m, start, size):
        return wf.at[pl.ds(pl.multiple_of(m * CHIP + start, 16), size), :]

    def piece(m, p):
        return rows_of(m, 64 * c, AHEAD) if p == 0 else rows_of(m, 64 * c + AHEAD, UNIT - AHEAD)

    def w_copy(src, dst, ident, who, send=None):
        return copy(src, dst, w_s.at[ident if send is None else send], w_r.at[ident], who)

    w_sent = []

    def w_go(src, ident, who):
        d = w_copy(src, src, ident, who)
        d.start()
        w_sent.append(d)

    mine = chip(yh, 0)
    theirs = chip(1 - yh, 0)
    w_swap.wait_recv()
    own_rows = wsh[...].astype(F32)
    sib_rows = wtmp[...].astype(F32)
    first = c == 0
    wf[pl.ds(pl.multiple_of(mine * CHIP, 16), CHIP), :] = jnp.concatenate(
        [jnp.where(first, own_rows, sib_rows), jnp.where(first, sib_rows, own_rows)], axis=0
    ).astype(BF16)

    edge_up = [w_copy(piece(mine, p), piece(mine, p), 13 + p, up) for p in range(2)]
    edge_dn = [w_copy(piece(mine, p), piece(mine, p), 13 + p, dn) for p in range(2)]
    pass_up = [w_copy(piece(theirs, p), piece(theirs, p), 13 + p, up, 15 + p) for p in range(2)]
    pass_dn = [w_copy(piece(theirs, p), piece(theirs, p), 13 + p, dn, 15 + p) for p in range(2)]

    @pl.when(j == 3)
    def _():
        for d in edge_up:
            d.start()

    @pl.when(j == 0)
    def _():
        for d in edge_dn:
            d.start()

    def along_x(r, m):
        return {
            (d, p): w_copy(piece(m, p), piece(m, p), 1 + 4 * r + 2 * d + p, xp if d == 0 else xm)
            for d in range(2)
            for p in range(2)
        }

    mine_x = along_x(0, mine)
    theirs_x = along_x(1, theirs)
    for key in ((0, 0), (1, 1), (0, 1), (1, 0)):
        mine_x[key].start()
    w_sent.extend(mine_x.values())
    w_sent.extend(theirs_x.values())
    pool_swap.start()

    def slab_rows(n):
        m = chip(1 - yh if n < 4 else yh, ORDER[n % 4])
        return ptf[pl.ds(pl.multiple_of(m * CHIP + SHARD * c, 8), SHARD), :]

    def transpose_into(ref, start):
        ptf[...] = ref[...].astype(F32).T
        for n in range(0, 8, 2):
            pt[SHARD * n:SHARD * (n + 2), start:start + ROWS] = jnp.concatenate(
                [slab_rows(n), slab_rows(n + 1)], axis=0
            ).astype(BF16)

    def to_sibling(m, ident):
        w_go(rows_of(m, 80 * c, PART), ident, sib)

    def near_first(r, h):
        for d, (off, onward) in enumerate(((3, xp), (1, xm))):
            got = piece(chip(h, off), d)
            w_copy(got, got, 1 + 4 * r + 3 * d, xp).wait_recv()
            w_go(got, 9 + 2 * r + d, onward)

    def near_rest(r, h):
        for d, off in enumerate((3, 1)):
            m = chip(h, off)
            got = piece(m, 1 - d)
            w_copy(got, got, 2 + 4 * r + d, xp).wait_recv()
            to_sibling(m, 17 + 4 * r + d)

    def far_units(r, h):
        m = chip(h, 2)
        for p in range(2):
            w_copy(piece(m, p), piece(m, p), 9 + 2 * r + p, xp).wait_recv()
        to_sibling(m, 19 + 4 * r)

    edge_in = [w_copy(piece(theirs, p), piece(theirs, p), 13 + p, xp) for p in range(2)]
    theirs_part = rows_of(theirs, 80 * c, PART)
    theirs_sib = w_copy(theirs_part, theirs_part, 20, sib)
    w_sent.append(theirs_sib)

    def theirs_first():
        edge_in[0].wait_recv()

        @pl.when(j == 0)
        def _():
            pass_up[0].start()

        @pl.when(j == 3)
        def _():
            pass_dn[0].start()

        theirs_x[0, 0].start()

    def theirs_rest():
        edge_in[1].wait_recv()

        @pl.when(j == 0)
        def _():
            pass_up[1].start()

        @pl.when(j == 3)
        def _():
            pass_dn[1].start()

        for key in ((1, 1), (0, 1), (1, 0)):
            theirs_x[key].start()
        theirs_sib.start()

    def hop_on(h):
        @pl.when(j <= 2)
        def _():
            for q in (2 * h, 2 * h + 1):
                hop_in[q].wait_recv()
                hop_up[q].start()

        @pl.when(inner)
        def _():
            pass_x(1, h)

    hop_on(0)
    transpose_into(pool, 0)

    @pl.when(outer)
    def _():
        theirs_first()

    near_first(0, yh)

    @pl.when(outer)
    def _():
        theirs_rest()

    hop_on(1)
    near_rest(0, yh)
    pool_swap.wait_recv()
    transpose_into(psib, ROWS)

    @pl.when(j == 0)
    def _():
        send_p(0, pool, 0)
        send_p(0, pool, 1)
        guest.start()

    @pl.when(j == 3)
    def _():
        pass_p(4)

    @pl.when(inner)
    def _():
        pass_x(3, 0)
        theirs_first()

    far_units(0, yh)

    @pl.when(inner)
    def _():
        pass_x(3, 1)
        theirs_rest()
        pass_x(2, 0)

    @pl.when(j == 2)
    def _():
        pass_p(4)

    @pl.when(j == 1)
    def _():
        pass_x(2, 1)

    near_first(1, 1 - yh)

    @pl.when(j == 2)
    def _():
        pass_x(2, 1)

    @pl.when(j == 1)
    def _():
        send_p(0, pool, 1)

    near_rest(1, 1 - yh)

    @pl.when(j == 1)
    def _():
        pass_p(1)

    @pl.when(j == 2)
    def _():
        pass_p(3)

    far_units(1, 1 - yh)

    def ready(k):
        xb[k] = normalize(xbuf[k].astype(F32))[0].astype(BF16)

    @pl.when(inner)
    def _():
        for k in range(1, 4):
            ready(k)

    for ident, m in (
        (17, chip(yh, 3)), (18, chip(yh, 1)), (19, chip(yh, 2)), (20, theirs),
        (21, chip(1 - yh, 3)), (22, chip(1 - yh, 1)), (23, chip(1 - yh, 2)),
    ):
        got = rows_of(m, 80 - 80 * c, PART)
        w_copy(got, got, ident, sib).wait_recv()

    temper = jnp.exp(jnp.full((1, 1), log_scale[0], F32))
    offset = jnp.full((1, 1), bias[0], F32)
    gain = temper * (1.0 / ROWS)

    def project(block, out):
        for start in range(0, WIDTH, 512):
            cols = pl.ds(start, min(512, WIDTH - start))
            out[:, cols] = jnp.dot(block, wf[:, cols], preferred_element_type=F32) + hb[:, cols]

    def weights(a, b, own):
        l = temper * lax.dot_general(a, b, NT, preferred_element_type=F32) + offset
        if own:
            eye = lax.broadcasted_iota(jnp.int32, l.shape, 0) == lax.broadcasted_iota(jnp.int32, l.shape, 1)
            l = jnp.where(eye, -l, l)
        g = gain / (1.0 + jnp.exp(-l))
        if own:
            g = jnp.where(eye, -g, g)
        return l, g.astype(BF16)

    def losses(m):
        e = jnp.maximum(m, 0.0) + jnp.log1p(jnp.exp(-jnp.abs(m)))
        total = e[:, :ROWS]
        for start in range(ROWS, m.shape[1], ROWS):
            total = total + e[:, start:start + ROWS]
        return jnp.sum(total.T, axis=0, keepdims=True)

    def image_side(d, row):
        loss_out[...] = row * (1.0 / ROWS)
        v = ximg[...]
        img_out[...] = (xr * (d - v * jnp.sum(v * d, axis=-1, keepdims=True))).astype(BF16)

    project(pool[...], ztxt)
    v, zr = normalize(ztxt[...])
    ztxt[...] = v
    zb[0] = v.astype(BF16)

    def text_grad(a, own):
        _, g = weights(zb[0], a, own)
        return jnp.dot(g, a, preferred_element_type=F32)

    def text_side(d):
        v = ztxt[...]
        dzb[:ROWS] = (zr * (d - v * jnp.sum(v * d, axis=-1, keepdims=True))).astype(BF16)

    @pl.when(inner)
    def _():
        text_side(text_grad(xb[0:4].reshape(4 * ROWS, WIDTH), True))

    @pl.when(outer)
    def _():
        for k in (xk0, xk1):
            wait_x(k, 0)
            wait_x(k, 1)
            ready(k)
        u[:ROWS] = text_grad(xb[0], True) + text_grad(xb[xk0], False) + text_grad(xb[xk1], False)
        wait_x(xk2, 0)
        wait_x(xk2, 1)
        ready(xk2)
        text_side(u[:ROWS] + text_grad(xb[xk2], False))

    pair = copy(dzb.at[:ROWS], dzb.at[ROWS:], h_s.at[3], h_r.at[3], sib)
    pair.start()

    def make(n):
        t = jnp.dot(pt[SHARD * n:SHARD * (n + 2), :], dzb[...], preferred_element_type=F32)
        terms[n] = t[:SHARD]
        terms[n + 1] = t[SHARD:]

    def cols(n, q):
        start, size, _ = PIECES[q]
        return terms[n, :, start:start + size]

    g_sent = []

    def g_go(src, value, ident, dst, who):
        src[...] = value.astype(BF16)
        d = copy(src, dst, g_s.at[ident], g_r.at[ident], who)
        d.start()
        g_sent.append(d)

    def g_wait(ref, ident):
        copy(ref, ref, g_s.at[ident], g_r.at[ident], xp).wait_recv()
        return ref[...].astype(F32)

    def slot(refs, q, *index):
        return refs[q].at[index] if index else refs[q]

    def far_sends(g):
        for q, (_, _, way) in enumerate(PIECES):
            g_go(slot(g_out, q, g, 0), cols(4 * g, q), 12 * g + q, slot(g_far, q, g), xp if way > 0 else xm)

    def near_sends(g):
        for q, (_, _, way) in enumerate(PIECES):
            n, who = (2, xm) if way > 0 else (1, xp)
            g_go(slot(g_out, q, g, 1), cols(4 * g + n, q), 12 * g + 4 + q, slot(g_near, q, g, 0), who)

    def second_sends(g):
        for q, (_, _, way) in enumerate(PIECES):
            n, who = (1, xp) if way > 0 else (2, xm)
            value = cols(4 * g + n, q) + g_wait(slot(g_far, q, g), 12 * g + q)
            g_go(slot(g_out, q, g, 2), value, 12 * g + 8 + q, slot(g_near, q, g, 1), who)

    def total(g, q):
        value = cols(4 * g + 3, q) + g_wait(slot(g_near, q, g, 0), 12 * g + 4 + q)
        return value + g_wait(slot(g_near, q, g, 1), 12 * g + 8 + q)

    def back():
        @pl.loop(0, WIDTH // TILE)
        def _(n):
            cols = pl.ds(pl.multiple_of(n * TILE, TILE), TILE)
            pool_out[:, cols] = lax.dot_general(
                dzb[:ROWS], wf[cols, :], NT, preferred_element_type=F32
            ).astype(BF16)

    gdx_up = copy(gdx_out, gdx_in, h_s.at[0], h_r.at[0], up)
    gdx_dn = copy(gdx_out, gdx_in, h_s.at[0], h_r.at[0], dn)
    gsum_up = copy(gsum_out, gsum_in, h_s.at[1], h_r.at[1], up)
    gsum_dn = copy(gsum_out, gsum_in, h_s.at[1], h_r.at[1], dn)

    @pl.when(outer)
    def _():
        m, g = weights(xb[0], zb[0], True)
        u[ROWS:2 * ROWS] = jnp.dot(g, zb[0], preferred_element_type=F32)
        loss_out[...] = losses(m)

    def texts_done(first, last):
        for n in range(first, last):
            v = u[ROWS * (n - 1):ROWS * n]
            zb[n] = normalize(v)[0].astype(BF16)

    def meet(image, texts, own):
        m, g = weights(image, texts, own)
        return jnp.dot(g, texts, preferred_element_type=F32), losses(m)

    @pl.when(j == 1)
    def _():
        for h in range(2):
            wait_p(3, h)
            wait_p(4, h)

    @pl.when(j == 2)
    def _():
        for h in range(2):
            wait_p(1, h)

    @pl.when(inner)
    def _():
        project(pbuf[0:3].reshape(3 * ROWS, WIDTH), u.at[:3 * ROWS])

    pair.wait_recv()
    make(0)
    far_sends(0)
    make(2)
    near_sends(0)
    make(4)
    make(6)

    @pl.when(j == 1)
    def _():
        wait_x(5, 0, whole=True)
        ready(5)

    @pl.when(inner)
    def _():
        texts_done(1, 4)
        d, row = meet(xb[9 - 4 * j], zb[pl.ds(4 - 2 * j, 2)].reshape(2 * ROWS, WIDTH), False)
        gdx[...] = d
        gsum_out[...] = row

    @pl.when(outer)
    def _():
        back()

    second_sends(0)
    far_sends(1)
    near_sends(1)

    for q, (_, _, way) in enumerate(PIECES):
        g_go(slot(y_out, q), total(0, q), 24 + q, slot(y_pass, q), up2 if way > 0 else dn2)

    onward = [
        copy(slot(y_pass, q), slot(y_in, q), g_s.at[28 + q], g_r.at[28 + q], up2 if way > 0 else dn2)
        for q, (_, _, way) in enumerate(PIECES)
    ]

    def relay():
        for q in range(4):
            copy(slot(y_pass, q), slot(y_pass, q), g_s.at[24 + q], g_r.at[24 + q], xp).wait_recv()
            onward[q].start()

    @pl.when(outer)
    def _():
        relay()

    @pl.when(inner)
    def _():
        for h in range(2):
            wait_p(2, h)
        project(pbuf[3], u.at[3 * ROWS:])
        texts_done(4, 5)
        d, row = meet(xb[9 - 4 * j], zb[4], False)
        gdx_out[...] = (gdx[...] + d).astype(BF16)
        gsum_out[...] += row

        @pl.when(j == 1)
        def _():
            gdx_dn.start()
            gsum_dn.start()

        @pl.when(j == 2)
        def _():
            gdx_up.start()
            gsum_up.start()

    second_sends(1)

    @pl.when(inner)
    def _():
        d, row = meet(xb[0], zb[0:3].reshape(3 * ROWS, WIDTH), True)
        e, more = meet(xb[0], zb[4], False)
        image_side(d + e, row + more)

    @pl.when(inner)
    def _():
        relay()
        back()

    for q, (start, size, _) in enumerate(PIECES):
        head_out[:, start:start + size] = total(1, q)

    @pl.when(outer)
    def _():
        gsum_up.wait_recv()
        gdx_up.wait_recv()
        image_side(u[ROWS:2 * ROWS] + gdx_in[...].astype(F32), loss_out[...] + gsum_in[...])

    for q, (start, size, _) in enumerate(PIECES):
        head_out[:, start:start + size] += g_wait(slot(y_in, q), 28 + q)

    w_swap.wait_send()
    for d in w_sent:
        d.wait_send()

    @pl.when(j == 3)
    def _():
        for d in edge_up + pass_dn:
            d.wait_send()

    @pl.when(j == 0)
    def _():
        for d in edge_dn + pass_up:
            d.wait_send()

    @pl.when(j <= 2)
    def _():
        for d in x_hop + hop_up:
            d.wait_send()

    @pl.when(j >= 1)
    def _():
        for d in p_hop:
            d.wait_send()

    @pl.when(j == 0)
    def _():
        guest.wait_send()

    @pl.when(inner)
    def _():
        gdx_up.wait_send()
        gsum_up.wait_send()

    x_done(0, img)
    p_done(0, pool)
    for k in range(1, 4):
        x_done(k, xbuf.at[k])
        p_done(k, pbuf.at[0])
    p_done(4, pbuf.at[0])
    pool_swap.wait_send()
    pair.wait_send()
    for d in g_sent + onward:
        d.wait_send()


def finish(*refs):
    moves = [pltpu.make_async_copy(refs[i], refs[4 + i], refs[8].at[i]) for i in range(4)]
    for d in moves:
        d.start()
    for d in moves:
        d.wait()


def per_device(images, pooled, head_weight, head_bias, log_scale, bias):
    smem = pl.BlockSpec(memory_space=pltpu.SMEM)
    vmem = pl.BlockSpec(memory_space=pltpu.VMEM)
    hbm = pl.BlockSpec(memory_space=pltpu.HBM)
    block = (ROWS, WIDTH)
    slab = (SHARD, WIDTH)
    parts = [(SHARD, size) for _, size, _ in PIECES]
    dma = pltpu.SemaphoreType.DMA
    results = (
        jax.ShapeDtypeStruct((1, ROWS), F32),
        jax.ShapeDtypeStruct(block, BF16),
        jax.ShapeDtypeStruct(block, BF16),
        jax.ShapeDtypeStruct(slab, F32),
    )
    made = pl.pallas_call(
        kernel,
        out_shape=results,
        in_specs=[hbm, hbm, hbm, hbm, smem, smem],
        out_specs=(vmem,) * 4,
        scratch_shapes=[
            pltpu.VMEM(block, BF16),
            pltpu.VMEM(block, BF16),
            pltpu.VMEM(slab, BF16),
            pltpu.VMEM((1, WIDTH), F32),
            pltpu.VMEM(slab, BF16),
            pltpu.VMEM((WIDTH, WIDTH), BF16),
            pltpu.VMEM((6,) + block, BF16),
            pltpu.VMEM((4,) + block, BF16),
            pltpu.VMEM((6,) + block, BF16),
            pltpu.VMEM((5,) + block, BF16),
            pltpu.VMEM(block, F32),
            pltpu.VMEM(block, F32),
            pltpu.VMEM((4 * ROWS, WIDTH), F32),
            pltpu.VMEM((2 * ROWS, WIDTH), BF16),
            pltpu.VMEM(block, BF16),
            pltpu.VMEM((WIDTH, ROWS), F32),
            pltpu.VMEM((8 * SHARD, 2 * ROWS), BF16),
            pltpu.VMEM((8,) + slab, F32),
            [pltpu.VMEM((2, 3) + p, BF16) for p in parts],
            [pltpu.VMEM((2,) + p, BF16) for p in parts],
            [pltpu.VMEM((2, 2) + p, BF16) for p in parts],
            [pltpu.VMEM(p, BF16) for p in parts],
            [pltpu.VMEM(p, BF16) for p in parts],
            [pltpu.VMEM(p, BF16) for p in parts],
            pltpu.VMEM(block, F32),
            pltpu.VMEM(block, BF16),
            pltpu.VMEM((1, ROWS), F32),
            pltpu.VMEM(block, BF16),
            pltpu.VMEM((1, ROWS), F32),
            dma((4,)),
            dma((24,)), dma((24,)),
            dma((7, 4)), dma((6, 4)),
            dma((6, 2)), dma((5, 2)),
            dma((32,)), dma((32,)),
            dma((4,)), dma((4,)),
        ],
        compiler_params=pltpu.CompilerParams(
            collective_id=0, has_side_effects=True, vmem_limit_bytes=VMEM_GRANT
        ),
        cost_estimate=pl.CostEstimate(flops=4_000_000_000, bytes_accessed=6_000_000, transcendentals=300_000),
    )(*[pltpu.with_memory_space_constraint(v, pltpu.HBM) for v in (images, pooled, head_weight, head_bias)], log_scale, bias)
    loss, image_grad, pooled_grad, head_grad = pl.pallas_call(
        finish,
        out_shape=results,
        in_specs=[vmem] * 4,
        out_specs=(hbm,) * 4,
        scratch_shapes=[dma((4,))],
    )(*made)
    return loss.reshape(ROWS), image_grad, pooled_grad, head_grad


def solution(mesh):
    in_specs = (P(("dp", "fsdp"), None), P(("dp", "fsdp"), None), P("fsdp", None), P(), P(), P())
    out_specs = (
        P(("dp", "fsdp")),
        P(("dp", "fsdp"), None),
        P(("dp", "fsdp"), None),
        P(("dp", "fsdp"), None),
    )
    return jax.shard_map(
        per_device, mesh=mesh, in_specs=in_specs, out_specs=out_specs, check_vma=False
    )
```

```python
import jax
import jax.numpy as jnp
from jax import lax
from jax.experimental import pallas as pl
from jax.experimental.pallas import tpu as pltpu
from jax.sharding import PartitionSpec as P

MESH = pl.DeviceIdType.MESH
F32 = jnp.float32
BF16 = jnp.bfloat16
NT = (((1,), (1,)), ((), ()))

ROWS = 128
WIDTH = 1152
SHARD = 72
CHIP = 144
UNIT = 80
PART = 64
AHEAD = 48
TILE = 384
VMEM_GRANT = 44 * 1024 * 1024
HALF = 64
PIECES = ((0, 384, 1), (640, 256, -1), (384, 256, 1), (896, 256, -1))
PLACE = {1: 0, 3: 1, 4: 2, 2: 3}
ORDER = (2, 1, 3, 0)


def normalize(v):
    r = lax.rsqrt(jnp.sum(v * v, axis=-1, keepdims=True) + 1e-06)
    return v * r, r


def kernel(
    img_hbm, pool_hbm, wsh_hbm, hb_hbm, log_scale, bias,
    loss_out, img_out, pool_out, head_out,
    img, pool, wsh, hb,
    wtmp, wf, xbuf, pbuf, xb, zb, ximg, ztxt, u, dzb, psib, ptf, pt, terms,
    g_out, g_far, g_near,
    y_out, y_pass, y_in,
    gdx, gdx_out, gsum_out, gdx_in, gsum_in,
    l_s, w_s, w_r, x_s, x_r, p_s, p_r, g_s, g_r, h_s, h_r,
):
    loads = [
        pltpu.make_async_copy(src, dst, l_s.at[i])
        for i, (src, dst) in enumerate(
            ((wsh_hbm, wsh), (img_hbm, img), (pool_hbm, pool), (hb_hbm, hb.at[0]))
        )
    ]
    for d in loads:
        d.start()
    dp = lax.axis_index("dp")
    f = lax.axis_index("fsdp")
    j = lax.rem(dp, 4)
    yh = lax.div(f, 8)
    x = lax.rem(lax.div(f, 2), 4)
    c = lax.rem(f, 2)
    base = yh * 8 + c

    sib = (dp, f + 1 - 2 * c)
    xp = (dp, base + 2 * lax.rem(x + 1, 4))
    xm = (dp, base + 2 * lax.rem(x + 3, 4))
    zp = (lax.rem(dp + 4, 32), f)
    zm = (lax.rem(dp + 28, 32), f)
    wrap_up = lax.div(j + 1, 4)
    up = (dp + 1 - 4 * wrap_up, lax.rem(f + 8 * wrap_up, 16))
    wrap_dn = lax.div(3 - j, 3)
    dn = (dp - 1 + 4 * wrap_dn, lax.rem(f + 8 * wrap_dn, 16))
    odd = lax.rem(j, 2)
    step = 3 - 2 * odd
    wrap = lax.div(j + step, 4)
    y_up = (dp + step - 4 * wrap, lax.rem(f + 8 * wrap, 16))
    step = 1 + 2 * odd
    wrap = lax.div(3 - j, 2)
    y_dn = (dp - step + 4 * wrap, lax.rem(f + 8 * wrap, 16))

    barrier = pltpu.get_barrier_semaphore()
    for who in (sib, xp, xm, zp, zm, up, dn):
        pl.semaphore_signal(barrier, inc=1, device_id=who, device_id_type=MESH)

    @pl.when(odd == 0)
    def _():
        pl.semaphore_signal(barrier, inc=1, device_id=y_up, device_id_type=MESH)

    @pl.when(odd == 1)
    def _():
        pl.semaphore_signal(barrier, inc=1, device_id=y_dn, device_id_type=MESH)

    pl.semaphore_wait(barrier, 8)
    for d in loads:
        d.wait()

    def copy(src, dst, send, recv, who):
        return pltpu.make_async_remote_copy(
            src_ref=src, dst_ref=dst, send_sem=send, recv_sem=recv, device_id=who, device_id_type=MESH
        )

    def part(ref, h):
        return ref.at[pl.ds(HALF * h, HALF), :]

    def send_x(k, src, h):
        @pl.when(jnp.logical_and(k <= 3 - j, j >= 1))
        def _():
            copy(part(src, h), part(xbuf.at[k + 1], h), x_s.at[k, h], x_r.at[k + 1, h], dn).start()

        @pl.when(jnp.logical_and(k > 3 - j, j <= 2))
        def _():
            copy(part(src, h), part(xbuf.at[k - 1], h), x_s.at[k, h], x_r.at[k - 1, h], up).start()

    def send_p(k, src, h):
        if k < 4:
          @pl.when(jnp.logical_and(k <= j, j <= 1))
          def _():
            copy(part(src, h), part(pbuf.at[PLACE[k + 1]], h), p_s.at[k, h], p_r.at[k + 1, h], up).start()

        if k > 2:
          @pl.when(jnp.logical_and(k > j, j >= 2))
          def _():
            copy(part(src, h), part(pbuf.at[PLACE[k - 1]], h), p_s.at[k, h], p_r.at[k - 1, h], dn).start()

    def wait_x(k, h, whole=False):
        dst = xbuf.at[k] if whole else part(xbuf.at[k], h)
        copy(dst, dst, x_s.at[k, h], x_r.at[k, h], up).wait_recv()

    def quarter(k, q):
        return xbuf.at[k, pl.ds(HALF // 2 * q, HALF // 2), :]

    hop_in = [copy(quarter(4, q), quarter(4, q), x_s.at[5, q], x_r.at[4, q], zm) for q in range(4)]
    hop_up = [copy(quarter(4, q), quarter(3, q), x_s.at[4, q], x_r.at[3, q // 2], up) for q in range(4)]

    def wait_p(k, h):
        dst = part(pbuf.at[PLACE[k]], h)
        copy(dst, dst, p_s.at[k, h], p_r.at[k, h], up).wait_recv()

    def pass_x(k, h):
        wait_x(k, h)
        send_x(k, xbuf.at[k], h)

    def pass_p(k):
        for h in range(2):
            wait_p(k, h)
            send_p(k, pbuf.at[PLACE[k]], h)

    def x_done(k, src):
        @pl.when(jnp.logical_or(jnp.logical_and(k <= 3 - j, j >= 1), jnp.logical_and(k > 3 - j, j <= 2)))
        def _():
            for h in range(2):
                copy(part(src, h), part(xbuf.at[1], h), x_s.at[k, h], x_r.at[1, h], up).wait_send()

    def p_done(k, src):
        @pl.when(jnp.logical_or(jnp.logical_and(k <= j, j <= 1), jnp.logical_and(k > j, j >= 2)))
        def _():
            for h in range(2):
                copy(part(src, h), part(pbuf.at[0], h), p_s.at[k, h], p_r.at[1, h], up).wait_send()

    middle = lax.rem(lax.div(j + 1, 2), 2)
    outer = middle == 0
    inner = middle == 1
    xk0 = 1 + 2 * lax.div(j, 3)
    xk1 = 2 + middle
    xk2 = 6 - xk0 - xk1
    guest = copy(img, xbuf.at[5], x_s.at[6, 0], x_r.at[5, 0], up)

    w_swap = copy(wsh, wtmp, w_s.at[0], w_r.at[0], sib)
    w_swap.start()
    pool_swap = copy(pool, psib, h_s.at[2], h_r.at[2], sib)
    x_hop = [
        copy(img.at[pl.ds(HALF // 2 * q, HALF // 2), :], quarter(4, q), x_s.at[5, q], x_r.at[4, q], zm)
        for q in range(4)
    ]
    p_hop = [copy(part(pool, h), part(pbuf.at[PLACE[4]], h), p_s.at[5, h], p_r.at[4, h], zp) for h in range(2)]

    @pl.when(j <= 2)
    def _():
        for d in x_hop:
            d.start()

    send_x(0, img, 0)
    send_x(0, img, 1)

    @pl.when(j == 1)
    def _():
        send_p(0, pool, 0)

    @pl.when(j >= 1)
    def _():
        for d in p_hop:
            d.start()

    v, xr = normalize(img[...].astype(F32))
    ximg[...] = v
    xb[0] = v.astype(BF16)

    def chip(h, off):
        return h * 4 + lax.rem(x + off, 4)

    def rows_of(m, start, size):
        return wf.at[pl.ds(pl.multiple_of(m * CHIP + start, 16), size), :]

    def piece(m, p):
        return rows_of(m, 64 * c, AHEAD) if p == 0 else rows_of(m, 64 * c + AHEAD, UNIT - AHEAD)

    def w_copy(src, dst, ident, who, send=None):
        return copy(src, dst, w_s.at[ident if send is None else send], w_r.at[ident], who)

    w_sent = []

    def w_go(src, ident, who):
        d = w_copy(src, src, ident, who)
        d.start()
        w_sent.append(d)

    mine = chip(yh, 0)
    theirs = chip(1 - yh, 0)
    w_swap.wait_recv()
    own_rows = wsh[...].astype(F32)
    sib_rows = wtmp[...].astype(F32)
    first = c == 0
    wf[pl.ds(pl.multiple_of(mine * CHIP, 16), CHIP), :] = jnp.concatenate(
        [jnp.where(first, own_rows, sib_rows), jnp.where(first, sib_rows, own_rows)], axis=0
    ).astype(BF16)

    edge_up = [w_copy(piece(mine, p), piece(mine, p), 13 + p, up) for p in range(2)]
    edge_dn = [w_copy(piece(mine, p), piece(mine, p), 13 + p, dn) for p in range(2)]
    pass_up = [w_copy(piece(theirs, p), piece(theirs, p), 13 + p, up, 15 + p) for p in range(2)]
    pass_dn = [w_copy(piece(theirs, p), piece(theirs, p), 13 + p, dn, 15 + p) for p in range(2)]

    @pl.when(j == 3)
    def _():
        for d in edge_up:
            d.start()

    @pl.when(j == 0)
    def _():
        for d in edge_dn:
            d.start()

    def along_x(r, m):
        return {
            (d, p): w_copy(piece(m, p), piece(m, p), 1 + 4 * r + 2 * d + p, xp if d == 0 else xm)
            for d in range(2)
            for p in range(2)
        }

    mine_x = along_x(0, mine)
    theirs_x = along_x(1, theirs)
    for key in ((0, 0), (1, 1), (0, 1), (1, 0)):
        mine_x[key].start()
    w_sent.extend(mine_x.values())
    w_sent.extend(theirs_x.values())
    pool_swap.start()

    def slab_rows(n):
        m = chip(1 - yh if n < 4 else yh, ORDER[n % 4])
        return ptf[pl.ds(pl.multiple_of(m * CHIP + SHARD * c, 8), SHARD), :]

    def transpose_into(ref, start):
        ptf[...] = ref[...].astype(F32).T
        for n in range(0, 8, 2):
            pt[SHARD * n:SHARD * (n + 2), start:start + ROWS] = jnp.concatenate(
                [slab_rows(n), slab_rows(n + 1)], axis=0
            ).astype(BF16)

    def to_sibling(m, ident):
        w_go(rows_of(m, 80 * c, PART), ident, sib)

    def near_first(r, h):
        for d, (off, onward) in enumerate(((3, xp), (1, xm))):
            got = piece(chip(h, off), d)
            w_copy(got, got, 1 + 4 * r + 3 * d, xp).wait_recv()
            w_go(got, 9 + 2 * r + d, onward)

    def near_rest(r, h):
        for d, off in enumerate((3, 1)):
            m = chip(h, off)
            got = piece(m, 1 - d)
            w_copy(got, got, 2 + 4 * r + d, xp).wait_recv()
            to_sibling(m, 17 + 4 * r + d)

    def far_units(r, h):
        m = chip(h, 2)
        for p in range(2):
            w_copy(piece(m, p), piece(m, p), 9 + 2 * r + p, xp).wait_recv()
        to_sibling(m, 19 + 4 * r)

    edge_in = [w_copy(piece(theirs, p), piece(theirs, p), 13 + p, xp) for p in range(2)]
    theirs_part = rows_of(theirs, 80 * c, PART)
    theirs_sib = w_copy(theirs_part, theirs_part, 20, sib)
    w_sent.append(theirs_sib)

    def theirs_first():
        edge_in[0].wait_recv()

        @pl.when(j == 0)
        def _():
            pass_up[0].start()

        @pl.when(j == 3)
        def _():
            pass_dn[0].start()

        theirs_x[0, 0].start()

    def theirs_rest():
        edge_in[1].wait_recv()

        @pl.when(j == 0)
        def _():
            pass_up[1].start()

        @pl.when(j == 3)
        def _():
            pass_dn[1].start()

        for key in ((1, 1), (0, 1), (1, 0)):
            theirs_x[key].start()
        theirs_sib.start()

    def hop_on(h):
        @pl.when(j <= 2)
        def _():
            for q in (2 * h, 2 * h + 1):
                hop_in[q].wait_recv()
                hop_up[q].start()

        @pl.when(inner)
        def _():
            pass_x(1, h)

    hop_on(0)
    transpose_into(pool, 0)

    @pl.when(outer)
    def _():
        theirs_first()

    near_first(0, yh)

    @pl.when(outer)
    def _():
        theirs_rest()

    hop_on(1)
    near_rest(0, yh)
    pool_swap.wait_recv()
    transpose_into(psib, ROWS)

    @pl.when(j == 0)
    def _():
        send_p(0, pool, 0)
        send_p(0, pool, 1)
        guest.start()

    @pl.when(j == 3)
    def _():
        pass_p(4)

    @pl.when(inner)
    def _():
        pass_x(3, 0)
        theirs_first()

    far_units(0, yh)

    @pl.when(inner)
    def _():
        pass_x(3, 1)
        theirs_rest()
        pass_x(2, 0)

    @pl.when(j == 2)
    def _():
        pass_p(4)

    @pl.when(j == 1)
    def _():
        pass_x(2, 1)

    near_first(1, 1 - yh)

    @pl.when(j == 2)
    def _():
        pass_x(2, 1)

    @pl.when(j == 1)
    def _():
        send_p(0, pool, 1)

    near_rest(1, 1 - yh)

    @pl.when(j == 1)
    def _():
        pass_p(1)

    @pl.when(j == 2)
    def _():
        pass_p(3)

    far_units(1, 1 - yh)

    def ready(k):
        xb[k] = normalize(xbuf[k].astype(F32))[0].astype(BF16)

    @pl.when(inner)
    def _():
        for k in range(1, 4):
            ready(k)

    for ident, m in (
        (17, chip(yh, 3)), (18, chip(yh, 1)), (19, chip(yh, 2)), (20, theirs),
        (21, chip(1 - yh, 3)), (22, chip(1 - yh, 1)), (23, chip(1 - yh, 2)),
    ):
        got = rows_of(m, 80 - 80 * c, PART)
        w_copy(got, got, ident, sib).wait_recv()

    temper = jnp.exp(jnp.full((1, 1), log_scale[0], F32))
    offset = jnp.full((1, 1), bias[0], F32)
    gain = temper * (1.0 / ROWS)

    def project(block, out):
        for start in range(0, WIDTH, 512):
            cols = pl.ds(start, min(512, WIDTH - start))
            out[:, cols] = jnp.dot(block, wf[:, cols], preferred_element_type=F32) + hb[:, cols]

    def weights(a, b, own):
        l = temper * lax.dot_general(a, b, NT, preferred_element_type=F32) + offset
        if own:
            eye = lax.broadcasted_iota(jnp.int32, l.shape, 0) == lax.broadcasted_iota(jnp.int32, l.shape, 1)
            l = jnp.where(eye, -l, l)
        g = gain / (1.0 + jnp.exp(-l))
        if own:
            g = jnp.where(eye, -g, g)
        return l, g.astype(BF16)

    def losses(m):
        e = jnp.maximum(m, 0.0) + jnp.log1p(jnp.exp(-jnp.abs(m)))
        total = e[:, :ROWS]
        for start in range(ROWS, m.shape[1], ROWS):
            total = total + e[:, start:start + ROWS]
        return jnp.sum(total.T, axis=0, keepdims=True)

    def image_side(d, row):
        loss_out[...] = row * (1.0 / ROWS)
        v = ximg[...]
        img_out[...] = (xr * (d - v * jnp.sum(v * d, axis=-1, keepdims=True))).astype(BF16)

    project(pool[...], ztxt)
    v, zr = normalize(ztxt[...])
    ztxt[...] = v
    zb[0] = v.astype(BF16)

    def text_grad(a, own):
        _, g = weights(zb[0], a, own)
        return jnp.dot(g, a, preferred_element_type=F32)

    def text_side(d):
        v = ztxt[...]
        dzb[:ROWS] = (zr * (d - v * jnp.sum(v * d, axis=-1, keepdims=True))).astype(BF16)

    @pl.when(inner)
    def _():
        text_side(text_grad(xb[0:4].reshape(4 * ROWS, WIDTH), True))

    @pl.when(outer)
    def _():
        for k in (xk0, xk1):
            wait_x(k, 0)
            wait_x(k, 1)
            ready(k)
        u[:ROWS] = text_grad(xb[0], True) + text_grad(xb[xk0], False) + text_grad(xb[xk1], False)
        wait_x(xk2, 0)
        wait_x(xk2, 1)
        ready(xk2)
        text_side(u[:ROWS] + text_grad(xb[xk2], False))

    pair = copy(dzb.at[:ROWS], dzb.at[ROWS:], h_s.at[3], h_r.at[3], sib)
    pair.start()

    def make(n):
        t = jnp.dot(pt[SHARD * n:SHARD * (n + 2), :], dzb[...], preferred_element_type=F32)
        terms[n] = t[:SHARD]
        terms[n + 1] = t[SHARD:]

    def cols(n, q):
        start, size, _ = PIECES[q]
        return terms[n, :, start:start + size]

    g_sent = []

    def g_go(src, value, ident, dst, who):
        src[...] = value.astype(BF16)
        d = copy(src, dst, g_s.at[ident], g_r.at[ident], who)
        d.start()
        g_sent.append(d)

    def g_wait(ref, ident):
        copy(ref, ref, g_s.at[ident], g_r.at[ident], xp).wait_recv()
        return ref[...].astype(F32)

    def slot(refs, q, *index):
        return refs[q].at[index] if index else refs[q]

    def far_sends(g):
        for q, (_, _, way) in enumerate(PIECES):
            g_go(slot(g_out, q, g, 0), cols(4 * g, q), 12 * g + q, slot(g_far, q, g), xp if way > 0 else xm)

    def near_sends(g):
        for q, (_, _, way) in enumerate(PIECES):
            n, who = (2, xm) if way > 0 else (1, xp)
            g_go(slot(g_out, q, g, 1), cols(4 * g + n, q), 12 * g + 4 + q, slot(g_near, q, g, 0), who)

    def second_sends(g):
        for q, (_, _, way) in enumerate(PIECES):
            n, who = (1, xp) if way > 0 else (2, xm)
            value = cols(4 * g + n, q) + g_wait(slot(g_far, q, g), 12 * g + q)
            g_go(slot(g_out, q, g, 2), value, 12 * g + 8 + q, slot(g_near, q, g, 1), who)

    def total(g, q):
        value = cols(4 * g + 3, q) + g_wait(slot(g_near, q, g, 0), 12 * g + 4 + q)
        return value + g_wait(slot(g_near, q, g, 1), 12 * g + 8 + q)

    def back():
        @pl.loop(0, WIDTH // TILE)
        def _(n):
            cols = pl.ds(pl.multiple_of(n * TILE, TILE), TILE)
            pool_out[:, cols] = lax.dot_general(
                dzb[:ROWS], wf[cols, :], NT, preferred_element_type=F32
            ).astype(BF16)

    gdx_up = copy(gdx_out, gdx_in, h_s.at[0], h_r.at[0], up)
    gdx_dn = copy(gdx_out, gdx_in, h_s.at[0], h_r.at[0], dn)
    gsum_up = copy(gsum_out, gsum_in, h_s.at[1], h_r.at[1], up)
    gsum_dn = copy(gsum_out, gsum_in, h_s.at[1], h_r.at[1], dn)

    @pl.when(outer)
    def _():
        m, g = weights(xb[0], zb[0], True)
        u[ROWS:2 * ROWS] = jnp.dot(g, zb[0], preferred_element_type=F32)
        loss_out[...] = losses(m)

    def texts_done(first, last):
        for n in range(first, last):
            v = u[ROWS * (n - 1):ROWS * n]
            zb[n] = normalize(v)[0].astype(BF16)

    def meet(image, texts, own):
        m, g = weights(image, texts, own)
        return jnp.dot(g, texts, preferred_element_type=F32), losses(m)

    @pl.when(j == 1)
    def _():
        for h in range(2):
            wait_p(3, h)
            wait_p(4, h)

    @pl.when(j == 2)
    def _():
        for h in range(2):
            wait_p(1, h)

    @pl.when(inner)
    def _():
        project(pbuf[0:3].reshape(3 * ROWS, WIDTH), u.at[:3 * ROWS])

    pair.wait_recv()
    make(0)
    far_sends(0)
    make(2)
    near_sends(0)
    make(4)
    make(6)

    @pl.when(j == 1)
    def _():
        wait_x(5, 0, whole=True)
        ready(5)

    @pl.when(inner)
    def _():
        texts_done(1, 4)
        d, row = meet(xb[9 - 4 * j], zb[pl.ds(4 - 2 * j, 2)].reshape(2 * ROWS, WIDTH), False)
        gdx[...] = d
        gsum_out[...] = row

    @pl.when(outer)
    def _():
        back()

    second_sends(0)
    far_sends(1)
    near_sends(1)

    @pl.when(inner)
    def _():
        for h in range(2):
            wait_p(2, h)
        project(pbuf[3], u.at[3 * ROWS:])
        texts_done(4, 5)
        d, row = meet(xb[9 - 4 * j], zb[4], False)
        gdx_out[...] = (gdx[...] + d).astype(BF16)
        gsum_out[...] += row

        @pl.when(j == 1)
        def _():
            gdx_dn.start()
            gsum_dn.start()

        @pl.when(j == 2)
        def _():
            gdx_up.start()
            gsum_up.start()

    for q, (_, _, way) in enumerate(PIECES):
        g_go(slot(y_out, q), total(0, q), 24 + q, slot(y_pass, q), y_up if way > 0 else y_dn)

    onward = [
        copy(slot(y_pass, q), slot(y_in, q), g_s.at[28 + q], g_r.at[28 + q], y_up if way > 0 else y_dn)
        for q, (_, _, way) in enumerate(PIECES)
    ]

    def relay():
        for q in range(4):
            copy(slot(y_pass, q), slot(y_pass, q), g_s.at[24 + q], g_r.at[24 + q], xp).wait_recv()
            onward[q].start()

    second_sends(1)

    @pl.when(inner)
    def _():
        d, row = meet(xb[0], zb[0:3].reshape(3 * ROWS, WIDTH), True)
        e, more = meet(xb[0], zb[4], False)
        image_side(d + e, row + more)

    relay()

    @pl.when(inner)
    def _():
        back()

    for q, (start, size, _) in enumerate(PIECES):
        head_out[:, start:start + size] = total(1, q)

    @pl.when(outer)
    def _():
        gsum_up.wait_recv()
        gdx_up.wait_recv()
        image_side(u[ROWS:2 * ROWS] + gdx_in[...].astype(F32), loss_out[...] + gsum_in[...])

    for q, (start, size, _) in enumerate(PIECES):
        head_out[:, start:start + size] += g_wait(slot(y_in, q), 28 + q)

    w_swap.wait_send()
    for d in w_sent:
        d.wait_send()

    @pl.when(j == 3)
    def _():
        for d in edge_up + pass_dn:
            d.wait_send()

    @pl.when(j == 0)
    def _():
        for d in edge_dn + pass_up:
            d.wait_send()

    @pl.when(j <= 2)
    def _():
        for d in x_hop + hop_up:
            d.wait_send()

    @pl.when(j >= 1)
    def _():
        for d in p_hop:
            d.wait_send()

    @pl.when(j == 0)
    def _():
        guest.wait_send()

    @pl.when(inner)
    def _():
        gdx_up.wait_send()
        gsum_up.wait_send()

    x_done(0, img)
    p_done(0, pool)
    for k in range(1, 4):
        x_done(k, xbuf.at[k])
        p_done(k, pbuf.at[0])
    p_done(4, pbuf.at[0])
    pool_swap.wait_send()
    pair.wait_send()
    for d in g_sent + onward:
        d.wait_send()


def finish(*refs):
    moves = [pltpu.make_async_copy(refs[i], refs[4 + i], refs[8].at[i]) for i in range(4)]
    for d in moves:
        d.start()
    for d in moves:
        d.wait()


def per_device(images, pooled, head_weight, head_bias, log_scale, bias):
    smem = pl.BlockSpec(memory_space=pltpu.SMEM)
    vmem = pl.BlockSpec(memory_space=pltpu.VMEM)
    hbm = pl.BlockSpec(memory_space=pltpu.HBM)
    block = (ROWS, WIDTH)
    slab = (SHARD, WIDTH)
    parts = [(SHARD, size) for _, size, _ in PIECES]
    dma = pltpu.SemaphoreType.DMA
    results = (
        jax.ShapeDtypeStruct((1, ROWS), F32),
        jax.ShapeDtypeStruct(block, BF16),
        jax.ShapeDtypeStruct(block, BF16),
        jax.ShapeDtypeStruct(slab, F32),
    )
    made = pl.pallas_call(
        kernel,
        out_shape=results,
        in_specs=[hbm, hbm, hbm, hbm, smem, smem],
        out_specs=(vmem,) * 4,
        scratch_shapes=[
            pltpu.VMEM(block, BF16),
            pltpu.VMEM(block, BF16),
            pltpu.VMEM(slab, BF16),
            pltpu.VMEM((1, WIDTH), F32),
            pltpu.VMEM(slab, BF16),
            pltpu.VMEM((WIDTH, WIDTH), BF16),
            pltpu.VMEM((6,) + block, BF16),
            pltpu.VMEM((4,) + block, BF16),
            pltpu.VMEM((6,) + block, BF16),
            pltpu.VMEM((5,) + block, BF16),
            pltpu.VMEM(block, F32),
            pltpu.VMEM(block, F32),
            pltpu.VMEM((4 * ROWS, WIDTH), F32),
            pltpu.VMEM((2 * ROWS, WIDTH), BF16),
            pltpu.VMEM(block, BF16),
            pltpu.VMEM((WIDTH, ROWS), F32),
            pltpu.VMEM((8 * SHARD, 2 * ROWS), BF16),
            pltpu.VMEM((8,) + slab, F32),
            [pltpu.VMEM((2, 3) + p, BF16) for p in parts],
            [pltpu.VMEM((2,) + p, BF16) for p in parts],
            [pltpu.VMEM((2, 2) + p, BF16) for p in parts],
            [pltpu.VMEM(p, BF16) for p in parts],
            [pltpu.VMEM(p, BF16) for p in parts],
            [pltpu.VMEM(p, BF16) for p in parts],
            pltpu.VMEM(block, F32),
            pltpu.VMEM(block, BF16),
            pltpu.VMEM((1, ROWS), F32),
            pltpu.VMEM(block, BF16),
            pltpu.VMEM((1, ROWS), F32),
            dma((4,)),
            dma((24,)), dma((24,)),
            dma((7, 4)), dma((6, 4)),
            dma((6, 2)), dma((5, 2)),
            dma((32,)), dma((32,)),
            dma((4,)), dma((4,)),
        ],
        compiler_params=pltpu.CompilerParams(
            collective_id=0, has_side_effects=True, vmem_limit_bytes=VMEM_GRANT
        ),
        cost_estimate=pl.CostEstimate(flops=4_000_000_000, bytes_accessed=6_000_000, transcendentals=300_000),
    )(*[pltpu.with_memory_space_constraint(v, pltpu.HBM) for v in (images, pooled, head_weight, head_bias)], log_scale, bias)
    loss, image_grad, pooled_grad, head_grad = pl.pallas_call(
        finish,
        out_shape=results,
        in_specs=[vmem] * 4,
        out_specs=(hbm,) * 4,
        scratch_shapes=[dma((4,))],
        compiler_params=pltpu.CompilerParams(vmem_limit_bytes=4 * 1024 * 1024),
    )(*made)
    return loss.reshape(ROWS), image_grad, pooled_grad, head_grad


def solution(mesh):
    in_specs = (P(("dp", "fsdp"), None), P(("dp", "fsdp"), None), P("fsdp", None), P(), P(), P())
    out_specs = (
        P(("dp", "fsdp")),
        P(("dp", "fsdp"), None),
        P(("dp", "fsdp"), None),
        P(("dp", "fsdp"), None),
    )
    return jax.shard_map(
        per_device, mesh=mesh, in_specs=in_specs, out_specs=out_specs, check_vma=False
    )
```

```python
import jax
import jax.numpy as jnp
from jax import lax
from jax.experimental import pallas as pl
from jax.experimental.pallas import tpu as pltpu
from jax.sharding import PartitionSpec as P

MESH = pl.DeviceIdType.MESH
F32 = jnp.float32
BF16 = jnp.bfloat16
NT = (((1,), (1,)), ((), ()))

ROWS = 128
WIDTH = 1152
SHARD = 72
CHIP = 144
UNIT = 80
PART = 64
AHEAD = 48
TILE = 384
VMEM_GRANT = 44 * 1024 * 1024
HALF = 64
PIECES = ((0, 384, 1), (640, 256, -1), (384, 256, 1), (896, 256, -1))
PLACE = {1: 0, 3: 1, 4: 2, 2: 3}
ORDER = (2, 1, 3, 0)


def normalize(v):
    r = lax.rsqrt(jnp.sum(v * v, axis=-1, keepdims=True) + 1e-06)
    return v * r, r


def kernel(
    img_hbm, pool_hbm, wsh_hbm, hb_hbm, log_scale, bias,
    loss_out, img_out, pool_out, head_out,
    img, pool, wsh, hb,
    wtmp, wf, xbuf, pbuf, xb, zb, ximg, ztxt, u, dzb, psib, ptf, pt, terms,
    g_out, g_far, g_near,
    y_out, y_pass, y_in,
    gdx, gdx_out, gsum_out, gdx_in, gsum_in,
    l_s, w_s, w_r, x_s, x_r, p_s, p_r, g_s, g_r, h_s, h_r,
):
    loads = [
        pltpu.make_async_copy(src, dst, l_s.at[i])
        for i, (src, dst) in enumerate(
            ((wsh_hbm, wsh), (img_hbm, img), (pool_hbm, pool), (hb_hbm, hb.at[0]))
        )
    ]
    for d in loads:
        d.start()
    dp = lax.axis_index("dp")
    f = lax.axis_index("fsdp")
    j = lax.rem(dp, 4)
    yh = lax.div(f, 8)
    x = lax.rem(lax.div(f, 2), 4)
    c = lax.rem(f, 2)
    base = yh * 8 + c

    sib = (dp, f + 1 - 2 * c)
    xp = (dp, base + 2 * lax.rem(x + 1, 4))
    xm = (dp, base + 2 * lax.rem(x + 3, 4))
    zp = (lax.rem(dp + 4, 32), f)
    zm = (lax.rem(dp + 28, 32), f)
    wrap_up = lax.div(j + 1, 4)
    up = (dp + 1 - 4 * wrap_up, lax.rem(f + 8 * wrap_up, 16))
    wrap_dn = lax.div(3 - j, 3)
    dn = (dp - 1 + 4 * wrap_dn, lax.rem(f + 8 * wrap_dn, 16))
    odd = lax.rem(j, 2)
    step = 3 - 2 * odd
    wrap = lax.div(j + step, 4)
    y_up = (dp + step - 4 * wrap, lax.rem(f + 8 * wrap, 16))
    step = 1 + 2 * odd
    wrap = lax.div(3 - j, 2)
    y_dn = (dp - step + 4 * wrap, lax.rem(f + 8 * wrap, 16))

    barrier = pltpu.get_barrier_semaphore()
    for who in (sib, xp, xm, zp, zm, up, dn):
        pl.semaphore_signal(barrier, inc=1, device_id=who, device_id_type=MESH)

    @pl.when(odd == 0)
    def _():
        pl.semaphore_signal(barrier, inc=1, device_id=y_up, device_id_type=MESH)

    @pl.when(odd == 1)
    def _():
        pl.semaphore_signal(barrier, inc=1, device_id=y_dn, device_id_type=MESH)

    pl.semaphore_wait(barrier, 8)
    for d in loads:
        d.wait()

    def copy(src, dst, send, recv, who):
        return pltpu.make_async_remote_copy(
            src_ref=src, dst_ref=dst, send_sem=send, recv_sem=recv, device_id=who, device_id_type=MESH
        )

    def part(ref, h):
        return ref.at[pl.ds(HALF * h, HALF), :]

    def send_x(k, src, h):
        @pl.when(jnp.logical_and(k <= 3 - j, j >= 1))
        def _():
            copy(part(src, h), part(xbuf.at[k + 1], h), x_s.at[k, h], x_r.at[k + 1, h], dn).start()

        @pl.when(jnp.logical_and(k > 3 - j, j <= 2))
        def _():
            copy(part(src, h), part(xbuf.at[k - 1], h), x_s.at[k, h], x_r.at[k - 1, h], up).start()

    def send_p(k, src, h):
        if k < 4:
          @pl.when(jnp.logical_and(k <= j, j <= 1))
          def _():
            copy(part(src, h), part(pbuf.at[PLACE[k + 1]], h), p_s.at[k, h], p_r.at[k + 1, h], up).start()

        if k > 2:
          @pl.when(jnp.logical_and(k > j, j >= 2))
          def _():
            copy(part(src, h), part(pbuf.at[PLACE[k - 1]], h), p_s.at[k, h], p_r.at[k - 1, h], dn).start()

    def wait_x(k, h, whole=False):
        dst = xbuf.at[k] if whole else part(xbuf.at[k], h)
        copy(dst, dst, x_s.at[k, h], x_r.at[k, h], up).wait_recv()

    def quarter(k, q):
        return xbuf.at[k, pl.ds(HALF // 2 * q, HALF // 2), :]

    hop_in = [copy(quarter(4, q), quarter(4, q), x_s.at[5, q], x_r.at[4, q], zm) for q in range(4)]
    hop_up = [copy(quarter(4, q), quarter(3, q), x_s.at[4, q], x_r.at[3, q // 2], up) for q in range(4)]

    def wait_p(k, h):
        dst = part(pbuf.at[PLACE[k]], h)
        copy(dst, dst, p_s.at[k, h], p_r.at[k, h], up).wait_recv()

    def pass_x(k, h):
        wait_x(k, h)
        send_x(k, xbuf.at[k], h)

    def pass_p(k):
        for h in range(2):
            wait_p(k, h)
            send_p(k, pbuf.at[PLACE[k]], h)

    def x_done(k, src):
        @pl.when(jnp.logical_or(jnp.logical_and(k <= 3 - j, j >= 1), jnp.logical_and(k > 3 - j, j <= 2)))
        def _():
            for h in range(2):
                copy(part(src, h), part(xbuf.at[1], h), x_s.at[k, h], x_r.at[1, h], up).wait_send()

    def p_done(k, src):
        @pl.when(jnp.logical_or(jnp.logical_and(k <= j, j <= 1), jnp.logical_and(k > j, j >= 2)))
        def _():
            for h in range(2):
                copy(part(src, h), part(pbuf.at[0], h), p_s.at[k, h], p_r.at[1, h], up).wait_send()

    middle = lax.rem(lax.div(j + 1, 2), 2)
    outer = middle == 0
    inner = middle == 1
    xk0 = 1 + 2 * lax.div(j, 3)
    xk1 = 2 + middle
    xk2 = 6 - xk0 - xk1
    guest = copy(img, xbuf.at[5], x_s.at[6, 0], x_r.at[5, 0], up)

    w_swap = copy(wsh, wtmp, w_s.at[0], w_r.at[0], sib)
    w_swap.start()
    pool_swap = copy(pool, psib, h_s.at[2], h_r.at[2], sib)
    x_hop = [
        copy(img.at[pl.ds(HALF // 2 * q, HALF // 2), :], quarter(4, q), x_s.at[5, q], x_r.at[4, q], zm)
        for q in range(4)
    ]
    p_hop = [copy(part(pool, h), part(pbuf.at[PLACE[4]], h), p_s.at[5, h], p_r.at[4, h], zp) for h in range(2)]

    @pl.when(j <= 2)
    def _():
        for d in x_hop:
            d.start()

    send_x(0, img, 0)
    send_x(0, img, 1)

    @pl.when(j == 1)
    def _():
        send_p(0, pool, 0)

    @pl.when(j >= 1)
    def _():
        for d in p_hop:
            d.start()

    v, xr = normalize(img[...].astype(F32))
    ximg[...] = v
    xb[0] = v.astype(BF16)

    def chip(h, off):
        return h * 4 + lax.rem(x + off, 4)

    def rows_of(m, start, size):
        return wf.at[pl.ds(pl.multiple_of(m * CHIP + start, 16), size), :]

    def piece(m, p):
        return rows_of(m, 64 * c, AHEAD) if p == 0 else rows_of(m, 64 * c + AHEAD, UNIT - AHEAD)

    def w_copy(src, dst, ident, who, send=None):
        return copy(src, dst, w_s.at[ident if send is None else send], w_r.at[ident], who)

    w_sent = []

    def w_go(src, ident, who):
        d = w_copy(src, src, ident, who)
        d.start()
        w_sent.append(d)

    mine = chip(yh, 0)
    theirs = chip(1 - yh, 0)
    w_swap.wait_recv()
    own_rows = wsh[...].astype(F32)
    sib_rows = wtmp[...].astype(F32)
    first = c == 0
    wf[pl.ds(pl.multiple_of(mine * CHIP, 16), CHIP), :] = jnp.concatenate(
        [jnp.where(first, own_rows, sib_rows), jnp.where(first, sib_rows, own_rows)], axis=0
    ).astype(BF16)

    edge_up = [w_copy(piece(mine, p), piece(mine, p), 13 + p, up) for p in range(2)]
    edge_dn = [w_copy(piece(mine, p), piece(mine, p), 13 + p, dn) for p in range(2)]
    pass_up = [w_copy(piece(theirs, p), piece(theirs, p), 13 + p, up, 15 + p) for p in range(2)]
    pass_dn = [w_copy(piece(theirs, p), piece(theirs, p), 13 + p, dn, 15 + p) for p in range(2)]

    @pl.when(j == 3)
    def _():
        for d in edge_up:
            d.start()

    @pl.when(j == 0)
    def _():
        for d in edge_dn:
            d.start()

    def along_x(r, m):
        return {
            (d, p): w_copy(piece(m, p), piece(m, p), 1 + 4 * r + 2 * d + p, xp if d == 0 else xm)
            for d in range(2)
            for p in range(2)
        }

    mine_x = along_x(0, mine)
    theirs_x = along_x(1, theirs)
    for key in ((0, 0), (1, 1), (0, 1), (1, 0)):
        mine_x[key].start()
    w_sent.extend(mine_x.values())
    w_sent.extend(theirs_x.values())
    pool_swap.start()

    def slab_rows(n):
        m = chip(1 - yh if n < 4 else yh, ORDER[n % 4])
        return ptf[pl.ds(pl.multiple_of(m * CHIP + SHARD * c, 8), SHARD), :]

    def transpose_into(ref, start):
        ptf[...] = ref[...].astype(F32).T
        for n in range(0, 8, 2):
            pt[SHARD * n:SHARD * (n + 2), start:start + ROWS] = jnp.concatenate(
                [slab_rows(n), slab_rows(n + 1)], axis=0
            ).astype(BF16)

    def to_sibling(m, ident):
        w_go(rows_of(m, 80 * c, PART), ident, sib)

    def near_first(r, h):
        for d, (off, onward) in enumerate(((3, xp), (1, xm))):
            got = piece(chip(h, off), d)
            w_copy(got, got, 1 + 4 * r + 3 * d, xp).wait_recv()
            w_go(got, 9 + 2 * r + d, onward)

    def near_rest(r, h):
        for d, off in enumerate((3, 1)):
            m = chip(h, off)
            got = piece(m, 1 - d)
            w_copy(got, got, 2 + 4 * r + d, xp).wait_recv()
            to_sibling(m, 17 + 4 * r + d)

    def far_units(r, h):
        m = chip(h, 2)
        for p in range(2):
            w_copy(piece(m, p), piece(m, p), 9 + 2 * r + p, xp).wait_recv()
        to_sibling(m, 19 + 4 * r)

    edge_in = [w_copy(piece(theirs, p), piece(theirs, p), 13 + p, xp) for p in range(2)]
    theirs_part = rows_of(theirs, 80 * c, PART)
    theirs_sib = w_copy(theirs_part, theirs_part, 20, sib)
    w_sent.append(theirs_sib)

    def theirs_first():
        edge_in[0].wait_recv()

        @pl.when(j == 0)
        def _():
            pass_up[0].start()

        @pl.when(j == 3)
        def _():
            pass_dn[0].start()

        theirs_x[0, 0].start()

    def theirs_rest():
        edge_in[1].wait_recv()

        @pl.when(j == 0)
        def _():
            pass_up[1].start()

        @pl.when(j == 3)
        def _():
            pass_dn[1].start()

        for key in ((1, 1), (0, 1), (1, 0)):
            theirs_x[key].start()
        theirs_sib.start()

    def hop_on(h):
        @pl.when(j <= 2)
        def _():
            for q in (2 * h, 2 * h + 1):
                hop_in[q].wait_recv()
                hop_up[q].start()

        @pl.when(inner)
        def _():
            pass_x(1, h)

    hop_on(0)
    transpose_into(pool, 0)

    @pl.when(outer)
    def _():
        theirs_first()

    near_first(0, yh)

    @pl.when(outer)
    def _():
        theirs_rest()

    hop_on(1)
    near_rest(0, yh)
    pool_swap.wait_recv()
    transpose_into(psib, ROWS)

    @pl.when(j == 0)
    def _():
        send_p(0, pool, 0)
        send_p(0, pool, 1)
        guest.start()

    @pl.when(j == 3)
    def _():
        pass_p(4)

    @pl.when(inner)
    def _():
        pass_x(3, 0)
        theirs_first()

    far_units(0, yh)

    @pl.when(inner)
    def _():
        pass_x(3, 1)
        theirs_rest()
        pass_x(2, 0)

    @pl.when(j == 2)
    def _():
        pass_p(4)

    @pl.when(j == 1)
    def _():
        pass_x(2, 1)

    near_first(1, 1 - yh)

    @pl.when(j == 2)
    def _():
        pass_x(2, 1)

    @pl.when(j == 1)
    def _():
        send_p(0, pool, 1)

    near_rest(1, 1 - yh)

    @pl.when(j == 1)
    def _():
        pass_p(1)

    @pl.when(j == 2)
    def _():
        pass_p(3)

    far_units(1, 1 - yh)

    def ready(k):
        xb[k] = normalize(xbuf[k].astype(F32))[0].astype(BF16)

    @pl.when(inner)
    def _():
        for k in range(1, 4):
            ready(k)

    for ident, m in (
        (17, chip(yh, 3)), (18, chip(yh, 1)), (19, chip(yh, 2)), (20, theirs),
        (21, chip(1 - yh, 3)), (22, chip(1 - yh, 1)), (23, chip(1 - yh, 2)),
    ):
        got = rows_of(m, 80 - 80 * c, PART)
        w_copy(got, got, ident, sib).wait_recv()

    temper = jnp.exp(jnp.full((1, 1), log_scale[0], F32))
    offset = jnp.full((1, 1), bias[0], F32)
    gain = temper * (1.0 / ROWS)

    def project(block, out):
        for start in range(0, WIDTH, 512):
            cols = pl.ds(start, min(512, WIDTH - start))
            out[:, cols] = jnp.dot(block, wf[:, cols], preferred_element_type=F32) + hb[:, cols]

    def weights(a, b, own):
        l = temper * lax.dot_general(a, b, NT, preferred_element_type=F32) + offset
        if own:
            eye = lax.broadcasted_iota(jnp.int32, l.shape, 0) == lax.broadcasted_iota(jnp.int32, l.shape, 1)
            l = jnp.where(eye, -l, l)
        g = gain / (1.0 + jnp.exp(-l))
        if own:
            g = jnp.where(eye, -g, g)
        return l, g.astype(BF16)

    def losses(m):
        e = jnp.maximum(m, 0.0) + jnp.log1p(jnp.exp(-jnp.abs(m)))
        total = e[:, :ROWS]
        for start in range(ROWS, m.shape[1], ROWS):
            total = total + e[:, start:start + ROWS]
        return jnp.sum(total.T, axis=0, keepdims=True)

    def image_side(d, row):
        loss_out[...] = row * (1.0 / ROWS)
        v = ximg[...]
        img_out[...] = (xr * (d - v * jnp.sum(v * d, axis=-1, keepdims=True))).astype(BF16)

    project(pool[...], ztxt)
    v, zr = normalize(ztxt[...])
    ztxt[...] = v
    zb[0] = v.astype(BF16)

    def text_grad(a, own):
        _, g = weights(zb[0], a, own)
        return jnp.dot(g, a, preferred_element_type=F32)

    def text_side(d):
        v = ztxt[...]
        dzb[:ROWS] = (zr * (d - v * jnp.sum(v * d, axis=-1, keepdims=True))).astype(BF16)

    @pl.when(inner)
    def _():
        text_side(text_grad(xb[0:4].reshape(4 * ROWS, WIDTH), True))

    @pl.when(outer)
    def _():
        for k in (xk0, xk1):
            wait_x(k, 0)
            wait_x(k, 1)
            ready(k)
        u[:ROWS] = text_grad(xb[0], True) + text_grad(xb[xk0], False) + text_grad(xb[xk1], False)
        wait_x(xk2, 0)
        wait_x(xk2, 1)
        ready(xk2)
        text_side(u[:ROWS] + text_grad(xb[xk2], False))

    pair = copy(dzb.at[:ROWS], dzb.at[ROWS:], h_s.at[3], h_r.at[3], sib)
    pair.start()

    def make(n):
        t = jnp.dot(pt[SHARD * n:SHARD * (n + 2), :], dzb[...], preferred_element_type=F32)
        terms[n] = t[:SHARD]
        terms[n + 1] = t[SHARD:]

    def cols(n, q):
        start, size, _ = PIECES[q]
        return terms[n, :, start:start + size]

    g_sent = []

    def g_go(src, value, ident, dst, who):
        src[...] = value.astype(BF16)
        d = copy(src, dst, g_s.at[ident], g_r.at[ident], who)
        d.start()
        g_sent.append(d)

    def g_wait(ref, ident):
        copy(ref, ref, g_s.at[ident], g_r.at[ident], xp).wait_recv()
        return ref[...].astype(F32)

    def slot(refs, q, *index):
        return refs[q].at[index] if index else refs[q]

    def far_sends(g):
        for q, (_, _, way) in enumerate(PIECES):
            g_go(slot(g_out, q, g, 0), cols(4 * g, q), 12 * g + q, slot(g_far, q, g), xp if way > 0 else xm)

    def near_sends(g):
        for q, (_, _, way) in enumerate(PIECES):
            n, who = (2, xm) if way > 0 else (1, xp)
            g_go(slot(g_out, q, g, 1), cols(4 * g + n, q), 12 * g + 4 + q, slot(g_near, q, g, 0), who)

    def second_sends(g):
        for q, (_, _, way) in enumerate(PIECES):
            n, who = (1, xp) if way > 0 else (2, xm)
            value = cols(4 * g + n, q) + g_wait(slot(g_far, q, g), 12 * g + q)
            g_go(slot(g_out, q, g, 2), value, 12 * g + 8 + q, slot(g_near, q, g, 1), who)

    def total(g, q):
        value = cols(4 * g + 3, q) + g_wait(slot(g_near, q, g, 0), 12 * g + 4 + q)
        return value + g_wait(slot(g_near, q, g, 1), 12 * g + 8 + q)

    def back():
        @pl.loop(0, WIDTH // TILE)
        def _(n):
            cols = pl.ds(pl.multiple_of(n * TILE, TILE), TILE)
            pool_out[:, cols] = lax.dot_general(
                dzb[:ROWS], wf[cols, :], NT, preferred_element_type=F32
            ).astype(BF16)

    gdx_up = copy(gdx_out, gdx_in, h_s.at[0], h_r.at[0], up)
    gdx_dn = copy(gdx_out, gdx_in, h_s.at[0], h_r.at[0], dn)
    gsum_up = copy(gsum_out, gsum_in, h_s.at[1], h_r.at[1], up)
    gsum_dn = copy(gsum_out, gsum_in, h_s.at[1], h_r.at[1], dn)

    @pl.when(outer)
    def _():
        m, g = weights(xb[0], zb[0], True)
        u[ROWS:2 * ROWS] = jnp.dot(g, zb[0], preferred_element_type=F32)
        loss_out[...] = losses(m)

    def texts_done(first, last):
        for n in range(first, last):
            v = u[ROWS * (n - 1):ROWS * n]
            zb[n] = normalize(v)[0].astype(BF16)

    def meet(image, texts, own):
        m, g = weights(image, texts, own)
        return jnp.dot(g, texts, preferred_element_type=F32), losses(m)

    @pl.when(inner)
    def _():
        back()

    pair.wait_recv()
    make(0)
    far_sends(0)
    make(2)
    near_sends(0)

    @pl.when(j == 1)
    def _():
        for h in range(2):
            wait_p(3, h)
            wait_p(4, h)

    @pl.when(j == 2)
    def _():
        for h in range(2):
            wait_p(1, h)

    @pl.when(inner)
    def _():
        project(pbuf[0:3].reshape(3 * ROWS, WIDTH), u.at[:3 * ROWS])

    @pl.when(outer)
    def _():
        make(4)
        make(6)
        back()

    second_sends(0)

    @pl.when(inner)
    def _():
        make(4)
        make(6)

    far_sends(1)
    near_sends(1)

    @pl.when(j == 1)
    def _():
        wait_x(5, 0, whole=True)
        ready(5)

    @pl.when(inner)
    def _():
        texts_done(1, 4)
        d, row = meet(xb[9 - 4 * j], zb[pl.ds(4 - 2 * j, 2)].reshape(2 * ROWS, WIDTH), False)
        gdx[...] = d
        gsum_out[...] = row

    for q, (_, _, way) in enumerate(PIECES):
        g_go(slot(y_out, q), total(0, q), 24 + q, slot(y_pass, q), y_up if way > 0 else y_dn)

    onward = [
        copy(slot(y_pass, q), slot(y_in, q), g_s.at[28 + q], g_r.at[28 + q], y_up if way > 0 else y_dn)
        for q, (_, _, way) in enumerate(PIECES)
    ]

    def relay():
        for q in range(4):
            copy(slot(y_pass, q), slot(y_pass, q), g_s.at[24 + q], g_r.at[24 + q], xp).wait_recv()
            onward[q].start()

    @pl.when(inner)
    def _():
        for h in range(2):
            wait_p(2, h)
        project(pbuf[3], u.at[3 * ROWS:])
        texts_done(4, 5)
        d, row = meet(xb[9 - 4 * j], zb[4], False)
        gdx_out[...] = (gdx[...] + d).astype(BF16)
        gsum_out[...] += row

        @pl.when(j == 1)
        def _():
            gdx_dn.start()
            gsum_dn.start()

        @pl.when(j == 2)
        def _():
            gdx_up.start()
            gsum_up.start()

    second_sends(1)

    @pl.when(inner)
    def _():
        d, row = meet(xb[0], zb[0:3].reshape(3 * ROWS, WIDTH), True)
        e, more = meet(xb[0], zb[4], False)
        image_side(d + e, row + more)

    relay()

    for q, (start, size, _) in enumerate(PIECES):
        head_out[:, start:start + size] = total(1, q)

    @pl.when(outer)
    def _():
        gsum_up.wait_recv()
        gdx_up.wait_recv()
        image_side(u[ROWS:2 * ROWS] + gdx_in[...].astype(F32), loss_out[...] + gsum_in[...])

    for q, (start, size, _) in enumerate(PIECES):
        head_out[:, start:start + size] += g_wait(slot(y_in, q), 28 + q)

    w_swap.wait_send()
    for d in w_sent:
        d.wait_send()

    @pl.when(j == 3)
    def _():
        for d in edge_up + pass_dn:
            d.wait_send()

    @pl.when(j == 0)
    def _():
        for d in edge_dn + pass_up:
            d.wait_send()

    @pl.when(j <= 2)
    def _():
        for d in x_hop + hop_up:
            d.wait_send()

    @pl.when(j >= 1)
    def _():
        for d in p_hop:
            d.wait_send()

    @pl.when(j == 0)
    def _():
        guest.wait_send()

    @pl.when(inner)
    def _():
        gdx_up.wait_send()
        gsum_up.wait_send()

    x_done(0, img)
    p_done(0, pool)
    for k in range(1, 4):
        x_done(k, xbuf.at[k])
        p_done(k, pbuf.at[0])
    p_done(4, pbuf.at[0])
    pool_swap.wait_send()
    pair.wait_send()
    for d in g_sent + onward:
        d.wait_send()


def finish(*refs):
    moves = [pltpu.make_async_copy(refs[i], refs[4 + i], refs[8].at[i]) for i in range(4)]
    for d in moves:
        d.start()
    for d in moves:
        d.wait()


def per_device(images, pooled, head_weight, head_bias, log_scale, bias):
    smem = pl.BlockSpec(memory_space=pltpu.SMEM)
    vmem = pl.BlockSpec(memory_space=pltpu.VMEM)
    hbm = pl.BlockSpec(memory_space=pltpu.HBM)
    block = (ROWS, WIDTH)
    slab = (SHARD, WIDTH)
    parts = [(SHARD, size) for _, size, _ in PIECES]
    dma = pltpu.SemaphoreType.DMA
    results = (
        jax.ShapeDtypeStruct((1, ROWS), F32),
        jax.ShapeDtypeStruct(block, BF16),
        jax.ShapeDtypeStruct(block, BF16),
        jax.ShapeDtypeStruct(slab, F32),
    )
    made = pl.pallas_call(
        kernel,
        out_shape=results,
        in_specs=[hbm, hbm, hbm, hbm, smem, smem],
        out_specs=(vmem,) * 4,
        scratch_shapes=[
            pltpu.VMEM(block, BF16),
            pltpu.VMEM(block, BF16),
            pltpu.VMEM(slab, BF16),
            pltpu.VMEM((1, WIDTH), F32),
            pltpu.VMEM(slab, BF16),
            pltpu.VMEM((WIDTH, WIDTH), BF16),
            pltpu.VMEM((6,) + block, BF16),
            pltpu.VMEM((4,) + block, BF16),
            pltpu.VMEM((6,) + block, BF16),
            pltpu.VMEM((5,) + block, BF16),
            pltpu.VMEM(block, F32),
            pltpu.VMEM(block, F32),
            pltpu.VMEM((4 * ROWS, WIDTH), F32),
            pltpu.VMEM((2 * ROWS, WIDTH), BF16),
            pltpu.VMEM(block, BF16),
            pltpu.VMEM((WIDTH, ROWS), F32),
            pltpu.VMEM((8 * SHARD, 2 * ROWS), BF16),
            pltpu.VMEM((8,) + slab, F32),
            [pltpu.VMEM((2, 3) + p, BF16) for p in parts],
            [pltpu.VMEM((2,) + p, BF16) for p in parts],
            [pltpu.VMEM((2, 2) + p, BF16) for p in parts],
            [pltpu.VMEM(p, BF16) for p in parts],
            [pltpu.VMEM(p, BF16) for p in parts],
            [pltpu.VMEM(p, BF16) for p in parts],
            pltpu.VMEM(block, F32),
            pltpu.VMEM(block, BF16),
            pltpu.VMEM((1, ROWS), F32),
            pltpu.VMEM(block, BF16),
            pltpu.VMEM((1, ROWS), F32),
            dma((4,)),
            dma((24,)), dma((24,)),
            dma((7, 4)), dma((6, 4)),
            dma((6, 2)), dma((5, 2)),
            dma((32,)), dma((32,)),
            dma((4,)), dma((4,)),
        ],
        compiler_params=pltpu.CompilerParams(
            collective_id=0, has_side_effects=True, vmem_limit_bytes=VMEM_GRANT
        ),
        cost_estimate=pl.CostEstimate(flops=4_000_000_000, bytes_accessed=6_000_000, transcendentals=300_000),
    )(*[pltpu.with_memory_space_constraint(v, pltpu.HBM) for v in (images, pooled, head_weight, head_bias)], log_scale, bias)
    loss, image_grad, pooled_grad, head_grad = pl.pallas_call(
        finish,
        out_shape=results,
        in_specs=[vmem] * 4,
        out_specs=(hbm,) * 4,
        scratch_shapes=[dma((4,))],
        compiler_params=pltpu.CompilerParams(vmem_limit_bytes=4 * 1024 * 1024),
    )(*made)
    return loss.reshape(ROWS), image_grad, pooled_grad, head_grad


def solution(mesh):
    in_specs = (P(("dp", "fsdp"), None), P(("dp", "fsdp"), None), P("fsdp", None), P(), P(), P())
    out_specs = (
        P(("dp", "fsdp")),
        P(("dp", "fsdp"), None),
        P(("dp", "fsdp"), None),
        P(("dp", "fsdp"), None),
    )
    return jax.shard_map(
        per_device, mesh=mesh, in_specs=in_specs, out_specs=out_specs, check_vma=False
    )
```

```python
import jax
import jax.numpy as jnp
from jax import lax
from jax.experimental import pallas as pl
from jax.experimental.pallas import tpu as pltpu
from jax.sharding import PartitionSpec as P

MESH = pl.DeviceIdType.MESH
F32 = jnp.float32
BF16 = jnp.bfloat16
NT = (((1,), (1,)), ((), ()))

ROWS = 128
WIDTH = 1152
SHARD = 72
CHIP = 144
FIRST = 640
TILE = 384
VMEM_GRANT = 44 * 1024 * 1024
HALF = 64
PIECES = ((0, 384, 1), (640, 256, -1), (384, 256, 1), (896, 256, -1))
PLACE = {1: 0, 3: 1, 4: 2, 2: 3}
ORDER = (2, 1, 3, 0)


def normalize(v):
    r = lax.rsqrt(jnp.sum(v * v, axis=-1, keepdims=True) + 1e-06)
    return v * r, r


def kernel(
    img_hbm, pool_hbm, wsh_hbm, hb_hbm, log_scale, bias,
    loss_out, img_out, pool_out, head_out,
    img, pool, hb,
    wa, wb, wf, xbuf, pbuf, xb, zb, ximg, ztxt, u, dzb, psib, ptf, pt, terms,
    g_out, g_far, g_near,
    y_out, y_pass, y_in,
    gdx, gdx_out, gsum_out, gdx_in, gsum_in,
    l_s, w_s, w_r, x_s, x_r, p_s, p_r, g_s, g_r, h_s, h_r,
):
    dp = lax.axis_index("dp")
    f = lax.axis_index("fsdp")
    j = lax.rem(dp, 4)
    yh = lax.div(f, 8)
    x = lax.rem(lax.div(f, 2), 4)
    c = lax.rem(f, 2)
    base = yh * 8 + c

    sib = (dp, f + 1 - 2 * c)
    xp = (dp, base + 2 * lax.rem(x + 1, 4))
    xm = (dp, base + 2 * lax.rem(x + 3, 4))
    zp = (lax.rem(dp + 4, 32), f)
    zm = (lax.rem(dp + 28, 32), f)
    wrap_up = lax.div(j + 1, 4)
    up = (dp + 1 - 4 * wrap_up, lax.rem(f + 8 * wrap_up, 16))
    wrap_dn = lax.div(3 - j, 3)
    dn = (dp - 1 + 4 * wrap_dn, lax.rem(f + 8 * wrap_dn, 16))
    odd = lax.rem(j, 2)
    step = 3 - 2 * odd
    wrap = lax.div(j + step, 4)
    y_up = (dp + step - 4 * wrap, lax.rem(f + 8 * wrap, 16))
    step = 1 + 2 * odd
    wrap = lax.div(3 - j, 2)
    y_dn = (dp - step + 4 * wrap, lax.rem(f + 8 * wrap, 16))

    across = (dp - j + lax.rem(j + 2, 4), lax.rem(f + 8, 16))
    mine = yh * 4 + x
    theirs = 4 - yh * 4 + x

    loads = [
        pltpu.make_async_copy(src, dst, l_s.at[i])
        for i, (src, dst) in enumerate(
            (
                (wsh_hbm.at[:, :FIRST], wa.at[c, mine]),
                (wsh_hbm.at[:, FIRST:], wb.at[c, mine]),
                (img_hbm, img),
                (pool_hbm, pool),
                (hb_hbm, hb.at[0]),
            )
        )
    ]
    for d in loads:
        d.start()

    barrier = pltpu.get_barrier_semaphore()
    for who in (sib, xp, xm, zp, zm, up, dn, across):
        pl.semaphore_signal(barrier, inc=1, device_id=who, device_id_type=MESH)

    @pl.when(odd == 0)
    def _():
        pl.semaphore_signal(barrier, inc=1, device_id=y_up, device_id_type=MESH)

    @pl.when(odd == 1)
    def _():
        pl.semaphore_signal(barrier, inc=1, device_id=y_dn, device_id_type=MESH)

    pl.semaphore_wait(barrier, 9)
    for d in loads:
        d.wait()

    def copy(src, dst, send, recv, who):
        return pltpu.make_async_remote_copy(
            src_ref=src, dst_ref=dst, send_sem=send, recv_sem=recv, device_id=who, device_id_type=MESH
        )

    def part(ref, h):
        return ref.at[pl.ds(HALF * h, HALF), :]

    def send_x(k, src, h):
        @pl.when(jnp.logical_and(k <= 3 - j, j >= 1))
        def _():
            copy(part(src, h), part(xbuf.at[k + 1], h), x_s.at[k, h], x_r.at[k + 1, h], dn).start()

        @pl.when(jnp.logical_and(k > 3 - j, j <= 2))
        def _():
            copy(part(src, h), part(xbuf.at[k - 1], h), x_s.at[k, h], x_r.at[k - 1, h], up).start()

    def send_p(k, src, h):
        if k < 4:
          @pl.when(jnp.logical_and(k <= j, j <= 1))
          def _():
            copy(part(src, h), part(pbuf.at[PLACE[k + 1]], h), p_s.at[k, h], p_r.at[k + 1, h], up).start()

        if k > 2:
          @pl.when(jnp.logical_and(k > j, j >= 2))
          def _():
            copy(part(src, h), part(pbuf.at[PLACE[k - 1]], h), p_s.at[k, h], p_r.at[k - 1, h], dn).start()

    def wait_x(k, h, whole=False):
        dst = xbuf.at[k] if whole else part(xbuf.at[k], h)
        copy(dst, dst, x_s.at[k, h], x_r.at[k, h], up).wait_recv()

    def quarter(k, q):
        return xbuf.at[k, pl.ds(HALF // 2 * q, HALF // 2), :]

    hop_in = [copy(quarter(4, q), quarter(4, q), x_s.at[5, q], x_r.at[4, q], zm) for q in range(4)]
    hop_up = [copy(quarter(4, q), quarter(3, q), x_s.at[4, q], x_r.at[3, q // 2], up) for q in range(4)]

    def wait_p(k, h):
        dst = part(pbuf.at[PLACE[k]], h)
        copy(dst, dst, p_s.at[k, h], p_r.at[k, h], up).wait_recv()

    def pass_x(k, h):
        wait_x(k, h)
        send_x(k, xbuf.at[k], h)

    def pass_p(k):
        for h in range(2):
            wait_p(k, h)
            send_p(k, pbuf.at[PLACE[k]], h)

    def x_done(k, src):
        @pl.when(jnp.logical_or(jnp.logical_and(k <= 3 - j, j >= 1), jnp.logical_and(k > 3 - j, j <= 2)))
        def _():
            for h in range(2):
                copy(part(src, h), part(xbuf.at[1], h), x_s.at[k, h], x_r.at[1, h], up).wait_send()

    def p_done(k, src):
        @pl.when(jnp.logical_or(jnp.logical_and(k <= j, j <= 1), jnp.logical_and(k > j, j >= 2)))
        def _():
            for h in range(2):
                copy(part(src, h), part(pbuf.at[0], h), p_s.at[k, h], p_r.at[1, h], up).wait_send()

    middle = lax.rem(lax.div(j + 1, 2), 2)
    outer = middle == 0
    inner = middle == 1
    xk0 = 1 + 2 * lax.div(j, 3)
    xk1 = 2 + middle
    xk2 = 6 - xk0 - xk1
    guest = copy(img, xbuf.at[5], x_s.at[6, 0], x_r.at[5, 0], up)

    pool_swap = copy(pool, psib, h_s.at[2], h_r.at[2], sib)
    x_hop = [
        copy(img.at[pl.ds(HALF // 2 * q, HALF // 2), :], quarter(4, q), x_s.at[5, q], x_r.at[4, q], zm)
        for q in range(4)
    ]
    p_hop = [copy(part(pool, h), part(pbuf.at[PLACE[4]], h), p_s.at[5, h], p_r.at[4, h], zp) for h in range(2)]

    @pl.when(j <= 2)
    def _():
        for d in x_hop:
            d.start()

    send_x(0, img, 0)
    send_x(0, img, 1)

    def chip(h, off):
        return h * 4 + lax.rem(x + off, 4)

    def piece(m, p):
        return (wa if p == 0 else wb).at[c, m]

    def w_copy(src, dst, ident, who, send=None):
        return copy(src, dst, w_s.at[ident if send is None else send], w_r.at[ident], who)

    w_sent = []

    def w_go(src, ident, who):
        d = w_copy(src, src, ident, who)
        d.start()
        w_sent.append(d)

    def to_sibling(n, m, p):
        w_go(piece(m, p), 17 + 2 * n + p, sib)

    def assemble(n, m):
        for p in range(2):
            src = (wa if p == 0 else wb).at[1 - c, m]
            w_copy(src, src, 17 + 2 * n + p, sib).wait_recv()
        rows = pl.ds(pl.multiple_of(m * CHIP, 16), CHIP)
        for ref, cols in ((wa, slice(0, FIRST)), (wb, slice(FIRST, WIDTH))):
            wf[rows, cols] = jnp.concatenate(
                [ref[0, m].astype(F32), ref[1, m].astype(F32)], axis=0
            ).astype(BF16)

    edge_up = [w_copy(piece(mine, p), piece(mine, p), 13 + p, up) for p in range(2)]
    edge_dn = [w_copy(piece(mine, p), piece(mine, p), 13 + p, dn) for p in range(2)]
    edge_far = [w_copy(piece(mine, p), piece(mine, p), 13 + p, across, 15 + p) for p in range(2)]

    @pl.when(j == 3)
    def _():
        for d in edge_up:
            d.start()

    @pl.when(j == 0)
    def _():
        for d in edge_dn:
            d.start()

    @pl.when(outer)
    def _():
        for d in edge_far:
            d.start()

    def along_x(r, m):
        return {
            (d, p): w_copy(piece(m, p), piece(m, p), 1 + 4 * r + 2 * d + p, xp if d == 0 else xm)
            for d in range(2)
            for p in range(2)
        }

    mine_x = along_x(0, mine)
    theirs_x = along_x(1, theirs)
    for key in ((0, 0), (1, 1), (0, 1), (1, 0)):
        mine_x[key].start()
    w_sent.extend(mine_x.values())
    w_sent.extend(theirs_x.values())
    to_sibling(0, mine, 0)
    to_sibling(0, mine, 1)
    pool_swap.start()

    @pl.when(j == 1)
    def _():
        send_p(0, pool, 0)

    @pl.when(j >= 1)
    def _():
        for d in p_hop:
            d.start()

    v, xr = normalize(img[...].astype(F32))
    ximg[...] = v
    xb[0] = v.astype(BF16)

    def slab_rows(n):
        m = chip(1 - yh if n < 4 else yh, ORDER[n % 4])
        return ptf[pl.ds(pl.multiple_of(m * CHIP + SHARD * c, 8), SHARD), :]

    def transpose_into(ref, start):
        ptf[...] = ref[...].astype(F32).T
        for n in range(0, 8, 2):
            pt[SHARD * n:SHARD * (n + 2), start:start + ROWS] = jnp.concatenate(
                [slab_rows(n), slab_rows(n + 1)], axis=0
            ).astype(BF16)

    def near_first(r, h):
        for d, (off, onward) in enumerate(((3, xp), (1, xm))):
            got = piece(chip(h, off), d)
            w_copy(got, got, 1 + 4 * r + 3 * d, xp).wait_recv()
            w_go(got, 9 + 2 * r + d, onward)
            to_sibling(1 + 4 * r + d, chip(h, off), d)

    def near_rest(r, h):
        for d, off in enumerate((3, 1)):
            m = chip(h, off)
            got = piece(m, 1 - d)
            w_copy(got, got, 2 + 4 * r + d, xp).wait_recv()
            to_sibling(1 + 4 * r + d, m, 1 - d)

    def far_units(r, h):
        m = chip(h, 2)
        for p in range(2):
            w_copy(piece(m, p), piece(m, p), 9 + 2 * r + p, xp).wait_recv()
            to_sibling(3 + 4 * r, m, p)

    edge_in = [w_copy(piece(theirs, p), piece(theirs, p), 13 + p, xp) for p in range(2)]

    def theirs_first():
        edge_in[0].wait_recv()
        theirs_x[0, 0].start()
        theirs_sib[0].start()

    def theirs_rest():
        edge_in[1].wait_recv()
        for key in ((1, 1), (0, 1), (1, 0)):
            theirs_x[key].start()
        theirs_sib[1].start()

    theirs_sib = [w_copy(piece(theirs, p), piece(theirs, p), 25 + p, sib) for p in range(2)]
    w_sent.extend(theirs_sib)

    def hop_on(h):
        @pl.when(j <= 2)
        def _():
            for q in (2 * h, 2 * h + 1):
                hop_in[q].wait_recv()
                hop_up[q].start()

        @pl.when(inner)
        def _():
            pass_x(1, h)

    hop_on(0)
    transpose_into(pool, 0)

    @pl.when(outer)
    def _():
        theirs_first()

    near_first(0, yh)

    @pl.when(outer)
    def _():
        theirs_rest()

    hop_on(1)
    near_rest(0, yh)
    pool_swap.wait_recv()
    transpose_into(psib, ROWS)

    @pl.when(j == 0)
    def _():
        send_p(0, pool, 0)
        send_p(0, pool, 1)
        guest.start()

    @pl.when(j == 3)
    def _():
        pass_p(4)

    @pl.when(inner)
    def _():
        pass_x(3, 0)
        theirs_first()

    far_units(0, yh)
    assemble(0, mine)

    @pl.when(inner)
    def _():
        pass_x(3, 1)
        theirs_rest()
        pass_x(2, 0)

    @pl.when(j == 2)
    def _():
        pass_p(4)

    @pl.when(j == 1)
    def _():
        pass_x(2, 1)

    near_first(1, 1 - yh)
    for n, off in ((1, 3), (2, 1), (3, 2)):
        assemble(n, chip(yh, off))

    @pl.when(j == 2)
    def _():
        pass_x(2, 1)

    @pl.when(j == 1)
    def _():
        send_p(0, pool, 1)

    near_rest(1, 1 - yh)

    @pl.when(j == 1)
    def _():
        pass_p(1)

    @pl.when(j == 2)
    def _():
        pass_p(3)

    far_units(1, 1 - yh)

    def ready(k):
        xb[k] = normalize(xbuf[k].astype(F32))[0].astype(BF16)

    @pl.when(inner)
    def _():
        for k in range(1, 4):
            ready(k)

    assemble(4, theirs)
    for n, off in ((5, 3), (6, 1), (7, 2)):
        assemble(n, chip(1 - yh, off))

    temper = jnp.exp(jnp.full((1, 1), log_scale[0], F32))
    offset = jnp.full((1, 1), bias[0], F32)
    gain = temper * (1.0 / ROWS)

    def project(block, out):
        for start in range(0, WIDTH, 512):
            cols = pl.ds(start, min(512, WIDTH - start))
            out[:, cols] = jnp.dot(block, wf[:, cols], preferred_element_type=F32) + hb[:, cols]

    def weights(a, b, own):
        l = temper * lax.dot_general(a, b, NT, preferred_element_type=F32) + offset
        if own:
            eye = lax.broadcasted_iota(jnp.int32, l.shape, 0) == lax.broadcasted_iota(jnp.int32, l.shape, 1)
            l = jnp.where(eye, -l, l)
        g = gain / (1.0 + jnp.exp(-l))
        if own:
            g = jnp.where(eye, -g, g)
        return l, g.astype(BF16)

    def losses(m):
        e = jnp.maximum(m, 0.0) + jnp.log1p(jnp.exp(-jnp.abs(m)))
        total = e[:, :ROWS]
        for start in range(ROWS, m.shape[1], ROWS):
            total = total + e[:, start:start + ROWS]
        return jnp.sum(total.T, axis=0, keepdims=True)

    def image_side(d, row):
        loss_out[...] = row * (1.0 / ROWS)
        v = ximg[...]
        img_out[...] = (xr * (d - v * jnp.sum(v * d, axis=-1, keepdims=True))).astype(BF16)

    project(pool[...], ztxt)
    v, zr = normalize(ztxt[...])
    ztxt[...] = v
    zb[0] = v.astype(BF16)

    def text_grad(a, own):
        _, g = weights(zb[0], a, own)
        return jnp.dot(g, a, preferred_element_type=F32)

    def text_side(d):
        v = ztxt[...]
        dzb[:ROWS] = (zr * (d - v * jnp.sum(v * d, axis=-1, keepdims=True))).astype(BF16)

    @pl.when(inner)
    def _():
        text_side(text_grad(xb[0:4].reshape(4 * ROWS, WIDTH), True))

    @pl.when(outer)
    def _():
        for k in (xk0, xk1):
            wait_x(k, 0)
            wait_x(k, 1)
            ready(k)
        u[:ROWS] = text_grad(xb[0], True) + text_grad(xb[xk0], False) + text_grad(xb[xk1], False)
        wait_x(xk2, 0)
        wait_x(xk2, 1)
        ready(xk2)
        text_side(u[:ROWS] + text_grad(xb[xk2], False))

    pair = copy(dzb.at[:ROWS], dzb.at[ROWS:], h_s.at[3], h_r.at[3], sib)
    pair.start()

    def make(n):
        t = jnp.dot(pt[SHARD * n:SHARD * (n + 2), :], dzb[...], preferred_element_type=F32)
        terms[n] = t[:SHARD]
        terms[n + 1] = t[SHARD:]

    def cols(n, q):
        start, size, _ = PIECES[q]
        return terms[n, :, start:start + size]

    g_sent = []

    def g_go(src, value, ident, dst, who):
        src[...] = value.astype(BF16)
        d = copy(src, dst, g_s.at[ident], g_r.at[ident], who)
        d.start()
        g_sent.append(d)

    def g_wait(ref, ident):
        copy(ref, ref, g_s.at[ident], g_r.at[ident], xp).wait_recv()
        return ref[...].astype(F32)

    def slot(refs, q, *index):
        return refs[q].at[index] if index else refs[q]

    def far_sends(g):
        for q, (_, _, way) in enumerate(PIECES):
            g_go(slot(g_out, q, g, 0), cols(4 * g, q), 12 * g + q, slot(g_far, q, g), xp if way > 0 else xm)

    def near_sends(g):
        for q, (_, _, way) in enumerate(PIECES):
            n, who = (2, xm) if way > 0 else (1, xp)
            g_go(slot(g_out, q, g, 1), cols(4 * g + n, q), 12 * g + 4 + q, slot(g_near, q, g, 0), who)

    def second_sends(g):
        for q, (_, _, way) in enumerate(PIECES):
            n, who = (1, xp) if way > 0 else (2, xm)
            value = cols(4 * g + n, q) + g_wait(slot(g_far, q, g), 12 * g + q)
            g_go(slot(g_out, q, g, 2), value, 12 * g + 8 + q, slot(g_near, q, g, 1), who)

    def total(g, q):
        value = cols(4 * g + 3, q) + g_wait(slot(g_near, q, g, 0), 12 * g + 4 + q)
        return value + g_wait(slot(g_near, q, g, 1), 12 * g + 8 + q)

    def back():
        @pl.loop(0, WIDTH // TILE)
        def _(n):
            cols = pl.ds(pl.multiple_of(n * TILE, TILE), TILE)
            pool_out[:, cols] = lax.dot_general(
                dzb[:ROWS], wf[cols, :], NT, preferred_element_type=F32
            ).astype(BF16)

    gdx_up = copy(gdx_out, gdx_in, h_s.at[0], h_r.at[0], up)
    gdx_dn = copy(gdx_out, gdx_in, h_s.at[0], h_r.at[0], dn)
    gsum_up = copy(gsum_out, gsum_in, h_s.at[1], h_r.at[1], up)
    gsum_dn = copy(gsum_out, gsum_in, h_s.at[1], h_r.at[1], dn)

    @pl.when(outer)
    def _():
        m, g = weights(xb[0], zb[0], True)
        u[ROWS:2 * ROWS] = jnp.dot(g, zb[0], preferred_element_type=F32)
        loss_out[...] = losses(m)

    def texts_done(first, last):
        for n in range(first, last):
            v = u[ROWS * (n - 1):ROWS * n]
            zb[n] = normalize(v)[0].astype(BF16)

    def meet(image, texts, own):
        m, g = weights(image, texts, own)
        return jnp.dot(g, texts, preferred_element_type=F32), losses(m)

    @pl.when(inner)
    def _():
        back()

    pair.wait_recv()
    make(0)
    far_sends(0)
    make(2)
    near_sends(0)

    @pl.when(j == 1)
    def _():
        for h in range(2):
            wait_p(3, h)
            wait_p(4, h)

    @pl.when(j == 2)
    def _():
        for h in range(2):
            wait_p(1, h)

    @pl.when(inner)
    def _():
        project(pbuf[0:3].reshape(3 * ROWS, WIDTH), u.at[:3 * ROWS])

    @pl.when(outer)
    def _():
        make(4)
        make(6)
        back()

    second_sends(0)

    @pl.when(inner)
    def _():
        make(4)
        make(6)

    far_sends(1)
    near_sends(1)

    @pl.when(j == 1)
    def _():
        wait_x(5, 0, whole=True)
        ready(5)

    @pl.when(inner)
    def _():
        texts_done(1, 4)
        d, row = meet(xb[9 - 4 * j], zb[pl.ds(4 - 2 * j, 2)].reshape(2 * ROWS, WIDTH), False)
        gdx[...] = d
        gsum_out[...] = row

    for q, (_, _, way) in enumerate(PIECES):
        g_go(slot(y_out, q), total(0, q), 24 + q, slot(y_pass, q), y_up if way > 0 else y_dn)

    onward = [
        copy(slot(y_pass, q), slot(y_in, q), g_s.at[28 + q], g_r.at[28 + q], y_up if way > 0 else y_dn)
        for q, (_, _, way) in enumerate(PIECES)
    ]

    def relay():
        for q in range(4):
            copy(slot(y_pass, q), slot(y_pass, q), g_s.at[24 + q], g_r.at[24 + q], xp).wait_recv()
            onward[q].start()

    @pl.when(inner)
    def _():
        for h in range(2):
            wait_p(2, h)
        project(pbuf[3], u.at[3 * ROWS:])
        texts_done(4, 5)
        d, row = meet(xb[9 - 4 * j], zb[4], False)
        gdx_out[...] = (gdx[...] + d).astype(BF16)
        gsum_out[...] += row

        @pl.when(j == 1)
        def _():
            gdx_dn.start()
            gsum_dn.start()

        @pl.when(j == 2)
        def _():
            gdx_up.start()
            gsum_up.start()

    second_sends(1)

    @pl.when(inner)
    def _():
        d, row = meet(xb[0], zb[0:3].reshape(3 * ROWS, WIDTH), True)
        e, more = meet(xb[0], zb[4], False)
        image_side(d + e, row + more)

    relay()

    for q, (start, size, _) in enumerate(PIECES):
        head_out[:, start:start + size] = total(1, q)

    @pl.when(outer)
    def _():
        gsum_up.wait_recv()
        gdx_up.wait_recv()
        image_side(u[ROWS:2 * ROWS] + gdx_in[...].astype(F32), loss_out[...] + gsum_in[...])

    for q, (start, size, _) in enumerate(PIECES):
        head_out[:, start:start + size] += g_wait(slot(y_in, q), 28 + q)

    for d in w_sent:
        d.wait_send()

    @pl.when(j == 3)
    def _():
        for d in edge_up:
            d.wait_send()

    @pl.when(j == 0)
    def _():
        for d in edge_dn:
            d.wait_send()

    @pl.when(outer)
    def _():
        for d in edge_far:
            d.wait_send()

    @pl.when(j <= 2)
    def _():
        for d in x_hop + hop_up:
            d.wait_send()

    @pl.when(j >= 1)
    def _():
        for d in p_hop:
            d.wait_send()

    @pl.when(j == 0)
    def _():
        guest.wait_send()

    @pl.when(inner)
    def _():
        gdx_up.wait_send()
        gsum_up.wait_send()

    x_done(0, img)
    p_done(0, pool)
    for k in range(1, 4):
        x_done(k, xbuf.at[k])
        p_done(k, pbuf.at[0])
    p_done(4, pbuf.at[0])
    pool_swap.wait_send()
    pair.wait_send()
    for d in g_sent + onward:
        d.wait_send()


def finish(*refs):
    moves = [pltpu.make_async_copy(refs[i], refs[4 + i], refs[8].at[i]) for i in range(4)]
    for d in moves:
        d.start()
    for d in moves:
        d.wait()


def per_device(images, pooled, head_weight, head_bias, log_scale, bias):
    smem = pl.BlockSpec(memory_space=pltpu.SMEM)
    vmem = pl.BlockSpec(memory_space=pltpu.VMEM)
    hbm = pl.BlockSpec(memory_space=pltpu.HBM)
    block = (ROWS, WIDTH)
    slab = (SHARD, WIDTH)
    parts = [(SHARD, size) for _, size, _ in PIECES]
    dma = pltpu.SemaphoreType.DMA
    results = (
        jax.ShapeDtypeStruct((1, ROWS), F32),
        jax.ShapeDtypeStruct(block, BF16),
        jax.ShapeDtypeStruct(block, BF16),
        jax.ShapeDtypeStruct(slab, F32),
    )
    made = pl.pallas_call(
        kernel,
        out_shape=results,
        in_specs=[hbm, hbm, hbm, hbm, smem, smem],
        out_specs=(vmem,) * 4,
        scratch_shapes=[
            pltpu.VMEM(block, BF16),
            pltpu.VMEM(block, BF16),
            pltpu.VMEM((1, WIDTH), F32),
            pltpu.VMEM((2, 8, SHARD, FIRST), BF16),
            pltpu.VMEM((2, 8, SHARD, WIDTH - FIRST), BF16),
            pltpu.VMEM((WIDTH, WIDTH), BF16),
            pltpu.VMEM((6,) + block, BF16),
            pltpu.VMEM((4,) + block, BF16),
            pltpu.VMEM((6,) + block, BF16),
            pltpu.VMEM((5,) + block, BF16),
            pltpu.VMEM(block, F32),
            pltpu.VMEM(block, F32),
            pltpu.VMEM((4 * ROWS, WIDTH), F32),
            pltpu.VMEM((2 * ROWS, WIDTH), BF16),
            pltpu.VMEM(block, BF16),
            pltpu.VMEM((WIDTH, ROWS), F32),
            pltpu.VMEM((8 * SHARD, 2 * ROWS), BF16),
            pltpu.VMEM((8,) + slab, F32),
            [pltpu.VMEM((2, 3) + p, BF16) for p in parts],
            [pltpu.VMEM((2,) + p, BF16) for p in parts],
            [pltpu.VMEM((2, 2) + p, BF16) for p in parts],
            [pltpu.VMEM(p, BF16) for p in parts],
            [pltpu.VMEM(p, BF16) for p in parts],
            [pltpu.VMEM(p, BF16) for p in parts],
            pltpu.VMEM(block, F32),
            pltpu.VMEM(block, BF16),
            pltpu.VMEM((1, ROWS), F32),
            pltpu.VMEM(block, BF16),
            pltpu.VMEM((1, ROWS), F32),
            dma((5,)),
            dma((33,)), dma((33,)),
            dma((7, 4)), dma((6, 4)),
            dma((6, 2)), dma((5, 2)),
            dma((32,)), dma((32,)),
            dma((4,)), dma((4,)),
        ],
        compiler_params=pltpu.CompilerParams(
            collective_id=0, has_side_effects=True, vmem_limit_bytes=VMEM_GRANT
        ),
        cost_estimate=pl.CostEstimate(flops=4_000_000_000, bytes_accessed=6_000_000, transcendentals=300_000),
    )(*[pltpu.with_memory_space_constraint(v, pltpu.HBM) for v in (images, pooled, head_weight, head_bias)], log_scale, bias)
    loss, image_grad, pooled_grad, head_grad = pl.pallas_call(
        finish,
        out_shape=results,
        in_specs=[vmem] * 4,
        out_specs=(hbm,) * 4,
        scratch_shapes=[dma((4,))],
        compiler_params=pltpu.CompilerParams(vmem_limit_bytes=4 * 1024 * 1024),
    )(*made)
    return loss.reshape(ROWS), image_grad, pooled_grad, head_grad


def solution(mesh):
    in_specs = (P(("dp", "fsdp"), None), P(("dp", "fsdp"), None), P("fsdp", None), P(), P(), P())
    out_specs = (
        P(("dp", "fsdp")),
        P(("dp", "fsdp"), None),
        P(("dp", "fsdp"), None),
        P(("dp", "fsdp"), None),
    )
    return jax.shard_map(
        per_device, mesh=mesh, in_specs=in_specs, out_specs=out_specs, check_vma=False
    )
```

```python
import jax
import jax.numpy as jnp
from jax import lax
from jax.experimental import pallas as pl
from jax.experimental.pallas import tpu as pltpu
from jax.sharding import PartitionSpec as P

MESH = pl.DeviceIdType.MESH
F32 = jnp.float32
BF16 = jnp.bfloat16
NT = (((1,), (1,)), ((), ()))

ROWS = 128
WIDTH = 1152
SHARD = 72
CHIP = 144
FIRST = 640
TILE = 384
VMEM_GRANT = 44 * 1024 * 1024
HALF = 64
PIECES = (
    ((0, 384, 1), (640, 256, -1), (384, 256, 1), (896, 256, -1)),
    ((0, 640, 1), (640, 512, -1)),
)
PLACE = {1: 0, 3: 1, 2: 2, 4: 3}
ORDER = (2, 1, 3, 0)


def normalize(v):
    r = lax.rsqrt(jnp.sum(v * v, axis=-1, keepdims=True) + 1e-06)
    return v * r, r


def kernel(
    img_hbm, pool_hbm, wsh_hbm, hb_hbm, log_scale, bias,
    loss_out, img_out, pool_out, head_out,
    img, pool, hb,
    wa, wb, wf, xbuf, pbuf, xb, zb, ximg, ztxt, u, dzb, psib, ptf, pt, terms,
    g_out, g_far, g_near,
    y_out, y_pass, y_in,
    gdx, gdx_out, gsum_out, gdx_in, gsum_in,
    l_s, w_s, w_r, x_s, x_r, p_s, p_r, g_s, g_r, h_s, h_r,
):
    dp = lax.axis_index("dp")
    f = lax.axis_index("fsdp")
    j = lax.rem(dp, 4)
    yh = lax.div(f, 8)
    x = lax.rem(lax.div(f, 2), 4)
    c = lax.rem(f, 2)
    base = yh * 8 + c

    sib = (dp, f + 1 - 2 * c)
    xp = (dp, base + 2 * lax.rem(x + 1, 4))
    xm = (dp, base + 2 * lax.rem(x + 3, 4))
    zp = (lax.rem(dp + 4, 32), f)
    zm = (lax.rem(dp + 28, 32), f)
    wrap_up = lax.div(j + 1, 4)
    up = (dp + 1 - 4 * wrap_up, lax.rem(f + 8 * wrap_up, 16))
    wrap_dn = lax.div(3 - j, 3)
    dn = (dp - 1 + 4 * wrap_dn, lax.rem(f + 8 * wrap_dn, 16))
    odd = lax.rem(j, 2)
    step = 3 - 2 * odd
    wrap = lax.div(j + step, 4)
    y_up = (dp + step - 4 * wrap, lax.rem(f + 8 * wrap, 16))
    step = 1 + 2 * odd
    wrap = lax.div(3 - j, 2)
    y_dn = (dp - step + 4 * wrap, lax.rem(f + 8 * wrap, 16))

    across = (dp - j + lax.rem(j + 2, 4), lax.rem(f + 8, 16))
    mine = yh * 4 + x
    theirs = 4 - yh * 4 + x

    loads = [
        pltpu.make_async_copy(src, dst, l_s.at[i])
        for i, (src, dst) in enumerate(
            (
                (wsh_hbm.at[:, :FIRST], wa.at[c, mine]),
                (wsh_hbm.at[:, FIRST:], wb.at[c, mine]),
                (img_hbm, img),
                (pool_hbm, pool),
                (hb_hbm, hb.at[0]),
            )
        )
    ]
    for d in loads:
        d.start()

    barrier = pltpu.get_barrier_semaphore()
    for who in (sib, xp, xm, zp, zm, up, dn, across):
        pl.semaphore_signal(barrier, inc=1, device_id=who, device_id_type=MESH)

    @pl.when(odd == 0)
    def _():
        pl.semaphore_signal(barrier, inc=1, device_id=y_up, device_id_type=MESH)

    @pl.when(odd == 1)
    def _():
        pl.semaphore_signal(barrier, inc=1, device_id=y_dn, device_id_type=MESH)

    pl.semaphore_wait(barrier, 9)
    for d in loads:
        d.wait()

    def copy(src, dst, send, recv, who):
        return pltpu.make_async_remote_copy(
            src_ref=src, dst_ref=dst, send_sem=send, recv_sem=recv, device_id=who, device_id_type=MESH
        )

    def part(ref, h):
        return ref.at[pl.ds(HALF * h, HALF), :]

    def send_x(k, src, h):
        @pl.when(jnp.logical_and(k <= 3 - j, j >= 1))
        def _():
            copy(part(src, h), part(xbuf.at[k + 1], h), x_s.at[k, h], x_r.at[k + 1, h], dn).start()

        @pl.when(jnp.logical_and(k > 3 - j, j <= 2))
        def _():
            copy(part(src, h), part(xbuf.at[k - 1], h), x_s.at[k, h], x_r.at[k - 1, h], up).start()

    def send_p(k, src, h):
        if k < 4:
          @pl.when(jnp.logical_and(k <= j, j <= (2 if k == 0 else 1)))
          def _():
            copy(part(src, h), part(pbuf.at[PLACE[k + 1]], h), p_s.at[k, h], p_r.at[k + 1, h], up).start()

        if k > 2:
          @pl.when(jnp.logical_and(k > j, j >= (1 if k == 4 else 2)))
          def _():
            copy(part(src, h), part(pbuf.at[PLACE[k - 1]], h), p_s.at[k, h], p_r.at[k - 1, h], dn).start()

    def wait_x(k, h, whole=False):
        dst = xbuf.at[k] if whole else part(xbuf.at[k], h)
        copy(dst, dst, x_s.at[k, h], x_r.at[k, h], up).wait_recv()

    def quarter(k, q):
        return xbuf.at[k, pl.ds(HALF // 2 * q, HALF // 2), :]

    hop_in = [copy(quarter(4, q), quarter(4, q), x_s.at[5, q], x_r.at[4, q], zm) for q in range(4)]
    hop_up = [copy(quarter(4, q), quarter(3, q), x_s.at[4, q], x_r.at[3, q // 2], up) for q in range(4)]

    def wait_p(k, h):
        dst = part(pbuf.at[PLACE[k]], h)
        copy(dst, dst, p_s.at[k, h], p_r.at[k, h], up).wait_recv()

    def pass_x(k, h):
        wait_x(k, h)
        send_x(k, xbuf.at[k], h)

    def pass_p(k):
        for h in range(2):
            wait_p(k, h)
            send_p(k, pbuf.at[PLACE[k]], h)

    def x_done(k, src):
        @pl.when(jnp.logical_or(jnp.logical_and(k <= 3 - j, j >= 1), jnp.logical_and(k > 3 - j, j <= 2)))
        def _():
            for h in range(2):
                copy(part(src, h), part(xbuf.at[1], h), x_s.at[k, h], x_r.at[1, h], up).wait_send()

    def p_done(k, src):
        @pl.when(
            jnp.logical_or(
                jnp.logical_and(k <= j, j <= (2 if k == 0 else 1)),
                jnp.logical_and(k > j, j >= (1 if k == 4 else 2)),
            )
        )
        def _():
            for h in range(2):
                copy(part(src, h), part(pbuf.at[0], h), p_s.at[k, h], p_r.at[1, h], up).wait_send()

    middle = lax.rem(lax.div(j + 1, 2), 2)
    outer = middle == 0
    inner = middle == 1
    xk0 = 1 + 2 * lax.div(j, 3)
    xk1 = 2 + middle
    xk2 = 6 - xk0 - xk1
    guest = copy(img, xbuf.at[5], x_s.at[6, 0], x_r.at[5, 0], up)

    pool_swap = copy(pool, psib, h_s.at[2], h_r.at[2], sib)
    x_hop = [
        copy(img.at[pl.ds(HALF // 2 * q, HALF // 2), :], quarter(4, q), x_s.at[5, q], x_r.at[4, q], zm)
        for q in range(4)
    ]
    p_hop = [copy(part(pool, h), part(pbuf.at[PLACE[4]], h), p_s.at[5, h], p_r.at[4, h], zp) for h in range(2)]

    @pl.when(j <= 2)
    def _():
        for d in x_hop:
            d.start()

    send_x(0, img, 0)
    send_x(0, img, 1)

    def chip(h, off):
        return h * 4 + lax.rem(x + off, 4)

    def piece(m, p):
        return (wa if p == 0 else wb).at[c, m]

    def w_copy(src, dst, ident, who, send=None):
        return copy(src, dst, w_s.at[ident if send is None else send], w_r.at[ident], who)

    w_sent = []

    def w_go(src, ident, who):
        d = w_copy(src, src, ident, who)
        d.start()
        w_sent.append(d)

    def to_sibling(n, m, p):
        w_go(piece(m, p), 17 + 2 * n + p, sib)

    def assemble(n, m):
        for p in range(2):
            src = (wa if p == 0 else wb).at[1 - c, m]
            w_copy(src, src, 17 + 2 * n + p, sib).wait_recv()
        rows = pl.ds(pl.multiple_of(m * CHIP, 16), CHIP)
        for ref, cols in ((wa, slice(0, FIRST)), (wb, slice(FIRST, WIDTH))):
            wf[rows, cols] = jnp.concatenate(
                [ref[0, m].astype(F32), ref[1, m].astype(F32)], axis=0
            ).astype(BF16)

    edge_up = [w_copy(piece(mine, p), piece(mine, p), 13 + p, up) for p in range(2)]
    edge_dn = [w_copy(piece(mine, p), piece(mine, p), 13 + p, dn) for p in range(2)]
    edge_far = [w_copy(piece(mine, p), piece(mine, p), 13 + p, across, 15 + p) for p in range(2)]

    @pl.when(j == 3)
    def _():
        for d in edge_up:
            d.start()

    @pl.when(j == 0)
    def _():
        for d in edge_dn:
            d.start()

    @pl.when(outer)
    def _():
        for d in edge_far:
            d.start()

    def along_x(r, m):
        return {
            (d, p): w_copy(piece(m, p), piece(m, p), 1 + 4 * r + 2 * d + p, xp if d == 0 else xm)
            for d in range(2)
            for p in range(2)
        }

    mine_x = along_x(0, mine)
    theirs_x = along_x(1, theirs)
    for key in ((0, 0), (1, 1), (0, 1), (1, 0)):
        mine_x[key].start()
    w_sent.extend(mine_x.values())
    w_sent.extend(theirs_x.values())
    to_sibling(0, mine, 0)
    to_sibling(0, mine, 1)
    pool_swap.start()

    @pl.when(j == 1)
    def _():
        send_p(0, pool, 0)

    @pl.when(j >= 1)
    def _():
        for d in p_hop:
            d.start()

    v, xr = normalize(img[...].astype(F32))
    ximg[...] = v
    xb[0] = v.astype(BF16)

    def slab_rows(n):
        m = chip(1 - yh if n < 4 else yh, ORDER[n % 4])
        return ptf[pl.ds(pl.multiple_of(m * CHIP + SHARD * c, 8), SHARD), :]

    def transpose_into(ref, start):
        ptf[...] = ref[...].astype(F32).T
        for n in range(0, 8, 2):
            pt[SHARD * n:SHARD * (n + 2), start:start + ROWS] = jnp.concatenate(
                [slab_rows(n), slab_rows(n + 1)], axis=0
            ).astype(BF16)

    def near_first(r, h):
        for d, (off, onward) in enumerate(((3, xp), (1, xm))):
            got = piece(chip(h, off), d)
            w_copy(got, got, 1 + 4 * r + 3 * d, xp).wait_recv()
            w_go(got, 9 + 2 * r + d, onward)
            to_sibling(1 + 4 * r + d, chip(h, off), d)

    def near_rest(r, h):
        for d, off in enumerate((3, 1)):
            m = chip(h, off)
            got = piece(m, 1 - d)
            w_copy(got, got, 2 + 4 * r + d, xp).wait_recv()
            to_sibling(1 + 4 * r + d, m, 1 - d)

    def far_units(r, h):
        m = chip(h, 2)
        for p in range(2):
            w_copy(piece(m, p), piece(m, p), 9 + 2 * r + p, xp).wait_recv()
            to_sibling(3 + 4 * r, m, p)

    edge_in = [w_copy(piece(theirs, p), piece(theirs, p), 13 + p, xp) for p in range(2)]

    def theirs_first():
        edge_in[0].wait_recv()
        theirs_x[0, 0].start()
        theirs_sib[0].start()

    def theirs_rest():
        edge_in[1].wait_recv()
        for key in ((1, 1), (0, 1), (1, 0)):
            theirs_x[key].start()
        theirs_sib[1].start()

    theirs_sib = [w_copy(piece(theirs, p), piece(theirs, p), 25 + p, sib) for p in range(2)]
    w_sent.extend(theirs_sib)

    def hop_on(h):
        @pl.when(j <= 2)
        def _():
            for q in (2 * h, 2 * h + 1):
                hop_in[q].wait_recv()
                hop_up[q].start()

        @pl.when(inner)
        def _():
            pass_x(1, h)

    hop_on(0)
    transpose_into(pool, 0)

    @pl.when(outer)
    def _():
        theirs_first()

    near_first(0, yh)

    @pl.when(outer)
    def _():
        theirs_rest()

    hop_on(1)
    near_rest(0, yh)
    pool_swap.wait_recv()
    transpose_into(psib, ROWS)

    @pl.when(j == 0)
    def _():
        send_p(0, pool, 0)
        send_p(0, pool, 1)
        guest.start()

    @pl.when(j == 3)
    def _():
        pass_p(4)

    @pl.when(inner)
    def _():
        pass_x(3, 0)
        theirs_first()

    far_units(0, yh)
    assemble(0, mine)

    @pl.when(inner)
    def _():
        pass_x(3, 1)
        theirs_rest()
        pass_x(2, 0)

    @pl.when(j == 2)
    def _():
        pass_p(4)

    @pl.when(j == 1)
    def _():
        pass_x(2, 1)

    near_first(1, 1 - yh)
    for n, off in ((1, 3), (2, 1), (3, 2)):
        assemble(n, chip(yh, off))

    @pl.when(j == 2)
    def _():
        pass_x(2, 1)

    @pl.when(j == 1)
    def _():
        send_p(0, pool, 1)

    near_rest(1, 1 - yh)

    @pl.when(j == 1)
    def _():
        pass_p(1)
        pass_p(4)

    @pl.when(j == 2)
    def _():
        pass_p(3)
        send_p(0, pool, 0)
        send_p(0, pool, 1)

    far_units(1, 1 - yh)

    def ready(k):
        xb[k] = normalize(xbuf[k].astype(F32))[0].astype(BF16)

    @pl.when(inner)
    def _():
        for k in range(1, 4):
            ready(k)

    assemble(4, theirs)
    for n, off in ((5, 3), (6, 1), (7, 2)):
        assemble(n, chip(1 - yh, off))

    temper = jnp.exp(jnp.full((1, 1), log_scale[0], F32))
    offset = jnp.full((1, 1), bias[0], F32)
    gain = temper * (1.0 / ROWS)

    def project(block, out):
        for start in range(0, WIDTH, 512):
            cols = pl.ds(start, min(512, WIDTH - start))
            out[:, cols] = jnp.dot(block, wf[:, cols], preferred_element_type=F32) + hb[:, cols]

    def weights(a, b, own):
        l = temper * lax.dot_general(a, b, NT, preferred_element_type=F32) + offset
        if own:
            eye = lax.broadcasted_iota(jnp.int32, l.shape, 0) == lax.broadcasted_iota(jnp.int32, l.shape, 1)
            l = jnp.where(eye, -l, l)
        g = gain / (1.0 + jnp.exp(-l))
        if own:
            g = jnp.where(eye, -g, g)
        return l, g.astype(BF16)

    def losses(m):
        e = jnp.maximum(m, 0.0) + jnp.log1p(jnp.exp(-jnp.abs(m)))
        total = e[:, :ROWS]
        for start in range(ROWS, m.shape[1], ROWS):
            total = total + e[:, start:start + ROWS]
        return jnp.sum(total.T, axis=0, keepdims=True)

    def image_side(d, row):
        loss_out[...] = row * (1.0 / ROWS)
        v = ximg[...]
        img_out[...] = (xr * (d - v * jnp.sum(v * d, axis=-1, keepdims=True))).astype(BF16)

    project(pool[...], ztxt)
    v, zr = normalize(ztxt[...])
    ztxt[...] = v
    zb[0] = v.astype(BF16)

    def text_grad(a, own):
        _, g = weights(zb[0], a, own)
        return jnp.dot(g, a, preferred_element_type=F32)

    def text_side(d):
        v = ztxt[...]
        dzb[:ROWS] = (zr * (d - v * jnp.sum(v * d, axis=-1, keepdims=True))).astype(BF16)

    @pl.when(inner)
    def _():
        text_side(text_grad(xb[0:4].reshape(4 * ROWS, WIDTH), True))

    @pl.when(outer)
    def _():
        for k in (xk0, xk1):
            wait_x(k, 0)
            wait_x(k, 1)
            ready(k)
        u[:ROWS] = text_grad(xb[0], True) + text_grad(xb[xk0], False) + text_grad(xb[xk1], False)
        wait_x(xk2, 0)
        wait_x(xk2, 1)
        ready(xk2)
        text_side(u[:ROWS] + text_grad(xb[xk2], False))

    pair = copy(dzb.at[:ROWS], dzb.at[ROWS:], h_s.at[3], h_r.at[3], sib)
    pair.start()

    def make(n):
        t = jnp.dot(pt[SHARD * n:SHARD * (n + 2), :], dzb[...], preferred_element_type=F32)
        terms[n] = t[:SHARD]
        terms[n + 1] = t[SHARD:]

    def cols(n, q):
        start, size, _ = PIECES[n // 4][q]
        return terms[n, :, start:start + size]

    g_sent = []

    def g_go(src, value, ident, dst, who):
        src[...] = value.astype(BF16)
        d = copy(src, dst, g_s.at[ident], g_r.at[ident], who)
        d.start()
        g_sent.append(d)

    def g_wait(ref, ident):
        copy(ref, ref, g_s.at[ident], g_r.at[ident], xp).wait_recv()
        return ref[...].astype(F32)

    def far_sends(g):
        for q, (_, _, way) in enumerate(PIECES[g]):
            g_go(g_out[g][q].at[0], cols(4 * g, q), 12 * g + q, g_far[g][q], xp if way > 0 else xm)

    def near_sends(g):
        for q, (_, _, way) in enumerate(PIECES[g]):
            n, who = (2, xm) if way > 0 else (1, xp)
            g_go(g_out[g][q].at[1], cols(4 * g + n, q), 12 * g + 4 + q, g_near[g][q].at[0], who)

    def second_sends(g):
        for q, (_, _, way) in enumerate(PIECES[g]):
            n, who = (1, xp) if way > 0 else (2, xm)
            value = cols(4 * g + n, q) + g_wait(g_far[g][q], 12 * g + q)
            g_go(g_out[g][q].at[2], value, 12 * g + 8 + q, g_near[g][q].at[1], who)

    def total(g, q):
        value = cols(4 * g + 3, q) + g_wait(g_near[g][q].at[0], 12 * g + 4 + q)
        return value + g_wait(g_near[g][q].at[1], 12 * g + 8 + q)

    def back():
        @pl.loop(0, WIDTH // TILE)
        def _(n):
            cols = pl.ds(pl.multiple_of(n * TILE, TILE), TILE)
            pool_out[:, cols] = lax.dot_general(
                dzb[:ROWS], wf[cols, :], NT, preferred_element_type=F32
            ).astype(BF16)

    gdx_up = copy(gdx_out, gdx_in, h_s.at[0], h_r.at[0], up)
    gdx_dn = copy(gdx_out, gdx_in, h_s.at[0], h_r.at[0], dn)
    gsum_up = copy(gsum_out, gsum_in, h_s.at[1], h_r.at[1], up)
    gsum_dn = copy(gsum_out, gsum_in, h_s.at[1], h_r.at[1], dn)

    @pl.when(outer)
    def _():
        m, g = weights(xb[0], zb[0], True)
        u[ROWS:2 * ROWS] = jnp.dot(g, zb[0], preferred_element_type=F32)
        loss_out[...] = losses(m)

    def texts_done(first, last):
        for n in range(first, last):
            v = u[ROWS * (n - 1):ROWS * n]
            zb[n] = normalize(v)[0].astype(BF16)

    def meet(image, texts, own):
        m, g = weights(image, texts, own)
        return jnp.dot(g, texts, preferred_element_type=F32), losses(m)

    @pl.when(inner)
    def _():
        back()

    pair.wait_recv()
    make(0)
    far_sends(0)
    make(2)
    near_sends(0)

    @pl.when(j == 1)
    def _():
        for h in range(2):
            wait_p(3, h)

    @pl.when(j == 2)
    def _():
        for h in range(2):
            wait_p(1, h)

    @pl.when(inner)
    def _():
        project(pbuf[0:2].reshape(2 * ROWS, WIDTH), u.at[:2 * ROWS])

    @pl.when(outer)
    def _():
        make(4)
        make(6)
        back()

    second_sends(0)

    @pl.when(inner)
    def _():
        make(4)
        make(6)

    far_sends(1)
    near_sends(1)

    @pl.when(j == 1)
    def _():
        wait_x(5, 0, whole=True)
        ready(5)

    @pl.when(inner)
    def _():
        texts_done(1, 3)
        d, row = meet(xb[9 - 4 * j], zb[3 - j], False)
        gdx[...] = d
        gsum_out[...] = row

    for q, (_, _, way) in enumerate(PIECES[0]):
        g_go(y_out[q], total(0, q), 24 + q, y_pass[q], y_up if way > 0 else y_dn)

    onward = [
        copy(y_pass[q], y_in[q], g_s.at[28 + q], g_r.at[28 + q], y_up if way > 0 else y_dn)
        for q, (_, _, way) in enumerate(PIECES[0])
    ]

    def relay():
        for q in range(4):
            copy(y_pass[q], y_pass[q], g_s.at[24 + q], g_r.at[24 + q], xp).wait_recv()
            onward[q].start()

    @pl.when(inner)
    def _():
        for h in range(2):
            wait_p(2, h)
        project(pbuf[2], u.at[2 * ROWS:3 * ROWS])
        texts_done(3, 4)
        d, row = meet(xb[9 - 4 * j], zb[3], False)
        gdx_out[...] = (gdx[...] + d).astype(BF16)
        gsum_out[...] += row

        @pl.when(j == 1)
        def _():
            gdx_dn.start()
            gsum_dn.start()

        @pl.when(j == 2)
        def _():
            gdx_up.start()
            gsum_up.start()

    second_sends(1)

    @pl.when(j == 0)
    def _():
        for h in range(2):
            wait_p(3, h)

    @pl.when(j == 3)
    def _():
        for h in range(2):
            wait_p(1, h)

    @pl.when(outer)
    def _():
        project(pbuf[1 - lax.div(j, 3)], u.at[2 * ROWS:3 * ROWS])
        texts_done(3, 4)
        d, row = meet(xb[0], zb[3], False)
        u[ROWS:2 * ROWS] += d
        loss_out[...] += row

    @pl.when(inner)
    def _():
        d, row = meet(xb[0], zb[0:3].reshape(3 * ROWS, WIDTH), True)
        e, more = meet(xb[0], zb[3], False)
        image_side(d + e, row + more)

    relay()

    for d in w_sent:
        d.wait_send()

    @pl.when(j == 3)
    def _():
        for d in edge_up:
            d.wait_send()

    @pl.when(j == 0)
    def _():
        for d in edge_dn:
            d.wait_send()

    @pl.when(outer)
    def _():
        for d in edge_far:
            d.wait_send()

    @pl.when(j <= 2)
    def _():
        for d in x_hop + hop_up:
            d.wait_send()

    @pl.when(j >= 1)
    def _():
        for d in p_hop:
            d.wait_send()

    @pl.when(j == 0)
    def _():
        guest.wait_send()

    x_done(0, img)
    p_done(0, pool)
    for k in range(1, 4):
        x_done(k, xbuf.at[k])
        p_done(k, pbuf.at[0])
    p_done(4, pbuf.at[0])
    pool_swap.wait_send()
    pair.wait_send()
    for d in g_sent[:24]:
        d.wait_send()

    for q, (start, size, _) in enumerate(PIECES[1]):
        head_out[:, start:start + size] = total(1, q)

    @pl.when(outer)
    def _():
        gsum_up.wait_recv()
        gdx_up.wait_recv()
        image_side(u[ROWS:2 * ROWS] + gdx_in[...].astype(F32), loss_out[...] + gsum_in[...])

    for q, (start, size, _) in enumerate(PIECES[0]):
        head_out[:, start:start + size] += g_wait(y_in[q], 28 + q)

    @pl.when(inner)
    def _():
        gdx_up.wait_send()
        gsum_up.wait_send()

    for d in g_sent[24:] + onward:
        d.wait_send()


def finish(*refs):
    moves = [pltpu.make_async_copy(refs[i], refs[4 + i], refs[8].at[i]) for i in range(4)]
    for d in moves:
        d.start()
    for d in moves:
        d.wait()


def per_device(images, pooled, head_weight, head_bias, log_scale, bias):
    smem = pl.BlockSpec(memory_space=pltpu.SMEM)
    vmem = pl.BlockSpec(memory_space=pltpu.VMEM)
    hbm = pl.BlockSpec(memory_space=pltpu.HBM)
    block = (ROWS, WIDTH)
    slab = (SHARD, WIDTH)
    parts = [[(SHARD, size) for _, size, _ in pieces] for pieces in PIECES]
    dma = pltpu.SemaphoreType.DMA
    results = (
        jax.ShapeDtypeStruct((1, ROWS), F32),
        jax.ShapeDtypeStruct(block, BF16),
        jax.ShapeDtypeStruct(block, BF16),
        jax.ShapeDtypeStruct(slab, F32),
    )
    made = pl.pallas_call(
        kernel,
        out_shape=results,
        in_specs=[hbm, hbm, hbm, hbm, smem, smem],
        out_specs=(vmem,) * 4,
        scratch_shapes=[
            pltpu.VMEM(block, BF16),
            pltpu.VMEM(block, BF16),
            pltpu.VMEM((1, WIDTH), F32),
            pltpu.VMEM((2, 8, SHARD, FIRST), BF16),
            pltpu.VMEM((2, 8, SHARD, WIDTH - FIRST), BF16),
            pltpu.VMEM((WIDTH, WIDTH), BF16),
            pltpu.VMEM((6,) + block, BF16),
            pltpu.VMEM((4,) + block, BF16),
            pltpu.VMEM((6,) + block, BF16),
            pltpu.VMEM((4,) + block, BF16),
            pltpu.VMEM(block, F32),
            pltpu.VMEM(block, F32),
            pltpu.VMEM((3 * ROWS, WIDTH), F32),
            pltpu.VMEM((2 * ROWS, WIDTH), BF16),
            pltpu.VMEM(block, BF16),
            pltpu.VMEM((WIDTH, ROWS), F32),
            pltpu.VMEM((8 * SHARD, 2 * ROWS), BF16),
            pltpu.VMEM((8,) + slab, F32),
            [[pltpu.VMEM((3,) + p, BF16) for p in ps] for ps in parts],
            [[pltpu.VMEM(p, BF16) for p in ps] for ps in parts],
            [[pltpu.VMEM((2,) + p, BF16) for p in ps] for ps in parts],
            [pltpu.VMEM(p, BF16) for p in parts[0]],
            [pltpu.VMEM(p, BF16) for p in parts[0]],
            [pltpu.VMEM(p, BF16) for p in parts[0]],
            pltpu.VMEM(block, F32),
            pltpu.VMEM(block, BF16),
            pltpu.VMEM((1, ROWS), F32),
            pltpu.VMEM(block, BF16),
            pltpu.VMEM((1, ROWS), F32),
            dma((5,)),
            dma((33,)), dma((33,)),
            dma((7, 4)), dma((6, 4)),
            dma((6, 2)), dma((5, 2)),
            dma((32,)), dma((32,)),
            dma((4,)), dma((4,)),
        ],
        compiler_params=pltpu.CompilerParams(
            collective_id=0, has_side_effects=True, vmem_limit_bytes=VMEM_GRANT
        ),
        cost_estimate=pl.CostEstimate(flops=4_000_000_000, bytes_accessed=6_000_000, transcendentals=300_000),
    )(*[pltpu.with_memory_space_constraint(v, pltpu.HBM) for v in (images, pooled, head_weight, head_bias)], log_scale, bias)
    loss, image_grad, pooled_grad, head_grad = pl.pallas_call(
        finish,
        out_shape=results,
        in_specs=[vmem] * 4,
        out_specs=(hbm,) * 4,
        scratch_shapes=[dma((4,))],
        compiler_params=pltpu.CompilerParams(vmem_limit_bytes=4 * 1024 * 1024),
    )(*made)
    return loss.reshape(ROWS), image_grad, pooled_grad, head_grad


def solution(mesh):
    in_specs = (P(("dp", "fsdp"), None), P(("dp", "fsdp"), None), P("fsdp", None), P(), P(), P())
    out_specs = (
        P(("dp", "fsdp")),
        P(("dp", "fsdp"), None),
        P(("dp", "fsdp"), None),
        P(("dp", "fsdp"), None),
    )
    return jax.shard_map(
        per_device, mesh=mesh, in_specs=in_specs, out_specs=out_specs, check_vma=False
    )
```

```python
import jax
import jax.numpy as jnp
from jax import lax
from jax.experimental import pallas as pl
from jax.experimental.pallas import tpu as pltpu
from jax.sharding import PartitionSpec as P

MESH = pl.DeviceIdType.MESH
F32 = jnp.float32
BF16 = jnp.bfloat16
NT = (((1,), (1,)), ((), ()))

ROWS = 128
WIDTH = 1152
SHARD = 72
CHIP = 144
FIRST = 640
TILE = 384
VMEM_GRANT = 44 * 1024 * 1024
HALF = 64
PIECES = ((0, 384, 1), (640, 256, -1), (384, 256, 1), (896, 256, -1))
PLACE = {1: 0, 3: 1, 4: 2, 2: 3}
ORDER = (2, 1, 3, 0)


def normalize(v):
    r = lax.rsqrt(jnp.sum(v * v, axis=-1, keepdims=True) + 1e-06)
    return v * r, r


def kernel(
    img_hbm, pool_hbm, wsh_hbm, hb_hbm, log_scale, bias,
    loss_out, img_out, pool_out, head_out,
    img, pool, hb,
    wa, wb, wf, xbuf, pbuf, xb, zb, ximg, ztxt, u, dzb, psib, ptf, pt, terms,
    g_out, g_far, g_near,
    y_out, y_pass, y_in,
    gdx, gdx_out, gsum_out, gdx_in, gsum_in,
    l_s, w_s, w_r, x_s, x_r, p_s, p_r, g_s, g_r, h_s, h_r,
):
    dp = lax.axis_index("dp")
    f = lax.axis_index("fsdp")
    j = lax.rem(dp, 4)
    yh = lax.div(f, 8)
    x = lax.rem(lax.div(f, 2), 4)
    c = lax.rem(f, 2)
    base = yh * 8 + c

    sib = (dp, f + 1 - 2 * c)
    xp = (dp, base + 2 * lax.rem(x + 1, 4))
    xm = (dp, base + 2 * lax.rem(x + 3, 4))
    zp = (lax.rem(dp + 4, 32), f)
    zm = (lax.rem(dp + 28, 32), f)
    wrap_up = lax.div(j + 1, 4)
    up = (dp + 1 - 4 * wrap_up, lax.rem(f + 8 * wrap_up, 16))
    wrap_dn = lax.div(3 - j, 3)
    dn = (dp - 1 + 4 * wrap_dn, lax.rem(f + 8 * wrap_dn, 16))
    odd = lax.rem(j, 2)
    step = 3 - 2 * odd
    wrap = lax.div(j + step, 4)
    y_up = (dp + step - 4 * wrap, lax.rem(f + 8 * wrap, 16))
    step = 1 + 2 * odd
    wrap = lax.div(3 - j, 2)
    y_dn = (dp - step + 4 * wrap, lax.rem(f + 8 * wrap, 16))

    across = (dp - j + lax.rem(j + 2, 4), lax.rem(f + 8, 16))
    mine = yh * 4 + x
    theirs = 4 - yh * 4 + x

    loads = [
        pltpu.make_async_copy(src, dst, l_s.at[i])
        for i, (src, dst) in enumerate(
            (
                (wsh_hbm.at[:, :FIRST], wa.at[c, mine]),
                (wsh_hbm.at[:, FIRST:], wb.at[c, mine]),
                (img_hbm, img),
                (pool_hbm, pool),
                (hb_hbm, hb.at[0]),
            )
        )
    ]
    for d in loads:
        d.start()

    barrier = pltpu.get_barrier_semaphore()
    for who in (sib, xp, xm, zp, zm, up, dn, across):
        pl.semaphore_signal(barrier, inc=1, device_id=who, device_id_type=MESH)

    @pl.when(odd == 0)
    def _():
        pl.semaphore_signal(barrier, inc=1, device_id=y_up, device_id_type=MESH)

    @pl.when(odd == 1)
    def _():
        pl.semaphore_signal(barrier, inc=1, device_id=y_dn, device_id_type=MESH)

    pl.semaphore_wait(barrier, 9)
    for d in loads:
        d.wait()

    def copy(src, dst, send, recv, who):
        return pltpu.make_async_remote_copy(
            src_ref=src, dst_ref=dst, send_sem=send, recv_sem=recv, device_id=who, device_id_type=MESH
        )

    def part(ref, h):
        return ref.at[pl.ds(HALF * h, HALF), :]

    def send_x(k, src, h):
        @pl.when(jnp.logical_and(k <= 3 - j, j >= 1))
        def _():
            copy(part(src, h), part(xbuf.at[k + 1], h), x_s.at[k, h], x_r.at[k + 1, h], dn).start()

        @pl.when(jnp.logical_and(k > 3 - j, j <= 2))
        def _():
            copy(part(src, h), part(xbuf.at[k - 1], h), x_s.at[k, h], x_r.at[k - 1, h], up).start()

    def send_p(k, src, h):
        if k < 4:
          @pl.when(jnp.logical_and(k <= j, j <= 1))
          def _():
            copy(part(src, h), part(pbuf.at[PLACE[k + 1]], h), p_s.at[k, h], p_r.at[k + 1, h], up).start()

        if k > 2:
          @pl.when(jnp.logical_and(k > j, j >= 2))
          def _():
            copy(part(src, h), part(pbuf.at[PLACE[k - 1]], h), p_s.at[k, h], p_r.at[k - 1, h], dn).start()

    def wait_x(k, h, whole=False):
        dst = xbuf.at[k] if whole else part(xbuf.at[k], h)
        copy(dst, dst, x_s.at[k, h], x_r.at[k, h], up).wait_recv()

    def quarter(k, q):
        return xbuf.at[k, pl.ds(HALF // 2 * q, HALF // 2), :]

    hop_in = [copy(quarter(4, q), quarter(4, q), x_s.at[5, q], x_r.at[4, q], zm) for q in range(4)]
    hop_up = [copy(quarter(4, q), quarter(3, q), x_s.at[4, q], x_r.at[3, q // 2], up) for q in range(4)]

    def wait_p(k, h):
        dst = part(pbuf.at[PLACE[k]], h)
        copy(dst, dst, p_s.at[k, h], p_r.at[k, h], up).wait_recv()

    def pass_x(k, h):
        wait_x(k, h)
        send_x(k, xbuf.at[k], h)

    def pass_p(k):
        for h in range(2):
            wait_p(k, h)
            send_p(k, pbuf.at[PLACE[k]], h)

    def x_done(k, src):
        @pl.when(jnp.logical_or(jnp.logical_and(k <= 3 - j, j >= 1), jnp.logical_and(k > 3 - j, j <= 2)))
        def _():
            for h in range(2):
                copy(part(src, h), part(xbuf.at[1], h), x_s.at[k, h], x_r.at[1, h], up).wait_send()

    def p_done(k, src):
        @pl.when(jnp.logical_or(jnp.logical_and(k <= j, j <= 1), jnp.logical_and(k > j, j >= 2)))
        def _():
            for h in range(2):
                copy(part(src, h), part(pbuf.at[0], h), p_s.at[k, h], p_r.at[1, h], up).wait_send()

    middle = lax.rem(lax.div(j + 1, 2), 2)
    outer = middle == 0
    inner = middle == 1
    xk0 = 1 + 2 * lax.div(j, 3)
    xk1 = 2 + middle
    xk2 = 6 - xk0 - xk1
    guest = copy(img, xbuf.at[5], x_s.at[6, 0], x_r.at[5, 0], up)

    pool_swap = copy(pool, psib, h_s.at[2], h_r.at[2], sib)
    x_hop = [
        copy(img.at[pl.ds(HALF // 2 * q, HALF // 2), :], quarter(4, q), x_s.at[5, q], x_r.at[4, q], zm)
        for q in range(4)
    ]
    p_hop = [copy(part(pool, h), part(pbuf.at[PLACE[4]], h), p_s.at[5, h], p_r.at[4, h], zp) for h in range(2)]

    @pl.when(j <= 2)
    def _():
        for d in x_hop:
            d.start()

    send_x(0, img, 0)
    send_x(0, img, 1)

    def chip(h, off):
        return h * 4 + lax.rem(x + off, 4)

    def piece(m, p):
        return (wa if p == 0 else wb).at[c, m]

    def w_copy(src, dst, ident, who, send=None):
        return copy(src, dst, w_s.at[ident if send is None else send], w_r.at[ident], who)

    w_sent = []

    def w_go(src, ident, who):
        d = w_copy(src, src, ident, who)
        d.start()
        w_sent.append(d)

    def to_sibling(n, m, p):
        w_go(piece(m, p), 17 + 2 * n + p, sib)

    def assemble(n, m):
        for p in range(2):
            src = (wa if p == 0 else wb).at[1 - c, m]
            w_copy(src, src, 17 + 2 * n + p, sib).wait_recv()
        rows = pl.ds(pl.multiple_of(m * CHIP, 16), CHIP)
        for ref, cols in ((wa, slice(0, FIRST)), (wb, slice(FIRST, WIDTH))):
            wf[rows, cols] = jnp.concatenate(
                [ref[0, m].astype(F32), ref[1, m].astype(F32)], axis=0
            ).astype(BF16)

    edge_up = [w_copy(piece(mine, p), piece(mine, p), 13 + p, up) for p in range(2)]
    edge_dn = [w_copy(piece(mine, p), piece(mine, p), 13 + p, dn) for p in range(2)]
    edge_far = [w_copy(piece(mine, p), piece(mine, p), 13 + p, across, 15 + p) for p in range(2)]

    @pl.when(j == 3)
    def _():
        for d in edge_up:
            d.start()

    @pl.when(j == 0)
    def _():
        for d in edge_dn:
            d.start()

    @pl.when(outer)
    def _():
        for d in edge_far:
            d.start()

    def along_x(r, m):
        return {
            (d, p): w_copy(piece(m, p), piece(m, p), 1 + 4 * r + 2 * d + p, xp if d == 0 else xm)
            for d in range(2)
            for p in range(2)
        }

    mine_x = along_x(0, mine)
    theirs_x = along_x(1, theirs)
    for key in ((0, 0), (1, 1), (0, 1), (1, 0)):
        mine_x[key].start()
    w_sent.extend(mine_x.values())
    w_sent.extend(theirs_x.values())
    to_sibling(0, mine, 0)
    to_sibling(0, mine, 1)
    pool_swap.start()

    @pl.when(j == 1)
    def _():
        send_p(0, pool, 0)

    @pl.when(j >= 1)
    def _():
        for d in p_hop:
            d.start()

    v, xr = normalize(img[...].astype(F32))
    ximg[...] = v
    xb[0] = v.astype(BF16)

    def slab_rows(n):
        m = chip(1 - yh if n < 4 else yh, ORDER[n % 4])
        return ptf[pl.ds(pl.multiple_of(m * CHIP + SHARD * c, 8), SHARD), :]

    def transpose_into(ref, start):
        ptf[...] = ref[...].astype(F32).T
        for n in range(0, 8, 2):
            pt[SHARD * n:SHARD * (n + 2), start:start + ROWS] = jnp.concatenate(
                [slab_rows(n), slab_rows(n + 1)], axis=0
            ).astype(BF16)

    def near_first(r, h):
        for d, (off, onward) in enumerate(((3, xp), (1, xm))):
            got = piece(chip(h, off), d)
            w_copy(got, got, 1 + 4 * r + 3 * d, xp).wait_recv()
            w_go(got, 9 + 2 * r + d, onward)
            to_sibling(1 + 4 * r + d, chip(h, off), d)

    def near_rest(r, h):
        for d, off in enumerate((3, 1)):
            m = chip(h, off)
            got = piece(m, 1 - d)
            w_copy(got, got, 2 + 4 * r + d, xp).wait_recv()
            to_sibling(1 + 4 * r + d, m, 1 - d)

    def far_units(r, h):
        m = chip(h, 2)
        for p in range(2):
            w_copy(piece(m, p), piece(m, p), 9 + 2 * r + p, xp).wait_recv()
            to_sibling(3 + 4 * r, m, p)

    edge_in = [w_copy(piece(theirs, p), piece(theirs, p), 13 + p, xp) for p in range(2)]

    def theirs_first():
        edge_in[0].wait_recv()
        theirs_x[0, 0].start()
        theirs_sib[0].start()

    def theirs_rest():
        edge_in[1].wait_recv()
        for key in ((1, 1), (0, 1), (1, 0)):
            theirs_x[key].start()
        theirs_sib[1].start()

    theirs_sib = [w_copy(piece(theirs, p), piece(theirs, p), 25 + p, sib) for p in range(2)]
    w_sent.extend(theirs_sib)

    def hop_on(h):
        @pl.when(j <= 2)
        def _():
            for q in (2 * h, 2 * h + 1):
                hop_in[q].wait_recv()
                hop_up[q].start()

        @pl.when(inner)
        def _():
            pass_x(1, h)

    hop_on(0)
    transpose_into(pool, 0)

    @pl.when(outer)
    def _():
        theirs_first()

    near_first(0, yh)

    @pl.when(outer)
    def _():
        theirs_rest()

    hop_on(1)
    near_rest(0, yh)
    pool_swap.wait_recv()
    transpose_into(psib, ROWS)

    @pl.when(j == 0)
    def _():
        send_p(0, pool, 0)
        send_p(0, pool, 1)
        guest.start()

    @pl.when(j == 3)
    def _():
        pass_p(4)

    @pl.when(inner)
    def _():
        pass_x(3, 0)
        theirs_first()

    far_units(0, yh)
    assemble(0, mine)

    @pl.when(inner)
    def _():
        pass_x(3, 1)
        theirs_rest()
        pass_x(2, 0)

    @pl.when(j == 2)
    def _():
        pass_p(4)

    @pl.when(j == 1)
    def _():
        pass_x(2, 1)

    near_first(1, 1 - yh)
    for n, off in ((1, 3), (2, 1), (3, 2)):
        assemble(n, chip(yh, off))

    @pl.when(j == 2)
    def _():
        pass_x(2, 1)

    @pl.when(j == 1)
    def _():
        send_p(0, pool, 1)

    near_rest(1, 1 - yh)

    @pl.when(j == 1)
    def _():
        pass_p(1)

    @pl.when(j == 2)
    def _():
        pass_p(3)

    far_units(1, 1 - yh)

    def ready(k):
        xb[k] = normalize(xbuf[k].astype(F32))[0].astype(BF16)

    @pl.when(inner)
    def _():
        for k in range(1, 4):
            ready(k)

    assemble(4, theirs)
    for n, off in ((5, 3), (6, 1), (7, 2)):
        assemble(n, chip(1 - yh, off))

    temper = jnp.exp(jnp.full((1, 1), log_scale[0], F32))
    offset = jnp.full((1, 1), bias[0], F32)
    gain = temper * (1.0 / ROWS)

    def project(block, out):
        for start in range(0, WIDTH, 512):
            cols = pl.ds(start, min(512, WIDTH - start))
            out[:, cols] = jnp.dot(block, wf[:, cols], preferred_element_type=F32) + hb[:, cols]

    def weights(a, b, own):
        l = temper * lax.dot_general(a, b, NT, preferred_element_type=F32) + offset
        if own:
            eye = lax.broadcasted_iota(jnp.int32, l.shape, 0) == lax.broadcasted_iota(jnp.int32, l.shape, 1)
            l = jnp.where(eye, -l, l)
        g = gain / (1.0 + jnp.exp(-l))
        if own:
            g = jnp.where(eye, -g, g)
        return l, g.astype(BF16)

    def losses(m):
        e = jnp.maximum(m, 0.0) + jnp.log1p(jnp.exp(-jnp.abs(m)))
        total = e[:, :ROWS]
        for start in range(ROWS, m.shape[1], ROWS):
            total = total + e[:, start:start + ROWS]
        return jnp.sum(total.T, axis=0, keepdims=True)

    def image_side(d, row):
        loss_out[...] = row * (1.0 / ROWS)
        v = ximg[...]
        img_out[...] = (xr * (d - v * jnp.sum(v * d, axis=-1, keepdims=True))).astype(BF16)

    project(pool[...], ztxt)
    v, zr = normalize(ztxt[...])
    ztxt[...] = v
    zb[0] = v.astype(BF16)

    def text_grad(a, own):
        _, g = weights(zb[0], a, own)
        return jnp.dot(g, a, preferred_element_type=F32)

    def text_side(d):
        v = ztxt[...]
        dzb[:ROWS] = (zr * (d - v * jnp.sum(v * d, axis=-1, keepdims=True))).astype(BF16)

    @pl.when(inner)
    def _():
        text_side(text_grad(xb[0:4].reshape(4 * ROWS, WIDTH), True))

    @pl.when(outer)
    def _():
        for k in (xk0, xk1):
            wait_x(k, 0)
            wait_x(k, 1)
            ready(k)
        u[:ROWS] = text_grad(xb[0], True) + text_grad(xb[xk0], False) + text_grad(xb[xk1], False)
        wait_x(xk2, 0)
        wait_x(xk2, 1)
        ready(xk2)
        text_side(u[:ROWS] + text_grad(xb[xk2], False))

    pair = copy(dzb.at[:ROWS], dzb.at[ROWS:], h_s.at[3], h_r.at[3], sib)
    pair.start()

    def make(n):
        t = jnp.dot(pt[SHARD * n:SHARD * (n + 2), :], dzb[...], preferred_element_type=F32)
        terms[n] = t[:SHARD]
        terms[n + 1] = t[SHARD:]

    def cols(n, q):
        start, size, _ = PIECES[q]
        return terms[n, :, start:start + size]

    g_sent = []

    def g_go(src, value, ident, dst, who):
        src[...] = value.astype(BF16)
        d = copy(src, dst, g_s.at[ident], g_r.at[ident], who)
        d.start()
        g_sent.append(d)

    def g_wait(ref, ident):
        copy(ref, ref, g_s.at[ident], g_r.at[ident], xp).wait_recv()
        return ref[...].astype(F32)

    def slot(refs, q, *index):
        return refs[q].at[index] if index else refs[q]

    def far_sends(g):
        for q, (_, _, way) in enumerate(PIECES):
            g_go(slot(g_out, q, g, 0), cols(4 * g, q), 12 * g + q, slot(g_far, q, g), xp if way > 0 else xm)

    def near_sends(g):
        for q, (_, _, way) in enumerate(PIECES):
            n, who = (2, xm) if way > 0 else (1, xp)
            g_go(slot(g_out, q, g, 1), cols(4 * g + n, q), 12 * g + 4 + q, slot(g_near, q, g, 0), who)

    def second_sends(g):
        for q, (_, _, way) in enumerate(PIECES):
            n, who = (1, xp) if way > 0 else (2, xm)
            value = cols(4 * g + n, q) + g_wait(slot(g_far, q, g), 12 * g + q)
            g_go(slot(g_out, q, g, 2), value, 12 * g + 8 + q, slot(g_near, q, g, 1), who)

    def total(g, q):
        value = cols(4 * g + 3, q) + g_wait(slot(g_near, q, g, 0), 12 * g + 4 + q)
        return value + g_wait(slot(g_near, q, g, 1), 12 * g + 8 + q)

    def back():
        @pl.loop(0, WIDTH // TILE)
        def _(n):
            cols = pl.ds(pl.multiple_of(n * TILE, TILE), TILE)
            pool_out[:, cols] = lax.dot_general(
                dzb[:ROWS], wf[cols, :], NT, preferred_element_type=F32
            ).astype(BF16)

    gdx_up = copy(gdx_out, gdx_in, h_s.at[0], h_r.at[0], up)
    gdx_dn = copy(gdx_out, gdx_in, h_s.at[0], h_r.at[0], dn)
    gsum_up = copy(gsum_out, gsum_in, h_s.at[1], h_r.at[1], up)
    gsum_dn = copy(gsum_out, gsum_in, h_s.at[1], h_r.at[1], dn)

    @pl.when(outer)
    def _():
        m, g = weights(xb[0], zb[0], True)
        u[ROWS:2 * ROWS] = jnp.dot(g, zb[0], preferred_element_type=F32)
        loss_out[...] = losses(m)

    def texts_done(first, last):
        for n in range(first, last):
            v = u[ROWS * (n - 1):ROWS * n]
            zb[n] = normalize(v)[0].astype(BF16)

    def meet(image, texts, own):
        m, g = weights(image, texts, own)
        return jnp.dot(g, texts, preferred_element_type=F32), losses(m)

    @pl.when(inner)
    def _():
        back()

    pair.wait_recv()
    make(0)
    far_sends(0)
    make(2)
    near_sends(0)

    @pl.when(j == 1)
    def _():
        for h in range(2):
            wait_p(3, h)
            wait_p(4, h)

    @pl.when(j == 2)
    def _():
        for h in range(2):
            wait_p(1, h)

    @pl.when(inner)
    def _():
        project(pbuf[0:3].reshape(3 * ROWS, WIDTH), u.at[:3 * ROWS])

    @pl.when(outer)
    def _():
        make(4)
        make(6)
        back()

    second_sends(0)

    @pl.when(inner)
    def _():
        make(4)
        make(6)

    far_sends(1)
    near_sends(1)

    @pl.when(j == 1)
    def _():
        wait_x(5, 0, whole=True)
        ready(5)

    @pl.when(inner)
    def _():
        texts_done(1, 4)
        d, row = meet(xb[9 - 4 * j], zb[pl.ds(4 - 2 * j, 2)].reshape(2 * ROWS, WIDTH), False)
        gdx[...] = d
        gsum_out[...] = row

    for q, (_, _, way) in enumerate(PIECES):
        g_go(slot(y_out, q), total(0, q), 24 + q, slot(y_pass, q), y_up if way > 0 else y_dn)

    onward = [
        copy(slot(y_pass, q), slot(y_in, q), g_s.at[28 + q], g_r.at[28 + q], y_up if way > 0 else y_dn)
        for q, (_, _, way) in enumerate(PIECES)
    ]

    def relay():
        for q in range(4):
            copy(slot(y_pass, q), slot(y_pass, q), g_s.at[24 + q], g_r.at[24 + q], xp).wait_recv()
            onward[q].start()

    second_sends(1)

    @pl.when(inner)
    def _():
        d, row = meet(xb[0], zb[0:3].reshape(3 * ROWS, WIDTH), True)
        u[:ROWS] = d
        loss_out[...] = row

    relay()

    @pl.when(inner)
    def _():
        for h in range(2):
            wait_p(2, h)
        project(pbuf[3], u.at[3 * ROWS:])
        texts_done(4, 5)
        d, row = meet(xb[9 - 4 * j], zb[4], False)
        gdx_out[...] = (gdx[...] + d).astype(BF16)
        gsum_out[...] += row

        @pl.when(j == 1)
        def _():
            gdx_dn.start()
            gsum_dn.start()

        @pl.when(j == 2)
        def _():
            gdx_up.start()
            gsum_up.start()

    @pl.when(inner)
    def _():
        d, row = meet(xb[0], zb[4], False)
        image_side(u[:ROWS] + d, loss_out[...] + row)

    for d in w_sent:
        d.wait_send()

    @pl.when(j == 3)
    def _():
        for d in edge_up:
            d.wait_send()

    @pl.when(j == 0)
    def _():
        for d in edge_dn:
            d.wait_send()

    @pl.when(outer)
    def _():
        for d in edge_far:
            d.wait_send()

    @pl.when(j <= 2)
    def _():
        for d in x_hop + hop_up:
            d.wait_send()

    @pl.when(j >= 1)
    def _():
        for d in p_hop:
            d.wait_send()

    @pl.when(j == 0)
    def _():
        guest.wait_send()

    x_done(0, img)
    p_done(0, pool)
    for k in range(1, 4):
        x_done(k, xbuf.at[k])
        p_done(k, pbuf.at[0])
    p_done(4, pbuf.at[0])
    pool_swap.wait_send()
    pair.wait_send()
    for d in g_sent[:24]:
        d.wait_send()


    for q, (start, size, _) in enumerate(PIECES):
        head_out[:, start:start + size] = total(1, q)

    @pl.when(outer)
    def _():
        gsum_up.wait_recv()
        gdx_up.wait_recv()
        image_side(u[ROWS:2 * ROWS] + gdx_in[...].astype(F32), loss_out[...] + gsum_in[...])

    for q, (start, size, _) in enumerate(PIECES):
        head_out[:, start:start + size] += g_wait(slot(y_in, q), 28 + q)

    @pl.when(inner)
    def _():
        gdx_up.wait_send()
        gsum_up.wait_send()

    for d in g_sent[24:] + onward:
        d.wait_send()


def finish(*refs):
    moves = [pltpu.make_async_copy(refs[i], refs[4 + i], refs[8].at[i]) for i in range(4)]
    for d in moves:
        d.start()
    for d in moves:
        d.wait()


def per_device(images, pooled, head_weight, head_bias, log_scale, bias):
    smem = pl.BlockSpec(memory_space=pltpu.SMEM)
    vmem = pl.BlockSpec(memory_space=pltpu.VMEM)
    hbm = pl.BlockSpec(memory_space=pltpu.HBM)
    block = (ROWS, WIDTH)
    slab = (SHARD, WIDTH)
    parts = [(SHARD, size) for _, size, _ in PIECES]
    dma = pltpu.SemaphoreType.DMA
    results = (
        jax.ShapeDtypeStruct((1, ROWS), F32),
        jax.ShapeDtypeStruct(block, BF16),
        jax.ShapeDtypeStruct(block, BF16),
        jax.ShapeDtypeStruct(slab, F32),
    )
    made = pl.pallas_call(
        kernel,
        out_shape=results,
        in_specs=[hbm, hbm, hbm, hbm, smem, smem],
        out_specs=(vmem,) * 4,
        scratch_shapes=[
            pltpu.VMEM(block, BF16),
            pltpu.VMEM(block, BF16),
            pltpu.VMEM((1, WIDTH), F32),
            pltpu.VMEM((2, 8, SHARD, FIRST), BF16),
            pltpu.VMEM((2, 8, SHARD, WIDTH - FIRST), BF16),
            pltpu.VMEM((WIDTH, WIDTH), BF16),
            pltpu.VMEM((6,) + block, BF16),
            pltpu.VMEM((4,) + block, BF16),
            pltpu.VMEM((6,) + block, BF16),
            pltpu.VMEM((5,) + block, BF16),
            pltpu.VMEM(block, F32),
            pltpu.VMEM(block, F32),
            pltpu.VMEM((4 * ROWS, WIDTH), F32),
            pltpu.VMEM((2 * ROWS, WIDTH), BF16),
            pltpu.VMEM(block, BF16),
            pltpu.VMEM((WIDTH, ROWS), F32),
            pltpu.VMEM((8 * SHARD, 2 * ROWS), BF16),
            pltpu.VMEM((8,) + slab, F32),
            [pltpu.VMEM((2, 3) + p, BF16) for p in parts],
            [pltpu.VMEM((2,) + p, BF16) for p in parts],
            [pltpu.VMEM((2, 2) + p, BF16) for p in parts],
            [pltpu.VMEM(p, BF16) for p in parts],
            [pltpu.VMEM(p, BF16) for p in parts],
            [pltpu.VMEM(p, BF16) for p in parts],
            pltpu.VMEM(block, F32),
            pltpu.VMEM(block, BF16),
            pltpu.VMEM((1, ROWS), F32),
            pltpu.VMEM(block, BF16),
            pltpu.VMEM((1, ROWS), F32),
            dma((5,)),
            dma((33,)), dma((33,)),
            dma((7, 4)), dma((6, 4)),
            dma((6, 2)), dma((5, 2)),
            dma((32,)), dma((32,)),
            dma((4,)), dma((4,)),
        ],
        compiler_params=pltpu.CompilerParams(
            collective_id=0, has_side_effects=True, vmem_limit_bytes=VMEM_GRANT
        ),
        cost_estimate=pl.CostEstimate(flops=4_000_000_000, bytes_accessed=6_000_000, transcendentals=300_000),
    )(*[pltpu.with_memory_space_constraint(v, pltpu.HBM) for v in (images, pooled, head_weight, head_bias)], log_scale, bias)
    loss, image_grad, pooled_grad, head_grad = pl.pallas_call(
        finish,
        out_shape=results,
        in_specs=[vmem] * 4,
        out_specs=(hbm,) * 4,
        scratch_shapes=[dma((4,))],
        compiler_params=pltpu.CompilerParams(vmem_limit_bytes=4 * 1024 * 1024),
    )(*made)
    return loss.reshape(ROWS), image_grad, pooled_grad, head_grad


def solution(mesh):
    in_specs = (P(("dp", "fsdp"), None), P(("dp", "fsdp"), None), P("fsdp", None), P(), P(), P())
    out_specs = (
        P(("dp", "fsdp")),
        P(("dp", "fsdp"), None),
        P(("dp", "fsdp"), None),
        P(("dp", "fsdp"), None),
    )
    return jax.shard_map(
        per_device, mesh=mesh, in_specs=in_specs, out_specs=out_specs, check_vma=False
    )
```

```python
import jax
import jax.numpy as jnp
from jax import lax
from jax.experimental import pallas as pl
from jax.experimental.pallas import tpu as pltpu
from jax.sharding import PartitionSpec as P

MESH = pl.DeviceIdType.MESH
F32 = jnp.float32
BF16 = jnp.bfloat16
NT = (((1,), (1,)), ((), ()))

ROWS = 128
WIDTH = 1152
SHARD = 72
CHIP = 144
FIRST = 640
TILE = 384
VMEM_GRANT = 44 * 1024 * 1024
HALF = 64
PIECES = ((0, 384, 1), (640, 256, -1), (384, 256, 1), (896, 256, -1))
PLACE = {1: 0, 3: 1, 4: 2, 2: 3}
ORDER = (2, 1, 3, 0)


def normalize(v):
    r = lax.rsqrt(jnp.sum(v * v, axis=-1, keepdims=True) + 1e-06)
    return v * r, r


def kernel(
    img_hbm, pool_hbm, wsh_hbm, hb_hbm, log_scale, bias,
    loss_out, img_out, pool_out, head_out,
    img, pool, hb,
    wa, wb, wf, xbuf, pbuf, xb, zb, ximg, ztxt, u, dzb, psib, ptf, pt, terms,
    g_out, g_far, g_near,
    y_out, y_pass, y_in,
    gdx, gdx_out, gsum_out, gdx_in, gsum_in,
    l_s, w_s, w_r, x_s, x_r, p_s, p_r, g_s, g_r, h_s, h_r,
):
    dp = lax.axis_index("dp")
    f = lax.axis_index("fsdp")
    j = lax.rem(dp, 4)
    yh = lax.div(f, 8)
    x = lax.rem(lax.div(f, 2), 4)
    c = lax.rem(f, 2)
    base = yh * 8 + c

    sib = (dp, f + 1 - 2 * c)
    xp = (dp, base + 2 * lax.rem(x + 1, 4))
    xm = (dp, base + 2 * lax.rem(x + 3, 4))
    zp = (lax.rem(dp + 4, 32), f)
    zm = (lax.rem(dp + 28, 32), f)
    wrap_up = lax.div(j + 1, 4)
    up = (dp + 1 - 4 * wrap_up, lax.rem(f + 8 * wrap_up, 16))
    wrap_dn = lax.div(3 - j, 3)
    dn = (dp - 1 + 4 * wrap_dn, lax.rem(f + 8 * wrap_dn, 16))
    odd = lax.rem(j, 2)
    step = 3 - 2 * odd
    wrap = lax.div(j + step, 4)
    y_up = (dp + step - 4 * wrap, lax.rem(f + 8 * wrap, 16))
    step = 1 + 2 * odd
    wrap = lax.div(3 - j, 2)
    y_dn = (dp - step + 4 * wrap, lax.rem(f + 8 * wrap, 16))

    across = (dp - j + lax.rem(j + 2, 4), lax.rem(f + 8, 16))
    mine = yh * 4 + x
    theirs = 4 - yh * 4 + x

    loads = [
        pltpu.make_async_copy(src, dst, l_s.at[i])
        for i, (src, dst) in enumerate(
            (
                (wsh_hbm.at[:, :FIRST], wa.at[c, mine]),
                (wsh_hbm.at[:, FIRST:], wb.at[c, mine]),
                (img_hbm, img),
                (pool_hbm, pool),
                (hb_hbm, hb.at[0]),
            )
        )
    ]
    for d in loads:
        d.start()

    barrier = pltpu.get_barrier_semaphore()
    for who in (sib, xp, xm, zp, zm, up, dn, across):
        pl.semaphore_signal(barrier, inc=1, device_id=who, device_id_type=MESH)

    @pl.when(odd == 0)
    def _():
        pl.semaphore_signal(barrier, inc=1, device_id=y_up, device_id_type=MESH)

    @pl.when(odd == 1)
    def _():
        pl.semaphore_signal(barrier, inc=1, device_id=y_dn, device_id_type=MESH)

    pl.semaphore_wait(barrier, 9)
    for d in loads:
        d.wait()

    def copy(src, dst, send, recv, who):
        return pltpu.make_async_remote_copy(
            src_ref=src, dst_ref=dst, send_sem=send, recv_sem=recv, device_id=who, device_id_type=MESH
        )

    def part(ref, h):
        return ref.at[pl.ds(HALF * h, HALF), :]

    def send_x(k, src, h):
        @pl.when(jnp.logical_and(k <= 3 - j, j >= 1))
        def _():
            copy(part(src, h), part(xbuf.at[k + 1], h), x_s.at[k, h], x_r.at[k + 1, h], dn).start()

        @pl.when(jnp.logical_and(k > 3 - j, j <= 2))
        def _():
            copy(part(src, h), part(xbuf.at[k - 1], h), x_s.at[k, h], x_r.at[k - 1, h], up).start()

    def send_p(k, src, h):
        if k < 4:
          @pl.when(jnp.logical_and(k <= j, j <= 1))
          def _():
            copy(part(src, h), part(pbuf.at[PLACE[k + 1]], h), p_s.at[k, h], p_r.at[k + 1, h], up).start()

        if k > 2:
          @pl.when(jnp.logical_and(k > j, j >= 2))
          def _():
            copy(part(src, h), part(pbuf.at[PLACE[k - 1]], h), p_s.at[k, h], p_r.at[k - 1, h], dn).start()

    def wait_x(k, h, whole=False):
        dst = xbuf.at[k] if whole else part(xbuf.at[k], h)
        copy(dst, dst, x_s.at[k, h], x_r.at[k, h], up).wait_recv()

    def quarter(k, q):
        return xbuf.at[k, pl.ds(HALF // 2 * q, HALF // 2), :]

    hop_in = [copy(quarter(4, q), quarter(4, q), x_s.at[5, q], x_r.at[4, q], zm) for q in range(4)]
    hop_up = [copy(quarter(4, q), quarter(3, q), x_s.at[4, q], x_r.at[3, q // 2], up) for q in range(4)]

    def wait_p(k, h):
        dst = part(pbuf.at[PLACE[k]], h)
        copy(dst, dst, p_s.at[k, h], p_r.at[k, h], up).wait_recv()

    def pass_x(k, h):
        wait_x(k, h)
        send_x(k, xbuf.at[k], h)

    def pass_p(k):
        for h in range(2):
            wait_p(k, h)
            send_p(k, pbuf.at[PLACE[k]], h)

    def x_done(k, src):
        @pl.when(jnp.logical_or(jnp.logical_and(k <= 3 - j, j >= 1), jnp.logical_and(k > 3 - j, j <= 2)))
        def _():
            for h in range(2):
                copy(part(src, h), part(xbuf.at[1], h), x_s.at[k, h], x_r.at[1, h], up).wait_send()

    def p_done(k, src):
        @pl.when(jnp.logical_or(jnp.logical_and(k <= j, j <= 1), jnp.logical_and(k > j, j >= 2)))
        def _():
            for h in range(2):
                copy(part(src, h), part(pbuf.at[0], h), p_s.at[k, h], p_r.at[1, h], up).wait_send()

    middle = lax.rem(lax.div(j + 1, 2), 2)
    outer = middle == 0
    inner = middle == 1
    xk0 = 1 + 2 * lax.div(j, 3)
    xk1 = 2 + middle
    xk2 = 6 - xk0 - xk1
    guest = copy(img, xbuf.at[5], x_s.at[6, 0], x_r.at[5, 0], up)

    pool_swap = copy(pool, psib, h_s.at[2], h_r.at[2], sib)
    x_hop = [
        copy(img.at[pl.ds(HALF // 2 * q, HALF // 2), :], quarter(4, q), x_s.at[5, q], x_r.at[4, q], zm)
        for q in range(4)
    ]
    p_hop = [copy(part(pool, h), part(pbuf.at[PLACE[4]], h), p_s.at[5, h], p_r.at[4, h], zp) for h in range(2)]

    @pl.when(j <= 2)
    def _():
        for d in x_hop:
            d.start()

    send_x(0, img, 0)
    send_x(0, img, 1)

    def chip(h, off):
        return h * 4 + lax.rem(x + off, 4)

    def piece(m, p):
        return (wa if p == 0 else wb).at[c, m]

    def w_copy(src, dst, ident, who, send=None):
        return copy(src, dst, w_s.at[ident if send is None else send], w_r.at[ident], who)

    w_sent = []

    def w_go(src, ident, who):
        d = w_copy(src, src, ident, who)
        d.start()
        w_sent.append(d)

    def to_sibling(n, m, p):
        w_go(piece(m, p), 17 + 2 * n + p, sib)

    def assemble(n, m):
        for p in range(2):
            src = (wa if p == 0 else wb).at[1 - c, m]
            w_copy(src, src, 17 + 2 * n + p, sib).wait_recv()
        rows = pl.ds(pl.multiple_of(m * CHIP, 16), CHIP)
        for ref, cols in ((wa, slice(0, FIRST)), (wb, slice(FIRST, WIDTH))):
            wf[rows, cols] = jnp.concatenate(
                [ref[0, m].astype(F32), ref[1, m].astype(F32)], axis=0
            ).astype(BF16)

    edge_up = [w_copy(piece(mine, p), piece(mine, p), 13 + p, up) for p in range(2)]
    edge_dn = [w_copy(piece(mine, p), piece(mine, p), 13 + p, dn) for p in range(2)]
    edge_far = [w_copy(piece(mine, p), piece(mine, p), 13 + p, across, 15 + p) for p in range(2)]

    @pl.when(j == 3)
    def _():
        for d in edge_up:
            d.start()

    @pl.when(j == 0)
    def _():
        for d in edge_dn:
            d.start()

    @pl.when(outer)
    def _():
        for d in edge_far:
            d.start()

    def along_x(r, m):
        return {
            (d, p): w_copy(piece(m, p), piece(m, p), 1 + 4 * r + 2 * d + p, xp if d == 0 else xm)
            for d in range(2)
            for p in range(2)
        }

    mine_x = along_x(0, mine)
    theirs_x = along_x(1, theirs)
    for key in ((0, 0), (1, 1), (0, 1), (1, 0)):
        mine_x[key].start()
    w_sent.extend(mine_x.values())
    w_sent.extend(theirs_x.values())
    to_sibling(0, mine, 0)
    to_sibling(0, mine, 1)
    pool_swap.start()

    @pl.when(j == 1)
    def _():
        send_p(0, pool, 0)

    @pl.when(j >= 1)
    def _():
        for d in p_hop:
            d.start()

    v, xr = normalize(img[...].astype(F32))
    ximg[...] = v
    xb[0] = v.astype(BF16)

    def slab_rows(n):
        m = chip(1 - yh if n < 4 else yh, ORDER[n % 4])
        return ptf[pl.ds(pl.multiple_of(m * CHIP + SHARD * c, 8), SHARD), :]

    def transpose_into(ref, start):
        ptf[...] = ref[...].astype(F32).T
        for n in range(0, 8, 2):
            pt[SHARD * n:SHARD * (n + 2), start:start + ROWS] = jnp.concatenate(
                [slab_rows(n), slab_rows(n + 1)], axis=0
            ).astype(BF16)

    def near_first(r, h):
        for d, (off, onward) in enumerate(((3, xp), (1, xm))):
            got = piece(chip(h, off), d)
            w_copy(got, got, 1 + 4 * r + 3 * d, xp).wait_recv()
            w_go(got, 9 + 2 * r + d, onward)
            to_sibling(1 + 4 * r + d, chip(h, off), d)

    def near_rest(r, h):
        for d, off in enumerate((3, 1)):
            m = chip(h, off)
            got = piece(m, 1 - d)
            w_copy(got, got, 2 + 4 * r + d, xp).wait_recv()
            to_sibling(1 + 4 * r + d, m, 1 - d)

    def far_units(r, h):
        m = chip(h, 2)
        for p in range(2):
            w_copy(piece(m, p), piece(m, p), 9 + 2 * r + p, xp).wait_recv()
            to_sibling(3 + 4 * r, m, p)

    edge_in = [w_copy(piece(theirs, p), piece(theirs, p), 13 + p, xp) for p in range(2)]

    def theirs_first():
        edge_in[0].wait_recv()
        theirs_x[0, 0].start()
        theirs_sib[0].start()

    def theirs_rest():
        edge_in[1].wait_recv()
        for key in ((1, 1), (0, 1), (1, 0)):
            theirs_x[key].start()
        theirs_sib[1].start()

    theirs_sib = [w_copy(piece(theirs, p), piece(theirs, p), 25 + p, sib) for p in range(2)]
    w_sent.extend(theirs_sib)

    def hop_on(h):
        @pl.when(j <= 2)
        def _():
            for q in (2 * h, 2 * h + 1):
                hop_in[q].wait_recv()
                hop_up[q].start()

        @pl.when(inner)
        def _():
            pass_x(1, h)

    hop_on(0)
    transpose_into(pool, 0)

    @pl.when(outer)
    def _():
        theirs_first()

    near_first(0, yh)

    @pl.when(outer)
    def _():
        theirs_rest()

    hop_on(1)
    near_rest(0, yh)
    pool_swap.wait_recv()
    transpose_into(psib, ROWS)

    @pl.when(j == 0)
    def _():
        send_p(0, pool, 0)
        send_p(0, pool, 1)
        guest.start()

    @pl.when(j == 3)
    def _():
        pass_p(4)

    @pl.when(inner)
    def _():
        pass_x(3, 0)
        theirs_first()

    far_units(0, yh)
    assemble(0, mine)

    @pl.when(inner)
    def _():
        pass_x(3, 1)
        theirs_rest()
        pass_x(2, 0)

    @pl.when(j == 2)
    def _():
        pass_p(4)

    @pl.when(j == 1)
    def _():
        pass_x(2, 1)

    near_first(1, 1 - yh)
    for n, off in ((1, 3), (2, 1), (3, 2)):
        assemble(n, chip(yh, off))

    @pl.when(j == 2)
    def _():
        pass_x(2, 1)

    @pl.when(j == 1)
    def _():
        send_p(0, pool, 1)

    near_rest(1, 1 - yh)

    @pl.when(j == 1)
    def _():
        pass_p(1)

    @pl.when(j == 2)
    def _():
        pass_p(3)

    far_units(1, 1 - yh)

    def ready(k):
        xb[k] = normalize(xbuf[k].astype(F32))[0].astype(BF16)

    @pl.when(inner)
    def _():
        for k in range(1, 4):
            ready(k)

    assemble(4, theirs)
    for n, off in ((5, 3), (6, 1), (7, 2)):
        assemble(n, chip(1 - yh, off))

    temper = jnp.exp(jnp.full((1, 1), log_scale[0], F32))
    offset = jnp.full((1, 1), bias[0], F32)
    gain = temper * (1.0 / ROWS)

    def project(block, out):
        for start in range(0, WIDTH, 512):
            cols = pl.ds(start, min(512, WIDTH - start))
            out[:, cols] = jnp.dot(block, wf[:, cols], preferred_element_type=F32) + hb[:, cols]

    def weights(a, b, own):
        l = temper * lax.dot_general(a, b, NT, preferred_element_type=F32) + offset
        if own:
            eye = lax.broadcasted_iota(jnp.int32, l.shape, 0) == lax.broadcasted_iota(jnp.int32, l.shape, 1)
            l = jnp.where(eye, -l, l)
        g = gain / (1.0 + jnp.exp(-l))
        if own:
            g = jnp.where(eye, -g, g)
        return l, g.astype(BF16)

    def losses(m):
        e = jnp.maximum(m, 0.0) + jnp.log1p(jnp.exp(-jnp.abs(m)))
        total = e[:, :ROWS]
        for start in range(ROWS, m.shape[1], ROWS):
            total = total + e[:, start:start + ROWS]
        return jnp.sum(total.T, axis=0, keepdims=True)

    def image_side(d, row):
        loss_out[...] = row * (1.0 / ROWS)
        v = ximg[...]
        img_out[...] = (xr * (d - v * jnp.sum(v * d, axis=-1, keepdims=True))).astype(BF16)

    project(pool[...], ztxt)
    v, zr = normalize(ztxt[...])
    ztxt[...] = v
    zb[0] = v.astype(BF16)

    def text_grad(a, own):
        _, g = weights(zb[0], a, own)
        return jnp.dot(g, a, preferred_element_type=F32)

    def text_side(d):
        v = ztxt[...]
        dzb[:ROWS] = (zr * (d - v * jnp.sum(v * d, axis=-1, keepdims=True))).astype(BF16)

    @pl.when(inner)
    def _():
        text_side(text_grad(xb[0:4].reshape(4 * ROWS, WIDTH), True))

    @pl.when(outer)
    def _():
        for k in (xk0, xk1):
            wait_x(k, 0)
            wait_x(k, 1)
            ready(k)
        u[:ROWS] = text_grad(xb[0], True) + text_grad(xb[xk0], False) + text_grad(xb[xk1], False)
        wait_x(xk2, 0)
        wait_x(xk2, 1)
        ready(xk2)
        text_side(u[:ROWS] + text_grad(xb[xk2], False))

    pair = copy(dzb.at[:ROWS], dzb.at[ROWS:], h_s.at[3], h_r.at[3], sib)
    pair.start()

    def make(n):
        t = jnp.dot(pt[SHARD * n:SHARD * (n + 2), :], dzb[...], preferred_element_type=F32)
        terms[n] = t[:SHARD]
        terms[n + 1] = t[SHARD:]

    def cols(n, q):
        start, size, _ = PIECES[q]
        return terms[n, :, start:start + size]

    g_sent = []

    def g_go(src, value, ident, dst, who):
        src[...] = value.astype(BF16)
        d = copy(src, dst, g_s.at[ident], g_r.at[ident], who)
        d.start()
        g_sent.append(d)

    def g_wait(ref, ident):
        copy(ref, ref, g_s.at[ident], g_r.at[ident], xp).wait_recv()
        return ref[...].astype(F32)

    def slot(refs, q, *index):
        return refs[q].at[index] if index else refs[q]

    def far_sends(g):
        for q, (_, _, way) in enumerate(PIECES):
            g_go(slot(g_out, q, g, 0), cols(4 * g, q), 12 * g + q, slot(g_far, q, g), xp if way > 0 else xm)

    def near_sends(g):
        for q, (_, _, way) in enumerate(PIECES):
            n, who = (2, xm) if way > 0 else (1, xp)
            g_go(slot(g_out, q, g, 1), cols(4 * g + n, q), 12 * g + 4 + q, slot(g_near, q, g, 0), who)

    def second_sends(g):
        for q, (_, _, way) in enumerate(PIECES):
            n, who = (1, xp) if way > 0 else (2, xm)
            value = cols(4 * g + n, q) + g_wait(slot(g_far, q, g), 12 * g + q)
            g_go(slot(g_out, q, g, 2), value, 12 * g + 8 + q, slot(g_near, q, g, 1), who)

    def total(g, q):
        value = cols(4 * g + 3, q) + g_wait(slot(g_near, q, g, 0), 12 * g + 4 + q)
        return value + g_wait(slot(g_near, q, g, 1), 12 * g + 8 + q)

    def back():
        @pl.loop(0, WIDTH // TILE)
        def _(n):
            cols = pl.ds(pl.multiple_of(n * TILE, TILE), TILE)
            pool_out[:, cols] = lax.dot_general(
                dzb[:ROWS], wf[cols, :], NT, preferred_element_type=F32
            ).astype(BF16)

    gdx_up = copy(gdx_out, gdx_in, h_s.at[0], h_r.at[0], up)
    gdx_dn = copy(gdx_out, gdx_in, h_s.at[0], h_r.at[0], dn)
    gsum_up = copy(gsum_out, gsum_in, h_s.at[1], h_r.at[1], up)
    gsum_dn = copy(gsum_out, gsum_in, h_s.at[1], h_r.at[1], dn)

    @pl.when(outer)
    def _():
        m, g = weights(xb[0], zb[0], True)
        u[ROWS:2 * ROWS] = jnp.dot(g, zb[0], preferred_element_type=F32)
        loss_out[...] = losses(m)

    def texts_done(first, last):
        for n in range(first, last):
            v = u[ROWS * (n - 1):ROWS * n]
            zb[n] = normalize(v)[0].astype(BF16)

    def meet(image, texts, own):
        m, g = weights(image, texts, own)
        return jnp.dot(g, texts, preferred_element_type=F32), losses(m)

    @pl.when(inner)
    def _():
        back()

    pair.wait_recv()
    make(0)
    far_sends(0)
    make(2)
    near_sends(0)

    @pl.when(j == 1)
    def _():
        for h in range(2):
            wait_p(3, h)
            wait_p(4, h)

    @pl.when(j == 2)
    def _():
        for h in range(2):
            wait_p(1, h)

    @pl.when(inner)
    def _():
        project(pbuf[0:3].reshape(3 * ROWS, WIDTH), u.at[:3 * ROWS])

    @pl.when(outer)
    def _():
        make(4)
        make(6)
        back()

    second_sends(0)

    @pl.when(inner)
    def _():
        make(4)
        make(6)

    far_sends(1)
    near_sends(1)

    @pl.when(j == 1)
    def _():
        wait_x(5, 0, whole=True)
        ready(5)

    @pl.when(inner)
    def _():
        texts_done(1, 4)
        d, row = meet(xb[9 - 4 * j], zb[pl.ds(4 - 2 * j, 2)].reshape(2 * ROWS, WIDTH), False)
        gdx[...] = d
        gsum_out[...] = row

    for q, (_, _, way) in enumerate(PIECES):
        g_go(slot(y_out, q), total(0, q), 24 + q, slot(y_pass, q), y_up if way > 0 else y_dn)

    onward = [
        copy(slot(y_pass, q), slot(y_in, q), g_s.at[28 + q], g_r.at[28 + q], y_up if way > 0 else y_dn)
        for q, (_, _, way) in enumerate(PIECES)
    ]

    def relay():
        for q in range(4):
            copy(slot(y_pass, q), slot(y_pass, q), g_s.at[24 + q], g_r.at[24 + q], xp).wait_recv()
            onward[q].start()

    second_sends(1)

    @pl.when(inner)
    def _():
        for h in range(2):
            wait_p(2, h)
        project(pbuf[3], u.at[3 * ROWS:])
        texts_done(4, 5)
        d, row = meet(xb[9 - 4 * j], zb[4], False)
        gdx_out[...] = (gdx[...] + d).astype(BF16)
        gsum_out[...] += row

    relay()

    @pl.when(j == 1)
    def _():
        gdx_dn.start()
        gsum_dn.start()

    @pl.when(j == 2)
    def _():
        gdx_up.start()
        gsum_up.start()

    @pl.when(inner)
    def _():
        d, row = meet(xb[0], zb[0:3].reshape(3 * ROWS, WIDTH), True)
        e, more = meet(xb[0], zb[4], False)
        image_side(d + e, row + more)

    for d in w_sent:
        d.wait_send()

    @pl.when(j == 3)
    def _():
        for d in edge_up:
            d.wait_send()

    @pl.when(j == 0)
    def _():
        for d in edge_dn:
            d.wait_send()

    @pl.when(outer)
    def _():
        for d in edge_far:
            d.wait_send()

    @pl.when(j <= 2)
    def _():
        for d in x_hop + hop_up:
            d.wait_send()

    @pl.when(j >= 1)
    def _():
        for d in p_hop:
            d.wait_send()

    @pl.when(j == 0)
    def _():
        guest.wait_send()

    x_done(0, img)
    p_done(0, pool)
    for k in range(1, 4):
        x_done(k, xbuf.at[k])
        p_done(k, pbuf.at[0])
    p_done(4, pbuf.at[0])
    pool_swap.wait_send()
    pair.wait_send()
    for d in g_sent[:24]:
        d.wait_send()


    for q, (start, size, _) in enumerate(PIECES):
        head_out[:, start:start + size] = total(1, q)

    @pl.when(outer)
    def _():
        gsum_up.wait_recv()
        gdx_up.wait_recv()
        image_side(u[ROWS:2 * ROWS] + gdx_in[...].astype(F32), loss_out[...] + gsum_in[...])

    for q, (start, size, _) in enumerate(PIECES):
        head_out[:, start:start + size] += g_wait(slot(y_in, q), 28 + q)

    @pl.when(inner)
    def _():
        gdx_up.wait_send()
        gsum_up.wait_send()

    for d in g_sent[24:] + onward:
        d.wait_send()


def finish(*refs):
    moves = [pltpu.make_async_copy(refs[i], refs[4 + i], refs[8].at[i]) for i in range(4)]
    for d in moves:
        d.start()
    for d in moves:
        d.wait()


def per_device(images, pooled, head_weight, head_bias, log_scale, bias):
    smem = pl.BlockSpec(memory_space=pltpu.SMEM)
    vmem = pl.BlockSpec(memory_space=pltpu.VMEM)
    hbm = pl.BlockSpec(memory_space=pltpu.HBM)
    block = (ROWS, WIDTH)
    slab = (SHARD, WIDTH)
    parts = [(SHARD, size) for _, size, _ in PIECES]
    dma = pltpu.SemaphoreType.DMA
    results = (
        jax.ShapeDtypeStruct((1, ROWS), F32),
        jax.ShapeDtypeStruct(block, BF16),
        jax.ShapeDtypeStruct(block, BF16),
        jax.ShapeDtypeStruct(slab, F32),
    )
    made = pl.pallas_call(
        kernel,
        out_shape=results,
        in_specs=[hbm, hbm, hbm, hbm, smem, smem],
        out_specs=(vmem,) * 4,
        scratch_shapes=[
            pltpu.VMEM(block, BF16),
            pltpu.VMEM(block, BF16),
            pltpu.VMEM((1, WIDTH), F32),
            pltpu.VMEM((2, 8, SHARD, FIRST), BF16),
            pltpu.VMEM((2, 8, SHARD, WIDTH - FIRST), BF16),
            pltpu.VMEM((WIDTH, WIDTH), BF16),
            pltpu.VMEM((6,) + block, BF16),
            pltpu.VMEM((4,) + block, BF16),
            pltpu.VMEM((6,) + block, BF16),
            pltpu.VMEM((5,) + block, BF16),
            pltpu.VMEM(block, F32),
            pltpu.VMEM(block, F32),
            pltpu.VMEM((4 * ROWS, WIDTH), F32),
            pltpu.VMEM((2 * ROWS, WIDTH), BF16),
            pltpu.VMEM(block, BF16),
            pltpu.VMEM((WIDTH, ROWS), F32),
            pltpu.VMEM((8 * SHARD, 2 * ROWS), BF16),
            pltpu.VMEM((8,) + slab, F32),
            [pltpu.VMEM((2, 3) + p, BF16) for p in parts],
            [pltpu.VMEM((2,) + p, BF16) for p in parts],
            [pltpu.VMEM((2, 2) + p, BF16) for p in parts],
            [pltpu.VMEM(p, BF16) for p in parts],
            [pltpu.VMEM(p, BF16) for p in parts],
            [pltpu.VMEM(p, BF16) for p in parts],
            pltpu.VMEM(block, F32),
            pltpu.VMEM(block, BF16),
            pltpu.VMEM((1, ROWS), F32),
            pltpu.VMEM(block, BF16),
            pltpu.VMEM((1, ROWS), F32),
            dma((5,)),
            dma((33,)), dma((33,)),
            dma((7, 4)), dma((6, 4)),
            dma((6, 2)), dma((5, 2)),
            dma((32,)), dma((32,)),
            dma((4,)), dma((4,)),
        ],
        compiler_params=pltpu.CompilerParams(
            collective_id=0, has_side_effects=True, vmem_limit_bytes=VMEM_GRANT
        ),
        cost_estimate=pl.CostEstimate(flops=4_000_000_000, bytes_accessed=6_000_000, transcendentals=300_000),
    )(*[pltpu.with_memory_space_constraint(v, pltpu.HBM) for v in (images, pooled, head_weight, head_bias)], log_scale, bias)
    loss, image_grad, pooled_grad, head_grad = pl.pallas_call(
        finish,
        out_shape=results,
        in_specs=[vmem] * 4,
        out_specs=(hbm,) * 4,
        scratch_shapes=[dma((4,))],
        compiler_params=pltpu.CompilerParams(vmem_limit_bytes=4 * 1024 * 1024),
    )(*made)
    return loss.reshape(ROWS), image_grad, pooled_grad, head_grad


def solution(mesh):
    in_specs = (P(("dp", "fsdp"), None), P(("dp", "fsdp"), None), P("fsdp", None), P(), P(), P())
    out_specs = (
        P(("dp", "fsdp")),
        P(("dp", "fsdp"), None),
        P(("dp", "fsdp"), None),
        P(("dp", "fsdp"), None),
    )
    return jax.shard_map(
        per_device, mesh=mesh, in_specs=in_specs, out_specs=out_specs, check_vma=False
    )
```

```python
import jax
import jax.numpy as jnp
from jax import lax
from jax.experimental import pallas as pl
from jax.experimental.pallas import tpu as pltpu
from jax.sharding import PartitionSpec as P

MESH = pl.DeviceIdType.MESH
F32 = jnp.float32
BF16 = jnp.bfloat16
NT = (((1,), (1,)), ((), ()))

ROWS = 128
WIDTH = 1152
SHARD = 72
CHIP = 144
FIRST = 640
TILE = 384
VMEM_GRANT = 44 * 1024 * 1024
HALF = 64
PIECES = ((0, 384, 1), (640, 256, -1), (384, 256, 1), (896, 256, -1))
PLACE = {1: 0, 3: 1, 4: 2, 2: 3}
ORDER = (2, 1, 3, 0)


def normalize(v):
    r = lax.rsqrt(jnp.sum(v * v, axis=-1, keepdims=True) + 1e-06)
    return v * r, r


def kernel(
    img_hbm, pool_hbm, wsh_hbm, hb_hbm, log_scale, bias,
    loss_out, img_out, pool_out, head_out,
    img, pool, hb,
    wa, wb, wf, xbuf, pbuf, xb, zb, ximg, ztxt, u, dzb, psib, ptf, pt, terms,
    g_out, g_far, g_near,
    y_out, y_pass, y_in,
    gdx, gdx_out, gsum_out, gdx_in, gsum_in,
    l_s, w_s, w_r, x_s, x_r, p_s, p_r, g_s, g_r, h_s, h_r,
):
    dp = lax.axis_index("dp")
    f = lax.axis_index("fsdp")
    j = lax.rem(dp, 4)
    yh = lax.div(f, 8)
    x = lax.rem(lax.div(f, 2), 4)
    c = lax.rem(f, 2)
    base = yh * 8 + c

    sib = (dp, f + 1 - 2 * c)
    xp = (dp, base + 2 * lax.rem(x + 1, 4))
    xm = (dp, base + 2 * lax.rem(x + 3, 4))
    zp = (lax.rem(dp + 4, 32), f)
    zm = (lax.rem(dp + 28, 32), f)
    wrap_up = lax.div(j + 1, 4)
    up = (dp + 1 - 4 * wrap_up, lax.rem(f + 8 * wrap_up, 16))
    wrap_dn = lax.div(3 - j, 3)
    dn = (dp - 1 + 4 * wrap_dn, lax.rem(f + 8 * wrap_dn, 16))
    odd = lax.rem(j, 2)
    step = 3 - 2 * odd
    wrap = lax.div(j + step, 4)
    y_up = (dp + step - 4 * wrap, lax.rem(f + 8 * wrap, 16))
    step = 1 + 2 * odd
    wrap = lax.div(3 - j, 2)
    y_dn = (dp - step + 4 * wrap, lax.rem(f + 8 * wrap, 16))

    across = (dp - j + lax.rem(j + 2, 4), lax.rem(f + 8, 16))
    mine = yh * 4 + x
    theirs = 4 - yh * 4 + x

    loads = [
        pltpu.make_async_copy(src, dst, l_s.at[i])
        for i, (src, dst) in enumerate(
            (
                (wsh_hbm.at[:, :FIRST], wa.at[c, mine]),
                (wsh_hbm.at[:, FIRST:], wb.at[c, mine]),
                (img_hbm, img),
                (pool_hbm, pool),
                (hb_hbm, hb.at[0]),
            )
        )
    ]
    for d in loads:
        d.start()

    barrier = pltpu.get_barrier_semaphore()
    for who in (sib, xp, xm, zp, zm, up, dn, across):
        pl.semaphore_signal(barrier, inc=1, device_id=who, device_id_type=MESH)

    @pl.when(odd == 0)
    def _():
        pl.semaphore_signal(barrier, inc=1, device_id=y_up, device_id_type=MESH)

    @pl.when(odd == 1)
    def _():
        pl.semaphore_signal(barrier, inc=1, device_id=y_dn, device_id_type=MESH)

    pl.semaphore_wait(barrier, 9)
    for d in loads:
        d.wait()

    def copy(src, dst, send, recv, who):
        return pltpu.make_async_remote_copy(
            src_ref=src, dst_ref=dst, send_sem=send, recv_sem=recv, device_id=who, device_id_type=MESH
        )

    def part(ref, h):
        return ref.at[pl.ds(HALF * h, HALF), :]

    def send_x(k, src, h):
        @pl.when(jnp.logical_and(k <= 3 - j, j >= 1))
        def _():
            copy(part(src, h), part(xbuf.at[k + 1], h), x_s.at[k, h], x_r.at[k + 1, h], dn).start()

        @pl.when(jnp.logical_and(k > 3 - j, j <= 2))
        def _():
            copy(part(src, h), part(xbuf.at[k - 1], h), x_s.at[k, h], x_r.at[k - 1, h], up).start()

    def send_p(k, src, h):
        if k < 4:
          @pl.when(jnp.logical_and(k <= j, j <= 1))
          def _():
            copy(part(src, h), part(pbuf.at[PLACE[k + 1]], h), p_s.at[k, h], p_r.at[k + 1, h], up).start()

        if k > 2:
          @pl.when(jnp.logical_and(k > j, j >= 2))
          def _():
            copy(part(src, h), part(pbuf.at[PLACE[k - 1]], h), p_s.at[k, h], p_r.at[k - 1, h], dn).start()

    def wait_x(k, h, whole=False):
        dst = xbuf.at[k] if whole else part(xbuf.at[k], h)
        copy(dst, dst, x_s.at[k, h], x_r.at[k, h], up).wait_recv()

    def quarter(k, q):
        return xbuf.at[k, pl.ds(HALF // 2 * q, HALF // 2), :]

    hop_in = [copy(quarter(4, q), quarter(4, q), x_s.at[5, q], x_r.at[4, q], zm) for q in range(4)]
    hop_up = [copy(quarter(4, q), quarter(3, q), x_s.at[4, q], x_r.at[3, q // 2], up) for q in range(4)]

    def wait_p(k, h):
        dst = part(pbuf.at[PLACE[k]], h)
        copy(dst, dst, p_s.at[k, h], p_r.at[k, h], up).wait_recv()

    def pass_x(k, h):
        wait_x(k, h)
        send_x(k, xbuf.at[k], h)

    def pass_p(k):
        for h in range(2):
            wait_p(k, h)
            send_p(k, pbuf.at[PLACE[k]], h)

    def x_done(k, src):
        @pl.when(jnp.logical_or(jnp.logical_and(k <= 3 - j, j >= 1), jnp.logical_and(k > 3 - j, j <= 2)))
        def _():
            for h in range(2):
                copy(part(src, h), part(xbuf.at[1], h), x_s.at[k, h], x_r.at[1, h], up).wait_send()

    def p_done(k, src):
        @pl.when(jnp.logical_or(jnp.logical_and(k <= j, j <= 1), jnp.logical_and(k > j, j >= 2)))
        def _():
            for h in range(2):
                copy(part(src, h), part(pbuf.at[0], h), p_s.at[k, h], p_r.at[1, h], up).wait_send()

    middle = lax.rem(lax.div(j + 1, 2), 2)
    outer = middle == 0
    inner = middle == 1
    xk0 = 1 + 2 * lax.div(j, 3)
    xk1 = 2 + middle
    xk2 = 6 - xk0 - xk1
    guest = copy(img, xbuf.at[5], x_s.at[6, 0], x_r.at[5, 0], up)

    pool_swap = copy(pool, psib, h_s.at[2], h_r.at[2], sib)
    x_hop = [
        copy(img.at[pl.ds(HALF // 2 * q, HALF // 2), :], quarter(4, q), x_s.at[5, q], x_r.at[4, q], zm)
        for q in range(4)
    ]
    p_hop = [copy(part(pool, h), part(pbuf.at[PLACE[4]], h), p_s.at[5, h], p_r.at[4, h], zp) for h in range(2)]

    @pl.when(j <= 2)
    def _():
        for d in x_hop:
            d.start()

    send_x(0, img, 0)
    send_x(0, img, 1)

    def chip(h, off):
        return h * 4 + lax.rem(x + off, 4)

    def piece(m, p):
        return (wa if p == 0 else wb).at[c, m]

    def w_copy(src, dst, ident, who, send=None):
        return copy(src, dst, w_s.at[ident if send is None else send], w_r.at[ident], who)

    w_sent = []

    def w_go(src, ident, who):
        d = w_copy(src, src, ident, who)
        d.start()
        w_sent.append(d)

    def to_sibling(n, m, p):
        w_go(piece(m, p), 17 + 2 * n + p, sib)

    def assemble(n, m):
        for p in range(2):
            src = (wa if p == 0 else wb).at[1 - c, m]
            w_copy(src, src, 17 + 2 * n + p, sib).wait_recv()
        rows = pl.ds(pl.multiple_of(m * CHIP, 16), CHIP)
        for ref, cols in ((wa, slice(0, FIRST)), (wb, slice(FIRST, WIDTH))):
            wf[rows, cols] = jnp.concatenate(
                [ref[0, m].astype(F32), ref[1, m].astype(F32)], axis=0
            ).astype(BF16)

    edge_up = [w_copy(piece(mine, p), piece(mine, p), 13 + p, up) for p in range(2)]
    edge_dn = [w_copy(piece(mine, p), piece(mine, p), 13 + p, dn) for p in range(2)]
    edge_far = [w_copy(piece(mine, p), piece(mine, p), 13 + p, across, 15 + p) for p in range(2)]

    @pl.when(j == 3)
    def _():
        for d in edge_up:
            d.start()

    @pl.when(j == 0)
    def _():
        for d in edge_dn:
            d.start()

    @pl.when(outer)
    def _():
        for d in edge_far:
            d.start()

    def along_x(r, m):
        return {
            (d, p): w_copy(piece(m, p), piece(m, p), 1 + 4 * r + 2 * d + p, xp if d == 0 else xm)
            for d in range(2)
            for p in range(2)
        }

    mine_x = along_x(0, mine)
    theirs_x = along_x(1, theirs)
    for key in ((0, 0), (1, 1), (0, 1), (1, 0)):
        mine_x[key].start()
    w_sent.extend(mine_x.values())
    w_sent.extend(theirs_x.values())
    to_sibling(0, mine, 0)
    to_sibling(0, mine, 1)
    pool_swap.start()

    @pl.when(j == 1)
    def _():
        send_p(0, pool, 0)

    @pl.when(j >= 1)
    def _():
        for d in p_hop:
            d.start()

    v, xr = normalize(img[...].astype(F32))
    ximg[...] = v
    xb[0] = v.astype(BF16)

    def slab_rows(n):
        m = chip(1 - yh if n < 4 else yh, ORDER[n % 4])
        return ptf[pl.ds(pl.multiple_of(m * CHIP + SHARD * c, 8), SHARD), :]

    def transpose_into(ref, start):
        ptf[...] = ref[...].astype(F32).T
        for n in range(0, 8, 2):
            pt[SHARD * n:SHARD * (n + 2), start:start + ROWS] = jnp.concatenate(
                [slab_rows(n), slab_rows(n + 1)], axis=0
            ).astype(BF16)

    def near_first(r, h):
        for d, (off, onward) in enumerate(((3, xp), (1, xm))):
            got = piece(chip(h, off), d)
            w_copy(got, got, 1 + 4 * r + 3 * d, xp).wait_recv()
            w_go(got, 9 + 2 * r + d, onward)
            to_sibling(1 + 4 * r + d, chip(h, off), d)

    def near_rest(r, h):
        for d, off in enumerate((3, 1)):
            m = chip(h, off)
            got = piece(m, 1 - d)
            w_copy(got, got, 2 + 4 * r + d, xp).wait_recv()
            to_sibling(1 + 4 * r + d, m, 1 - d)

    def far_units(r, h):
        m = chip(h, 2)
        for p in range(2):
            w_copy(piece(m, p), piece(m, p), 9 + 2 * r + p, xp).wait_recv()
            to_sibling(3 + 4 * r, m, p)

    edge_in = [w_copy(piece(theirs, p), piece(theirs, p), 13 + p, xp) for p in range(2)]

    def theirs_first():
        edge_in[0].wait_recv()
        theirs_x[0, 0].start()
        theirs_sib[0].start()

    def theirs_rest():
        edge_in[1].wait_recv()
        for key in ((1, 1), (0, 1), (1, 0)):
            theirs_x[key].start()
        theirs_sib[1].start()

    theirs_sib = [w_copy(piece(theirs, p), piece(theirs, p), 25 + p, sib) for p in range(2)]
    w_sent.extend(theirs_sib)

    def hop_on(h):
        @pl.when(j <= 2)
        def _():
            for q in (2 * h, 2 * h + 1):
                hop_in[q].wait_recv()
                hop_up[q].start()

        @pl.when(inner)
        def _():
            pass_x(1, h)

    hop_on(0)
    transpose_into(pool, 0)

    @pl.when(outer)
    def _():
        theirs_first()

    near_first(0, yh)

    @pl.when(outer)
    def _():
        theirs_rest()

    hop_on(1)
    near_rest(0, yh)
    pool_swap.wait_recv()
    transpose_into(psib, ROWS)

    @pl.when(j == 0)
    def _():
        send_p(0, pool, 0)
        send_p(0, pool, 1)
        guest.start()

    @pl.when(j == 3)
    def _():
        pass_p(4)

    @pl.when(inner)
    def _():
        pass_x(3, 0)
        theirs_first()

    far_units(0, yh)
    assemble(0, mine)

    @pl.when(inner)
    def _():
        pass_x(3, 1)
        theirs_rest()
        pass_x(2, 0)

    @pl.when(j == 2)
    def _():
        pass_p(4)

    @pl.when(j == 1)
    def _():
        pass_x(2, 1)

    near_first(1, 1 - yh)
    for n, off in ((1, 3), (2, 1), (3, 2)):
        assemble(n, chip(yh, off))

    @pl.when(j == 2)
    def _():
        pass_x(2, 1)

    @pl.when(j == 1)
    def _():
        send_p(0, pool, 1)

    near_rest(1, 1 - yh)

    @pl.when(j == 1)
    def _():
        pass_p(1)

    @pl.when(j == 2)
    def _():
        pass_p(3)

    far_units(1, 1 - yh)

    def ready(k):
        xb[k] = normalize(xbuf[k].astype(F32))[0].astype(BF16)

    @pl.when(inner)
    def _():
        for k in range(1, 4):
            ready(k)

    assemble(4, theirs)
    for n, off in ((5, 3), (6, 1), (7, 2)):
        assemble(n, chip(1 - yh, off))

    temper = jnp.exp(jnp.full((1, 1), log_scale[0], F32))
    offset = jnp.full((1, 1), bias[0], F32)
    gain = temper * (1.0 / ROWS)

    def project(block, out):
        for start in range(0, WIDTH, 512):
            cols = pl.ds(start, min(512, WIDTH - start))
            out[:, cols] = jnp.dot(block, wf[:, cols], preferred_element_type=F32) + hb[:, cols]

    def weights(a, b, own):
        l = temper * lax.dot_general(a, b, NT, preferred_element_type=F32) + offset
        if own:
            eye = lax.broadcasted_iota(jnp.int32, l.shape, 0) == lax.broadcasted_iota(jnp.int32, l.shape, 1)
            l = jnp.where(eye, -l, l)
        g = gain / (1.0 + jnp.exp(-l))
        if own:
            g = jnp.where(eye, -g, g)
        return l, g.astype(BF16)

    def losses(m):
        e = jnp.maximum(m, 0.0) + jnp.log1p(jnp.exp(-jnp.abs(m)))
        total = e[:, :ROWS]
        for start in range(ROWS, m.shape[1], ROWS):
            total = total + e[:, start:start + ROWS]
        return jnp.sum(total.T, axis=0, keepdims=True)

    def image_side(d, row):
        loss_out[...] = row * (1.0 / ROWS)
        v = ximg[...]
        img_out[...] = (xr * (d - v * jnp.sum(v * d, axis=-1, keepdims=True))).astype(BF16)

    project(pool[...], ztxt)
    v, zr = normalize(ztxt[...])
    ztxt[...] = v
    zb[0] = v.astype(BF16)

    def text_grad(a, own):
        _, g = weights(zb[0], a, own)
        return jnp.dot(g, a, preferred_element_type=F32)

    def text_side(d):
        v = ztxt[...]
        dzb[:ROWS] = (zr * (d - v * jnp.sum(v * d, axis=-1, keepdims=True))).astype(BF16)

    @pl.when(inner)
    def _():
        text_side(text_grad(xb[0:4].reshape(4 * ROWS, WIDTH), True))

    @pl.when(outer)
    def _():
        for k in (xk0, xk1):
            wait_x(k, 0)
            wait_x(k, 1)
            ready(k)
        u[:ROWS] = text_grad(xb[0], True) + text_grad(xb[xk0], False) + text_grad(xb[xk1], False)
        wait_x(xk2, 0)
        wait_x(xk2, 1)
        ready(xk2)
        text_side(u[:ROWS] + text_grad(xb[xk2], False))

    pair = copy(dzb.at[:ROWS], dzb.at[ROWS:], h_s.at[3], h_r.at[3], sib)
    pair.start()

    def make(n):
        t = jnp.dot(pt[SHARD * n:SHARD * (n + 2), :], dzb[...], preferred_element_type=F32)
        terms[n] = t[:SHARD]
        terms[n + 1] = t[SHARD:]

    def cols(n, q):
        start, size, _ = PIECES[q]
        return terms[n, :, start:start + size]

    g_sent = []

    def g_go(src, value, ident, dst, who):
        src[...] = value.astype(BF16)
        d = copy(src, dst, g_s.at[ident], g_r.at[ident], who)
        d.start()
        g_sent.append(d)

    def g_wait(ref, ident):
        copy(ref, ref, g_s.at[ident], g_r.at[ident], xp).wait_recv()
        return ref[...].astype(F32)

    def slot(refs, q, *index):
        return refs[q].at[index] if index else refs[q]

    def far_sends(g):
        for q, (_, _, way) in enumerate(PIECES):
            g_go(slot(g_out, q, g, 0), cols(4 * g, q), 12 * g + q, slot(g_far, q, g), xp if way > 0 else xm)

    def near_sends(g):
        for q, (_, _, way) in enumerate(PIECES):
            n, who = (2, xm) if way > 0 else (1, xp)
            g_go(slot(g_out, q, g, 1), cols(4 * g + n, q), 12 * g + 4 + q, slot(g_near, q, g, 0), who)

    def second_sends(g):
        for q, (_, _, way) in enumerate(PIECES):
            n, who = (1, xp) if way > 0 else (2, xm)
            value = cols(4 * g + n, q) + g_wait(slot(g_far, q, g), 12 * g + q)
            g_go(slot(g_out, q, g, 2), value, 12 * g + 8 + q, slot(g_near, q, g, 1), who)

    def total(g, q):
        value = cols(4 * g + 3, q) + g_wait(slot(g_near, q, g, 0), 12 * g + 4 + q)
        return value + g_wait(slot(g_near, q, g, 1), 12 * g + 8 + q)

    def back():
        @pl.loop(0, WIDTH // TILE)
        def _(n):
            cols = pl.ds(pl.multiple_of(n * TILE, TILE), TILE)
            pool_out[:, cols] = lax.dot_general(
                dzb[:ROWS], wf[cols, :], NT, preferred_element_type=F32
            ).astype(BF16)

    gdx_up = [copy(part(gdx_out, h), part(gdx_in, h), h_s.at[4 * h], h_r.at[4 * h], up) for h in range(2)]
    gdx_dn = [copy(part(gdx_out, h), part(gdx_in, h), h_s.at[4 * h], h_r.at[4 * h], dn) for h in range(2)]
    gsum_up = copy(gsum_out, gsum_in, h_s.at[1], h_r.at[1], up)
    gsum_dn = copy(gsum_out, gsum_in, h_s.at[1], h_r.at[1], dn)

    @pl.when(outer)
    def _():
        m, g = weights(xb[0], zb[0], True)
        u[ROWS:2 * ROWS] = jnp.dot(g, zb[0], preferred_element_type=F32)
        loss_out[...] = losses(m)

    def texts_done(first, last):
        for n in range(first, last):
            v = u[ROWS * (n - 1):ROWS * n]
            zb[n] = normalize(v)[0].astype(BF16)

    def meet(image, texts, own):
        m, g = weights(image, texts, own)
        return jnp.dot(g, texts, preferred_element_type=F32), losses(m)

    @pl.when(inner)
    def _():
        back()

    pair.wait_recv()
    make(0)
    far_sends(0)
    make(2)
    near_sends(0)

    @pl.when(j == 1)
    def _():
        for h in range(2):
            wait_p(3, h)
            wait_p(4, h)

    @pl.when(j == 2)
    def _():
        for h in range(2):
            wait_p(1, h)

    @pl.when(inner)
    def _():
        project(pbuf[0:3].reshape(3 * ROWS, WIDTH), u.at[:3 * ROWS])

    @pl.when(outer)
    def _():
        make(4)
        make(6)
        back()

    second_sends(0)

    @pl.when(inner)
    def _():
        make(4)
        make(6)

    far_sends(1)
    near_sends(1)

    @pl.when(j == 1)
    def _():
        wait_x(5, 0, whole=True)
        ready(5)

    @pl.when(inner)
    def _():
        texts_done(1, 4)
        d, row = meet(xb[9 - 4 * j], zb[pl.ds(4 - 2 * j, 2)].reshape(2 * ROWS, WIDTH), False)
        gdx[...] = d
        gsum_out[...] = row

    for q, (_, _, way) in enumerate(PIECES):
        g_go(slot(y_out, q), total(0, q), 24 + q, slot(y_pass, q), y_up if way > 0 else y_dn)

    onward = [
        copy(slot(y_pass, q), slot(y_in, q), g_s.at[28 + q], g_r.at[28 + q], y_up if way > 0 else y_dn)
        for q, (_, _, way) in enumerate(PIECES)
    ]

    def relay():
        for q in range(4):
            copy(slot(y_pass, q), slot(y_pass, q), g_s.at[24 + q], g_r.at[24 + q], xp).wait_recv()
            onward[q].start()

    second_sends(1)

    @pl.when(inner)
    def _():
        for h in range(2):
            wait_p(2, h)
        project(pbuf[3], u.at[3 * ROWS:])
        texts_done(4, 5)
        d, row = meet(xb[9 - 4 * j], zb[4], False)
        gdx_out[...] = (gdx[...] + d).astype(BF16)
        gsum_out[...] += row

    @pl.when(j == 1)
    def _():
        gsum_dn.start()
        gdx_dn[0].start()

    @pl.when(j == 2)
    def _():
        gsum_up.start()
        gdx_up[0].start()

    relay()

    @pl.when(j == 1)
    def _():
        gdx_dn[1].start()

    @pl.when(j == 2)
    def _():
        gdx_up[1].start()

    @pl.when(inner)
    def _():
        d, row = meet(xb[0], zb[0:3].reshape(3 * ROWS, WIDTH), True)
        e, more = meet(xb[0], zb[4], False)
        image_side(d + e, row + more)

    for d in w_sent:
        d.wait_send()

    @pl.when(j == 3)
    def _():
        for d in edge_up:
            d.wait_send()

    @pl.when(j == 0)
    def _():
        for d in edge_dn:
            d.wait_send()

    @pl.when(outer)
    def _():
        for d in edge_far:
            d.wait_send()

    @pl.when(j <= 2)
    def _():
        for d in x_hop + hop_up:
            d.wait_send()

    @pl.when(j >= 1)
    def _():
        for d in p_hop:
            d.wait_send()

    @pl.when(j == 0)
    def _():
        guest.wait_send()

    x_done(0, img)
    p_done(0, pool)
    for k in range(1, 4):
        x_done(k, xbuf.at[k])
        p_done(k, pbuf.at[0])
    p_done(4, pbuf.at[0])
    pool_swap.wait_send()
    pair.wait_send()
    for d in g_sent[:24]:
        d.wait_send()


    for q, (start, size, _) in enumerate(PIECES):
        head_out[:, start:start + size] = total(1, q)

    @pl.when(outer)
    def _():
        gsum_up.wait_recv()
        gdx_up[0].wait_recv()
        gdx_up[1].wait_recv()
        image_side(u[ROWS:2 * ROWS] + gdx_in[...].astype(F32), loss_out[...] + gsum_in[...])

    for q, (start, size, _) in enumerate(PIECES):
        head_out[:, start:start + size] += g_wait(slot(y_in, q), 28 + q)

    @pl.when(inner)
    def _():
        gdx_up[0].wait_send()
        gdx_up[1].wait_send()
        gsum_up.wait_send()

    for d in g_sent[24:] + onward:
        d.wait_send()


def finish(*refs):
    moves = [pltpu.make_async_copy(refs[i], refs[4 + i], refs[8].at[i]) for i in range(4)]
    for d in moves:
        d.start()
    for d in moves:
        d.wait()


def per_device(images, pooled, head_weight, head_bias, log_scale, bias):
    smem = pl.BlockSpec(memory_space=pltpu.SMEM)
    vmem = pl.BlockSpec(memory_space=pltpu.VMEM)
    hbm = pl.BlockSpec(memory_space=pltpu.HBM)
    block = (ROWS, WIDTH)
    slab = (SHARD, WIDTH)
    parts = [(SHARD, size) for _, size, _ in PIECES]
    dma = pltpu.SemaphoreType.DMA
    results = (
        jax.ShapeDtypeStruct((1, ROWS), F32),
        jax.ShapeDtypeStruct(block, BF16),
        jax.ShapeDtypeStruct(block, BF16),
        jax.ShapeDtypeStruct(slab, F32),
    )
    made = pl.pallas_call(
        kernel,
        out_shape=results,
        in_specs=[hbm, hbm, hbm, hbm, smem, smem],
        out_specs=(vmem,) * 4,
        scratch_shapes=[
            pltpu.VMEM(block, BF16),
            pltpu.VMEM(block, BF16),
            pltpu.VMEM((1, WIDTH), F32),
            pltpu.VMEM((2, 8, SHARD, FIRST), BF16),
            pltpu.VMEM((2, 8, SHARD, WIDTH - FIRST), BF16),
            pltpu.VMEM((WIDTH, WIDTH), BF16),
            pltpu.VMEM((6,) + block, BF16),
            pltpu.VMEM((4,) + block, BF16),
            pltpu.VMEM((6,) + block, BF16),
            pltpu.VMEM((5,) + block, BF16),
            pltpu.VMEM(block, F32),
            pltpu.VMEM(block, F32),
            pltpu.VMEM((4 * ROWS, WIDTH), F32),
            pltpu.VMEM((2 * ROWS, WIDTH), BF16),
            pltpu.VMEM(block, BF16),
            pltpu.VMEM((WIDTH, ROWS), F32),
            pltpu.VMEM((8 * SHARD, 2 * ROWS), BF16),
            pltpu.VMEM((8,) + slab, F32),
            [pltpu.VMEM((2, 3) + p, BF16) for p in parts],
            [pltpu.VMEM((2,) + p, BF16) for p in parts],
            [pltpu.VMEM((2, 2) + p, BF16) for p in parts],
            [pltpu.VMEM(p, BF16) for p in parts],
            [pltpu.VMEM(p, BF16) for p in parts],
            [pltpu.VMEM(p, BF16) for p in parts],
            pltpu.VMEM(block, F32),
            pltpu.VMEM(block, BF16),
            pltpu.VMEM((1, ROWS), F32),
            pltpu.VMEM(block, BF16),
            pltpu.VMEM((1, ROWS), F32),
            dma((5,)),
            dma((33,)), dma((33,)),
            dma((7, 4)), dma((6, 4)),
            dma((6, 2)), dma((5, 2)),
            dma((32,)), dma((32,)),
            dma((5,)), dma((5,)),
        ],
        compiler_params=pltpu.CompilerParams(
            collective_id=0, has_side_effects=True, vmem_limit_bytes=VMEM_GRANT
        ),
        cost_estimate=pl.CostEstimate(flops=4_000_000_000, bytes_accessed=6_000_000, transcendentals=300_000),
    )(*[pltpu.with_memory_space_constraint(v, pltpu.HBM) for v in (images, pooled, head_weight, head_bias)], log_scale, bias)
    loss, image_grad, pooled_grad, head_grad = pl.pallas_call(
        finish,
        out_shape=results,
        in_specs=[vmem] * 4,
        out_specs=(hbm,) * 4,
        scratch_shapes=[dma((4,))],
        compiler_params=pltpu.CompilerParams(vmem_limit_bytes=4 * 1024 * 1024),
    )(*made)
    return loss.reshape(ROWS), image_grad, pooled_grad, head_grad


def solution(mesh):
    in_specs = (P(("dp", "fsdp"), None), P(("dp", "fsdp"), None), P("fsdp", None), P(), P(), P())
    out_specs = (
        P(("dp", "fsdp")),
        P(("dp", "fsdp"), None),
        P(("dp", "fsdp"), None),
        P(("dp", "fsdp"), None),
    )
    return jax.shard_map(
        per_device, mesh=mesh, in_specs=in_specs, out_specs=out_specs, check_vma=False
    )
```

```python
import jax
import jax.numpy as jnp
from jax import lax
from jax.experimental import pallas as pl
from jax.experimental.pallas import tpu as pltpu
from jax.sharding import PartitionSpec as P

MESH = pl.DeviceIdType.MESH
F32 = jnp.float32
BF16 = jnp.bfloat16
NT = (((1,), (1,)), ((), ()))

ROWS = 128
WIDTH = 1152
SHARD = 72
CHIP = 144
FIRST = 640
TILE = 384
VMEM_GRANT = 44 * 1024 * 1024
HALF = 64
PIECES = ((0, 384, 1), (640, 256, -1), (384, 256, 1), (896, 256, -1))
PLACE = {1: 0, 3: 1, 4: 2, 2: 3}
ORDER = (2, 1, 3, 0)


def normalize(v):
    r = lax.rsqrt(jnp.sum(v * v, axis=-1, keepdims=True) + 1e-06)
    return v * r, r


def kernel(
    img_hbm, pool_hbm, wsh_hbm, hb_hbm, log_scale, bias,
    loss_out, img_out, pool_out, head_out,
    img, pool, hb,
    wa, wb, wf, xbuf, pbuf, xb, zb, ximg, ztxt, u, dzb, psib, ptf, pt, terms,
    g_out, g_far, g_near,
    y_out, y_pass, y_in,
    gdx, gdx_out, gsum_out, gdx_in, gsum_in,
    l_s, w_s, w_r, x_s, x_r, p_s, p_r, g_s, g_r, h_s, h_r,
):
    dp = lax.axis_index("dp")
    f = lax.axis_index("fsdp")
    j = lax.rem(dp, 4)
    yh = lax.div(f, 8)
    x = lax.rem(lax.div(f, 2), 4)
    c = lax.rem(f, 2)
    base = yh * 8 + c

    sib = (dp, f + 1 - 2 * c)
    xp = (dp, base + 2 * lax.rem(x + 1, 4))
    xm = (dp, base + 2 * lax.rem(x + 3, 4))
    zp = (lax.rem(dp + 4, 32), f)
    zm = (lax.rem(dp + 28, 32), f)
    wrap_up = lax.div(j + 1, 4)
    up = (dp + 1 - 4 * wrap_up, lax.rem(f + 8 * wrap_up, 16))
    wrap_dn = lax.div(3 - j, 3)
    dn = (dp - 1 + 4 * wrap_dn, lax.rem(f + 8 * wrap_dn, 16))
    odd = lax.rem(j, 2)
    step = 3 - 2 * odd
    wrap = lax.div(j + step, 4)
    y_up = (dp + step - 4 * wrap, lax.rem(f + 8 * wrap, 16))
    step = 1 + 2 * odd
    wrap = lax.div(3 - j, 2)
    y_dn = (dp - step + 4 * wrap, lax.rem(f + 8 * wrap, 16))

    across = (dp - j + lax.rem(j + 2, 4), lax.rem(f + 8, 16))
    mine = yh * 4 + x
    theirs = 4 - yh * 4 + x

    loads = [
        pltpu.make_async_copy(src, dst, l_s.at[i])
        for i, (src, dst) in enumerate(
            (
                (wsh_hbm.at[:, :FIRST], wa.at[c, mine]),
                (wsh_hbm.at[:, FIRST:], wb.at[c, mine]),
                (img_hbm, img),
                (pool_hbm, pool),
                (hb_hbm, hb.at[0]),
            )
        )
    ]
    for d in loads:
        d.start()

    barrier = pltpu.get_barrier_semaphore()
    for who in (sib, xp, xm, zp, zm, up, dn, across):
        pl.semaphore_signal(barrier, inc=1, device_id=who, device_id_type=MESH)

    @pl.when(odd == 0)
    def _():
        pl.semaphore_signal(barrier, inc=1, device_id=y_up, device_id_type=MESH)

    @pl.when(odd == 1)
    def _():
        pl.semaphore_signal(barrier, inc=1, device_id=y_dn, device_id_type=MESH)

    pl.semaphore_wait(barrier, 9)
    for d in loads:
        d.wait()

    def copy(src, dst, send, recv, who):
        return pltpu.make_async_remote_copy(
            src_ref=src, dst_ref=dst, send_sem=send, recv_sem=recv, device_id=who, device_id_type=MESH
        )

    def part(ref, h):
        return ref.at[pl.ds(HALF * h, HALF), :]

    def send_x(k, src, h):
        @pl.when(jnp.logical_and(k <= 3 - j, j >= 1))
        def _():
            copy(part(src, h), part(xbuf.at[k + 1], h), x_s.at[k, h], x_r.at[k + 1, h], dn).start()

        @pl.when(jnp.logical_and(k > 3 - j, j <= 2))
        def _():
            copy(part(src, h), part(xbuf.at[k - 1], h), x_s.at[k, h], x_r.at[k - 1, h], up).start()

    def send_p(k, src, h):
        if k < 4:
          @pl.when(jnp.logical_and(k <= j, j <= 1))
          def _():
            copy(part(src, h), part(pbuf.at[PLACE[k + 1]], h), p_s.at[k, h], p_r.at[k + 1, h], up).start()

        if k > 2:
          @pl.when(jnp.logical_and(k > j, j >= 2))
          def _():
            copy(part(src, h), part(pbuf.at[PLACE[k - 1]], h), p_s.at[k, h], p_r.at[k - 1, h], dn).start()

    def wait_x(k, h, whole=False):
        dst = xbuf.at[k] if whole else part(xbuf.at[k], h)
        copy(dst, dst, x_s.at[k, h], x_r.at[k, h], up).wait_recv()

    def quarter(k, q):
        return xbuf.at[k, pl.ds(HALF // 2 * q, HALF // 2), :]

    hop_in = [copy(quarter(4, q), quarter(4, q), x_s.at[5, q], x_r.at[4, q], zm) for q in range(4)]
    hop_up = [copy(quarter(4, q), quarter(3, q), x_s.at[4, q], x_r.at[3, q // 2], up) for q in range(4)]

    def wait_p(k, h):
        dst = part(pbuf.at[PLACE[k]], h)
        copy(dst, dst, p_s.at[k, h], p_r.at[k, h], up).wait_recv()

    def pass_x(k, h):
        wait_x(k, h)
        send_x(k, xbuf.at[k], h)

    def pass_p(k):
        for h in range(2):
            wait_p(k, h)
            send_p(k, pbuf.at[PLACE[k]], h)

    def x_done(k, src):
        @pl.when(jnp.logical_or(jnp.logical_and(k <= 3 - j, j >= 1), jnp.logical_and(k > 3 - j, j <= 2)))
        def _():
            for h in range(2):
                copy(part(src, h), part(xbuf.at[1], h), x_s.at[k, h], x_r.at[1, h], up).wait_send()

    def p_done(k, src):
        @pl.when(jnp.logical_or(jnp.logical_and(k <= j, j <= 1), jnp.logical_and(k > j, j >= 2)))
        def _():
            for h in range(2):
                copy(part(src, h), part(pbuf.at[0], h), p_s.at[k, h], p_r.at[1, h], up).wait_send()

    middle = lax.rem(lax.div(j + 1, 2), 2)
    outer = middle == 0
    inner = middle == 1
    xk0 = 1 + 2 * lax.div(j, 3)
    xk1 = 2 + middle
    xk2 = 6 - xk0 - xk1
    guest = copy(img, xbuf.at[5], x_s.at[6, 0], x_r.at[5, 0], up)

    pool_swap = copy(pool, psib, h_s.at[2], h_r.at[2], sib)
    x_hop = [
        copy(img.at[pl.ds(HALF // 2 * q, HALF // 2), :], quarter(4, q), x_s.at[5, q], x_r.at[4, q], zm)
        for q in range(4)
    ]
    p_hop = [copy(part(pool, h), part(pbuf.at[PLACE[4]], h), p_s.at[5, h], p_r.at[4, h], zp) for h in range(2)]

    @pl.when(j <= 2)
    def _():
        for d in x_hop:
            d.start()

    send_x(0, img, 0)
    send_x(0, img, 1)

    def chip(h, off):
        return h * 4 + lax.rem(x + off, 4)

    def piece(m, p):
        return (wa if p == 0 else wb).at[c, m]

    def w_copy(src, dst, ident, who, send=None):
        return copy(src, dst, w_s.at[ident if send is None else send], w_r.at[ident], who)

    w_sent = []

    def w_go(src, ident, who):
        d = w_copy(src, src, ident, who)
        d.start()
        w_sent.append(d)

    def to_sibling(n, m, p):
        w_go(piece(m, p), 17 + 2 * n + p, sib)

    def assemble(n, m):
        for p in range(2):
            src = (wa if p == 0 else wb).at[1 - c, m]
            w_copy(src, src, 17 + 2 * n + p, sib).wait_recv()
        rows = pl.ds(pl.multiple_of(m * CHIP, 16), CHIP)
        for ref, cols in ((wa, slice(0, FIRST)), (wb, slice(FIRST, WIDTH))):
            wf[rows, cols] = jnp.concatenate(
                [ref[0, m].astype(F32), ref[1, m].astype(F32)], axis=0
            ).astype(BF16)

    edge_up = [w_copy(piece(mine, p), piece(mine, p), 13 + p, up) for p in range(2)]
    edge_dn = [w_copy(piece(mine, p), piece(mine, p), 13 + p, dn) for p in range(2)]
    edge_far = [w_copy(piece(mine, p), piece(mine, p), 13 + p, across, 15 + p) for p in range(2)]

    @pl.when(j == 3)
    def _():
        for d in edge_up:
            d.start()

    @pl.when(j == 0)
    def _():
        for d in edge_dn:
            d.start()

    @pl.when(outer)
    def _():
        for d in edge_far:
            d.start()

    def along_x(r, m):
        return {
            (d, p): w_copy(piece(m, p), piece(m, p), 1 + 4 * r + 2 * d + p, xp if d == 0 else xm)
            for d in range(2)
            for p in range(2)
        }

    mine_x = along_x(0, mine)
    theirs_x = along_x(1, theirs)
    for key in ((0, 0), (1, 1), (0, 1), (1, 0)):
        mine_x[key].start()
    w_sent.extend(mine_x.values())
    w_sent.extend(theirs_x.values())
    to_sibling(0, mine, 0)
    to_sibling(0, mine, 1)
    pool_swap.start()

    @pl.when(j == 1)
    def _():
        send_p(0, pool, 0)

    @pl.when(j >= 1)
    def _():
        for d in p_hop:
            d.start()

    v, xr = normalize(img[...].astype(F32))
    ximg[...] = v
    xb[0] = v.astype(BF16)

    def slab_rows(n):
        m = chip(1 - yh if n < 4 else yh, ORDER[n % 4])
        return ptf[pl.ds(pl.multiple_of(m * CHIP + SHARD * c, 8), SHARD), :]

    def transpose_into(ref, start):
        ptf[...] = ref[...].astype(F32).T
        for n in range(0, 8, 2):
            pt[SHARD * n:SHARD * (n + 2), start:start + ROWS] = jnp.concatenate(
                [slab_rows(n), slab_rows(n + 1)], axis=0
            ).astype(BF16)

    def near_first(r, h):
        for d, (off, onward) in enumerate(((3, xp), (1, xm))):
            got = piece(chip(h, off), d)
            w_copy(got, got, 1 + 4 * r + 3 * d, xp).wait_recv()
            w_go(got, 9 + 2 * r + d, onward)
            to_sibling(1 + 4 * r + d, chip(h, off), d)

    def near_rest(r, h):
        for d, off in enumerate((3, 1)):
            m = chip(h, off)
            got = piece(m, 1 - d)
            w_copy(got, got, 2 + 4 * r + d, xp).wait_recv()
            to_sibling(1 + 4 * r + d, m, 1 - d)

    def far_units(r, h):
        m = chip(h, 2)
        for p in range(2):
            w_copy(piece(m, p), piece(m, p), 9 + 2 * r + p, xp).wait_recv()
            to_sibling(3 + 4 * r, m, p)

    edge_in = [w_copy(piece(theirs, p), piece(theirs, p), 13 + p, xp) for p in range(2)]

    def theirs_first():
        edge_in[0].wait_recv()
        theirs_x[0, 0].start()
        theirs_sib[0].start()

    def theirs_rest():
        edge_in[1].wait_recv()
        for key in ((1, 1), (0, 1), (1, 0)):
            theirs_x[key].start()
        theirs_sib[1].start()

    theirs_sib = [w_copy(piece(theirs, p), piece(theirs, p), 25 + p, sib) for p in range(2)]
    w_sent.extend(theirs_sib)

    def hop_on(h, quarters):
        @pl.when(j <= 2)
        def _():
            for q in quarters:
                hop_in[q].wait_recv()
                hop_up[q].start()

        if h is None:
            return

        @pl.when(inner)
        def _():
            pass_x(1, h)

    hop_on(0, (0, 1))
    transpose_into(pool, 0)

    @pl.when(outer)
    def _():
        theirs_first()

    hop_on(None, (2,))
    near_first(0, yh)

    @pl.when(outer)
    def _():
        theirs_rest()

    hop_on(1, (3,))
    near_rest(0, yh)

    @pl.when(j == 0)
    def _():
        send_p(0, pool, 0)
        send_p(0, pool, 1)
        guest.start()

    @pl.when(j == 3)
    def _():
        pass_p(4)

    @pl.when(inner)
    def _():
        pass_x(3, 0)
        theirs_first()

    far_units(0, yh)
    assemble(0, mine)

    @pl.when(inner)
    def _():
        pass_x(3, 1)
        theirs_rest()
        pass_x(2, 0)

    @pl.when(j == 2)
    def _():
        pass_p(4)

    @pl.when(j == 1)
    def _():
        pass_x(2, 1)

    near_first(1, 1 - yh)
    for n, off in ((1, 3), (2, 1), (3, 2)):
        assemble(n, chip(yh, off))

    @pl.when(j == 2)
    def _():
        pass_x(2, 1)

    @pl.when(j == 1)
    def _():
        send_p(0, pool, 1)

    near_rest(1, 1 - yh)

    @pl.when(j == 1)
    def _():
        pass_p(1)

    @pl.when(j == 2)
    def _():
        pass_p(3)

    pool_swap.wait_recv()
    transpose_into(psib, ROWS)
    far_units(1, 1 - yh)

    def ready(k):
        xb[k] = normalize(xbuf[k].astype(F32))[0].astype(BF16)

    @pl.when(inner)
    def _():
        for k in range(1, 4):
            ready(k)

    assemble(4, theirs)
    for n, off in ((5, 3), (6, 1), (7, 2)):
        assemble(n, chip(1 - yh, off))

    temper = jnp.exp(jnp.full((1, 1), log_scale[0], F32))
    offset = jnp.full((1, 1), bias[0], F32)
    gain = temper * (1.0 / ROWS)

    def project(block, out):
        for start in range(0, WIDTH, 512):
            cols = pl.ds(start, min(512, WIDTH - start))
            out[:, cols] = jnp.dot(block, wf[:, cols], preferred_element_type=F32) + hb[:, cols]

    def weights(a, b, own):
        l = temper * lax.dot_general(a, b, NT, preferred_element_type=F32) + offset
        if own:
            eye = lax.broadcasted_iota(jnp.int32, l.shape, 0) == lax.broadcasted_iota(jnp.int32, l.shape, 1)
            l = jnp.where(eye, -l, l)
        g = gain / (1.0 + jnp.exp(-l))
        if own:
            g = jnp.where(eye, -g, g)
        return l, g.astype(BF16)

    def losses(m):
        e = jnp.maximum(m, 0.0) + jnp.log1p(jnp.exp(-jnp.abs(m)))
        total = e[:, :ROWS]
        for start in range(ROWS, m.shape[1], ROWS):
            total = total + e[:, start:start + ROWS]
        return jnp.sum(total.T, axis=0, keepdims=True)

    def image_side(d, row):
        loss_out[...] = row * (1.0 / ROWS)
        v = ximg[...]
        img_out[...] = (xr * (d - v * jnp.sum(v * d, axis=-1, keepdims=True))).astype(BF16)

    project(pool[...], ztxt)
    v, zr = normalize(ztxt[...])
    ztxt[...] = v
    zb[0] = v.astype(BF16)

    def text_grad(a, own):
        _, g = weights(zb[0], a, own)
        return jnp.dot(g, a, preferred_element_type=F32)

    def text_side(d):
        v = ztxt[...]
        dzb[:ROWS] = (zr * (d - v * jnp.sum(v * d, axis=-1, keepdims=True))).astype(BF16)

    @pl.when(inner)
    def _():
        text_side(text_grad(xb[0:4].reshape(4 * ROWS, WIDTH), True))

    @pl.when(outer)
    def _():
        for k in (xk0, xk1):
            wait_x(k, 0)
            wait_x(k, 1)
            ready(k)
        u[:ROWS] = text_grad(xb[0], True) + text_grad(xb[xk0], False) + text_grad(xb[xk1], False)
        wait_x(xk2, 0)
        wait_x(xk2, 1)
        ready(xk2)
        text_side(u[:ROWS] + text_grad(xb[xk2], False))

    pair = copy(dzb.at[:ROWS], dzb.at[ROWS:], h_s.at[3], h_r.at[3], sib)
    pair.start()

    def make(n):
        t = jnp.dot(pt[SHARD * n:SHARD * (n + 2), :], dzb[...], preferred_element_type=F32)
        terms[n] = t[:SHARD]
        terms[n + 1] = t[SHARD:]

    def cols(n, q):
        start, size, _ = PIECES[q]
        return terms[n, :, start:start + size]

    g_sent = []

    def g_go(src, value, ident, dst, who):
        src[...] = value.astype(BF16)
        d = copy(src, dst, g_s.at[ident], g_r.at[ident], who)
        d.start()
        g_sent.append(d)

    def g_wait(ref, ident):
        copy(ref, ref, g_s.at[ident], g_r.at[ident], xp).wait_recv()
        return ref[...].astype(F32)

    def slot(refs, q, *index):
        return refs[q].at[index] if index else refs[q]

    def far_sends(g):
        for q, (_, _, way) in enumerate(PIECES):
            g_go(slot(g_out, q, g, 0), cols(4 * g, q), 12 * g + q, slot(g_far, q, g), xp if way > 0 else xm)

    def near_sends(g):
        for q, (_, _, way) in enumerate(PIECES):
            n, who = (2, xm) if way > 0 else (1, xp)
            g_go(slot(g_out, q, g, 1), cols(4 * g + n, q), 12 * g + 4 + q, slot(g_near, q, g, 0), who)

    def second_sends(g):
        for q, (_, _, way) in enumerate(PIECES):
            n, who = (1, xp) if way > 0 else (2, xm)
            value = cols(4 * g + n, q) + g_wait(slot(g_far, q, g), 12 * g + q)
            g_go(slot(g_out, q, g, 2), value, 12 * g + 8 + q, slot(g_near, q, g, 1), who)

    def total(g, q):
        value = cols(4 * g + 3, q) + g_wait(slot(g_near, q, g, 0), 12 * g + 4 + q)
        return value + g_wait(slot(g_near, q, g, 1), 12 * g + 8 + q)

    def back():
        @pl.loop(0, WIDTH // TILE)
        def _(n):
            cols = pl.ds(pl.multiple_of(n * TILE, TILE), TILE)
            pool_out[:, cols] = lax.dot_general(
                dzb[:ROWS], wf[cols, :], NT, preferred_element_type=F32
            ).astype(BF16)

    gdx_up = [copy(part(gdx_out, h), part(gdx_in, h), h_s.at[4 * h], h_r.at[4 * h], up) for h in range(2)]
    gdx_dn = [copy(part(gdx_out, h), part(gdx_in, h), h_s.at[4 * h], h_r.at[4 * h], dn) for h in range(2)]
    gsum_up = copy(gsum_out, gsum_in, h_s.at[1], h_r.at[1], up)
    gsum_dn = copy(gsum_out, gsum_in, h_s.at[1], h_r.at[1], dn)

    @pl.when(outer)
    def _():
        m, g = weights(xb[0], zb[0], True)
        u[ROWS:2 * ROWS] = jnp.dot(g, zb[0], preferred_element_type=F32)
        loss_out[...] = losses(m)

    def texts_done(first, last):
        for n in range(first, last):
            v = u[ROWS * (n - 1):ROWS * n]
            zb[n] = normalize(v)[0].astype(BF16)

    def meet(image, texts, own):
        m, g = weights(image, texts, own)
        return jnp.dot(g, texts, preferred_element_type=F32), losses(m)

    @pl.when(inner)
    def _():
        back()

    pair.wait_recv()
    make(0)
    far_sends(0)
    make(2)
    near_sends(0)

    @pl.when(j == 1)
    def _():
        for h in range(2):
            wait_p(3, h)
            wait_p(4, h)

    @pl.when(j == 2)
    def _():
        for h in range(2):
            wait_p(1, h)

    @pl.when(inner)
    def _():
        project(pbuf[0:3].reshape(3 * ROWS, WIDTH), u.at[:3 * ROWS])

    @pl.when(outer)
    def _():
        make(4)
        make(6)
        back()

    second_sends(0)

    @pl.when(inner)
    def _():
        make(4)
        make(6)

    far_sends(1)
    near_sends(1)

    @pl.when(j == 1)
    def _():
        wait_x(5, 0, whole=True)
        ready(5)

    @pl.when(inner)
    def _():
        texts_done(1, 4)
        d, row = meet(xb[9 - 4 * j], zb[pl.ds(4 - 2 * j, 2)].reshape(2 * ROWS, WIDTH), False)
        gdx[...] = d
        gsum_out[...] = row

    for q, (_, _, way) in enumerate(PIECES):
        g_go(slot(y_out, q), total(0, q), 24 + q, slot(y_pass, q), y_up if way > 0 else y_dn)

    onward = [
        copy(slot(y_pass, q), slot(y_in, q), g_s.at[28 + q], g_r.at[28 + q], y_up if way > 0 else y_dn)
        for q, (_, _, way) in enumerate(PIECES)
    ]

    def relay():
        for q in range(4):
            copy(slot(y_pass, q), slot(y_pass, q), g_s.at[24 + q], g_r.at[24 + q], xp).wait_recv()
            onward[q].start()

    second_sends(1)

    @pl.when(inner)
    def _():
        for h in range(2):
            wait_p(2, h)
        project(pbuf[3], u.at[3 * ROWS:])
        texts_done(4, 5)
        d, row = meet(xb[9 - 4 * j], zb[4], False)
        gdx_out[...] = (gdx[...] + d).astype(BF16)
        gsum_out[...] += row

    @pl.when(j == 1)
    def _():
        gsum_dn.start()
        gdx_dn[0].start()

    @pl.when(j == 2)
    def _():
        gsum_up.start()
        gdx_up[0].start()

    relay()

    @pl.when(j == 1)
    def _():
        gdx_dn[1].start()

    @pl.when(j == 2)
    def _():
        gdx_up[1].start()

    @pl.when(inner)
    def _():
        d, row = meet(xb[0], zb[0:3].reshape(3 * ROWS, WIDTH), True)
        e, more = meet(xb[0], zb[4], False)
        image_side(d + e, row + more)

    for d in w_sent:
        d.wait_send()

    @pl.when(j == 3)
    def _():
        for d in edge_up:
            d.wait_send()

    @pl.when(j == 0)
    def _():
        for d in edge_dn:
            d.wait_send()

    @pl.when(outer)
    def _():
        for d in edge_far:
            d.wait_send()

    @pl.when(j <= 2)
    def _():
        for d in x_hop + hop_up:
            d.wait_send()

    @pl.when(j >= 1)
    def _():
        for d in p_hop:
            d.wait_send()

    @pl.when(j == 0)
    def _():
        guest.wait_send()

    x_done(0, img)
    p_done(0, pool)
    for k in range(1, 4):
        x_done(k, xbuf.at[k])
        p_done(k, pbuf.at[0])
    p_done(4, pbuf.at[0])
    pool_swap.wait_send()
    pair.wait_send()
    for d in g_sent[:24]:
        d.wait_send()


    for q, (start, size, _) in enumerate(PIECES):
        head_out[:, start:start + size] = total(1, q)

    @pl.when(outer)
    def _():
        gsum_up.wait_recv()
        gdx_up[0].wait_recv()
        gdx_up[1].wait_recv()
        image_side(u[ROWS:2 * ROWS] + gdx_in[...].astype(F32), loss_out[...] + gsum_in[...])

    for q, (start, size, _) in enumerate(PIECES):
        head_out[:, start:start + size] += g_wait(slot(y_in, q), 28 + q)

    @pl.when(inner)
    def _():
        gdx_up[0].wait_send()
        gdx_up[1].wait_send()
        gsum_up.wait_send()

    for d in g_sent[24:] + onward:
        d.wait_send()


def finish(*refs):
    moves = [pltpu.make_async_copy(refs[i], refs[4 + i], refs[8].at[i]) for i in range(4)]
    for d in moves:
        d.start()
    for d in moves:
        d.wait()


def per_device(images, pooled, head_weight, head_bias, log_scale, bias):
    smem = pl.BlockSpec(memory_space=pltpu.SMEM)
    vmem = pl.BlockSpec(memory_space=pltpu.VMEM)
    hbm = pl.BlockSpec(memory_space=pltpu.HBM)
    block = (ROWS, WIDTH)
    slab = (SHARD, WIDTH)
    parts = [(SHARD, size) for _, size, _ in PIECES]
    dma = pltpu.SemaphoreType.DMA
    results = (
        jax.ShapeDtypeStruct((1, ROWS), F32),
        jax.ShapeDtypeStruct(block, BF16),
        jax.ShapeDtypeStruct(block, BF16),
        jax.ShapeDtypeStruct(slab, F32),
    )
    made = pl.pallas_call(
        kernel,
        out_shape=results,
        in_specs=[hbm, hbm, hbm, hbm, smem, smem],
        out_specs=(vmem,) * 4,
        scratch_shapes=[
            pltpu.VMEM(block, BF16),
            pltpu.VMEM(block, BF16),
            pltpu.VMEM((1, WIDTH), F32),
            pltpu.VMEM((2, 8, SHARD, FIRST), BF16),
            pltpu.VMEM((2, 8, SHARD, WIDTH - FIRST), BF16),
            pltpu.VMEM((WIDTH, WIDTH), BF16),
            pltpu.VMEM((6,) + block, BF16),
            pltpu.VMEM((4,) + block, BF16),
            pltpu.VMEM((6,) + block, BF16),
            pltpu.VMEM((5,) + block, BF16),
            pltpu.VMEM(block, F32),
            pltpu.VMEM(block, F32),
            pltpu.VMEM((4 * ROWS, WIDTH), F32),
            pltpu.VMEM((2 * ROWS, WIDTH), BF16),
            pltpu.VMEM(block, BF16),
            pltpu.VMEM((WIDTH, ROWS), F32),
            pltpu.VMEM((8 * SHARD, 2 * ROWS), BF16),
            pltpu.VMEM((8,) + slab, F32),
            [pltpu.VMEM((2, 3) + p, BF16) for p in parts],
            [pltpu.VMEM((2,) + p, BF16) for p in parts],
            [pltpu.VMEM((2, 2) + p, BF16) for p in parts],
            [pltpu.VMEM(p, BF16) for p in parts],
            [pltpu.VMEM(p, BF16) for p in parts],
            [pltpu.VMEM(p, BF16) for p in parts],
            pltpu.VMEM(block, F32),
            pltpu.VMEM(block, BF16),
            pltpu.VMEM((1, ROWS), F32),
            pltpu.VMEM(block, BF16),
            pltpu.VMEM((1, ROWS), F32),
            dma((5,)),
            dma((33,)), dma((33,)),
            dma((7, 4)), dma((6, 4)),
            dma((6, 2)), dma((5, 2)),
            dma((32,)), dma((32,)),
            dma((5,)), dma((5,)),
        ],
        compiler_params=pltpu.CompilerParams(
            collective_id=0, has_side_effects=True, vmem_limit_bytes=VMEM_GRANT
        ),
        cost_estimate=pl.CostEstimate(flops=4_000_000_000, bytes_accessed=6_000_000, transcendentals=300_000),
    )(*[pltpu.with_memory_space_constraint(v, pltpu.HBM) for v in (images, pooled, head_weight, head_bias)], log_scale, bias)
    loss, image_grad, pooled_grad, head_grad = pl.pallas_call(
        finish,
        out_shape=results,
        in_specs=[vmem] * 4,
        out_specs=(hbm,) * 4,
        scratch_shapes=[dma((4,))],
        compiler_params=pltpu.CompilerParams(vmem_limit_bytes=4 * 1024 * 1024),
    )(*made)
    return loss.reshape(ROWS), image_grad, pooled_grad, head_grad


def solution(mesh):
    in_specs = (P(("dp", "fsdp"), None), P(("dp", "fsdp"), None), P("fsdp", None), P(), P(), P())
    out_specs = (
        P(("dp", "fsdp")),
        P(("dp", "fsdp"), None),
        P(("dp", "fsdp"), None),
        P(("dp", "fsdp"), None),
    )
    return jax.shard_map(
        per_device, mesh=mesh, in_specs=in_specs, out_specs=out_specs, check_vma=False
    )
```

```python
import jax
import jax.numpy as jnp
from jax import lax
from jax.experimental import pallas as pl
from jax.experimental.pallas import tpu as pltpu
from jax.sharding import PartitionSpec as P

MESH = pl.DeviceIdType.MESH
F32 = jnp.float32
BF16 = jnp.bfloat16
NT = (((1,), (1,)), ((), ()))

ROWS = 128
WIDTH = 1152
SHARD = 72
CHIP = 144
FIRST = 640
TILE = 384
VMEM_GRANT = 44 * 1024 * 1024
HALF = 64
PIECES = ((0, 384, 1), (640, 256, -1), (384, 256, 1), (896, 256, -1))
PLACE = {1: 0, 3: 1, 4: 2, 2: 3}
ORDER = (2, 1, 3, 0)


def normalize(v):
    r = lax.rsqrt(jnp.sum(v * v, axis=-1, keepdims=True) + 1e-06)
    return v * r, r


def kernel(
    img_hbm, pool_hbm, wsh_hbm, hb_hbm, log_scale, bias,
    loss_out, img_out, pool_out, head_out,
    img, pool, hb,
    wa, wb, wf, xbuf, pbuf, xb, zb, ximg, ztxt, u, dzb, psib, ptf, pt, terms,
    g_out, g_far, g_near,
    y_out, y_pass, y_in,
    gdx, gdx_out, gsum_out, gdx_in, gsum_in,
    l_s, w_s, w_r, x_s, x_r, p_s, p_r, g_s, g_r, h_s, h_r,
):
    dp = lax.axis_index("dp")
    f = lax.axis_index("fsdp")
    j = lax.rem(dp, 4)
    yh = lax.div(f, 8)
    x = lax.rem(lax.div(f, 2), 4)
    c = lax.rem(f, 2)
    base = yh * 8 + c

    sib = (dp, f + 1 - 2 * c)
    xp = (dp, base + 2 * lax.rem(x + 1, 4))
    xm = (dp, base + 2 * lax.rem(x + 3, 4))
    zp = (lax.rem(dp + 4, 32), f)
    zm = (lax.rem(dp + 28, 32), f)
    wrap_up = lax.div(j + 1, 4)
    up = (dp + 1 - 4 * wrap_up, lax.rem(f + 8 * wrap_up, 16))
    wrap_dn = lax.div(3 - j, 3)
    dn = (dp - 1 + 4 * wrap_dn, lax.rem(f + 8 * wrap_dn, 16))
    odd = lax.rem(j, 2)
    step = 3 - 2 * odd
    wrap = lax.div(j + step, 4)
    y_up = (dp + step - 4 * wrap, lax.rem(f + 8 * wrap, 16))
    step = 1 + 2 * odd
    wrap = lax.div(3 - j, 2)
    y_dn = (dp - step + 4 * wrap, lax.rem(f + 8 * wrap, 16))

    across = (dp - j + lax.rem(j + 2, 4), lax.rem(f + 8, 16))
    mine = yh * 4 + x
    theirs = 4 - yh * 4 + x

    loads = [
        pltpu.make_async_copy(src, dst, l_s.at[i])
        for i, (src, dst) in enumerate(
            (
                (wsh_hbm.at[:, :FIRST], wa.at[c, mine]),
                (wsh_hbm.at[:, FIRST:], wb.at[c, mine]),
                (img_hbm, img),
                (pool_hbm, pool),
                (hb_hbm, hb.at[0]),
            )
        )
    ]
    for d in loads:
        d.start()

    barrier = pltpu.get_barrier_semaphore()
    for who in (sib, xp, xm, zp, zm, up, dn, across):
        pl.semaphore_signal(barrier, inc=1, device_id=who, device_id_type=MESH)

    @pl.when(odd == 0)
    def _():
        pl.semaphore_signal(barrier, inc=1, device_id=y_up, device_id_type=MESH)

    @pl.when(odd == 1)
    def _():
        pl.semaphore_signal(barrier, inc=1, device_id=y_dn, device_id_type=MESH)

    pl.semaphore_wait(barrier, 9)
    for d in loads:
        d.wait()

    def copy(src, dst, send, recv, who):
        return pltpu.make_async_remote_copy(
            src_ref=src, dst_ref=dst, send_sem=send, recv_sem=recv, device_id=who, device_id_type=MESH
        )

    def part(ref, h):
        return ref.at[pl.ds(HALF * h, HALF), :]

    def send_x(k, src, h):
        @pl.when(jnp.logical_and(k <= 3 - j, j >= 1))
        def _():
            copy(part(src, h), part(xbuf.at[k + 1], h), x_s.at[k, h], x_r.at[k + 1, h], dn).start()

        @pl.when(jnp.logical_and(k > 3 - j, j <= 2))
        def _():
            copy(part(src, h), part(xbuf.at[k - 1], h), x_s.at[k, h], x_r.at[k - 1, h], up).start()

    def send_p(k, src, h):
        if k < 4:
          @pl.when(jnp.logical_and(k <= j, j <= 1))
          def _():
            copy(part(src, h), part(pbuf.at[PLACE[k + 1]], h), p_s.at[k, h], p_r.at[k + 1, h], up).start()

        if k > 2:
          @pl.when(jnp.logical_and(k > j, j >= 2))
          def _():
            copy(part(src, h), part(pbuf.at[PLACE[k - 1]], h), p_s.at[k, h], p_r.at[k - 1, h], dn).start()

    def wait_x(k, h, whole=False):
        dst = xbuf.at[k] if whole else part(xbuf.at[k], h)
        copy(dst, dst, x_s.at[k, h], x_r.at[k, h], up).wait_recv()

    def quarter(k, q):
        return xbuf.at[k, pl.ds(HALF // 2 * q, HALF // 2), :]

    hop_in = [copy(quarter(4, q), quarter(4, q), x_s.at[5, q], x_r.at[4, q], zm) for q in range(4)]
    hop_up = [copy(quarter(4, q), quarter(3, q), x_s.at[4, q], x_r.at[3, q // 2], up) for q in range(4)]

    def wait_p(k, h):
        dst = part(pbuf.at[PLACE[k]], h)
        copy(dst, dst, p_s.at[k, h], p_r.at[k, h], up).wait_recv()

    def pass_x(k, h):
        wait_x(k, h)
        send_x(k, xbuf.at[k], h)

    def pass_p(k):
        for h in range(2):
            wait_p(k, h)
            send_p(k, pbuf.at[PLACE[k]], h)

    def x_done(k, src):
        @pl.when(jnp.logical_or(jnp.logical_and(k <= 3 - j, j >= 1), jnp.logical_and(k > 3 - j, j <= 2)))
        def _():
            for h in range(2):
                copy(part(src, h), part(xbuf.at[1], h), x_s.at[k, h], x_r.at[1, h], up).wait_send()

    def p_done(k, src):
        @pl.when(jnp.logical_or(jnp.logical_and(k <= j, j <= 1), jnp.logical_and(k > j, j >= 2)))
        def _():
            for h in range(2):
                copy(part(src, h), part(pbuf.at[0], h), p_s.at[k, h], p_r.at[1, h], up).wait_send()

    middle = lax.rem(lax.div(j + 1, 2), 2)
    outer = middle == 0
    inner = middle == 1
    xk0 = 1 + 2 * lax.div(j, 3)
    xk1 = 2 + middle
    xk2 = 6 - xk0 - xk1
    guest = copy(img, xbuf.at[5], x_s.at[6, 0], x_r.at[5, 0], up)

    pool_swap = copy(pool, psib, h_s.at[2], h_r.at[2], sib)
    x_hop = [
        copy(img.at[pl.ds(HALF // 2 * q, HALF // 2), :], quarter(4, q), x_s.at[5, q], x_r.at[4, q], zm)
        for q in range(4)
    ]
    p_hop = [copy(part(pool, h), part(pbuf.at[PLACE[4]], h), p_s.at[5, h], p_r.at[4, h], zp) for h in range(2)]

    @pl.when(j <= 2)
    def _():
        for d in x_hop:
            d.start()

    send_x(0, img, 0)
    send_x(0, img, 1)

    def chip(h, off):
        return h * 4 + lax.rem(x + off, 4)

    def piece(m, p):
        return (wa if p == 0 else wb).at[c, m]

    def w_copy(src, dst, ident, who, send=None):
        return copy(src, dst, w_s.at[ident if send is None else send], w_r.at[ident], who)

    w_sent = []

    def w_go(src, ident, who):
        d = w_copy(src, src, ident, who)
        d.start()
        w_sent.append(d)

    def to_sibling(n, m, p):
        w_go(piece(m, p), 17 + 2 * n + p, sib)

    def assemble(n, m):
        for p in range(2):
            src = (wa if p == 0 else wb).at[1 - c, m]
            w_copy(src, src, 17 + 2 * n + p, sib).wait_recv()
        rows = pl.ds(pl.multiple_of(m * CHIP, 16), CHIP)
        for ref, cols in ((wa, slice(0, FIRST)), (wb, slice(FIRST, WIDTH))):
            wf[rows, cols] = jnp.concatenate(
                [ref[0, m].astype(F32), ref[1, m].astype(F32)], axis=0
            ).astype(BF16)

    edge_up = [w_copy(piece(mine, p), piece(mine, p), 13 + p, up) for p in range(2)]
    edge_dn = [w_copy(piece(mine, p), piece(mine, p), 13 + p, dn) for p in range(2)]
    edge_far = [w_copy(piece(mine, p), piece(mine, p), 13 + p, across, 15 + p) for p in range(2)]

    @pl.when(j == 3)
    def _():
        for d in edge_up:
            d.start()

    @pl.when(j == 0)
    def _():
        for d in edge_dn:
            d.start()

    @pl.when(outer)
    def _():
        for d in edge_far:
            d.start()

    def along_x(r, m):
        return {
            (d, p): w_copy(piece(m, p), piece(m, p), 1 + 4 * r + 2 * d + p, xp if d == 0 else xm)
            for d in range(2)
            for p in range(2)
        }

    mine_x = along_x(0, mine)
    theirs_x = along_x(1, theirs)
    for key in ((0, 0), (1, 1), (0, 1), (1, 0)):
        mine_x[key].start()
    w_sent.extend(mine_x.values())
    w_sent.extend(theirs_x.values())
    to_sibling(0, mine, 0)
    to_sibling(0, mine, 1)
    pool_swap.start()

    @pl.when(j == 1)
    def _():
        send_p(0, pool, 0)

    @pl.when(j >= 1)
    def _():
        for d in p_hop:
            d.start()

    v, xr = normalize(img[...].astype(F32))
    ximg[...] = v
    xb[0] = v.astype(BF16)

    def slab_rows(n):
        m = chip(1 - yh if n < 4 else yh, ORDER[n % 4])
        return ptf[pl.ds(pl.multiple_of(m * CHIP + SHARD * c, 8), SHARD), :]

    def transpose_into(ref, start):
        ptf[...] = ref[...].astype(F32).T
        for n in range(0, 8, 2):
            pt[SHARD * n:SHARD * (n + 2), start:start + ROWS] = jnp.concatenate(
                [slab_rows(n), slab_rows(n + 1)], axis=0
            ).astype(BF16)

    def near_first(r, h):
        for d, (off, onward) in enumerate(((3, xp), (1, xm))):
            got = piece(chip(h, off), d)
            w_copy(got, got, 1 + 4 * r + 3 * d, xp).wait_recv()
            w_go(got, 9 + 2 * r + d, onward)
            to_sibling(1 + 4 * r + d, chip(h, off), d)

    def near_rest(r, h):
        for d, off in enumerate((3, 1)):
            m = chip(h, off)
            got = piece(m, 1 - d)
            w_copy(got, got, 2 + 4 * r + d, xp).wait_recv()
            to_sibling(1 + 4 * r + d, m, 1 - d)

    def far_units(r, h):
        m = chip(h, 2)
        for p in range(2):
            w_copy(piece(m, p), piece(m, p), 9 + 2 * r + p, xp).wait_recv()
            to_sibling(3 + 4 * r, m, p)

    edge_in = [w_copy(piece(theirs, p), piece(theirs, p), 13 + p, xp) for p in range(2)]

    def theirs_first():
        edge_in[0].wait_recv()
        theirs_x[0, 0].start()
        theirs_sib[0].start()

    def theirs_rest():
        edge_in[1].wait_recv()
        for key in ((1, 1), (0, 1), (1, 0)):
            theirs_x[key].start()
        theirs_sib[1].start()

    theirs_sib = [w_copy(piece(theirs, p), piece(theirs, p), 25 + p, sib) for p in range(2)]
    w_sent.extend(theirs_sib)

    def hop_on(h):
        @pl.when(j <= 2)
        def _():
            for q in (2 * h, 2 * h + 1):
                hop_in[q].wait_recv()
                hop_up[q].start()

        @pl.when(inner)
        def _():
            pass_x(1, h)

    hop_on(0)
    transpose_into(pool, 0)

    @pl.when(outer)
    def _():
        theirs_first()

    near_first(0, yh)

    @pl.when(outer)
    def _():
        theirs_rest()

    hop_on(1)
    near_rest(0, yh)
    pool_swap.wait_recv()
    transpose_into(psib, ROWS)

    @pl.when(j == 0)
    def _():
        send_p(0, pool, 0)
        send_p(0, pool, 1)
        guest.start()

    @pl.when(j == 3)
    def _():
        pass_p(4)

    @pl.when(inner)
    def _():
        pass_x(3, 0)
        theirs_first()

    far_units(0, yh)
    assemble(0, mine)

    @pl.when(inner)
    def _():
        pass_x(3, 1)
        theirs_rest()
        pass_x(2, 0)

    @pl.when(j == 2)
    def _():
        pass_p(4)

    @pl.when(j == 1)
    def _():
        pass_x(2, 1)

    near_first(1, 1 - yh)
    for n, off in ((1, 3), (2, 1), (3, 2)):
        assemble(n, chip(yh, off))

    @pl.when(j == 2)
    def _():
        pass_x(2, 1)

    @pl.when(j == 1)
    def _():
        send_p(0, pool, 1)

    near_rest(1, 1 - yh)

    @pl.when(j == 1)
    def _():
        pass_p(1)

    @pl.when(j == 2)
    def _():
        pass_p(3)

    far_units(1, 1 - yh)

    def ready(k):
        xb[k] = normalize(xbuf[k].astype(F32))[0].astype(BF16)

    @pl.when(inner)
    def _():
        for k in range(1, 4):
            ready(k)

    assemble(4, theirs)
    for n, off in ((5, 3), (6, 1), (7, 2)):
        assemble(n, chip(1 - yh, off))

    temper = jnp.exp(jnp.full((1, 1), log_scale[0], F32))
    offset = jnp.full((1, 1), bias[0], F32)
    gain = temper * (1.0 / ROWS)

    def project(block, out):
        for start in range(0, WIDTH, 512):
            cols = pl.ds(start, min(512, WIDTH - start))
            out[:, cols] = jnp.dot(block, wf[:, cols], preferred_element_type=F32) + hb[:, cols]

    def weights(a, b, own):
        l = temper * lax.dot_general(a, b, NT, preferred_element_type=F32) + offset
        if own:
            eye = lax.broadcasted_iota(jnp.int32, l.shape, 0) == lax.broadcasted_iota(jnp.int32, l.shape, 1)
            l = jnp.where(eye, -l, l)
        g = gain / (1.0 + jnp.exp(-l))
        if own:
            g = jnp.where(eye, -g, g)
        return l, g.astype(BF16)

    def losses(m):
        e = jnp.maximum(m, 0.0) + jnp.log1p(jnp.exp(-jnp.abs(m)))
        total = e[:, :ROWS]
        for start in range(ROWS, m.shape[1], ROWS):
            total = total + e[:, start:start + ROWS]
        return jnp.sum(total.T, axis=0, keepdims=True)

    def image_side(d, row):
        loss_out[...] = row * (1.0 / ROWS)
        v = ximg[...]
        img_out[...] = (xr * (d - v * jnp.sum(v * d, axis=-1, keepdims=True))).astype(BF16)

    project(pool[...], ztxt)
    v, zr = normalize(ztxt[...])
    ztxt[...] = v
    zb[0] = v.astype(BF16)

    def text_grad(a, own):
        _, g = weights(zb[0], a, own)
        return jnp.dot(g, a, preferred_element_type=F32)

    def text_side(d):
        v = ztxt[...]
        dzb[:ROWS] = (zr * (d - v * jnp.sum(v * d, axis=-1, keepdims=True))).astype(BF16)

    @pl.when(inner)
    def _():
        text_side(text_grad(xb[0:4].reshape(4 * ROWS, WIDTH), True))

    @pl.when(outer)
    def _():
        for k in (xk0, xk1):
            wait_x(k, 0)
            wait_x(k, 1)
            ready(k)
        u[:ROWS] = text_grad(xb[0], True) + text_grad(xb[xk0], False) + text_grad(xb[xk1], False)
        wait_x(xk2, 0)
        wait_x(xk2, 1)
        ready(xk2)
        text_side(u[:ROWS] + text_grad(xb[xk2], False))

    pair = copy(dzb.at[:ROWS], dzb.at[ROWS:], h_s.at[3], h_r.at[3], sib)
    pair.start()

    def make(n):
        t = jnp.dot(pt[SHARD * n:SHARD * (n + 2), :], dzb[...], preferred_element_type=F32)
        terms[n] = t[:SHARD]
        terms[n + 1] = t[SHARD:]

    def cols(n, q):
        start, size, _ = PIECES[q]
        return terms[n, :, start:start + size]

    g_sent = []

    def g_go(src, value, ident, dst, who):
        src[...] = value.astype(BF16)
        d = copy(src, dst, g_s.at[ident], g_r.at[ident], who)
        d.start()
        g_sent.append(d)

    def g_wait(ref, ident):
        copy(ref, ref, g_s.at[ident], g_r.at[ident], xp).wait_recv()
        return ref[...].astype(F32)

    def slot(refs, q, *index):
        return refs[q].at[index] if index else refs[q]

    def far_sends(g):
        for q, (_, _, way) in enumerate(PIECES):
            g_go(slot(g_out, q, g, 0), cols(4 * g, q), 12 * g + q, slot(g_far, q, g), xp if way > 0 else xm)

    def near_sends(g):
        for q, (_, _, way) in enumerate(PIECES):
            n, who = (2, xm) if way > 0 else (1, xp)
            g_go(slot(g_out, q, g, 1), cols(4 * g + n, q), 12 * g + 4 + q, slot(g_near, q, g, 0), who)

    def second_sends(g):
        for q, (_, _, way) in enumerate(PIECES):
            n, who = (1, xp) if way > 0 else (2, xm)
            value = cols(4 * g + n, q) + g_wait(slot(g_far, q, g), 12 * g + q)
            g_go(slot(g_out, q, g, 2), value, 12 * g + 8 + q, slot(g_near, q, g, 1), who)

    def total(g, q):
        value = cols(4 * g + 3, q) + g_wait(slot(g_near, q, g, 0), 12 * g + 4 + q)
        return value + g_wait(slot(g_near, q, g, 1), 12 * g + 8 + q)

    def back():
        @pl.loop(0, WIDTH // TILE)
        def _(n):
            cols = pl.ds(pl.multiple_of(n * TILE, TILE), TILE)
            pool_out[:, cols] = lax.dot_general(
                dzb[:ROWS], wf[cols, :], NT, preferred_element_type=F32
            ).astype(BF16)

    gdx_up = [copy(part(gdx_out, h), part(gdx_in, h), h_s.at[4 * h], h_r.at[4 * h], up) for h in range(2)]
    gdx_dn = [copy(part(gdx_out, h), part(gdx_in, h), h_s.at[4 * h], h_r.at[4 * h], dn) for h in range(2)]
    gsum_up = copy(gsum_out, gsum_in, h_s.at[1], h_r.at[1], up)
    gsum_dn = copy(gsum_out, gsum_in, h_s.at[1], h_r.at[1], dn)

    @pl.when(outer)
    def _():
        m, g = weights(xb[0], zb[0], True)
        u[ROWS:2 * ROWS] = jnp.dot(g, zb[0], preferred_element_type=F32)
        loss_out[...] = losses(m)

    def texts_done(first, last):
        for n in range(first, last):
            v = u[ROWS * (n - 1):ROWS * n]
            zb[n] = normalize(v)[0].astype(BF16)

    def meet(image, texts, own):
        m, g = weights(image, texts, own)
        return jnp.dot(g, texts, preferred_element_type=F32), losses(m)

    @pl.when(inner)
    def _():
        back()

    pair.wait_recv()
    make(0)
    far_sends(0)
    make(2)
    near_sends(0)

    @pl.when(j == 1)
    def _():
        for h in range(2):
            wait_p(3, h)
            wait_p(4, h)

    @pl.when(j == 2)
    def _():
        for h in range(2):
            wait_p(1, h)

    @pl.when(inner)
    def _():
        project(pbuf[0:3].reshape(3 * ROWS, WIDTH), u.at[:3 * ROWS])

    @pl.when(outer)
    def _():
        make(4)
        make(6)
        back()

    second_sends(0)

    @pl.when(inner)
    def _():
        make(4)
        make(6)

    far_sends(1)
    near_sends(1)

    @pl.when(j == 1)
    def _():
        wait_x(5, 0, whole=True)
        ready(5)

    @pl.when(inner)
    def _():
        texts_done(1, 4)
        d, row = meet(xb[9 - 4 * j], zb[pl.ds(4 - 2 * j, 2)].reshape(2 * ROWS, WIDTH), False)
        gdx[...] = d
        gsum_out[...] = row

    for q, (_, _, way) in enumerate(PIECES):
        g_go(slot(y_out, q), total(0, q), 24 + q, slot(y_pass, q), y_up if way > 0 else y_dn)

    onward = [
        copy(slot(y_pass, q), slot(y_in, q), g_s.at[28 + q], g_r.at[28 + q], y_up if way > 0 else y_dn)
        for q, (_, _, way) in enumerate(PIECES)
    ]

    def relay():
        for q in range(4):
            copy(slot(y_pass, q), slot(y_pass, q), g_s.at[24 + q], g_r.at[24 + q], xp).wait_recv()
            onward[q].start()

    @pl.when(inner)
    def _():
        for h in range(2):
            wait_p(2, h)
        project(pbuf[3], u.at[3 * ROWS:])
        texts_done(4, 5)
        d, row = meet(xb[9 - 4 * j], zb[4], False)
        gdx_out[...] = (gdx[...] + d).astype(BF16)
        gsum_out[...] += row

    @pl.when(j == 1)
    def _():
        gsum_dn.start()
        gdx_dn[0].start()

    @pl.when(j == 2)
    def _():
        gsum_up.start()
        gdx_up[0].start()

    second_sends(1)
    relay()

    @pl.when(j == 1)
    def _():
        gdx_dn[1].start()

    @pl.when(j == 2)
    def _():
        gdx_up[1].start()

    @pl.when(inner)
    def _():
        d, row = meet(xb[0], zb[0:3].reshape(3 * ROWS, WIDTH), True)
        e, more = meet(xb[0], zb[4], False)
        image_side(d + e, row + more)

    for d in w_sent:
        d.wait_send()

    @pl.when(j == 3)
    def _():
        for d in edge_up:
            d.wait_send()

    @pl.when(j == 0)
    def _():
        for d in edge_dn:
            d.wait_send()

    @pl.when(outer)
    def _():
        for d in edge_far:
            d.wait_send()

    @pl.when(j <= 2)
    def _():
        for d in x_hop + hop_up:
            d.wait_send()

    @pl.when(j >= 1)
    def _():
        for d in p_hop:
            d.wait_send()

    @pl.when(j == 0)
    def _():
        guest.wait_send()

    x_done(0, img)
    p_done(0, pool)
    for k in range(1, 4):
        x_done(k, xbuf.at[k])
        p_done(k, pbuf.at[0])
    p_done(4, pbuf.at[0])
    pool_swap.wait_send()
    pair.wait_send()
    for d in g_sent[:24]:
        d.wait_send()


    for q, (start, size, _) in enumerate(PIECES):
        head_out[:, start:start + size] = total(1, q)

    @pl.when(outer)
    def _():
        gsum_up.wait_recv()
        gdx_up[0].wait_recv()
        gdx_up[1].wait_recv()
        image_side(u[ROWS:2 * ROWS] + gdx_in[...].astype(F32), loss_out[...] + gsum_in[...])

    for q, (start, size, _) in enumerate(PIECES):
        head_out[:, start:start + size] += g_wait(slot(y_in, q), 28 + q)

    @pl.when(inner)
    def _():
        gdx_up[0].wait_send()
        gdx_up[1].wait_send()
        gsum_up.wait_send()

    for d in g_sent[24:] + onward:
        d.wait_send()


def finish(*refs):
    moves = [pltpu.make_async_copy(refs[i], refs[4 + i], refs[8].at[i]) for i in range(4)]
    for d in moves:
        d.start()
    for d in moves:
        d.wait()


def per_device(images, pooled, head_weight, head_bias, log_scale, bias):
    smem = pl.BlockSpec(memory_space=pltpu.SMEM)
    vmem = pl.BlockSpec(memory_space=pltpu.VMEM)
    hbm = pl.BlockSpec(memory_space=pltpu.HBM)
    block = (ROWS, WIDTH)
    slab = (SHARD, WIDTH)
    parts = [(SHARD, size) for _, size, _ in PIECES]
    dma = pltpu.SemaphoreType.DMA
    results = (
        jax.ShapeDtypeStruct((1, ROWS), F32),
        jax.ShapeDtypeStruct(block, BF16),
        jax.ShapeDtypeStruct(block, BF16),
        jax.ShapeDtypeStruct(slab, F32),
    )
    made = pl.pallas_call(
        kernel,
        out_shape=results,
        in_specs=[hbm, hbm, hbm, hbm, smem, smem],
        out_specs=(vmem,) * 4,
        scratch_shapes=[
            pltpu.VMEM(block, BF16),
            pltpu.VMEM(block, BF16),
            pltpu.VMEM((1, WIDTH), F32),
            pltpu.VMEM((2, 8, SHARD, FIRST), BF16),
            pltpu.VMEM((2, 8, SHARD, WIDTH - FIRST), BF16),
            pltpu.VMEM((WIDTH, WIDTH), BF16),
            pltpu.VMEM((6,) + block, BF16),
            pltpu.VMEM((4,) + block, BF16),
            pltpu.VMEM((6,) + block, BF16),
            pltpu.VMEM((5,) + block, BF16),
            pltpu.VMEM(block, F32),
            pltpu.VMEM(block, F32),
            pltpu.VMEM((4 * ROWS, WIDTH), F32),
            pltpu.VMEM((2 * ROWS, WIDTH), BF16),
            pltpu.VMEM(block, BF16),
            pltpu.VMEM((WIDTH, ROWS), F32),
            pltpu.VMEM((8 * SHARD, 2 * ROWS), BF16),
            pltpu.VMEM((8,) + slab, F32),
            [pltpu.VMEM((2, 3) + p, BF16) for p in parts],
            [pltpu.VMEM((2,) + p, BF16) for p in parts],
            [pltpu.VMEM((2, 2) + p, BF16) for p in parts],
            [pltpu.VMEM(p, BF16) for p in parts],
            [pltpu.VMEM(p, BF16) for p in parts],
            [pltpu.VMEM(p, BF16) for p in parts],
            pltpu.VMEM(block, F32),
            pltpu.VMEM(block, BF16),
            pltpu.VMEM((1, ROWS), F32),
            pltpu.VMEM(block, BF16),
            pltpu.VMEM((1, ROWS), F32),
            dma((5,)),
            dma((33,)), dma((33,)),
            dma((7, 4)), dma((6, 4)),
            dma((6, 2)), dma((5, 2)),
            dma((32,)), dma((32,)),
            dma((5,)), dma((5,)),
        ],
        compiler_params=pltpu.CompilerParams(
            collective_id=0, has_side_effects=True, vmem_limit_bytes=VMEM_GRANT
        ),
        cost_estimate=pl.CostEstimate(flops=4_000_000_000, bytes_accessed=6_000_000, transcendentals=300_000),
    )(*[pltpu.with_memory_space_constraint(v, pltpu.HBM) for v in (images, pooled, head_weight, head_bias)], log_scale, bias)
    loss, image_grad, pooled_grad, head_grad = pl.pallas_call(
        finish,
        out_shape=results,
        in_specs=[vmem] * 4,
        out_specs=(hbm,) * 4,
        scratch_shapes=[dma((4,))],
        compiler_params=pltpu.CompilerParams(vmem_limit_bytes=4 * 1024 * 1024),
    )(*made)
    return loss.reshape(ROWS), image_grad, pooled_grad, head_grad


def solution(mesh):
    in_specs = (P(("dp", "fsdp"), None), P(("dp", "fsdp"), None), P("fsdp", None), P(), P(), P())
    out_specs = (
        P(("dp", "fsdp")),
        P(("dp", "fsdp"), None),
        P(("dp", "fsdp"), None),
        P(("dp", "fsdp"), None),
    )
    return jax.shard_map(
        per_device, mesh=mesh, in_specs=in_specs, out_specs=out_specs, check_vma=False
    )
```
